32 devices in a mesh: tok: 4 (over y, x), vocab: 8 (over z, core).
Axes of the slice: x: 2, y: 2, z: 4, core: 2. Of those that a mesh axis runs over, the one named last changes fastest.
Arguments:
- teacher_logits: bfloat16 [512, 32768], P('tok', 'vocab'), may hold values from -18 to 240
- hidden: bfloat16 [512, 4608], P('tok'), may hold values from -6 to 6
- new_head: bfloat16 [4608, 32768], P(None, ('tok', 'vocab')), may hold values from -0.26516504 to 0.26516504
- labels: int32 [512], replicated, may hold values from 0 to 32767
- map_target: int32 [256, 4], P('vocab'), may hold values from 0 to 255, as said below
- map_weight: bfloat16 [256, 4, 128, 128], P('vocab'), may hold values from 0 to 0.017578125, as said below
Outputs:
- loss: float32 [512], P('tok')
- head_grad: bfloat16 [4608, 32768], P(None, ('tok', 'vocab'))
The draws below stay inside these ranges and needn't reach their ends.
Inputs may be any that keep to these rules, and one draw needn't show every extreme that they name: `map_target`: values are ids of new blocks; new block b belongs to the device at index b // 8 of tok and vocab together, tok first. Of the 128 entries of one vocab index, at most 8 belong to one device, and some device gets exactly 8. `map_weight`: entries are non-negative.
All inputs are finite; a program needn't handle non-finite values.
Results may differ from the reference program's by a relative error of at most 0.001.
The reference program's roundings to bfloat16 on the way count: a program that leaves them out, or rounds other values in their place, can miss the bound.
Values may be sent and summed in bfloat16 or wider, within the bound.
No kernel may reach another device: no remote copies, remote signals or barrier semaphores. Data moves between devices by JAX's collectives and lax.ppermute only.
A program may use at most 128 MiB of HBM per device.

```python
import math
import jax
import jax.numpy as jnp
import numpy as np
from jax import lax

D = 4608
VN_DEV = 1024
BLK = 128
FAN = 4
TOKENS = 512
V_OLD = 32768
V_NEW = 32768
OLD_BLOCKS = 32
OB_ALL = 256
NEW_BLOCKS = 256
CAP = 8
N_TOK = 4
N_VOCAB = 8


def draw_hidden(key, part):
    key = jax.random.fold_in(key, 11)
    rows = jnp.clip(jax.random.normal(jax.random.fold_in(key, 1), (TOKENS, D), jnp.float32), -6.0, 6.0)
    return rows.astype(jnp.bfloat16)


def draw_new_head(key, part):
    key = jax.random.fold_in(key, 12)
    spread = 3.0 * D ** (-0.5)
    weights = jnp.clip(jax.random.normal(jax.random.fold_in(key, 1), (D, V_NEW), jnp.float32), -6.0, 6.0) * spread
    return weights.astype(jnp.bfloat16)


def draw_teacher_logits(key, part):
    key = jax.random.fold_in(key, 13)
    values = jnp.clip(3.0 * jax.random.normal(jax.random.fold_in(key, 1), (TOKENS, V_OLD), jnp.float32), -18.0, 18.0)
    return values.astype(jnp.bfloat16)


def draw_map_weight(key, part):
    key = jax.random.fold_in(key, 14)
    uniform_part = jax.random.uniform(key, (OB_ALL, FAN, BLK, BLK), jnp.float32)
    diagonal = (jnp.arange(BLK)[:, None] == jnp.arange(BLK)[None, :]).astype(jnp.float32)
    return ((uniform_part + 8.0 * diagonal) * (1.0 / (FAN * BLK))).astype(jnp.bfloat16)


def shard_targets(key):
    entries = OLD_BLOCKS * FAN
    order = jax.random.permutation(jax.random.fold_in(key, 1), N_TOK * N_VOCAB)
    index = jnp.arange(entries, dtype=jnp.int32)
    groups = jnp.where(index < entries - 2, index // CAP, entries // CAP + index - (entries - 2))
    owners = order[groups]
    shuffle = jax.random.permutation(jax.random.fold_in(key, 2), entries)
    owners = owners[shuffle]
    within = jax.random.randint(jax.random.fold_in(key, 3), (entries,), 0, VN_DEV // BLK)
    return (owners * (VN_DEV // BLK) + within).astype(jnp.int32).reshape(OLD_BLOCKS, FAN)


def draw_map_target(key, part):
    key = jax.random.fold_in(key, 15)
    shard_keys = jax.vmap(lambda number: jax.random.fold_in(key, number))(jnp.arange(N_VOCAB))
    return jax.vmap(shard_targets)(shard_keys).reshape(OB_ALL, FAN)


def with_ends(values, own_key, smallest, largest):
    longest = values.shape.index(max(values.shape))
    spots = []
    for shift in (0, 1):
        where = [jax.random.randint(jax.random.fold_in(own_key, axis), (), 0, length) for axis, length in enumerate(values.shape)]
        where[longest] = (where[longest] + shift) % values.shape[longest]
        spots.append(tuple(where))
    return values.at[spots[0]].set(smallest).at[spots[1]].set(largest)


def rank_table(count, lean):
    portions = [(1 << 20) // math.isqrt(grade ** lean) + 1 for grade in range(1, count + 1)]
    scale = 1 + sum(portions) // (1 << 30)
    return np.cumsum(np.array([max(1, weight // scale) for weight in portions]))


def ranked_ids(rng, shape, amount, lean):
    table = rank_table(amount, lean)
    pick = jax.random.randint(jax.random.fold_in(rng, 1), shape, 0, int(table[amount - 1]))
    rank = jnp.searchsorted(jnp.asarray(table, jnp.int32), pick, side="right")
    return jax.random.permutation(jax.random.fold_in(rng, 2), amount)[rank].astype(jnp.int32)


def setup_inputs(seed: int = 0) -> dict:
    key_list = jax.random.split(jax.random.key(seed), 7)
    return {
        "teacher_logits": draw_teacher_logits(jax.random.fold_in(key_list[6], 71), 0),
        "hidden": draw_hidden(jax.random.fold_in(key_list[6], 71), 0),
        "new_head": draw_new_head(jax.random.fold_in(key_list[6], 71), 0),
        "labels": with_ends(ranked_ids(key_list[3], (TOKENS,), V_NEW, 2), jax.random.fold_in(key_list[3], 3), 0, V_NEW - 1).astype(jnp.int32),
        "map_target": draw_map_target(jax.random.fold_in(key_list[6], 71), 0),
        "map_weight": draw_map_weight(jax.random.fold_in(key_list[6], 71), 0),
    }


def reference(teacher_logits, hidden, new_head, labels, map_target, map_weight):
    scores = teacher_logits.astype(jnp.float32)
    highest = jnp.max(scores, axis=1, keepdims=True)
    raised = jnp.exp(scores - highest)
    teacher_prob = (raised / jnp.sum(raised, axis=1, keepdims=True)).astype(jnp.bfloat16)
    blocks = teacher_prob.reshape(TOKENS, OB_ALL, BLK).astype(jnp.float32)
    target = jnp.zeros((TOKENS, NEW_BLOCKS, BLK), jnp.float32)
    for column in range(FAN):
        mapped = jnp.einsum('tjb,jbc->tjc', blocks, map_weight[:, column].astype(jnp.float32))
        mapped = lax.optimization_barrier(mapped.astype(jnp.bfloat16)).astype(jnp.float32)
        target = target.at[:, map_target[:, column], :].add(mapped)
    target = target.reshape(TOKENS, V_NEW)
    logits = jnp.dot(hidden, new_head, preferred_element_type=jnp.float32)
    row_top = jnp.max(logits, axis=1)
    log_total = row_top + jnp.log(jnp.sum(jnp.exp(logits - row_top[:, None]), axis=1))
    target_mass = jnp.sum(target, axis=1)
    inner = jnp.sum(target * logits, axis=1)
    label_hit = jnp.arange(V_NEW, dtype=jnp.int32)[None, :] == labels[:, None]
    label_logit = jnp.sum(jnp.where(label_hit, logits, 0.0), axis=1)
    loss = target_mass * log_total - inner + log_total - label_logit
    probs = jnp.exp(logits - log_total[:, None])
    grad_logits = ((target_mass + 1.0)[:, None] * probs - target - label_hit.astype(jnp.float32)).astype(jnp.bfloat16)
    head_grad = lax.dot_general(hidden, grad_logits, (((0,), (0,)), ((), ())), preferred_element_type=jnp.float32)
    return loss, head_grad.astype(jnp.bfloat16)
```

```python
import functools

import jax
import jax.numpy as jnp
from jax import lax
from jax.experimental import pallas as pl
from jax.experimental.pallas import tpu as pltpu
from jax.sharding import PartitionSpec as P

F32 = jnp.float32
BF16 = jnp.bfloat16
LANES = 128
GROUP = 8
VMEM_LIMIT = 56 * 1024 * 1024


def rows_from_columns(columns):
    n = columns[0].shape[0]
    lane = lax.broadcasted_iota(jnp.int32, (n, LANES), 1)
    tile = jnp.zeros((n, LANES), F32)
    for place, column in enumerate(columns):
        tile = jnp.where(lane == place, column, tile)
    return tile.T[0:8, :]


def teacher_kernel(x_ref, stat_ref):
    rows, cols = x_ref.shape
    pieces = [x_ref[:, j : j + LANES].astype(F32) for j in range(0, cols, LANES)]
    top = jnp.max(functools.reduce(jnp.maximum, pieces), axis=1, keepdims=True)
    total = jnp.zeros((rows, LANES), F32)
    for j in range(0, cols, LANES):
        total = total + jnp.exp(x_ref[:, j : j + LANES].astype(F32) - top)
    stat_ref[...] = rows_from_columns([top, jnp.sum(total, axis=1, keepdims=True)])


def teacher_stats(x):
    vmem = pl.BlockSpec(memory_space=pltpu.VMEM)
    return pl.pallas_call(
        teacher_kernel,
        in_specs=[vmem],
        out_specs=vmem,
        out_shape=jax.ShapeDtypeStruct((8, x.shape[0]), F32),
        compiler_params=pltpu.CompilerParams(vmem_limit_bytes=VMEM_LIMIT),
        cost_estimate=pl.CostEstimate(flops=4 * x.size, bytes_accessed=2 * x.size, transcendentals=x.size),
        name="teacher_stats",
    )(x)


def contrib_kernel(
    core_ref, own_code, peer_code, stats_ref, x_own, x_peer, w_own, w_peer, out_ref, mass_ref, acc, probs, *, steps, fan
):
    chunk, step = pl.program_id(0), pl.program_id(1)
    blocks = x_own.shape[1] // LANES
    rows = x_own.shape[0]
    slots = out_ref.shape[0]

    @pl.when((chunk == 0) & (step == 0))
    def _():
        n_vocab = stats_ref.shape[0]
        row = lambda v, k: stats_ref[v, k : k + 1, :]
        top = functools.reduce(jnp.maximum, [row(v, 0) for v in range(n_vocab)])
        total = functools.reduce(jnp.add, [row(v, 1) * jnp.exp(row(v, 0) - top) for v in range(n_vocab)])
        columns = jnp.concatenate([top, total, jnp.zeros((LANES - 2, rows), F32)], axis=0).T
        top, total = columns[:, 0:1], columns[:, 1:2]
        for side, x in enumerate((x_own, x_peer)):
            for j in range(blocks):
                raised = jnp.exp(x[:, j * LANES : (j + 1) * LANES].astype(F32) - top)
                probs[side * blocks + j] = (raised / total).astype(BF16)

    @pl.when(step == 0)
    def _():
        acc[...] = jnp.zeros_like(acc)

    def add(code_ref, w_ref, first, offset):
        for jj in range(GROUP):
            piece = probs[offset + first + jj]
            for f in range(fan):
                code = code_ref[(first + jj) * fan + f]
                slot = lax.shift_right_logical(code, 1) - chunk * slots
                mine = ((code & 1) == core_ref[0]) & (slot >= 0) & (slot < slots)
                slot = jnp.where(mine, slot, slots)
                part = jnp.dot(piece, w_ref[jj, f], preferred_element_type=F32)
                acc[slot] += part.astype(BF16).astype(F32)

    @pl.when(step < steps)
    def _():
        add(own_code, w_own, step * GROUP, 0)

    @pl.when(step >= steps)
    def _():
        add(peer_code, w_peer, (step - steps) * GROUP, blocks)

    @pl.when(step == 2 * steps - 1)
    def _():
        def body(i, mass):
            block = acc[i]
            out_ref[i] = block.astype(BF16)
            return mass + block

        mass = lax.fori_loop(0, slots, body, jnp.zeros((rows, LANES), F32), unroll=4)
        mass = jnp.sum(mass, axis=1, keepdims=True)
        part = rows_from_columns([mass])

        @pl.when(chunk == 0)
        def _():
            mass_ref[...] = part

        @pl.when(chunk > 0)
        def _():
            mass_ref[...] += part


def contributions(core, own_code, peer_code, stats, x_own, x_peer, w_own, w_peer, slots_all, slots):
    rows = x_own.shape[0]
    old_blocks, fan = w_own.shape[:2]
    steps = old_blocks // GROUP
    chunks = slots_all // slots
    smem = pl.BlockSpec(memory_space=pltpu.SMEM)
    whole = lambda shape: pl.BlockSpec(shape, lambda c, s: (0,) * len(shape))
    weights = (GROUP, fan, LANES, LANES)
    return pl.pallas_call(
        functools.partial(contrib_kernel, steps=steps, fan=fan),
        grid=(chunks, 2 * steps),
        in_specs=[
            smem,
            smem,
            smem,
            whole(stats.shape),
            whole(x_own.shape),
            whole(x_peer.shape),
            pl.BlockSpec(weights, lambda c, s: (jnp.minimum(s, steps - 1), 0, 0, 0)),
            pl.BlockSpec(weights, lambda c, s: (jnp.maximum(s - steps, 0), 0, 0, 0)),
        ],
        out_specs=[
            pl.BlockSpec((slots, rows, LANES), lambda c, s: (c, 0, 0)),
            whole((8, rows)),
        ],
        out_shape=[
            jax.ShapeDtypeStruct((slots_all, rows, LANES), BF16),
            jax.ShapeDtypeStruct((8, rows), F32),
        ],
        scratch_shapes=[
            pltpu.VMEM((slots + 1, rows, LANES), F32),
            pltpu.VMEM((2 * old_blocks, rows, LANES), BF16),
        ],
        compiler_params=pltpu.CompilerParams(vmem_limit_bytes=VMEM_LIMIT),
        cost_estimate=pl.CostEstimate(
            flops=4 * old_blocks * fan * rows * LANES * LANES,
            bytes_accessed=2 * x_own.size * 2 + 2 * w_own.size * 2 + slots_all * rows * LANES * 2,
            transcendentals=2 * x_own.size,
        ),
        name="chip_sums",
    )(core, own_code, peer_code, stats, x_own, x_peer, w_own, w_peer)


def student_kernel(base_ref, logits_ref, labels_ref, mass_ref, stat_ref):
    n_tok, rows, cols = logits_ref.shape
    lane = lax.broadcasted_iota(jnp.int32, (rows, LANES), 1)
    label = labels_ref[...]
    top = jnp.full((rows, LANES), -jnp.inf, F32)
    hit = jnp.zeros((rows, LANES), F32)
    for t in range(n_tok):
        for b in range(cols // LANES):
            block = logits_ref[t, :, b * LANES : (b + 1) * LANES]
            top = jnp.maximum(top, block)
            hit = hit + jnp.where(lane == label - (base_ref[t] + b * LANES), block, 0.0)
    top = jnp.max(top, axis=1, keepdims=True)
    total = jnp.zeros((rows, LANES), F32)
    for t in range(n_tok):
        for b in range(cols // LANES):
            total = total + jnp.exp(logits_ref[t, :, b * LANES : (b + 1) * LANES] - top)
    total = jnp.sum(total, axis=1, keepdims=True)
    hit = jnp.sum(hit, axis=1, keepdims=True)
    zero = jnp.zeros_like(hit)
    stat_ref[...] = mass_ref[...] + rows_from_columns([zero, top, total, hit])


def student_stats(base, logits, label_column, mass):
    smem = pl.BlockSpec(memory_space=pltpu.SMEM)
    vmem = pl.BlockSpec(memory_space=pltpu.VMEM)
    return pl.pallas_call(
        student_kernel,
        in_specs=[smem, vmem, vmem, vmem],
        out_specs=vmem,
        out_shape=jax.ShapeDtypeStruct(mass.shape, F32),
        compiler_params=pltpu.CompilerParams(vmem_limit_bytes=VMEM_LIMIT),
        cost_estimate=pl.CostEstimate(
            flops=4 * logits.size, bytes_accessed=4 * logits.size, transcendentals=logits.size
        ),
        name="student_stats",
    )(base, logits, label_column, mass)


def grad_kernel(base_ref, stats_ref, sums_ref, logits_ref, labels_ref, grad_ref, loss_ref, columns, inner):
    t = pl.program_id(0)
    n_vocab = stats_ref.shape[0]
    n_z, per, rows, _ = sums_ref.shape

    @pl.when(t == 0)
    def _():
        row = lambda v, k: stats_ref[v, k : k + 1, :]
        mass = functools.reduce(jnp.add, [row(v, 0) for v in range(n_vocab)])
        high = functools.reduce(jnp.maximum, [row(v, 1) for v in range(n_vocab)])
        spread = functools.reduce(jnp.add, [row(v, 2) * jnp.exp(row(v, 1) - high) for v in range(n_vocab)])
        log_total = high + jnp.log(spread)
        label_logit = functools.reduce(jnp.add, [row(v, 3) for v in range(n_vocab)])
        head = [mass + 1.0, log_total]
        fill = jnp.zeros((LANES - len(head), rows), F32)
        columns[...] = jnp.concatenate(head + [fill], axis=0).T
        inner[...] = jnp.zeros_like(inner)
        loss_ref[0:1, :] = mass * log_total + log_total - label_logit

    lane = lax.broadcasted_iota(jnp.int32, (rows, LANES), 1)
    label = labels_ref[...] - base_ref[t]
    lift = columns[:, 0:1]
    log_total = columns[:, 1:2]
    running = inner[...]
    for b in range(per):
        target = sums_ref[0, b].astype(F32)
        for z in range(1, n_z):
            target = target + sums_ref[z, b].astype(F32)
        logits = logits_ref[0, :, b * LANES : (b + 1) * LANES]
        running = running + target * logits
        hit = jnp.where(lane == label - b * LANES, 1.0, 0.0)
        grad = lift * jnp.exp(logits - log_total) - target - hit
        grad_ref[0, :, b * LANES : (b + 1) * LANES] = grad.astype(BF16)
    inner[...] = running

    @pl.when(t == pl.num_programs(0) - 1)
    def _():
        part = jnp.sum(inner[...], axis=1, keepdims=True)
        loss_ref[1:2, :] = rows_from_columns([part])[0:1, :]


def grad_logits(base, stats, sums, logits, label_column):
    n_tok, rows, cols = logits.shape
    n_z, slots = sums.shape[:2]
    per = slots // n_tok
    smem = pl.BlockSpec(memory_space=pltpu.SMEM)
    return pl.pallas_call(
        grad_kernel,
        grid=(n_tok,),
        in_specs=[
            smem,
            pl.BlockSpec(stats.shape, lambda t: (0, 0, 0)),
            pl.BlockSpec((n_z, per, rows, LANES), lambda t: (0, t, 0, 0)),
            pl.BlockSpec((1, rows, cols), lambda t: (t, 0, 0)),
            pl.BlockSpec((rows, 1), lambda t: (0, 0)),
        ],
        out_specs=[
            pl.BlockSpec((1, rows, cols), lambda t: (t, 0, 0)),
            pl.BlockSpec((8, rows), lambda t: (0, 0)),
        ],
        out_shape=[
            jax.ShapeDtypeStruct((n_tok, rows, cols), BF16),
            jax.ShapeDtypeStruct((8, rows), F32),
        ],
        scratch_shapes=[pltpu.VMEM((rows, LANES), F32), pltpu.VMEM((rows, LANES), F32)],
        compiler_params=pltpu.CompilerParams(vmem_limit_bytes=VMEM_LIMIT),
        cost_estimate=pl.CostEstimate(
            flops=16 * logits.size, bytes_accessed=2 * sums.size + 6 * logits.size, transcendentals=logits.size
        ),
        name="grad_logits",
    )(base, stats, sums, logits, label_column)


def matmul_kernel(a_ref, b_ref, o_ref):
    o_ref[...] = jnp.dot(a_ref[...], b_ref[...], preferred_element_type=F32).astype(o_ref.dtype)


def head_product(a, b):
    m, k = a.shape
    n = b.shape[1]
    tile = 512
    while m % tile:
        tile //= 2
    return pl.pallas_call(
        matmul_kernel,
        grid=(m // tile,),
        in_specs=[
            pl.BlockSpec((tile, k), lambda i: (i, 0)),
            pl.BlockSpec((k, n), lambda i: (0, 0)),
        ],
        out_specs=pl.BlockSpec((tile, n), lambda i: (i, 0)),
        out_shape=jax.ShapeDtypeStruct((m, n), BF16),
        compiler_params=pltpu.CompilerParams(vmem_limit_bytes=VMEM_LIMIT),
        cost_estimate=pl.CostEstimate(
            flops=2 * m * n * k, bytes_accessed=2 * (m * k + k * n + m * n), transcendentals=0
        ),
        name="head_product",
    )(a, b)


def local(teacher_logits, hidden, new_head, labels, map_target, map_weight):
    rows = teacher_logits.shape[0]
    block = map_weight.shape[2]
    n_tok = lax.axis_size("tok")
    n_vocab = lax.axis_size("vocab")
    n_z = n_vocab // 2
    new_cols = new_head.shape[1]
    per = new_cols // block
    tok = lax.axis_index("tok")
    vocab = lax.axis_index("vocab")
    slots = n_tok * per
    slots_all = n_z * slots

    everyone = lax.all_gather(hidden, "tok", axis=0, tiled=True)

    owner = map_target // per
    owner_vocab = owner % n_vocab
    slot = (owner_vocab // 2) * slots + (owner // n_vocab) * per + map_target % per
    own_code = (slot * 2 + owner_vocab % 2).astype(jnp.int32).reshape(-1)
    swap = [(v, v ^ 1) for v in range(n_vocab)]
    peer_logits = lax.ppermute(teacher_logits, "vocab", swap)
    peer_code = lax.ppermute(own_code, "vocab", swap)
    peer_weight = lax.ppermute(map_weight, "vocab", swap)
    core = (vocab % 2).astype(jnp.int32).reshape(1)
    at_once = min(slots_all, 128)
    totals = lax.all_gather(teacher_stats(teacher_logits), "vocab", axis=0)
    sums, mass = contributions(
        core, own_code, peer_code, totals, teacher_logits, peer_logits, map_weight, peer_weight, slots_all, at_once
    )

    sums = sums.reshape(n_z, slots, rows, block)
    lines = [[2 * z + c for z in range(n_z)] for c in range(2)]
    sums = lax.all_to_all(sums, "vocab", split_axis=0, concat_axis=0, axis_index_groups=lines, tiled=True)

    logits = jnp.dot(everyone, new_head, preferred_element_type=F32)
    turned = everyone.T
    logits = lax.all_to_all(
        logits.reshape(n_tok, rows, new_cols), "tok", split_axis=0, concat_axis=0, tiled=True
    )
    label_column = lax.dynamic_slice_in_dim(labels, tok * rows, rows).reshape(rows, 1)
    base = (jnp.arange(n_tok, dtype=jnp.int32) * n_vocab + vocab) * new_cols
    stats = student_stats(base, logits, label_column, mass)
    stats = lax.all_gather(stats, "vocab", axis=0)

    grad, loss_rows = grad_logits(base, stats, sums, logits, label_column)
    grad = lax.all_to_all(grad, "tok", split_axis=0, concat_axis=0, tiled=True)
    inner = lax.psum(loss_rows[1], "vocab")
    loss = loss_rows[0] - inner
    head_grad = head_product(turned, grad.reshape(n_tok * rows, new_cols))
    return (loss, head_grad)


def solution(mesh):
    return jax.shard_map(
        local,
        mesh=mesh,
        in_specs=(
            P("tok", "vocab"),
            P("tok", None),
            P(None, ("tok", "vocab")),
            P(),
            P("vocab", None),
            P("vocab", None, None, None),
        ),
        out_specs=(P("tok"), P(None, ("tok", "vocab"))),
        check_vma=False,
    )
```

```python
import functools

import jax
import jax.numpy as jnp
from jax import lax
from jax.experimental import pallas as pl
from jax.experimental.pallas import tpu as pltpu
from jax.sharding import PartitionSpec as P

F32 = jnp.float32
BF16 = jnp.bfloat16
LANES = 128
GROUP = 8
VMEM_LIMIT = 56 * 1024 * 1024
SMEM_SPEC = pl.BlockSpec(memory_space=pltpu.SMEM)
VMEM_SPEC = pl.BlockSpec(memory_space=pltpu.VMEM)


def params():
    return pltpu.CompilerParams(vmem_limit_bytes=VMEM_LIMIT)


def tree(op, items):
    while len(items) > 1:
        items = [op(items[i], items[i + 1]) if i + 1 < len(items) else items[i] for i in range(0, len(items), 2)]
    return items[0]


def total_at(rows_of, top_row, total_row):
    top = tree(jnp.maximum, [r[top_row] for r in rows_of])
    total = tree(jnp.add, [r[total_row] * jnp.exp(r[top_row] - top) for r in rows_of])
    return top, total


def split_rows(refs):
    return [[ref[k : k + 1, :] for k in range(8)] for ref in refs]


def rows_from_columns(columns):
    n = columns[0].shape[0]
    lane = lax.broadcasted_iota(jnp.int32, (n, LANES), 1)
    tile = jnp.zeros((n, LANES), F32)
    for place, column in enumerate(columns):
        tile = jnp.where(lane == place, column, tile)
    return tile.T[0:8, :]


def columns_from_rows(rows):
    n = rows[0].shape[1]
    return jnp.concatenate(rows + [jnp.zeros((LANES - len(rows), n), F32)], axis=0).T


def teacher_kernel(*refs):
    shards, stat_ref = refs[:-1], refs[-1]
    rows, cols = shards[0].shape
    places = [(ref, j) for ref in shards for j in range(0, cols, LANES)]
    read = lambda place: place[0][:, place[1] : place[1] + LANES].astype(F32)
    top = jnp.full((rows, LANES), -jnp.inf, F32)
    for place in places:
        top = jnp.maximum(top, read(place))
    top = jnp.max(top, axis=1, keepdims=True)
    total = jnp.zeros((rows, LANES), F32)
    for place in places:
        total = total + jnp.exp(read(place) - top)
    stat_ref[...] = rows_from_columns([top, jnp.sum(total, axis=1, keepdims=True)])


def teacher_stats(*shards):
    size = sum(x.size for x in shards)
    return pl.pallas_call(
        teacher_kernel,
        in_specs=[VMEM_SPEC] * len(shards),
        out_specs=VMEM_SPEC,
        out_shape=jax.ShapeDtypeStruct((8, shards[0].shape[0]), F32),
        compiler_params=params(),
        cost_estimate=pl.CostEstimate(flops=4 * size, bytes_accessed=2 * size, transcendentals=size),
        name="teacher_stats",
    )(*shards)


def sums_kernel(core_ref, own_code, peer_code, *refs, steps, fan, n_stats, n_out):
    stats, (x_own, x_peer, w_own, w_peer) = refs[:n_stats], refs[n_stats : n_stats + 4]
    outs = refs[n_stats + 4 : n_stats + 4 + n_out]
    mass_ref, acc, probs = refs[n_stats + 4 + n_out :]
    chunk, step = pl.program_id(0), pl.program_id(1)
    rows = x_own.shape[0]
    blocks = x_own.shape[1] // LANES
    piece_slots = outs[0].shape[0]
    slots = n_out * piece_slots

    @pl.when((chunk == 0) & (step == 0))
    def _():
        top, total = total_at(split_rows(stats), 0, 1)
        columns = columns_from_rows([top, 1.0 / total])
        top, scale = columns[:, 0:1], columns[:, 1:2]
        for side, x in enumerate((x_own, x_peer)):
            for j in range(blocks):
                raised = jnp.exp(x[:, j * LANES : (j + 1) * LANES].astype(F32) - top)
                probs[side * blocks + j] = (raised * scale).astype(BF16)

    @pl.when(step == 0)
    def _():
        acc[...] = jnp.zeros_like(acc)

    def add(code_ref, w_ref, first, offset):
        for jj in range(GROUP):
            weights = jnp.concatenate([w_ref[jj, f] for f in range(fan)], axis=1)
            mapped = jnp.dot(probs[offset + first + jj], weights, preferred_element_type=F32)
            mapped = mapped.astype(BF16).astype(F32)
            for f in range(fan):
                code = code_ref[(first + jj) * fan + f]
                slot = lax.shift_right_logical(code, 1) - chunk * slots
                mine = ((code & 1) == core_ref[0]) & (slot >= 0) & (slot < slots)
                slot = jnp.where(mine, slot, slots)
                acc[slot] += mapped[:, f * LANES : (f + 1) * LANES]

    @pl.when(step < steps)
    def _():
        add(own_code, w_own, step * GROUP, 0)

    @pl.when(step >= steps)
    def _():
        add(peer_code, w_peer, (step - steps) * GROUP, blocks)

    @pl.when(step == 2 * steps - 1)
    def _():
        mass = jnp.zeros((rows, LANES), F32)
        for place, out in enumerate(outs):

            def body(i, mass):
                block = acc[place * piece_slots + i]
                out[i] = block.astype(BF16)
                return mass + block

            mass = lax.fori_loop(0, piece_slots, body, mass, unroll=4)
        part = rows_from_columns([jnp.sum(mass, axis=1, keepdims=True)])

        @pl.when(chunk == 0)
        def _():
            mass_ref[...] = part

        @pl.when(chunk > 0)
        def _():
            mass_ref[...] += part


def chip_sums(core, own_code, peer_code, stats, x_own, x_peer, w_own, w_peer, chunks, n_out, piece_slots):
    rows = x_own.shape[0]
    old_blocks, fan = w_own.shape[:2]
    steps = old_blocks // GROUP
    whole = lambda shape: pl.BlockSpec(shape, lambda c, s: (0,) * len(shape))
    weights = (GROUP, fan, LANES, LANES)
    out = jax.ShapeDtypeStruct((chunks * piece_slots, rows, LANES), BF16)
    return pl.pallas_call(
        functools.partial(sums_kernel, steps=steps, fan=fan, n_stats=len(stats), n_out=n_out),
        grid=(chunks, 2 * steps),
        in_specs=[SMEM_SPEC] * 3
        + [whole(s.shape) for s in stats]
        + [
            whole(x_own.shape),
            whole(x_peer.shape),
            pl.BlockSpec(weights, lambda c, s: (jnp.minimum(s, steps - 1), 0, 0, 0)),
            pl.BlockSpec(weights, lambda c, s: (jnp.maximum(s - steps, 0), 0, 0, 0)),
        ],
        out_specs=[pl.BlockSpec((piece_slots, rows, LANES), lambda c, s: (c, 0, 0))] * n_out + [whole((8, rows))],
        out_shape=[out] * n_out + [jax.ShapeDtypeStruct((8, rows), F32)],
        scratch_shapes=[
            pltpu.VMEM((n_out * piece_slots + 1, rows, LANES), F32),
            pltpu.VMEM((2 * old_blocks, rows, LANES), BF16),
        ],
        compiler_params=params(),
        cost_estimate=pl.CostEstimate(
            flops=4 * old_blocks * fan * rows * LANES * LANES,
            bytes_accessed=4 * x_own.size + 4 * w_own.size + 2 * n_out * out.size,
            transcendentals=2 * x_own.size,
        ),
        name="chip_sums",
    )(core, own_code, peer_code, *stats, x_own, x_peer, w_own, w_peer)


def logits_kernel(spot_ref, after_ref, near_ref, far_ref, head_ref, *refs):
    outs, everyone = refs[:-1], refs[-1]
    n_tok = len(outs)
    half = near_ref.shape[0] // n_tok
    del after_ref

    @pl.when(pl.program_id(0) == 0)
    def _():
        core, tok = spot_ref[0], spot_ref[1]
        for r in range(n_tok):
            source = pl.ds(pl.multiple_of((tok ^ r) * half, half), half)
            for side, ref in ((core, near_ref), (1 - core, far_ref)):
                start = pl.multiple_of((2 * r + side) * half, half)
                everyone[pl.ds(start, half), :] = ref[source, :]

    result = jnp.dot(everyone[...], head_ref[...], preferred_element_type=F32)
    for r, out in enumerate(outs):
        out[...] = result[2 * r * half : 2 * (r + 1) * half, :]


def student_logits(spot, after, near, far, head, n_tok):
    every, depth = 2 * near.shape[0], near.shape[1]
    rows = every // n_tok
    cols = head.shape[1]
    tile = 256
    whole = lambda shape: pl.BlockSpec(shape, lambda i: (0, 0))
    return pl.pallas_call(
        logits_kernel,
        grid=(cols // tile,),
        in_specs=[SMEM_SPEC, whole(after.shape), whole(near.shape), whole(far.shape)]
        + [pl.BlockSpec((depth, tile), lambda i: (0, i))],
        out_specs=[pl.BlockSpec((rows, tile), lambda i: (0, i))] * n_tok + [whole((every, depth))],
        out_shape=[jax.ShapeDtypeStruct((rows, cols), F32)] * n_tok + [jax.ShapeDtypeStruct((every, depth), BF16)],
        compiler_params=params(),
        cost_estimate=pl.CostEstimate(
            flops=2 * every * depth * cols,
            bytes_accessed=2 * (2 * every * depth + depth * cols) + 4 * every * cols,
            transcendentals=0,
        ),
        name="student_logits",
    )(spot, after, near, far, head)


def student_kernel(base_ref, labels_ref, mass_ref, *refs):
    logits, stat_ref = refs[:-1], refs[-1]
    rows, cols = logits[0].shape
    lane = lax.broadcasted_iota(jnp.int32, (rows, LANES), 1)
    label = labels_ref[...]
    top = jnp.full((rows, LANES), -jnp.inf, F32)
    hit = jnp.zeros((rows, LANES), F32)
    for r, ref in enumerate(logits):
        for b in range(0, cols, LANES):
            block = ref[:, b : b + LANES]
            top = jnp.maximum(top, block)
            hit = hit + jnp.where(lane == label - (base_ref[r] + b), block, 0.0)
    top = jnp.max(top, axis=1, keepdims=True)
    total = jnp.zeros((rows, LANES), F32)
    for ref in logits:
        for b in range(0, cols, LANES):
            total = total + jnp.exp(ref[:, b : b + LANES] - top)
    total = jnp.sum(total, axis=1, keepdims=True)
    hit = jnp.sum(hit, axis=1, keepdims=True)
    stat_ref[...] = mass_ref[...] + rows_from_columns([jnp.zeros_like(hit), top, total, hit])


def student_stats(base, label_column, mass, logits):
    size = len(logits) * logits[0].size
    return pl.pallas_call(
        student_kernel,
        in_specs=[SMEM_SPEC] + [VMEM_SPEC] * (2 + len(logits)),
        out_specs=VMEM_SPEC,
        out_shape=jax.ShapeDtypeStruct(mass.shape, F32),
        compiler_params=params(),
        cost_estimate=pl.CostEstimate(flops=4 * size, bytes_accessed=4 * size, transcendentals=size),
        name="student_stats",
    )(base, label_column, mass, *logits)


def grad_kernel(base_ref, labels_ref, *refs, n_stats, n_sums, n_tok):
    stats, sums = refs[:n_stats], refs[n_stats : n_stats + n_sums]
    logits = refs[n_stats + n_sums : n_stats + n_sums + n_tok]
    grads = refs[n_stats + n_sums + n_tok : n_stats + n_sums + 2 * n_tok]
    loss_ref, columns, inner = refs[n_stats + n_sums + 2 * n_tok :]
    step = pl.program_id(0)
    rows, cols = logits[0].shape

    @pl.when(step == 0)
    def _():
        parts = split_rows(stats)
        mass = tree(jnp.add, [r[0] for r in parts])
        top, total = total_at(parts, 1, 2)
        log_total = top + jnp.log(total)
        label_logit = tree(jnp.add, [r[3] for r in parts])
        columns[...] = columns_from_rows([mass + 1.0, log_total])
        inner[...] = jnp.zeros_like(inner)
        loss_ref[...] = jnp.zeros_like(loss_ref)
        loss_ref[0:1, :] = mass * log_total + log_total - label_logit

    lane = lax.broadcasted_iota(jnp.int32, (rows, LANES), 1)
    lift, log_total = columns[:, 0:1], columns[:, 1:2]
    for r in range(n_tok):

        @pl.when(step == r)
        def _():
            label = labels_ref[...] - base_ref[r]
            running = inner[...]
            for b in range(cols // LANES):
                place = slice(b * LANES, (b + 1) * LANES)
                target = functools.reduce(
                    jnp.add, [ref[z, b].astype(F32) for ref in sums for z in range(ref.shape[0])]
                )
                score = logits[r][:, place]
                running = running + target * score
                hit = jnp.where(lane == label - b * LANES, 1.0, 0.0)
                grads[r][:, place] = (lift * jnp.exp(score - log_total) - target - hit).astype(BF16)
            inner[...] = running

    @pl.when(step == n_tok - 1)
    def _():
        loss_ref[1:2, :] = rows_from_columns([jnp.sum(inner[...], axis=1, keepdims=True)])[0:1, :]


def grad_logits(base, label_column, stats, sums, logits):
    n_tok = len(logits)
    rows, cols = logits[0].shape
    per = cols // LANES
    whole = lambda shape: pl.BlockSpec(shape, lambda t: (0,) * len(shape))
    size = n_tok * rows * cols
    return pl.pallas_call(
        functools.partial(grad_kernel, n_stats=len(stats), n_sums=len(sums), n_tok=n_tok),
        grid=(n_tok,),
        in_specs=[SMEM_SPEC, whole(label_column.shape)]
        + [whole(s.shape) for s in stats]
        + [pl.BlockSpec((s.shape[0], per, rows, LANES), lambda t: (0, t, 0, 0)) for s in sums]
        + [whole(x.shape) for x in logits],
        out_specs=[whole((rows, cols))] * n_tok + [whole((8, rows))],
        out_shape=[jax.ShapeDtypeStruct((rows, cols), BF16)] * n_tok + [jax.ShapeDtypeStruct((8, rows), F32)],
        scratch_shapes=[pltpu.VMEM((rows, LANES), F32), pltpu.VMEM((rows, LANES), F32)],
        compiler_params=params(),
        cost_estimate=pl.CostEstimate(
            flops=16 * size, bytes_accessed=2 * sum(s.size for s in sums) + 6 * size, transcendentals=size
        ),
        name="grad_logits",
    )(base, label_column, *stats, *sums, *logits)


def product_kernel(a_ref, *refs):
    pieces, (o_ref, b) = refs[:-2], refs[-2:]

    @pl.when(pl.program_id(0) == 0)
    def _():
        rows = pieces[0].shape[0]
        for r, piece in enumerate(pieces):
            b[r * rows : (r + 1) * rows, :] = piece[...]

    o_ref[...] = jnp.dot(a_ref[...], b[...], preferred_element_type=F32).astype(o_ref.dtype)


def head_product(a, pieces):
    m, k = a.shape
    rows, n = pieces[0].shape
    tile = m // 4
    return pl.pallas_call(
        product_kernel,
        grid=(m // tile,),
        in_specs=[pl.BlockSpec((tile, k), lambda i: (i, 0))] + [pl.BlockSpec((rows, n), lambda i: (0, 0))] * len(pieces),
        out_specs=pl.BlockSpec((tile, n), lambda i: (i, 0)),
        out_shape=jax.ShapeDtypeStruct((m, n), BF16),
        scratch_shapes=[pltpu.VMEM((k, n), BF16)],
        compiler_params=params(),
        cost_estimate=pl.CostEstimate(
            flops=2 * m * n * k, bytes_accessed=2 * (m * k + k * n + m * n), transcendentals=0
        ),
        name="head_product",
    )(a, *pieces)


def swap(x, axis, mask):
    return lax.ppermute(x, axis, [(i, i ^ mask) for i in range(lax.axis_size(axis))])


def gather_chips(x):
    n = lax.axis_size("vocab")
    if n > 8:
        everything = lax.all_gather(x, "vocab", axis=0)
        return [everything[v] for v in range(0, n, 2)]
    return [x] + [swap(x, "vocab", r) for r in range(2, n, 2)]


def plus(a, b):
    return (a.astype(F32) + b.astype(F32)).astype(BF16)


def line_exchange(far_outer, far_inner, near, own):
    def send(x, hops):
        return lax.ppermute(x, "vocab", [(2 * a + c, 2 * b + c) for a, b in hops for c in range(2)])

    inward, across, outward = [(0, 1), (3, 2)], [(1, 2), (2, 1)], [(1, 0), (2, 3)]
    first = send(far_outer, inward)
    second = send(far_inner, inward)
    third = send(near, inward)
    crossed_outer = send(plus(far_outer, first), across)
    crossed_inner = send(plus(far_inner, second), across)
    arrived = send(plus(near, crossed_outer), outward)
    return [own, third, crossed_inner, arrived]


def local(teacher_logits, hidden, new_head, labels, map_target, map_weight):
    rows = teacher_logits.shape[0]
    block = map_weight.shape[2]
    n_tok = lax.axis_size("tok")
    n_vocab = lax.axis_size("vocab")
    n_z = n_vocab // 2
    new_cols = new_head.shape[1]
    per = new_cols // block
    tok = lax.axis_index("tok")
    vocab = lax.axis_index("vocab")
    core = (vocab % 2).astype(jnp.int32).reshape(1)
    spot = jnp.stack([vocab % 2, tok]).astype(jnp.int32)
    slots = n_tok * per
    in_line = n_z == 4

    owner = map_target // per
    owner_vocab = owner % n_vocab
    owner_z = owner_vocab // 2
    if in_line:
        z = vocab // 2
        same = (owner_z // 2) == (z // 2)
        outer = (owner_z == 0) | (owner_z == n_z - 1)
        place = jnp.where(same, jnp.where(owner_z == z, 3, 2), jnp.where(outer, 0, 1))
    else:
        place = owner_z
    slot = place * slots + ((owner // n_vocab) ^ tok) * per + map_target % per
    own_code = (slot * 2 + owner_vocab % 2).astype(jnp.int32).reshape(-1)

    half = lax.dynamic_slice_in_dim(hidden, core[0] * (rows // 2), rows // 2)
    near = lax.all_gather(half, "tok", axis=0, tiled=True)

    peer_logits = swap(teacher_logits, "vocab", 1)
    peer_code = swap(own_code, "vocab", 1)
    peer_weight = swap(map_weight, "vocab", 1)
    totals = gather_chips(teacher_stats(teacher_logits, peer_logits))

    args = (core, own_code, peer_code, totals, teacher_logits, peer_logits, map_weight, peer_weight)
    if in_line:
        *pieces, mass = chip_sums(*args, 1, n_z, slots)
        sums = [x[None] for x in line_exchange(*pieces)]
    else:
        at_once = 4
        sums, mass = chip_sums(*args, n_z // at_once, 1, at_once * slots)
        lines = [[2 * z + c for z in range(n_z)] for c in range(2)]
        sums = lax.all_to_all(
            sums.reshape(n_z, slots, rows, block),
            "vocab",
            split_axis=0,
            concat_axis=0,
            axis_index_groups=lines,
            tiled=True,
        )
        sums = [sums]

    near, mass = lax.optimization_barrier((near, mass))
    far = swap(near, "vocab", 1)
    *scores, everyone = student_logits(spot, mass, near, far, new_head, n_tok)
    turned = everyone.T
    scores = [scores[0]] + [swap(scores[r], "tok", r) for r in range(1, n_tok)]
    label_column = lax.dynamic_slice_in_dim(labels, tok * rows, rows).reshape(rows, 1)
    base = ((jnp.arange(n_tok, dtype=jnp.int32) ^ tok) * n_vocab + vocab) * new_cols
    stats = student_stats(base, label_column, mass, scores)
    stats = gather_chips(stats) + gather_chips(swap(stats, "vocab", 1))

    *grads, loss_rows = grad_logits(base, label_column, stats, sums, scores)
    grads = [grads[0]] + [swap(grads[r], "tok", r) for r in range(1, n_tok)]
    inner = loss_rows[1]
    inner = tree(jnp.add, gather_chips(inner + swap(inner, "vocab", 1)))
    loss = loss_rows[0] - inner
    return (loss, head_product(turned, grads))


def solution(mesh):
    return jax.shard_map(
        local,
        mesh=mesh,
        in_specs=(
            P("tok", "vocab"),
            P("tok", None),
            P(None, ("tok", "vocab")),
            P(),
            P("vocab", None),
            P("vocab", None, None, None),
        ),
        out_specs=(P("tok"), P(None, ("tok", "vocab"))),
        check_vma=False,
    )
```

```python
import functools

import jax
import jax.numpy as jnp
from jax import lax
from jax.experimental import pallas as pl
from jax.experimental.pallas import tpu as pltpu
from jax.sharding import PartitionSpec as P

F32 = jnp.float32
BF16 = jnp.bfloat16
LANES = 128
BATCH = 4
COST = pl.CostEstimate(flops=1024, bytes_accessed=1024, transcendentals=0)
SLOT_BASE = 1024
SMEM_SPEC = pl.BlockSpec(memory_space=pltpu.SMEM)
VMEM_SPEC = pl.BlockSpec(memory_space=pltpu.VMEM)


def params(mebibytes):
    return pltpu.CompilerParams(vmem_limit_bytes=mebibytes * 1024 * 1024)


def tree(op, items):
    while len(items) > 1:
        items = [op(items[i], items[i + 1]) if i + 1 < len(items) else items[i] for i in range(0, len(items), 2)]
    return items[0]


def total_at(rows_of, top_row, total_row):
    top = tree(jnp.maximum, [r[top_row] for r in rows_of])
    total = tree(jnp.add, [r[total_row] * jnp.exp(r[top_row] - top) for r in rows_of])
    return top, total


def split_rows(refs):
    return [[ref[k : k + 1, :] for k in range(8)] for ref in refs]


def rows_from_columns(columns):
    n = columns[0].shape[0]
    lane = lax.broadcasted_iota(jnp.int32, (n, LANES), 1)
    tile = jnp.zeros((n, LANES), F32)
    for place, column in enumerate(columns):
        tile = jnp.where(lane == place, column, tile)
    return tile.T[0:8, :]


def columns_from_rows(rows):
    n = rows[0].shape[1]
    return jnp.concatenate(rows + [jnp.zeros((LANES - len(rows), n), F32)], axis=0).T


def teacher_kernel(*refs):
    shards, stat_ref = refs[:-1], refs[-1]
    rows, cols = shards[0].shape
    places = [(ref, j) for ref in shards for j in range(0, cols, LANES)]
    read = lambda place: place[0][:, place[1] : place[1] + LANES].astype(F32)
    top = jnp.full((rows, LANES), -jnp.inf, F32)
    for place in places:
        top = jnp.maximum(top, read(place))
    top = jnp.max(top, axis=1, keepdims=True)
    total = jnp.zeros((rows, LANES), F32)
    for place in places:
        total = total + jnp.exp(read(place) - top)
    stat_ref[...] = rows_from_columns([top, jnp.sum(total, axis=1, keepdims=True)])


def teacher_stats(*shards):
    size = sum(x.size for x in shards)
    return pl.pallas_call(
        teacher_kernel,
        in_specs=[VMEM_SPEC] * len(shards),
        out_specs=VMEM_SPEC,
        out_shape=jax.ShapeDtypeStruct((8, shards[0].shape[0]), F32),
        compiler_params=params(40),
        cost_estimate=COST,
        name="teacher_stats",
    )(*shards)


def divide(x, n):
    return lax.shift_right_logical(x, n.bit_length() - 1) if n & (n - 1) == 0 else x // n


def plan_kernel(spot_ref, own_ref, peer_ref, list_ref, count_ref, *, per, n_vocab, in_line):
    core, z = spot_ref[0], spot_ref[1]
    pieces, room = list_ref.shape
    entries, fan = own_ref.shape
    for p in range(pieces):
        count_ref[p] = 0

    def visit(i, carry):
        for side, ref in enumerate((own_ref, peer_ref)):
            for f in range(fan):
                block = ref[i, f]
                owner = divide(block, per)
                owner_tok = divide(owner, n_vocab)
                owner_vocab = owner - owner_tok * n_vocab
                owner_z = divide(owner_vocab, 2)
                slot = owner_tok * per + block - owner * per
                if in_line:
                    outer = (owner_z == 0) | (owner_z == 3)
                    near = jnp.where(owner_z == z, 3, 2)
                    place = jnp.where(divide(owner_z, 2) == divide(z, 2), near, jnp.where(outer, 0, 1))
                else:
                    place = owner_z

                @pl.when(owner_vocab - owner_z * 2 == core)
                def _():
                    n = count_ref[place]
                    list_ref[place, n] = ((side * entries + i) * fan + f) * SLOT_BASE + slot
                    count_ref[place] = n + 1

        return carry

    lax.fori_loop(0, entries, visit, 0)
    for p in range(pieces):
        n = count_ref[p]
        for k in range(BATCH - 1):
            list_ref[p, n + k] = SLOT_BASE - 1


def plan(spot, own_target, peer_target, pieces, per, n_vocab, in_line):
    room = 2 * own_target.size + BATCH
    return pl.pallas_call(
        functools.partial(plan_kernel, per=per, n_vocab=n_vocab, in_line=in_line),
        in_specs=[SMEM_SPEC] * 3,
        out_specs=[SMEM_SPEC] * 2,
        out_shape=[jax.ShapeDtypeStruct((pieces, room), jnp.int32), jax.ShapeDtypeStruct((pieces,), jnp.int32)],
        cost_estimate=COST,
        name="entry_lists",
    )(spot, own_target, peer_target)


def probs_kernel(x_own, x_peer, *refs):
    stats, probs = refs[:-1], refs[-1]
    blocks = x_own.shape[1] // LANES
    top, total = total_at(split_rows(stats), 0, 1)
    columns = columns_from_rows([top, 1.0 / total])
    top, scale = columns[:, 0:1], columns[:, 1:2]
    for side, x in enumerate((x_own, x_peer)):
        for j in range(blocks):
            raised = jnp.exp(x[:, j * LANES : (j + 1) * LANES].astype(F32) - top)
            probs[side * blocks + j] = (raised * scale).astype(BF16)


def sums_kernel(list_ref, count_ref, probs, w_own, w_peer, *refs, first, fan):
    outs, mass_ref, acc = refs[:-2], refs[-2], refs[-1]
    step = pl.program_id(0)
    slots, rows, _ = outs[0].shape
    side = w_own.shape[0] * fan
    mass = jnp.zeros((rows, LANES), F32)
    for k, out in enumerate(outs):
        piece = first + k + step
        acc[...] = jnp.zeros_like(acc)

        def add(i, carry):
            parts = []
            for u in range(BATCH):
                item = list_ref[piece, i * BATCH + u]
                slot = item & (SLOT_BASE - 1)
                entry = lax.shift_right_logical(item, SLOT_BASE.bit_length() - 1)
                weight = jnp.where(entry < side, 0, 1)
                parts.append((entry, slot, weight))
            for entry, slot, peer in parts:
                j = divide(entry, fan)
                f = entry - j * fan
                local_j = j - peer * (side // fan)
                weight = jnp.where(peer == 1, w_peer[local_j, f], w_own[local_j, f])
                part = jnp.dot(probs[j], weight, preferred_element_type=F32)
                acc[jnp.minimum(slot, slots)] += part.astype(BF16).astype(F32)
            return carry

        lax.fori_loop(0, divide(count_ref[piece] + BATCH - 1, BATCH), add, 0)

        def drain(i, mass):
            block = acc[i]
            out[i] = block.astype(BF16)
            return mass + block

        mass = lax.fori_loop(0, slots, drain, mass, unroll=4)
    part = rows_from_columns([jnp.sum(mass, axis=1, keepdims=True)])

    @pl.when(step == 0)
    def _():
        mass_ref[...] = part

    @pl.when(step > 0)
    def _():
        mass_ref[...] += part


def teacher_probs(x_own, x_peer, stats):
    rows, cols = x_own.shape
    return pl.pallas_call(
        probs_kernel,
        in_specs=[VMEM_SPEC] * (2 + len(stats)),
        out_specs=VMEM_SPEC,
        out_shape=jax.ShapeDtypeStruct((2 * cols // LANES, rows, LANES), BF16),
        compiler_params=params(16),
        cost_estimate=COST,
        name="teacher_probs",
    )(x_own, x_peer, *stats)


def chip_sums(lists, counts, probs, w_own, w_peer, first, n_out, steps, slots):
    rows = probs.shape[1]
    fan = w_own.shape[1]
    whole = lambda shape: pl.BlockSpec(shape, lambda s: (0,) * len(shape))
    out = jax.ShapeDtypeStruct((steps * slots, rows, LANES), BF16)
    return pl.pallas_call(
        functools.partial(sums_kernel, first=first, fan=fan),
        grid=(steps,),
        in_specs=[SMEM_SPEC] * 2 + [VMEM_SPEC] * 3,
        out_specs=[pl.BlockSpec((slots, rows, LANES), lambda s: (s, 0, 0))] * n_out + [whole((8, rows))],
        out_shape=[out] * n_out + [jax.ShapeDtypeStruct((8, rows), F32)],
        scratch_shapes=[pltpu.VMEM((slots + 1, rows, LANES), F32)],
        compiler_params=params(32),
        cost_estimate=COST,
        name="chip_sums",
    )(lists, counts, probs, w_own, w_peer)


def logits_kernel(spot_ref, after_ref, near_ref, far_ref, head_ref, *refs):
    out_ref, turned_ref, everyone = refs
    n_tok = out_ref.shape[0]
    half = near_ref.shape[0] // n_tok
    del after_ref

    @pl.when(pl.program_id(0) == 0)
    def _():
        core = spot_ref[0]
        for r in range(n_tok):
            source = slice(r * half, (r + 1) * half)
            for side, ref in ((core, near_ref), (1 - core, far_ref)):
                start = pl.multiple_of((2 * r + side) * half, half)
                everyone[pl.ds(start, half), :] = ref[source, :]

    result = jnp.dot(everyone[...], head_ref[...], preferred_element_type=F32)
    for r in range(n_tok):
        out_ref[r] = result[2 * r * half : 2 * (r + 1) * half, :]
    part = turned_ref.shape[0]
    start = pl.multiple_of(pl.program_id(0) * part, part)
    turned_ref[...] = everyone[:, pl.ds(start, part)].T


def student_logits(spot, after, near, far, head, n_tok):
    every, depth = 2 * near.shape[0], near.shape[1]
    rows = every // n_tok
    cols = head.shape[1]
    tile = 256
    whole = lambda shape: pl.BlockSpec(shape, lambda i: (0, 0))
    return pl.pallas_call(
        logits_kernel,
        grid=(cols // tile,),
        in_specs=[SMEM_SPEC, pl.BlockSpec(memory_space=pl.ANY), whole(near.shape), whole(far.shape)]
        + [pl.BlockSpec((depth, tile), lambda i: (0, i))],
        out_specs=[pl.BlockSpec((n_tok, rows, tile), lambda i: (0, 0, i))]
        + [pl.BlockSpec((depth * tile // cols, every), lambda i: (i, 0))],
        out_shape=[jax.ShapeDtypeStruct((n_tok, rows, cols), F32), jax.ShapeDtypeStruct((depth, every), BF16)],
        scratch_shapes=[pltpu.VMEM((every, depth), BF16)],
        compiler_params=params(40),
        cost_estimate=COST,
        name="student_logits",
    )(spot, after, near, far, head)


def student_kernel(base_ref, labels_ref, mass_ref, logits_ref, stat_ref):
    n_tok, rows, cols = logits_ref.shape
    lane = lax.broadcasted_iota(jnp.int32, (rows, LANES), 1)
    label = labels_ref[...]
    top = jnp.full((rows, LANES), -jnp.inf, F32)
    hit = jnp.zeros((rows, LANES), F32)
    for t in range(n_tok):
        for b in range(0, cols, LANES):
            block = logits_ref[t, :, b : b + LANES]
            top = jnp.maximum(top, block)
            hit = hit + jnp.where(lane == label - (base_ref[t] + b), block, 0.0)
    top = jnp.max(top, axis=1, keepdims=True)
    total = jnp.zeros((rows, LANES), F32)
    for t in range(n_tok):
        for b in range(0, cols, LANES):
            total = total + jnp.exp(logits_ref[t, :, b : b + LANES] - top)
    total = jnp.sum(total, axis=1, keepdims=True)
    hit = jnp.sum(hit, axis=1, keepdims=True)
    stat_ref[...] = mass_ref[...] + rows_from_columns([jnp.zeros_like(hit), top, total, hit])


def student_stats(base, label_column, mass, logits):
    return pl.pallas_call(
        student_kernel,
        in_specs=[SMEM_SPEC] + [VMEM_SPEC] * 3,
        out_specs=VMEM_SPEC,
        out_shape=jax.ShapeDtypeStruct(mass.shape, F32),
        compiler_params=params(16),
        cost_estimate=COST,
        name="student_stats",
    )(base, label_column, mass, logits)


def grad_kernel(base_ref, labels_ref, *refs, n_stats, n_sums):
    stats, sums = refs[:n_stats], refs[n_stats : n_stats + n_sums]
    logits_ref, grad_ref, loss_ref, columns, inner = refs[n_stats + n_sums :]
    step = pl.program_id(0)
    _, rows, cols = logits_ref.shape

    @pl.when(step == 0)
    def _():
        parts = split_rows(stats)
        mass = tree(jnp.add, [r[0] for r in parts])
        top, total = total_at(parts, 1, 2)
        log_total = top + jnp.log(total)
        label_logit = tree(jnp.add, [r[3] for r in parts])
        columns[...] = columns_from_rows([mass + 1.0, log_total])
        inner[...] = jnp.zeros_like(inner)
        loss_ref[...] = jnp.zeros_like(loss_ref)
        loss_ref[0:1, :] = mass * log_total + log_total - label_logit

    lane = lax.broadcasted_iota(jnp.int32, (rows, LANES), 1)
    lift, log_total = columns[:, 0:1], columns[:, 1:2]
    label = labels_ref[...] - base_ref[step]
    running = inner[...]
    for b in range(cols // LANES):
        place = slice(b * LANES, (b + 1) * LANES)
        target = functools.reduce(jnp.add, [ref[z, b].astype(F32) for ref in sums for z in range(ref.shape[0])])
        score = logits_ref[0, :, place]
        running = running + target * score
        hit = jnp.where(lane == label - b * LANES, 1.0, 0.0)
        grad_ref[0, :, place] = (lift * jnp.exp(score - log_total) - target - hit).astype(BF16)
    inner[...] = running

    @pl.when(step == pl.num_programs(0) - 1)
    def _():
        loss_ref[1:2, :] = rows_from_columns([jnp.sum(inner[...], axis=1, keepdims=True)])[0:1, :]


def grad_logits(base, label_column, stats, sums, logits):
    n_tok, rows, cols = logits.shape
    per = cols // LANES
    whole = lambda shape: pl.BlockSpec(shape, lambda t: (0,) * len(shape))
    one = pl.BlockSpec((1, rows, cols), lambda t: (t, 0, 0))
    return pl.pallas_call(
        functools.partial(grad_kernel, n_stats=len(stats), n_sums=len(sums)),
        grid=(n_tok,),
        in_specs=[SMEM_SPEC, whole(label_column.shape)]
        + [whole(s.shape) for s in stats]
        + [pl.BlockSpec((s.shape[0], per, rows, LANES), lambda t: (0, t, 0, 0)) for s in sums]
        + [one],
        out_specs=[one, whole((8, rows))],
        out_shape=[jax.ShapeDtypeStruct((n_tok, rows, cols), BF16), jax.ShapeDtypeStruct((8, rows), F32)],
        scratch_shapes=[pltpu.VMEM((rows, LANES), F32), pltpu.VMEM((rows, LANES), F32)],
        compiler_params=params(24),
        cost_estimate=COST,
        name="grad_logits",
    )(base, label_column, *stats, *sums, logits)


def product_kernel(a_ref, b_ref, o_ref):
    o_ref[...] = jnp.dot(a_ref[...], b_ref[...], preferred_element_type=F32).astype(o_ref.dtype)


def head_product(a, b):
    m, k = a.shape
    n = b.shape[1]
    tile = m // 4
    return pl.pallas_call(
        product_kernel,
        grid=(m // tile,),
        in_specs=[pl.BlockSpec((tile, k), lambda i: (i, 0)), pl.BlockSpec((k, n), lambda i: (0, 0))],
        out_specs=pl.BlockSpec((tile, n), lambda i: (i, 0)),
        out_shape=jax.ShapeDtypeStruct((m, n), BF16),
        compiler_params=params(32),
        cost_estimate=COST,
        name="head_product",
    )(a, b)


def swap(x, axis, mask):
    return lax.ppermute(x, axis, [(i, i ^ mask) for i in range(lax.axis_size(axis))])


def gather_chips(x):
    n = lax.axis_size("vocab")
    if n > 8:
        lines = [[2 * z + c for z in range(n // 2)] for c in range(2)]
        everything = lax.all_gather(x, "vocab", axis=0, axis_index_groups=lines)
        return [everything[z] for z in range(n // 2)]
    return [x] + [swap(x, "vocab", r) for r in range(2, n, 2)]


def gather_cores(x):
    chips = gather_chips(x)
    return chips + [swap(chip, "vocab", 1) for chip in chips]


def exchange_tok(x):
    return lax.all_to_all(x, "tok", split_axis=0, concat_axis=0, tiled=True)


def plus(a, b):
    return (a.astype(F32) + b.astype(F32)).astype(BF16)


def send(x, hops):
    return lax.ppermute(x, "vocab", [(2 * a + c, 2 * b + c) for a, b in hops for c in range(2)])


def local(teacher_logits, hidden, new_head, labels, map_target, map_weight):
    rows = teacher_logits.shape[0]
    block = map_weight.shape[2]
    n_tok = lax.axis_size("tok")
    n_vocab = lax.axis_size("vocab")
    n_z = n_vocab // 2
    new_cols = new_head.shape[1]
    per = new_cols // block
    tok = lax.axis_index("tok")
    vocab = lax.axis_index("vocab")
    spot = jnp.stack([vocab % 2, vocab // 2]).astype(jnp.int32)
    slots = n_tok * per
    in_line = n_z == 4

    half = lax.dynamic_slice_in_dim(hidden, spot[0] * (rows // 2), rows // 2)
    near = exchange_tok(jnp.broadcast_to(half, (n_tok,) + half.shape)).reshape(n_tok * (rows // 2), -1)
    peer_logits = swap(teacher_logits, "vocab", 1)
    peer_target = swap(map_target, "vocab", 1)
    peer_weight = swap(map_weight, "vocab", 1)
    totals = gather_cores(teacher_stats(teacher_logits))
    lists, counts = plan(spot, map_target, peer_target, n_z, per, n_vocab, in_line)
    probs = teacher_probs(teacher_logits, peer_logits, totals)

    sums_args = (lists, counts, probs, map_weight, peer_weight)
    if in_line:
        inward, across, outward = [(0, 1), (3, 2)], [(1, 2), (2, 1)], [(1, 0), (2, 3)]
        far_outer, mass_a = chip_sums(*sums_args, 0, 1, 1, slots)
        first = send(far_outer, inward)
        probs, mass_a = lax.optimization_barrier((probs, mass_a))
        far_inner, beside, own, mass_b = chip_sums(lists, counts, probs, map_weight, peer_weight, 1, 3, 1, slots)
        mass = mass_a + mass_b
        second = send(far_inner, inward)
        third = send(beside, inward)
    else:
        sums, mass = chip_sums(*sums_args, 0, 1, n_z, slots)
        lines = [[2 * z + c for z in range(n_z)] for c in range(2)]
        sums = lax.all_to_all(
            sums.reshape(n_z, slots, rows, block),
            "vocab",
            split_axis=0,
            concat_axis=0,
            axis_index_groups=lines,
            tiled=True,
        )
        sums = [sums]

    near, mass = lax.optimization_barrier((near, mass))
    far = swap(near, "vocab", 1)
    scores, turned = student_logits(spot, mass, near, far, new_head, n_tok)
    scores = exchange_tok(scores)
    if in_line:
        first, turned = lax.optimization_barrier((first, turned))
        merged = plus(far_outer, first)
        crossed_outer = send(merged, across)
        second, merged = lax.optimization_barrier((second, merged))
        merged_inner = plus(far_inner, second)
        crossed_inner = send(merged_inner, across)
        merged_near = plus(beside, crossed_outer)
        arrived = send(merged_near, outward)
        scores, merged_inner, merged_near = lax.optimization_barrier((scores, merged_inner, merged_near))
        sums = [x[None] for x in (own, third, crossed_inner, arrived)]
    label_column = lax.dynamic_slice_in_dim(labels, tok * rows, rows).reshape(rows, 1)
    base = (jnp.arange(n_tok, dtype=jnp.int32) * n_vocab + vocab) * new_cols
    stats = gather_cores(student_stats(base, label_column, mass, scores))

    grads, loss_rows = grad_logits(base, label_column, stats, sums, scores)
    grads = exchange_tok(grads).reshape(n_tok * rows, new_cols)
    inner = tree(jnp.add, gather_cores(loss_rows[1]))
    loss = loss_rows[0] - inner
    return (loss, head_product(turned, grads))


def solution(mesh):
    return jax.shard_map(
        local,
        mesh=mesh,
        in_specs=(
            P("tok", "vocab"),
            P("tok", None),
            P(None, ("tok", "vocab")),
            P(),
            P("vocab", None),
            P("vocab", None, None, None),
        ),
        out_specs=(P("tok"), P(None, ("tok", "vocab"))),
        check_vma=False,
    )
```

```python
import functools

import jax
import jax.numpy as jnp
from jax import lax
from jax.experimental import pallas as pl
from jax.experimental.pallas import tpu as pltpu
from jax.sharding import PartitionSpec as P

F32 = jnp.float32
BF16 = jnp.bfloat16
LANES = 128
BATCH = 4
COST = pl.CostEstimate(flops=1024, bytes_accessed=1024, transcendentals=0)
SLOT_BASE = 1024
SMEM_SPEC = pl.BlockSpec(memory_space=pltpu.SMEM)
VMEM_SPEC = pl.BlockSpec(memory_space=pltpu.VMEM)


def params(mebibytes):
    return pltpu.CompilerParams(vmem_limit_bytes=mebibytes * 1024 * 1024)


def tree(op, items):
    while len(items) > 1:
        items = [op(items[i], items[i + 1]) if i + 1 < len(items) else items[i] for i in range(0, len(items), 2)]
    return items[0]


def total_at(rows_of, top_row, total_row):
    top = tree(jnp.maximum, [r[top_row] for r in rows_of])
    total = tree(jnp.add, [r[total_row] * jnp.exp(r[top_row] - top) for r in rows_of])
    return top, total


def split_rows(ref):
    return [[ref[v, k : k + 1, :] for k in range(8)] for v in range(ref.shape[0])]


def rows_from_columns(columns):
    n = columns[0].shape[0]
    lane = lax.broadcasted_iota(jnp.int32, (n, LANES), 1)
    tile = jnp.zeros((n, LANES), F32)
    for place, column in enumerate(columns):
        tile = jnp.where(lane == place, column, tile)
    return tile.T[0:8, :]


def columns_from_rows(rows):
    n = rows[0].shape[1]
    return jnp.concatenate(rows + [jnp.zeros((LANES - len(rows), n), F32)], axis=0).T


def teacher_kernel(x_ref, stat_ref):
    rows, cols = x_ref.shape
    places = range(0, cols, LANES)
    read = lambda place: x_ref[:, place : place + LANES].astype(F32)
    top = jnp.full((rows, LANES), -jnp.inf, F32)
    for place in places:
        top = jnp.maximum(top, read(place))
    top = jnp.max(top, axis=1, keepdims=True)
    total = jnp.zeros((rows, LANES), F32)
    for place in places:
        total = total + jnp.exp(read(place) - top)
    stat_ref[...] = jnp.broadcast_to(rows_from_columns([top, jnp.sum(total, axis=1, keepdims=True)]), stat_ref.shape)


def teacher_stats(x, copies):
    return pl.pallas_call(
        teacher_kernel,
        in_specs=[VMEM_SPEC],
        out_specs=VMEM_SPEC,
        out_shape=jax.ShapeDtypeStruct((copies, 8, x.shape[0]), F32),
        compiler_params=params(16),
        cost_estimate=COST,
        name="teacher_stats",
    )(x)


def divide(x, n):
    return lax.shift_right_logical(x, n.bit_length() - 1) if n & (n - 1) == 0 else x // n


def plan_kernel(spot_ref, own_ref, peer_ref, list_ref, count_ref, *, per, n_vocab, in_line):
    core, z = spot_ref[0], spot_ref[1]
    pieces, room = list_ref.shape
    entries, fan = own_ref.shape
    for p in range(pieces):
        count_ref[p] = 0

    def visit(i, carry):
        for side, ref in enumerate((own_ref, peer_ref)):
            for f in range(fan):
                block = ref[i, f]
                owner = divide(block, per)
                owner_tok = divide(owner, n_vocab)
                owner_vocab = owner - owner_tok * n_vocab
                owner_z = divide(owner_vocab, 2)
                slot = owner_tok * per + block - owner * per
                if in_line:
                    outer = (owner_z == 0) | (owner_z == 3)
                    near = jnp.where(owner_z == z, 3, 2)
                    place = jnp.where(divide(owner_z, 2) == divide(z, 2), near, jnp.where(outer, 0, 1))
                else:
                    place = owner_z

                @pl.when(owner_vocab - owner_z * 2 == core)
                def _():
                    n = count_ref[place]
                    list_ref[place, n] = ((side * entries + i) * fan + f) * SLOT_BASE + slot
                    count_ref[place] = n + 1

        return carry

    lax.fori_loop(0, entries, visit, 0)
    for p in range(pieces):
        n = count_ref[p]
        for k in range(BATCH - 1):
            list_ref[p, n + k] = SLOT_BASE - 1


def plan(spot, own_target, peer_target, pieces, per, n_vocab, in_line):
    room = 2 * own_target.size + BATCH
    return pl.pallas_call(
        functools.partial(plan_kernel, per=per, n_vocab=n_vocab, in_line=in_line),
        in_specs=[SMEM_SPEC] * 3,
        out_specs=[SMEM_SPEC] * 2,
        out_shape=[jax.ShapeDtypeStruct((pieces, room), jnp.int32), jax.ShapeDtypeStruct((pieces,), jnp.int32)],
        cost_estimate=COST,
        name="entry_lists",
    )(spot, own_target, peer_target)


def probs_kernel(x_own, x_peer, stats, probs):
    blocks = x_own.shape[1] // LANES
    top, total = total_at(split_rows(stats), 0, 1)
    columns = columns_from_rows([top, 1.0 / total])
    top, scale = columns[:, 0:1], columns[:, 1:2]
    for side, x in enumerate((x_own, x_peer)):
        for j in range(blocks):
            raised = jnp.exp(x[:, j * LANES : (j + 1) * LANES].astype(F32) - top)
            probs[side * blocks + j] = (raised * scale).astype(BF16)


def sums_kernel(list_ref, count_ref, probs, w_own, w_peer, *refs, first, fan):
    outs, mass_ref, acc = refs[:-2], refs[-2], refs[-1]
    step = pl.program_id(0)
    slots, rows, _ = outs[0].shape
    side = w_own.shape[0] * fan
    mass = jnp.zeros((rows, LANES), F32)
    for k, out in enumerate(outs):
        piece = first + k + step
        acc[...] = jnp.zeros_like(acc)

        def add(i, carry):
            parts = []
            for u in range(BATCH):
                item = list_ref[piece, i * BATCH + u]
                slot = item & (SLOT_BASE - 1)
                entry = lax.shift_right_logical(item, SLOT_BASE.bit_length() - 1)
                weight = jnp.where(entry < side, 0, 1)
                parts.append((entry, slot, weight))
            for entry, slot, peer in parts:
                j = divide(entry, fan)
                f = entry - j * fan
                local_j = j - peer * (side // fan)
                weight = jnp.where(peer == 1, w_peer[local_j, f], w_own[local_j, f])
                part = jnp.dot(probs[j], weight, preferred_element_type=F32)
                acc[jnp.minimum(slot, slots)] += part.astype(BF16).astype(F32)
            return carry

        lax.fori_loop(0, divide(count_ref[piece] + BATCH - 1, BATCH), add, 0)

        def drain(i, mass):
            block = acc[i]
            out[i] = block.astype(BF16)
            return mass + block

        mass = lax.fori_loop(0, slots, drain, mass, unroll=4)
    part = rows_from_columns([jnp.sum(mass, axis=1, keepdims=True)])

    @pl.when(step == 0)
    def _():
        mass_ref[...] = part

    @pl.when(step > 0)
    def _():
        mass_ref[...] += part


def teacher_probs(x_own, x_peer, stats):
    rows, cols = x_own.shape
    return pl.pallas_call(
        probs_kernel,
        in_specs=[VMEM_SPEC] * 3,
        out_specs=VMEM_SPEC,
        out_shape=jax.ShapeDtypeStruct((2 * cols // LANES, rows, LANES), BF16),
        compiler_params=params(16),
        cost_estimate=COST,
        name="teacher_probs",
    )(x_own, x_peer, stats)


def chip_sums(lists, counts, probs, w_own, w_peer, first, n_out, steps, slots):
    rows = probs.shape[1]
    fan = w_own.shape[1]
    whole = lambda shape: pl.BlockSpec(shape, lambda s: (0,) * len(shape))
    out = jax.ShapeDtypeStruct((steps * slots, rows, LANES), BF16)
    return pl.pallas_call(
        functools.partial(sums_kernel, first=first, fan=fan),
        grid=(steps,),
        in_specs=[SMEM_SPEC] * 2 + [VMEM_SPEC] * 3,
        out_specs=[pl.BlockSpec((slots, rows, LANES), lambda s: (s, 0, 0))] * n_out + [whole((8, rows))],
        out_shape=[out] * n_out + [jax.ShapeDtypeStruct((8, rows), F32)],
        scratch_shapes=[pltpu.VMEM((slots + 1, rows, LANES), F32)],
        compiler_params=params(32),
        cost_estimate=COST,
        name="chip_sums",
    )(lists, counts, probs, w_own, w_peer)


def logits_kernel(spot_ref, after_ref, near_ref, far_ref, head_ref, *refs):
    out_ref, turned_ref, everyone = refs
    n_tok = out_ref.shape[0]
    half = near_ref.shape[0] // n_tok
    del after_ref

    @pl.when(pl.program_id(0) == 0)
    def _():
        core = spot_ref[0]
        for r in range(n_tok):
            source = slice(r * half, (r + 1) * half)
            for side, ref in ((core, near_ref), (1 - core, far_ref)):
                start = pl.multiple_of((2 * r + side) * half, half)
                everyone[pl.ds(start, half), :] = ref[source, :]

    result = jnp.dot(everyone[...], head_ref[...], preferred_element_type=F32)
    for r in range(n_tok):
        out_ref[r] = result[2 * r * half : 2 * (r + 1) * half, :]
    part = turned_ref.shape[0]
    start = pl.multiple_of(pl.program_id(0) * part, part)
    turned_ref[...] = everyone[:, pl.ds(start, part)].T


def student_logits(spot, after, near, far, head, n_tok):
    every, depth = 2 * near.shape[0], near.shape[1]
    rows = every // n_tok
    cols = head.shape[1]
    tile = 256
    whole = lambda shape: pl.BlockSpec(shape, lambda i: (0, 0))
    return pl.pallas_call(
        logits_kernel,
        grid=(cols // tile,),
        in_specs=[SMEM_SPEC, pl.BlockSpec(memory_space=pl.ANY), whole(near.shape), whole(far.shape)]
        + [pl.BlockSpec((depth, tile), lambda i: (0, i))],
        out_specs=[pl.BlockSpec((n_tok, rows, tile), lambda i: (0, 0, i))]
        + [pl.BlockSpec((depth * tile // cols, every), lambda i: (i, 0))],
        out_shape=[jax.ShapeDtypeStruct((n_tok, rows, cols), F32), jax.ShapeDtypeStruct((depth, every), BF16)],
        scratch_shapes=[pltpu.VMEM((every, depth), BF16)],
        compiler_params=params(40),
        cost_estimate=COST,
        name="student_logits",
    )(spot, after, near, far, head)


def student_kernel(base_ref, labels_ref, mass_ref, logits_ref, stat_ref):
    n_tok, rows, cols = logits_ref.shape
    lane = lax.broadcasted_iota(jnp.int32, (rows, LANES), 1)
    label = labels_ref[...]
    top = jnp.full((rows, LANES), -jnp.inf, F32)
    hit = jnp.zeros((rows, LANES), F32)
    for t in range(n_tok):
        for b in range(0, cols, LANES):
            block = logits_ref[t, :, b : b + LANES]
            top = jnp.maximum(top, block)
            hit = hit + jnp.where(lane == label - (base_ref[t] + b), block, 0.0)
    top = jnp.max(top, axis=1, keepdims=True)
    total = jnp.zeros((rows, LANES), F32)
    for t in range(n_tok):
        for b in range(0, cols, LANES):
            total = total + jnp.exp(logits_ref[t, :, b : b + LANES] - top)
    total = jnp.sum(total, axis=1, keepdims=True)
    hit = jnp.sum(hit, axis=1, keepdims=True)
    tile = mass_ref[...] + rows_from_columns([jnp.zeros_like(hit), top, total, hit])
    stat_ref[...] = jnp.broadcast_to(tile, stat_ref.shape)


def student_stats(base, label_column, mass, logits, copies):
    return pl.pallas_call(
        student_kernel,
        in_specs=[SMEM_SPEC] + [VMEM_SPEC] * 3,
        out_specs=VMEM_SPEC,
        out_shape=jax.ShapeDtypeStruct((copies,) + mass.shape, F32),
        compiler_params=params(16),
        cost_estimate=COST,
        name="student_stats",
    )(base, label_column, mass, logits)


def grad_kernel(base_ref, labels_ref, stats, *refs, n_sums, first):
    sums = refs[:n_sums]
    logits_ref, grad_ref, loss_ref, columns, inner = refs[n_sums:]
    step = pl.program_id(0)
    _, rows, cols = logits_ref.shape

    @pl.when(step == 0)
    def _():
        parts = split_rows(stats)
        mass = tree(jnp.add, [r[0] for r in parts])
        top, total = total_at(parts, 1, 2)
        log_total = top + jnp.log(total)
        label_logit = tree(jnp.add, [r[3] for r in parts])
        columns[...] = columns_from_rows([mass + 1.0, log_total])
        inner[...] = jnp.zeros_like(inner)
        loss_ref[...] = jnp.zeros_like(loss_ref)
        loss_ref[0:1, :] = mass * log_total + log_total - label_logit

    lane = lax.broadcasted_iota(jnp.int32, (rows, LANES), 1)
    lift, log_total = columns[:, 0:1], columns[:, 1:2]
    label = labels_ref[...] - (base_ref[step] + first)
    running = inner[...]
    for b in range(cols // LANES):
        place = slice(b * LANES, (b + 1) * LANES)
        target = functools.reduce(jnp.add, [ref[z, b].astype(F32) for ref in sums for z in range(ref.shape[0])])
        score = logits_ref[0, :, place]
        running = running + target * score
        hit = jnp.where(lane == label - b * LANES, 1.0, 0.0)
        grad_ref[0, :, place] = (lift * jnp.exp(score - log_total) - target - hit).astype(BF16)
    inner[...] = running

    @pl.when(step == pl.num_programs(0) - 1)
    def _():
        loss_ref[1:2, :] = rows_from_columns([jnp.sum(inner[...], axis=1, keepdims=True)])[0:1, :]


def grad_logits(base, label_column, stats, sums, logits, part, parts):
    n_tok, rows, cols = logits.shape
    cols //= parts
    per = cols // LANES
    whole = lambda shape: pl.BlockSpec(shape, lambda t: (0,) * len(shape))
    return pl.pallas_call(
        functools.partial(grad_kernel, n_sums=len(sums), first=part * cols),
        grid=(n_tok,),
        in_specs=[SMEM_SPEC, whole(label_column.shape), whole(stats.shape)]
        + [pl.BlockSpec((s.shape[0], per, rows, LANES), lambda t: (0, parts * t + part, 0, 0)) for s in sums]
        + [pl.BlockSpec((1, rows, cols), lambda t: (t, 0, part))],
        out_specs=[pl.BlockSpec((1, rows, cols), lambda t: (t, 0, 0)), whole((8, rows))],
        out_shape=[jax.ShapeDtypeStruct((n_tok, rows, cols), BF16), jax.ShapeDtypeStruct((8, rows), F32)],
        scratch_shapes=[pltpu.VMEM((rows, LANES), F32), pltpu.VMEM((rows, LANES), F32)],
        compiler_params=params(24),
        cost_estimate=COST,
        name="grad_logits",
    )(base, label_column, stats, *sums, logits)


def product_kernel(a_ref, b_ref, *refs):
    o_ref = refs[-1]
    o_ref[...] = jnp.dot(a_ref[...], b_ref[...], preferred_element_type=F32).astype(o_ref.dtype)


def head_product(a, b, part, parts, earlier):
    m, k = a.shape
    n = b.shape[1]
    tile = m // 4
    return pl.pallas_call(
        product_kernel,
        grid=(m // tile,),
        in_specs=[pl.BlockSpec((tile, k), lambda i: (i, 0)), pl.BlockSpec((k, n), lambda i: (0, 0))]
        + [pl.BlockSpec(memory_space=pl.ANY)] * len(earlier),
        out_specs=pl.BlockSpec((tile, n), lambda i: (i, part)),
        out_shape=jax.ShapeDtypeStruct((m, n * parts), BF16),
        input_output_aliases={2: 0} if earlier else {},
        compiler_params=params(32),
        cost_estimate=COST,
        name="head_product",
    )(a, b, *earlier)


def plus_kernel(a_ref, b_ref, o_ref):
    o_ref[...] = (a_ref[...].astype(F32) + b_ref[...].astype(F32)).astype(BF16)


def plus(a, b):
    blocks = 4
    spec = pl.BlockSpec((a.shape[0] // blocks,) + a.shape[1:], lambda i: (i, 0, 0))
    return pl.pallas_call(
        plus_kernel,
        grid=(blocks,),
        in_specs=[spec, spec],
        out_specs=spec,
        out_shape=jax.ShapeDtypeStruct(a.shape, BF16),
        compiler_params=params(16),
        cost_estimate=COST,
        name="merge",
    )(a, b)


def swap(x, axis, mask):
    return lax.ppermute(x, axis, [(i, i ^ mask) for i in range(lax.axis_size(axis))])


def gather_vocab(copies):
    return lax.all_to_all(copies, "vocab", split_axis=0, concat_axis=0, tiled=True)


def exchange_tok(x):
    return lax.all_to_all(x, "tok", split_axis=0, concat_axis=0, tiled=True)


def send(x, hops):
    return lax.ppermute(x, "vocab", [(2 * a + c, 2 * b + c) for a, b in hops for c in range(2)])


def local(teacher_logits, hidden, new_head, labels, map_target, map_weight):
    rows = teacher_logits.shape[0]
    block = map_weight.shape[2]
    n_tok = lax.axis_size("tok")
    n_vocab = lax.axis_size("vocab")
    n_z = n_vocab // 2
    new_cols = new_head.shape[1]
    per = new_cols // block
    tok = lax.axis_index("tok")
    vocab = lax.axis_index("vocab")
    spot = jnp.stack([vocab % 2, vocab // 2]).astype(jnp.int32)
    slots = n_tok * per
    in_line = n_z == 4

    peer_logits = swap(teacher_logits, "vocab", 1)
    peer_target = swap(map_target, "vocab", 1)
    peer_weight = swap(map_weight, "vocab", 1)
    teacher = teacher_stats(teacher_logits, n_vocab)
    totals = gather_vocab(teacher)
    half = lax.dynamic_slice_in_dim(hidden, spot[0] * (rows // 2), rows // 2)
    half, teacher = lax.optimization_barrier((half, teacher))
    near = exchange_tok(jnp.broadcast_to(half, (n_tok,) + half.shape)).reshape(n_tok * (rows // 2), -1)
    lists, counts = plan(spot, map_target, peer_target, n_z, per, n_vocab, in_line)
    probs = teacher_probs(teacher_logits, peer_logits, totals)

    if in_line:
        inward, across, outward = [(0, 1), (3, 2)], [(1, 2), (2, 1)], [(1, 0), (2, 3)]
        far_outer, far_inner, mass_a = chip_sums(lists, counts, probs, map_weight, peer_weight, 0, 2, 1, slots)
        first = send(far_outer, inward)
        second = send(far_inner, inward)
        probs, mass_a = lax.optimization_barrier((probs, mass_a))
        beside, own, mass_b = chip_sums(lists, counts, probs, map_weight, peer_weight, 2, 2, 1, slots)
        mass = mass_a + mass_b
    else:
        sums, mass = chip_sums(lists, counts, probs, map_weight, peer_weight, 0, 1, n_z, slots)
        lines = [[2 * z + c for z in range(n_z)] for c in range(2)]
        sums = lax.all_to_all(
            sums.reshape(n_z, slots, rows, block),
            "vocab",
            split_axis=0,
            concat_axis=0,
            axis_index_groups=lines,
            tiled=True,
        )
        sums = [sums]

    near, mass = lax.optimization_barrier((near, mass))
    far = swap(near, "vocab", 1)
    scores, turned = student_logits(spot, mass, near, far, new_head, n_tok)
    scores = exchange_tok(scores)
    label_column = lax.dynamic_slice_in_dim(labels, tok * rows, rows).reshape(rows, 1)
    base = (jnp.arange(n_tok, dtype=jnp.int32) * n_vocab + vocab) * new_cols
    if in_line:
        first, turned = lax.optimization_barrier((first, turned))
        merged = plus(far_outer, first)
        crossed_outer = send(merged, across)
        waited, merged = lax.optimization_barrier((beside, merged))
        third = send(waited, inward)
        scores, merged = lax.optimization_barrier((scores, merged))
        student = student_stats(base, label_column, mass, scores, n_vocab)
        second, student = lax.optimization_barrier((second, student))
        merged_inner = plus(far_inner, second)
        crossed_inner = send(merged_inner, across)
        crossed_outer, merged_inner = lax.optimization_barrier((crossed_outer, merged_inner))
        merged_near = plus(beside, crossed_outer)
        arrived = send(merged_near, outward)
        student, merged_near = lax.optimization_barrier((student, merged_near))
        sums = [x[None] for x in (own, third, crossed_inner, arrived)]
    else:
        student = student_stats(base, label_column, mass, scores, n_vocab)
    stats = gather_vocab(student)

    parts = 2
    swapped, inner = [], 0.0
    for part in range(parts):
        if part:
            scores, grads = lax.optimization_barrier((scores, grads))
        grads, loss_rows = grad_logits(base, label_column, stats, sums, scores, part, parts)
        swapped.append(exchange_tok(grads).reshape(n_tok * rows, -1))
        inner = inner + loss_rows[1]
    inner = gather_vocab(jnp.broadcast_to(inner, (n_vocab, 1, rows)))
    loss = loss_rows[0] - jnp.sum(inner, axis=(0, 1))
    head_grad = head_product(turned, swapped[0], 0, parts, [])
    for part in range(1, parts):
        late, head_grad = lax.optimization_barrier((swapped[part], head_grad))
        head_grad = head_product(turned, late, part, parts, [head_grad])
    return (loss, head_grad)


def solution(mesh):
    return jax.shard_map(
        local,
        mesh=mesh,
        in_specs=(
            P("tok", "vocab"),
            P("tok", None),
            P(None, ("tok", "vocab")),
            P(),
            P("vocab", None),
            P("vocab", None, None, None),
        ),
        out_specs=(P("tok"), P(None, ("tok", "vocab"))),
        check_vma=False,
    )
```

```python
import functools

import jax
import jax.numpy as jnp
from jax import lax
from jax.experimental import pallas as pl
from jax.experimental.pallas import tpu as pltpu
from jax.sharding import PartitionSpec as P

F32 = jnp.float32
BF16 = jnp.bfloat16
LANES = 128
BATCH = 4
COST = pl.CostEstimate(flops=1024, bytes_accessed=1024, transcendentals=0)
SLOT_BASE = 1024
SMEM_SPEC = pl.BlockSpec(memory_space=pltpu.SMEM)
VMEM_SPEC = pl.BlockSpec(memory_space=pltpu.VMEM)


def params(mebibytes):
    return pltpu.CompilerParams(vmem_limit_bytes=mebibytes * 1024 * 1024)


def tree(op, items):
    while len(items) > 1:
        items = [op(items[i], items[i + 1]) if i + 1 < len(items) else items[i] for i in range(0, len(items), 2)]
    return items[0]


def total_at(rows_of, top_row, total_row):
    top = tree(jnp.maximum, [r[top_row] for r in rows_of])
    total = tree(jnp.add, [r[total_row] * jnp.exp(r[top_row] - top) for r in rows_of])
    return top, total


def split_rows(refs):
    return [[ref[k : k + 1, :] for k in range(8)] for ref in refs]


def rows_from_columns(columns):
    n = columns[0].shape[0]
    lane = lax.broadcasted_iota(jnp.int32, (n, LANES), 1)
    tile = jnp.zeros((n, LANES), F32)
    for place, column in enumerate(columns):
        tile = jnp.where(lane == place, column, tile)
    return tile.T[0:8, :]


def columns_from_rows(rows):
    n = rows[0].shape[1]
    return jnp.concatenate(rows + [jnp.zeros((LANES - len(rows), n), F32)], axis=0).T


def teacher_kernel(x_ref, stat_ref):
    rows, cols = x_ref.shape
    places = range(0, cols, LANES)
    read = lambda place: x_ref[:, place : place + LANES].astype(F32)
    top = jnp.full((rows, LANES), -jnp.inf, F32)
    for place in places:
        top = jnp.maximum(top, read(place))
    top = jnp.max(top, axis=1, keepdims=True)
    total = jnp.zeros((rows, LANES), F32)
    for place in places:
        total = total + jnp.exp(read(place) - top)
    stat_ref[...] = rows_from_columns([top, jnp.sum(total, axis=1, keepdims=True)])


def teacher_stats(x):
    return pl.pallas_call(
        teacher_kernel,
        in_specs=[VMEM_SPEC],
        out_specs=VMEM_SPEC,
        out_shape=jax.ShapeDtypeStruct((8, x.shape[0]), F32),
        compiler_params=params(16),
        cost_estimate=COST,
        name="teacher_stats",
    )(x)


def divide(x, n):
    return lax.shift_right_logical(x, n.bit_length() - 1) if n & (n - 1) == 0 else x // n


def plan_kernel(spot_ref, own_ref, peer_ref, list_ref, count_ref, *, per, n_vocab, in_line):
    core, z = spot_ref[0], spot_ref[1]
    pieces = count_ref.shape[0]
    entries, fan = own_ref.shape

    def visit(i, counts):
        counts = list(counts)
        for side, ref in enumerate((own_ref, peer_ref)):
            for f in range(fan):
                block = ref[i, f]
                owner = divide(block, per)
                owner_tok = divide(owner, n_vocab)
                owner_vocab = owner - owner_tok * n_vocab
                owner_z = divide(owner_vocab, 2)
                slot = owner_tok * per + block - owner * per
                if in_line:
                    outer = (owner_z == 0) | (owner_z == 3)
                    near = jnp.where(owner_z == z, 3, 2)
                    place = jnp.where(divide(owner_z, 2) == divide(z, 2), near, jnp.where(outer, 0, 1))
                else:
                    place = owner_z
                place = jnp.where(owner_vocab - owner_z * 2 == core, place, pieces)
                n = 0
                for p in range(pieces):
                    n = jnp.where(place == p, counts[p], n)
                    counts[p] = counts[p] + jnp.where(place == p, 1, 0)
                list_ref[place, n] = ((side * entries + i) * fan + f) * SLOT_BASE + slot
        return tuple(counts)

    counts = lax.fori_loop(0, entries, visit, (jnp.int32(0),) * pieces)
    for p in range(pieces):
        count_ref[p] = counts[p]
        for k in range(BATCH - 1):
            list_ref[p, counts[p] + k] = SLOT_BASE - 1


def plan(spot, own_target, peer_target, pieces, per, n_vocab, in_line):
    room = 2 * own_target.size + BATCH
    return pl.pallas_call(
        functools.partial(plan_kernel, per=per, n_vocab=n_vocab, in_line=in_line),
        in_specs=[SMEM_SPEC] * 3,
        out_specs=[SMEM_SPEC] * 2,
        out_shape=[jax.ShapeDtypeStruct((pieces + 1, room), jnp.int32), jax.ShapeDtypeStruct((pieces,), jnp.int32)],
        cost_estimate=COST,
        name="entry_lists",
    )(spot, own_target, peer_target)


def probs_kernel(x_own, x_peer, *refs):
    stats, probs = refs[:-1], refs[-1]
    blocks = x_own.shape[1] // LANES
    top, total = total_at(split_rows(stats), 0, 1)
    columns = columns_from_rows([top, 1.0 / total])
    top, scale = columns[:, 0:1], columns[:, 1:2]
    for side, x in enumerate((x_own, x_peer)):
        for j in range(blocks):
            raised = jnp.exp(x[:, j * LANES : (j + 1) * LANES].astype(F32) - top)
            probs[side * blocks + j] = (raised * scale).astype(BF16)


def sums_kernel(list_ref, count_ref, probs, w_own, w_peer, *refs, first, fan):
    outs, mass_ref, acc = refs[:-2], refs[-2], refs[-1]
    step = pl.program_id(0)
    slots, rows, _ = outs[0].shape
    side = w_own.shape[0] * fan
    mass = jnp.zeros((rows, LANES), F32)
    for k, out in enumerate(outs):
        piece = first + k + step
        acc[...] = jnp.zeros_like(acc)

        def add(i, carry):
            parts = []
            for u in range(BATCH):
                item = list_ref[piece, i * BATCH + u]
                slot = item & (SLOT_BASE - 1)
                entry = lax.shift_right_logical(item, SLOT_BASE.bit_length() - 1)
                weight = jnp.where(entry < side, 0, 1)
                parts.append((entry, slot, weight))
            for entry, slot, peer in parts:
                j = divide(entry, fan)
                f = entry - j * fan
                local_j = j - peer * (side // fan)
                weight = jnp.where(peer == 1, w_peer[local_j, f], w_own[local_j, f])
                part = jnp.dot(probs[j], weight, preferred_element_type=F32)
                acc[jnp.minimum(slot, slots)] += part.astype(BF16).astype(F32)
            return carry

        lax.fori_loop(0, divide(count_ref[piece] + BATCH - 1, BATCH), add, 0)

        def drain(i, mass):
            block = acc[i]
            out[i] = block.astype(BF16)
            return mass + block

        mass = lax.fori_loop(0, slots, drain, mass, unroll=4)
    part = rows_from_columns([jnp.sum(mass, axis=1, keepdims=True)])

    @pl.when(step == 0)
    def _():
        mass_ref[...] = part

    @pl.when(step > 0)
    def _():
        mass_ref[...] += part


def teacher_probs(x_own, x_peer, stats):
    rows, cols = x_own.shape
    return pl.pallas_call(
        probs_kernel,
        in_specs=[VMEM_SPEC] * (2 + len(stats)),
        out_specs=VMEM_SPEC,
        out_shape=jax.ShapeDtypeStruct((2 * cols // LANES, rows, LANES), BF16),
        compiler_params=params(16),
        cost_estimate=COST,
        name="teacher_probs",
    )(x_own, x_peer, *stats)


def chip_sums(lists, counts, probs, w_own, w_peer, first, n_out, steps, slots):
    rows = probs.shape[1]
    fan = w_own.shape[1]
    whole = lambda shape: pl.BlockSpec(shape, lambda s: (0,) * len(shape))
    out = pltpu.HBM((steps * slots, rows, LANES), BF16)
    return pl.pallas_call(
        functools.partial(sums_kernel, first=first, fan=fan),
        grid=(steps,),
        in_specs=[SMEM_SPEC] * 2 + [VMEM_SPEC] * 3,
        out_specs=[pl.BlockSpec((slots, rows, LANES), lambda s: (s, 0, 0))] * n_out + [whole((8, rows))],
        out_shape=[out] * n_out + [jax.ShapeDtypeStruct((8, rows), F32)],
        scratch_shapes=[pltpu.VMEM((slots + 1, rows, LANES), F32)],
        compiler_params=params(32),
        cost_estimate=COST,
        name="chip_sums",
    )(lists, counts, probs, w_own, w_peer)


def logits_kernel(spot_ref, after_ref, near_ref, far_ref, head_ref, *refs):
    out_ref, turned_ref, everyone = refs
    n_tok = out_ref.shape[0]
    half = near_ref.shape[0] // n_tok
    del after_ref

    @pl.when(pl.program_id(0) == 0)
    def _():
        core = spot_ref[0]
        for r in range(n_tok):
            source = slice(r * half, (r + 1) * half)
            for side, ref in ((core, near_ref), (1 - core, far_ref)):
                start = pl.multiple_of((2 * r + side) * half, half)
                everyone[pl.ds(start, half), :] = ref[source, :]

    result = jnp.dot(everyone[...], head_ref[...], preferred_element_type=F32)
    for r in range(n_tok):
        out_ref[r] = result[2 * r * half : 2 * (r + 1) * half, :]
    part = turned_ref.shape[0]
    start = pl.multiple_of(pl.program_id(0) * part, part)
    turned_ref[...] = everyone[:, pl.ds(start, part)].T


def student_logits(spot, after, near, far, head, n_tok):
    every, depth = 2 * near.shape[0], near.shape[1]
    rows = every // n_tok
    cols = head.shape[1]
    tile = 256
    whole = lambda shape: pl.BlockSpec(shape, lambda i: (0, 0))
    return pl.pallas_call(
        logits_kernel,
        grid=(cols // tile,),
        in_specs=[SMEM_SPEC, pl.BlockSpec(memory_space=pl.ANY), whole(near.shape), whole(far.shape)]
        + [pl.BlockSpec((depth, tile), lambda i: (0, i))],
        out_specs=[pl.BlockSpec((n_tok, rows, tile), lambda i: (0, 0, i))]
        + [pl.BlockSpec((depth * tile // cols, every), lambda i: (i, 0))],
        out_shape=[pltpu.HBM((n_tok, rows, cols), F32), pltpu.HBM((depth, every), BF16)],
        scratch_shapes=[pltpu.VMEM((every, depth), BF16)],
        compiler_params=params(40),
        cost_estimate=COST,
        name="student_logits",
    )(spot, after, near, far, head)


def student_kernel(base_ref, labels_ref, mass_ref, logits_ref, stat_ref):
    n_tok, rows, cols = logits_ref.shape
    lane = lax.broadcasted_iota(jnp.int32, (rows, LANES), 1)
    label = labels_ref[...]
    top = jnp.full((rows, LANES), -jnp.inf, F32)
    hit = jnp.zeros((rows, LANES), F32)
    for t in range(n_tok):
        for b in range(0, cols, LANES):
            block = logits_ref[t, :, b : b + LANES]
            top = jnp.maximum(top, block)
            hit = hit + jnp.where(lane == label - (base_ref[t] + b), block, 0.0)
    top = jnp.max(top, axis=1, keepdims=True)
    total = jnp.zeros((rows, LANES), F32)
    for t in range(n_tok):
        for b in range(0, cols, LANES):
            total = total + jnp.exp(logits_ref[t, :, b : b + LANES] - top)
    total = jnp.sum(total, axis=1, keepdims=True)
    hit = jnp.sum(hit, axis=1, keepdims=True)
    stat_ref[...] = mass_ref[...] + rows_from_columns([jnp.zeros_like(hit), top, total, hit])


def student_stats(base, label_column, mass, logits):
    return pl.pallas_call(
        student_kernel,
        in_specs=[SMEM_SPEC] + [VMEM_SPEC] * 3,
        out_specs=VMEM_SPEC,
        out_shape=jax.ShapeDtypeStruct(mass.shape, F32),
        compiler_params=params(16),
        cost_estimate=COST,
        name="student_stats",
    )(base, label_column, mass, logits)


def grad_kernel(tok_ref, base_ref, labels_ref, *refs, n_stats, n_sums):
    stats, sums = refs[:n_stats], refs[n_stats : n_stats + n_sums]
    logits_ref, *grads, loss_ref, columns, inner = refs[n_stats + n_sums :]
    step = pl.program_id(0)
    _, rows, cols = logits_ref.shape

    @pl.when(step == 0)
    def _():
        parts = split_rows(stats)
        mass = tree(jnp.add, [r[0] for r in parts])
        top, total = total_at(parts, 1, 2)
        log_total = top + jnp.log(total)
        label_logit = tree(jnp.add, [r[3] for r in parts])
        columns[...] = columns_from_rows([mass + 1.0, log_total])
        inner[...] = jnp.zeros_like(inner)
        loss_ref[...] = jnp.zeros_like(loss_ref)
        loss_ref[0:1, :] = mass * log_total + log_total - label_logit

    lane = lax.broadcasted_iota(jnp.int32, (rows, LANES), 1)
    lift, log_total = columns[:, 0:1], columns[:, 1:2]
    label = labels_ref[...] - base_ref[token_group(step, tok_ref, len(grads))]
    for r in range(len(grads)):

        @pl.when(step == r)
        def _():
            running = inner[...]
            for b in range(cols // LANES):
                place = slice(b * LANES, (b + 1) * LANES)
                target = functools.reduce(
                    jnp.add, [ref[z, b].astype(F32) for ref in sums for z in range(ref.shape[0])]
                )
                score = logits_ref[0, :, place]
                running = running + target * score
                hit = jnp.where(lane == label - b * LANES, 1.0, 0.0)
                grads[r][:, place] = (lift * jnp.exp(score - log_total) - target - hit).astype(BF16)
            inner[...] = running

    @pl.when(step == pl.num_programs(0) - 1)
    def _():
        loss_ref[1:2, :] = rows_from_columns([jnp.sum(inner[...], axis=1, keepdims=True)])[0:1, :]


def token_group(step, tok_ref, n_tok):
    return tok_ref[0] ^ (n_tok - 1 - step)


def grad_logits(tok, base, label_column, stats, sums, logits):
    n_tok, rows, cols = logits.shape
    per = cols // LANES
    whole = lambda shape: pl.BlockSpec(shape, lambda t, tok_ref: (0,) * len(shape))
    group = lambda t, tok_ref: token_group(t, tok_ref, n_tok)
    return pl.pallas_call(
        functools.partial(grad_kernel, n_stats=len(stats), n_sums=len(sums)),
        grid_spec=pltpu.PrefetchScalarGridSpec(
            num_scalar_prefetch=1,
            grid=(n_tok,),
            in_specs=[SMEM_SPEC, whole(label_column.shape)]
            + [whole(s.shape) for s in stats]
            + [pl.BlockSpec((s.shape[0], per, rows, LANES), lambda t, r: (0, group(t, r), 0, 0)) for s in sums]
            + [pl.BlockSpec((1, rows, cols), lambda t, r: (group(t, r), 0, 0))],
            out_specs=[whole((rows, cols))] * n_tok + [whole((8, rows))],
            scratch_shapes=[pltpu.VMEM((rows, LANES), F32), pltpu.VMEM((rows, LANES), F32)],
        ),
        out_shape=[pltpu.HBM((rows, cols), BF16)] * n_tok + [jax.ShapeDtypeStruct((8, rows), F32)],
        compiler_params=params(24),
        cost_estimate=COST,
        name="grad_logits",
    )(tok, base, label_column, *stats, *sums, logits)


def product_kernel(tok_ref, a_ref, *refs):
    pieces, o_ref, b_ref = refs[:-2], refs[-2], refs[-1]
    rows = pieces[0].shape[0]

    @pl.when(pl.program_id(0) == 0)
    def _():
        for r, piece in enumerate(pieces):
            start = pl.multiple_of(token_group(r, tok_ref, len(pieces)) * rows, rows)
            b_ref[pl.ds(start, rows), :] = piece[...]

    o_ref[...] = jnp.dot(a_ref[...], b_ref[...], preferred_element_type=F32).astype(o_ref.dtype)


def head_product(tok, a, pieces):
    m, k = a.shape
    rows, n = pieces[0].shape
    tile = m // 4
    return pl.pallas_call(
        product_kernel,
        grid=(m // tile,),
        in_specs=[SMEM_SPEC, pl.BlockSpec((tile, k), lambda i: (i, 0))]
        + [pl.BlockSpec((rows, n), lambda i: (0, 0))] * len(pieces),
        out_specs=pl.BlockSpec((tile, n), lambda i: (i, 0)),
        out_shape=jax.ShapeDtypeStruct((m, n), BF16),
        scratch_shapes=[pltpu.VMEM((k, n), BF16)],
        compiler_params=params(32),
        cost_estimate=COST,
        name="head_product",
    )(tok, pltpu.with_memory_space_constraint(a, pltpu.HBM), *pieces)


def swap(x, axis, mask):
    return lax.ppermute(x, axis, [(i, i ^ mask) for i in range(lax.axis_size(axis))])


def gather_chips(x):
    n = lax.axis_size("vocab")
    if n > 8:
        lines = [[2 * z + c for z in range(n // 2)] for c in range(2)]
        everything = lax.all_gather(x, "vocab", axis=0, axis_index_groups=lines)
        return [everything[z] for z in range(n // 2)]
    return [x] + [swap(x, "vocab", r) for r in range(2, n, 2)]


def gather_cores(x):
    chips = gather_chips(x)
    return chips + [swap(chip, "vocab", 1) for chip in chips]


def plus(a, b):
    return (a.astype(F32) + b.astype(F32)).astype(BF16)


def exchange_tok(x):
    return lax.all_to_all(x, "tok", split_axis=0, concat_axis=0, tiled=True)


def send(x, hops):
    return lax.ppermute(x, "vocab", [(2 * a + c, 2 * b + c) for a, b in hops for c in range(2)])


def local(teacher_logits, hidden, new_head, labels, map_target, map_weight):
    rows = teacher_logits.shape[0]
    block = map_weight.shape[2]
    n_tok = lax.axis_size("tok")
    n_vocab = lax.axis_size("vocab")
    n_z = n_vocab // 2
    new_cols = new_head.shape[1]
    per = new_cols // block
    tok = lax.axis_index("tok")
    vocab = lax.axis_index("vocab")
    spot = jnp.stack([vocab % 2, vocab // 2]).astype(jnp.int32)
    slots = n_tok * per
    in_line = n_z == 4

    peer_logits = swap(teacher_logits, "vocab", 1)
    peer_target = swap(map_target, "vocab", 1)
    peer_weight = swap(map_weight, "vocab", 1)
    teacher = teacher_stats(teacher_logits)
    totals = gather_cores(teacher)
    half = lax.dynamic_slice_in_dim(hidden, spot[0] * (rows // 2), rows // 2)
    half, teacher = lax.optimization_barrier((half, teacher))
    near = exchange_tok(jnp.broadcast_to(half, (n_tok,) + half.shape)).reshape(n_tok * (rows // 2), -1)
    lists, counts = plan(spot, map_target, peer_target, n_z, per, n_vocab, in_line)
    probs = teacher_probs(teacher_logits, peer_logits, totals)

    if in_line:
        inward, across, outward = [(0, 1), (3, 2)], [(1, 2), (2, 1)], [(1, 0), (2, 3)]
        far_outer, far_inner, mass_a = chip_sums(lists, counts, probs, map_weight, peer_weight, 0, 2, 1, slots)
        first = send(far_outer, inward)
        second = send(far_inner, inward)
        probs, mass_a = lax.optimization_barrier((probs, mass_a))
        beside, own, mass_b = chip_sums(lists, counts, probs, map_weight, peer_weight, 2, 2, 1, slots)
        first, mass = lax.optimization_barrier((first, mass_a + mass_b))
        merged = plus(far_outer, first)
        crossed_outer = send(merged, across)
        waited, near, after = lax.optimization_barrier((beside, near, merged))
        third = send(waited, inward)
    else:
        sums, mass = chip_sums(lists, counts, probs, map_weight, peer_weight, 0, 1, n_z, slots)
        lines = [[2 * z + c for z in range(n_z)] for c in range(2)]
        sums = lax.all_to_all(
            sums.reshape(n_z, slots, rows, block),
            "vocab",
            split_axis=0,
            concat_axis=0,
            axis_index_groups=lines,
            tiled=True,
        )
        sums = [sums]
        after = mass

    far = swap(near, "vocab", 1)
    scores, turned = student_logits(spot, after, near, far, new_head, n_tok)
    scores = exchange_tok(scores)
    label_column = lax.dynamic_slice_in_dim(labels, tok * rows, rows).reshape(rows, 1)
    base = (jnp.arange(n_tok, dtype=jnp.int32) * n_vocab + vocab) * new_cols
    if in_line:
        second, turned = lax.optimization_barrier((second, turned))
        merged_inner = plus(far_inner, second)
        crossed_inner = send(merged_inner, across)
        crossed_outer, merged_inner = lax.optimization_barrier((crossed_outer, merged_inner))
        merged_near = plus(beside, crossed_outer)
        arrived = send(merged_near, outward)
        scores, merged_near = lax.optimization_barrier((scores, merged_near))
        sums = [x[None] for x in (own, third, crossed_inner, arrived)]
    stats = gather_cores(student_stats(base, label_column, mass, scores))

    group = tok.astype(jnp.int32).reshape(1)
    *grads, loss_rows = grad_logits(group, base, label_column, stats, sums, scores)
    grads = [swap(x, "tok", n_tok - 1 - r) for r, x in enumerate(grads[:-1])] + [grads[-1]]
    inner = loss_rows[1]
    mask = 1
    while mask < n_vocab:
        inner = inner + swap(inner, "vocab", mask)
        mask *= 2
    return (loss_rows[0] - inner, head_product(group, turned, grads))


def solution(mesh):
    return jax.shard_map(
        local,
        mesh=mesh,
        in_specs=(
            P("tok", "vocab"),
            P("tok", None),
            P(None, ("tok", "vocab")),
            P(),
            P("vocab", None),
            P("vocab", None, None, None),
        ),
        out_specs=(P("tok"), P(None, ("tok", "vocab"))),
        check_vma=False,
    )
```

```python
import functools

import jax
import jax.numpy as jnp
from jax import lax
from jax.experimental import pallas as pl
from jax.experimental.pallas import tpu as pltpu
from jax.sharding import PartitionSpec as P

F32 = jnp.float32
BF16 = jnp.bfloat16
LANES = 128
BATCH = 8
COST = pl.CostEstimate(flops=1024, bytes_accessed=1024, transcendentals=0)
SLOT_BITS = 10
SLOT_BASE = 1 << SLOT_BITS
SMEM_SPEC = pl.BlockSpec(memory_space=pltpu.SMEM)
VMEM_SPEC = pl.BlockSpec(memory_space=pltpu.VMEM)


def params(mebibytes):
    return pltpu.CompilerParams(vmem_limit_bytes=mebibytes * 1024 * 1024)


def tree(op, items):
    while len(items) > 1:
        items = [op(items[i], items[i + 1]) if i + 1 < len(items) else items[i] for i in range(0, len(items), 2)]
    return items[0]


def total_at(rows_of, top_row, total_row):
    top = tree(jnp.maximum, [r[top_row] for r in rows_of])
    total = tree(jnp.add, [r[total_row] * jnp.exp(r[top_row] - top) for r in rows_of])
    return top, total


def split_rows(refs):
    return [[ref[k : k + 1, :] for k in range(8)] for ref in refs]


def rows_from_columns(columns):
    n = columns[0].shape[0]
    lane = lax.broadcasted_iota(jnp.int32, (n, LANES), 1)
    tile = jnp.zeros((n, LANES), F32)
    for place, column in enumerate(columns):
        tile = jnp.where(lane == place, column, tile)
    return tile.T[0:8, :]


def columns_from_rows(rows):
    n = rows[0].shape[1]
    return jnp.concatenate(rows + [jnp.zeros((LANES - len(rows), n), F32)], axis=0).T


def teacher_kernel(x_ref, stat_ref):
    rows, cols = x_ref.shape
    places = range(0, cols, LANES)
    read = lambda place: x_ref[:, place : place + LANES].astype(F32)
    top = jnp.full((rows, LANES), -jnp.inf, F32)
    for place in places:
        top = jnp.maximum(top, read(place))
    top = jnp.max(top, axis=1, keepdims=True)
    total = jnp.zeros((rows, LANES), F32)
    for place in places:
        total = total + jnp.exp(read(place) - top)
    stat_ref[...] = rows_from_columns([top, jnp.sum(total, axis=1, keepdims=True)])


def teacher_stats(x):
    return pl.pallas_call(
        teacher_kernel,
        in_specs=[VMEM_SPEC],
        out_specs=VMEM_SPEC,
        out_shape=jax.ShapeDtypeStruct((8, x.shape[0]), F32),
        compiler_params=params(16),
        cost_estimate=COST,
        name="teacher_stats",
    )(x)


def divide(x, n):
    return lax.shift_right_logical(x, n.bit_length() - 1) if n & (n - 1) == 0 else x // n


def plan_kernel(own_ref, peer_ref, list_ref, count_ref):
    lists = count_ref.shape[0]
    entries = own_ref.shape[0]
    for p in range(lists):
        count_ref[p] = 0

    def visit(i, carry):
        for side, ref in enumerate((own_ref, peer_ref)):
            code = ref[i]
            row = lax.shift_right_logical(code, SLOT_BITS)
            n = count_ref[row]
            list_ref[row, n] = (side * entries + i) * SLOT_BASE + (code & (SLOT_BASE - 1))
            count_ref[row] = n + 1
        return carry

    lax.fori_loop(0, entries, visit, 0, unroll=8)
    for p in range(lists):
        n = count_ref[p]
        for k in range(BATCH - 1):
            list_ref[p, n + k] = SLOT_BASE - 1


def plan(own_code, peer_code, lists):
    room = 2 * own_code.size + BATCH
    return pl.pallas_call(
        plan_kernel,
        in_specs=[SMEM_SPEC] * 2,
        out_specs=[SMEM_SPEC] * 2,
        out_shape=[jax.ShapeDtypeStruct((lists, room), jnp.int32), jax.ShapeDtypeStruct((lists,), jnp.int32)],
        cost_estimate=COST,
        name="entry_lists",
    )(own_code, peer_code)


def probs_kernel(x_own, x_peer, *refs):
    stats, probs = refs[:-1], refs[-1]
    blocks = x_own.shape[1] // LANES
    top, total = total_at(split_rows(stats), 0, 1)
    columns = columns_from_rows([top, 1.0 / total])
    top, scale = columns[:, 0:1], columns[:, 1:2]
    for side, x in enumerate((x_own, x_peer)):
        for j in range(blocks):
            raised = jnp.exp(x[:, j * LANES : (j + 1) * LANES].astype(F32) - top)
            probs[side * blocks + j] = (raised * scale).astype(BF16)


def sums_kernel(spot_ref, list_ref, count_ref, probs, w_own, w_peer, *refs, first, fan, pieces):
    outs, mass_ref, acc = refs[:-2], refs[-2], refs[-1]
    step = pl.program_id(0)
    slots, rows, _ = outs[0].shape
    side = w_own.shape[0] * fan
    mass = jnp.zeros((rows, LANES), F32)
    for k, out in enumerate(outs):
        piece = spot_ref[0] * pieces + first + k + step
        acc[...] = jnp.zeros_like(acc)

        def add(i, carry):
            parts = []
            for u in range(BATCH):
                item = list_ref[piece, i * BATCH + u]
                slot = item & (SLOT_BASE - 1)
                entry = lax.shift_right_logical(item, SLOT_BITS)
                weight = jnp.where(entry < side, 0, 1)
                parts.append((entry, slot, weight))
            for entry, slot, peer in parts:
                j = divide(entry, fan)
                f = entry - j * fan
                local_j = j - peer * (side // fan)
                weight = jnp.where(peer == 1, w_peer[local_j, f], w_own[local_j, f])
                part = jnp.dot(probs[j], weight, preferred_element_type=F32)
                acc[jnp.minimum(slot, slots)] += part.astype(BF16).astype(F32)
            return carry

        lax.fori_loop(0, divide(count_ref[piece] + BATCH - 1, BATCH), add, 0)

        def drain(i, mass):
            block = acc[i]
            out[i] = block.astype(BF16)
            return mass + block

        mass = lax.fori_loop(0, slots, drain, mass, unroll=4)
    part = rows_from_columns([jnp.sum(mass, axis=1, keepdims=True)])

    @pl.when(step == 0)
    def _():
        mass_ref[...] = part

    @pl.when(step > 0)
    def _():
        mass_ref[...] += part


def teacher_probs(x_own, x_peer, stats):
    rows, cols = x_own.shape
    return pl.pallas_call(
        probs_kernel,
        in_specs=[VMEM_SPEC] * (2 + len(stats)),
        out_specs=VMEM_SPEC,
        out_shape=jax.ShapeDtypeStruct((2 * cols // LANES, rows, LANES), BF16),
        compiler_params=params(16),
        cost_estimate=COST,
        name="teacher_probs",
    )(x_own, x_peer, *stats)


def chip_sums(spot, lists, counts, probs, w_own, w_peer, first, n_out, steps, slots):
    rows = probs.shape[1]
    fan = w_own.shape[1]
    whole = lambda shape: pl.BlockSpec(shape, lambda s: (0,) * len(shape))
    out = pltpu.HBM((steps * slots, rows, LANES), BF16)
    return pl.pallas_call(
        functools.partial(sums_kernel, first=first, fan=fan, pieces=counts.shape[0] // 2),
        grid=(steps,),
        in_specs=[SMEM_SPEC] * 3 + [VMEM_SPEC] * 3,
        out_specs=[pl.BlockSpec((slots, rows, LANES), lambda s: (s, 0, 0))] * n_out + [whole((8, rows))],
        out_shape=[out] * n_out + [jax.ShapeDtypeStruct((8, rows), F32)],
        scratch_shapes=[pltpu.VMEM((slots + 1, rows, LANES), F32)],
        compiler_params=params(32),
        cost_estimate=COST,
        name="chip_sums",
    )(spot, lists, counts, probs, w_own, w_peer)


def logits_kernel(spot_ref, after_ref, near_ref, far_ref, head_ref, *refs):
    out_ref, turned_ref, everyone = refs
    n_tok = out_ref.shape[0]
    half = near_ref.shape[0] // n_tok
    del after_ref

    @pl.when(pl.program_id(0) == 0)
    def _():
        core = spot_ref[0]
        for r in range(n_tok):
            source = slice(r * half, (r + 1) * half)
            for side, ref in ((core, near_ref), (1 - core, far_ref)):
                start = pl.multiple_of((2 * r + side) * half, half)
                everyone[pl.ds(start, half), :] = ref[source, :]

    result = jnp.dot(everyone[...], head_ref[...], preferred_element_type=F32)
    for r in range(n_tok):
        out_ref[r] = result[2 * r * half : 2 * (r + 1) * half, :]
    part = turned_ref.shape[0]
    start = pl.multiple_of(pl.program_id(0) * part, part)
    turned_ref[...] = everyone[:, pl.ds(start, part)].T


def student_logits(spot, after, near, far, head, n_tok):
    every, depth = 2 * near.shape[0], near.shape[1]
    rows = every // n_tok
    cols = head.shape[1]
    tile = 256
    whole = lambda shape: pl.BlockSpec(shape, lambda i: (0, 0))
    return pl.pallas_call(
        logits_kernel,
        grid=(cols // tile,),
        in_specs=[SMEM_SPEC, pl.BlockSpec(memory_space=pl.ANY), whole(near.shape), whole(far.shape)]
        + [pl.BlockSpec((depth, tile), lambda i: (0, i))],
        out_specs=[pl.BlockSpec((n_tok, rows, tile), lambda i: (0, 0, i))]
        + [pl.BlockSpec((depth * tile // cols, every), lambda i: (i, 0))],
        out_shape=[pltpu.HBM((n_tok, rows, cols), F32), pltpu.HBM((depth, every), BF16)],
        scratch_shapes=[pltpu.VMEM((every, depth), BF16)],
        compiler_params=params(40),
        cost_estimate=COST,
        name="student_logits",
    )(spot, after, near, far, pltpu.with_memory_space_constraint(head, pltpu.HBM))


def student_kernel(base_ref, labels_ref, mass_ref, logits_ref, stat_ref):
    n_tok, rows, cols = logits_ref.shape
    lane = lax.broadcasted_iota(jnp.int32, (rows, LANES), 1)
    label = labels_ref[...]
    top = jnp.full((rows, LANES), -jnp.inf, F32)
    hit = jnp.zeros((rows, LANES), F32)
    for t in range(n_tok):
        for b in range(0, cols, LANES):
            block = logits_ref[t, :, b : b + LANES]
            top = jnp.maximum(top, block)
            hit = hit + jnp.where(lane == label - (base_ref[t] + b), block, 0.0)
    top = jnp.max(top, axis=1, keepdims=True)
    total = jnp.zeros((rows, LANES), F32)
    for t in range(n_tok):
        for b in range(0, cols, LANES):
            total = total + jnp.exp(logits_ref[t, :, b : b + LANES] - top)
    total = jnp.sum(total, axis=1, keepdims=True)
    hit = jnp.sum(hit, axis=1, keepdims=True)
    stat_ref[...] = mass_ref[...] + rows_from_columns([jnp.zeros_like(hit), top, total, hit])


def student_stats(base, label_column, mass, logits):
    return pl.pallas_call(
        student_kernel,
        in_specs=[SMEM_SPEC] + [VMEM_SPEC] * 3,
        out_specs=VMEM_SPEC,
        out_shape=jax.ShapeDtypeStruct(mass.shape, F32),
        compiler_params=params(16),
        cost_estimate=COST,
        name="student_stats",
    )(base, label_column, mass, logits)


def totals_kernel(*refs):
    stats, (columns, loss_ref) = refs[:-2], refs[-2:]
    parts = split_rows(stats)
    mass = tree(jnp.add, [r[0] for r in parts])
    top, total = total_at(parts, 1, 2)
    log_total = top + jnp.log(total)
    label_logit = tree(jnp.add, [r[3] for r in parts])
    columns[...] = columns_from_rows([mass + 1.0, log_total])
    loss_ref[...] = mass * log_total + log_total - label_logit


def token_totals(stats):
    rows = stats[0].shape[1]
    return pl.pallas_call(
        totals_kernel,
        in_specs=[VMEM_SPEC] * len(stats),
        out_specs=[VMEM_SPEC] * 2,
        out_shape=[jax.ShapeDtypeStruct((rows, LANES), F32), jax.ShapeDtypeStruct((1, rows), F32)],
        compiler_params=params(16),
        cost_estimate=COST,
        name="token_totals",
    )(*stats)


def grad_kernel(tok_ref, base_ref, labels_ref, columns, *refs, n_sums):
    sums = refs[:n_sums]
    logits_ref, *grads, inner_ref, inner = refs[n_sums:]
    step = pl.program_id(0)
    _, rows, cols = logits_ref.shape

    @pl.when(step == 0)
    def _():
        inner[...] = jnp.zeros_like(inner)

    lane = lax.broadcasted_iota(jnp.int32, (rows, LANES), 1)
    lift, log_total = columns[:, 0:1], columns[:, 1:2]
    label = labels_ref[...] - base_ref[token_group(step, tok_ref, len(grads))]
    for r in range(len(grads)):

        @pl.when(step == r)
        def _():
            running = inner[...]
            for b in range(cols // LANES):
                place = slice(b * LANES, (b + 1) * LANES)
                target = functools.reduce(
                    jnp.add, [ref[z, b].astype(F32) for ref in sums for z in range(ref.shape[0])]
                )
                score = logits_ref[0, :, place]
                running = running + target * score
                hit = jnp.where(lane == label - b * LANES, 1.0, 0.0)
                grads[r][:, place] = (lift * jnp.exp(score - log_total) - target - hit).astype(BF16)
            inner[...] = running

    @pl.when(step == pl.num_programs(0) - 1)
    def _():
        inner_ref[...] = rows_from_columns([jnp.sum(inner[...], axis=1, keepdims=True)])[0:1, :]


def token_group(step, tok_ref, n_tok):
    return tok_ref[0] ^ (n_tok - 1 - step)


def grad_logits(tok, base, label_column, columns, sums, logits):
    n_tok, rows, cols = logits.shape
    per = cols // LANES
    whole = lambda shape: pl.BlockSpec(shape, lambda t, tok_ref: (0,) * len(shape))
    group = lambda t, tok_ref: token_group(t, tok_ref, n_tok)
    return pl.pallas_call(
        functools.partial(grad_kernel, n_sums=len(sums)),
        grid_spec=pltpu.PrefetchScalarGridSpec(
            num_scalar_prefetch=1,
            grid=(n_tok,),
            in_specs=[SMEM_SPEC, whole(label_column.shape), whole(columns.shape)]
            + [pl.BlockSpec((s.shape[0], per, rows, LANES), lambda t, r: (0, group(t, r), 0, 0)) for s in sums]
            + [pl.BlockSpec((1, rows, cols), lambda t, r: (group(t, r), 0, 0))],
            out_specs=[whole((rows, cols))] * n_tok + [whole((1, rows))],
            scratch_shapes=[pltpu.VMEM((rows, LANES), F32)],
        ),
        out_shape=[pltpu.HBM((rows, cols), BF16)] * n_tok + [jax.ShapeDtypeStruct((1, rows), F32)],
        compiler_params=params(24),
        cost_estimate=COST,
        name="grad_logits",
    )(tok, base, label_column, columns, *sums, logits)


def product_kernel(tok_ref, a_ref, *refs):
    pieces, o_ref, b_ref = refs[:-2], refs[-2], refs[-1]
    rows = pieces[0].shape[0]

    @pl.when(pl.program_id(0) == 0)
    def _():
        for r, piece in enumerate(pieces):
            start = pl.multiple_of(token_group(r, tok_ref, len(pieces)) * rows, rows)
            b_ref[pl.ds(start, rows), :] = piece[...]

    o_ref[...] = jnp.dot(a_ref[...], b_ref[...], preferred_element_type=F32).astype(o_ref.dtype)


def head_product(tok, a, pieces):
    m, k = a.shape
    rows, n = pieces[0].shape
    tile = m // 4
    return pl.pallas_call(
        product_kernel,
        grid=(m // tile,),
        in_specs=[SMEM_SPEC, pl.BlockSpec((tile, k), lambda i: (i, 0))]
        + [pl.BlockSpec((rows, n), lambda i: (0, 0))] * len(pieces),
        out_specs=pl.BlockSpec((tile, n), lambda i: (i, 0)),
        out_shape=jax.ShapeDtypeStruct((m, n), BF16),
        scratch_shapes=[pltpu.VMEM((k, n), BF16)],
        compiler_params=params(32),
        cost_estimate=COST,
        name="head_product",
    )(tok, pltpu.with_memory_space_constraint(a, pltpu.HBM), *pieces)


def swap(x, axis, mask):
    return lax.ppermute(x, axis, [(i, i ^ mask) for i in range(lax.axis_size(axis))])


def gather_chips(x):
    n = lax.axis_size("vocab")
    if n > 8:
        lines = [[2 * z + c for z in range(n // 2)] for c in range(2)]
        everything = lax.all_gather(x, "vocab", axis=0, axis_index_groups=lines)
        return [everything[z] for z in range(n // 2)]
    return [x] + [swap(x, "vocab", r) for r in range(2, n, 2)]


def gather_cores(x):
    chips = gather_chips(x)
    return chips + [swap(chip, "vocab", 1) for chip in chips]


def plus(a, b):
    return (a.astype(F32) + b.astype(F32)).astype(BF16)


def exchange_tok(x):
    return lax.all_to_all(x, "tok", split_axis=0, concat_axis=0, tiled=True)


def send(x, hops):
    return lax.ppermute(x, "vocab", [(2 * a + c, 2 * b + c) for a, b in hops for c in range(2)])


def local(teacher_logits, hidden, new_head, labels, map_target, map_weight):
    rows = teacher_logits.shape[0]
    block = map_weight.shape[2]
    n_tok = lax.axis_size("tok")
    n_vocab = lax.axis_size("vocab")
    n_z = n_vocab // 2
    new_cols = new_head.shape[1]
    per = new_cols // block
    tok = lax.axis_index("tok")
    vocab = lax.axis_index("vocab")
    spot = jnp.stack([vocab % 2, vocab // 2]).astype(jnp.int32)
    slots = n_tok * per
    in_line = n_z == 4

    owner = map_target // per
    owner_vocab = owner % n_vocab
    owner_z = owner_vocab // 2
    if in_line:
        z = vocab // 2
        outer = (owner_z == 0) | (owner_z == n_z - 1)
        near_place = jnp.where(owner_z == z, 3, 2)
        place = jnp.where((owner_z // 2) == (z // 2), near_place, jnp.where(outer, 0, 1))
    else:
        place = owner_z
    slot = (owner // n_vocab) * per + map_target % per
    code = (((owner_vocab % 2) * n_z + place) * SLOT_BASE + slot).astype(jnp.int32).reshape(-1)

    peer_logits = swap(teacher_logits, "vocab", 1)
    peer_code = swap(code, "vocab", 1)
    peer_weight = swap(map_weight, "vocab", 1)
    teacher = teacher_stats(teacher_logits)
    totals = gather_cores(teacher)
    half = lax.dynamic_slice_in_dim(hidden, spot[0] * (rows // 2), rows // 2)
    half, teacher = lax.optimization_barrier((half, teacher))
    near = exchange_tok(jnp.broadcast_to(half, (n_tok,) + half.shape)).reshape(n_tok * (rows // 2), -1)
    lists, counts = plan(code, peer_code, 2 * n_z)
    probs = teacher_probs(teacher_logits, peer_logits, totals)

    if in_line:
        inward, across, outward = [(0, 1), (3, 2)], [(1, 2), (2, 1)], [(1, 0), (2, 3)]
        far_outer, mass_a = chip_sums(spot, lists, counts, probs, map_weight, peer_weight, 0, 1, 1, slots)
        first = send(far_outer, inward)
        near, mass_a = lax.optimization_barrier((near, mass_a))
        probs, far_outer = lax.optimization_barrier((probs, far_outer))
        far_inner, beside, own, mass_b = chip_sums(
            spot, lists, counts, probs, map_weight, peer_weight, 1, 3, 1, slots
        )
        second = send(far_inner, inward)
        mass = mass_a + mass_b
    else:
        sums, mass = chip_sums(spot, lists, counts, probs, map_weight, peer_weight, 0, 1, n_z, slots)
        lines = [[2 * z + c for z in range(n_z)] for c in range(2)]
        sums = lax.all_to_all(
            sums.reshape(n_z, slots, rows, block),
            "vocab",
            split_axis=0,
            concat_axis=0,
            axis_index_groups=lines,
            tiled=True,
        )
        sums = [sums]

    far = swap(near, "vocab", 1)
    scores, turned = student_logits(spot, mass, near, far, new_head, n_tok)
    scores = exchange_tok(scores)
    label_column = lax.dynamic_slice_in_dim(labels, tok * rows, rows).reshape(rows, 1)
    base = (jnp.arange(n_tok, dtype=jnp.int32) * n_vocab + vocab) * new_cols
    if in_line:
        first, turned = lax.optimization_barrier((first, turned))
        merged = plus(far_outer, first)
        crossed_outer = send(merged, across)
        scores, merged = lax.optimization_barrier((scores, merged))
        student = student_stats(base, label_column, mass, scores)
        second, waited, student = lax.optimization_barrier((second, beside, student))
        third = send(waited, inward)
        merged_inner = plus(far_inner, second)
        crossed_inner = send(merged_inner, across)
        crossed_outer, merged_inner = lax.optimization_barrier((crossed_outer, merged_inner))
        merged_near = plus(beside, crossed_outer)
        arrived = send(merged_near, outward)
        student, merged_near = lax.optimization_barrier((student, merged_near))
        sums = [x[None] for x in (own, third, crossed_inner, arrived)]
    else:
        student = student_stats(base, label_column, mass, scores)
    stats = gather_cores(student)

    group = tok.astype(jnp.int32).reshape(1)
    columns, base_loss = token_totals(stats)
    *grads, inner = grad_logits(group, base, label_column, columns, sums, scores)
    grads = [swap(x, "tok", n_tok - 1 - r) for r, x in enumerate(grads[:-1])] + [grads[-1]]
    mask = 1
    while mask < n_vocab:
        inner = inner + swap(inner, "vocab", mask)
        mask *= 2
    return ((base_loss - inner).reshape(rows), head_product(group, turned, grads))


def solution(mesh):
    return jax.shard_map(
        local,
        mesh=mesh,
        in_specs=(
            P("tok", "vocab"),
            P("tok", None),
            P(None, ("tok", "vocab")),
            P(),
            P("vocab", None),
            P("vocab", None, None, None),
        ),
        out_specs=(P("tok"), P(None, ("tok", "vocab"))),
        check_vma=False,
    )
```

```python
import functools

import jax
import jax.numpy as jnp
from jax import lax
from jax.experimental import pallas as pl
from jax.experimental.pallas import tpu as pltpu
from jax.sharding import PartitionSpec as P

F32 = jnp.float32
BF16 = jnp.bfloat16
LANES = 128
BATCH = 8
COST = pl.CostEstimate(flops=1024, bytes_accessed=1024, transcendentals=0)
SLOT_BITS = 10
SLOT_BASE = 1 << SLOT_BITS
SMEM_SPEC = pl.BlockSpec(memory_space=pltpu.SMEM)
VMEM_SPEC = pl.BlockSpec(memory_space=pltpu.VMEM)


def params(mebibytes):
    return pltpu.CompilerParams(vmem_limit_bytes=mebibytes * 1024 * 1024)


def tree(op, items):
    while len(items) > 1:
        items = [op(items[i], items[i + 1]) if i + 1 < len(items) else items[i] for i in range(0, len(items), 2)]
    return items[0]


def total_at(rows_of, top_row, total_row):
    top = tree(jnp.maximum, [r[top_row] for r in rows_of])
    total = tree(jnp.add, [r[total_row] * jnp.exp(r[top_row] - top) for r in rows_of])
    return top, total


def split_rows(refs):
    return [[ref[k : k + 1, :] for k in range(8)] for ref in refs]


def rows_from_columns(columns):
    n = columns[0].shape[0]
    lane = lax.broadcasted_iota(jnp.int32, (n, LANES), 1)
    tile = jnp.zeros((n, LANES), F32)
    for place, column in enumerate(columns):
        tile = jnp.where(lane == place, column, tile)
    return tile.T[0:8, :]


def columns_from_rows(rows):
    n = rows[0].shape[1]
    return jnp.concatenate(rows + [jnp.zeros((LANES - len(rows), n), F32)], axis=0).T


def teacher_kernel(x_ref, stat_ref):
    rows, cols = x_ref.shape
    places = range(0, cols, LANES)
    read = lambda place: x_ref[:, place : place + LANES].astype(F32)
    top = jnp.full((rows, LANES), -jnp.inf, F32)
    for place in places:
        top = jnp.maximum(top, read(place))
    top = jnp.max(top, axis=1, keepdims=True)
    total = jnp.zeros((rows, LANES), F32)
    for place in places:
        total = total + jnp.exp(read(place) - top)
    stat_ref[...] = rows_from_columns([top, jnp.sum(total, axis=1, keepdims=True)])


def teacher_stats(x):
    return pl.pallas_call(
        teacher_kernel,
        in_specs=[VMEM_SPEC],
        out_specs=VMEM_SPEC,
        out_shape=jax.ShapeDtypeStruct((8, x.shape[0]), F32),
        compiler_params=params(16),
        cost_estimate=COST,
        name="teacher_stats",
    )(x)


def divide(x, n):
    return lax.shift_right_logical(x, n.bit_length() - 1) if n & (n - 1) == 0 else x // n


def plan_kernel(own_ref, peer_ref, list_ref, count_ref):
    lists = count_ref.shape[0]
    entries = own_ref.shape[0]
    for p in range(lists):
        count_ref[p] = 0

    def visit(i, carry):
        for side, ref in enumerate((own_ref, peer_ref)):
            code = ref[i]
            row = lax.shift_right_logical(code, SLOT_BITS)
            n = count_ref[row]
            list_ref[row, n] = (side * entries + i) * SLOT_BASE + (code & (SLOT_BASE - 1))
            count_ref[row] = n + 1
        return carry

    lax.fori_loop(0, entries, visit, 0, unroll=8)
    for p in range(lists):
        n = count_ref[p]
        for k in range(BATCH - 1):
            list_ref[p, n + k] = SLOT_BASE - 1


def plan(own_code, peer_code, lists):
    room = 2 * own_code.size + BATCH
    return pl.pallas_call(
        plan_kernel,
        in_specs=[SMEM_SPEC] * 2,
        out_specs=[SMEM_SPEC] * 2,
        out_shape=[jax.ShapeDtypeStruct((lists, room), jnp.int32), jax.ShapeDtypeStruct((lists,), jnp.int32)],
        compiler_params=params(1),
        cost_estimate=COST,
        name="entry_lists",
    )(own_code, peer_code)


def probs_kernel(x_own, x_peer, *refs):
    stats, probs = refs[:-1], refs[-1]
    blocks = x_own.shape[1] // LANES
    top, total = total_at(split_rows(stats), 0, 1)
    columns = columns_from_rows([top, 1.0 / total])
    top, scale = columns[:, 0:1], columns[:, 1:2]
    for side, x in enumerate((x_own, x_peer)):
        for j in range(blocks):
            raised = jnp.exp(x[:, j * LANES : (j + 1) * LANES].astype(F32) - top)
            probs[side * blocks + j] = (raised * scale).astype(BF16)


def sums_kernel(spot_ref, list_ref, count_ref, probs, w_own, w_peer, *refs, first, fan, pieces):
    outs, mass_ref, acc = refs[:-2], refs[-2], refs[-1]
    step = pl.program_id(0)
    slots, rows, _ = outs[0].shape
    side = w_own.shape[0] * fan
    mass = jnp.zeros((rows, LANES), F32)
    for k, out in enumerate(outs):
        piece = spot_ref[0] * pieces + first + k + step
        acc[...] = jnp.zeros_like(acc)

        def add(i, carry):
            parts = []
            for u in range(BATCH):
                item = list_ref[piece, i * BATCH + u]
                slot = item & (SLOT_BASE - 1)
                entry = lax.shift_right_logical(item, SLOT_BITS)
                weight = jnp.where(entry < side, 0, 1)
                parts.append((entry, slot, weight))
            for entry, slot, peer in parts:
                j = divide(entry, fan)
                f = entry - j * fan
                local_j = j - peer * (side // fan)
                weight = jnp.where(peer == 1, w_peer[local_j, f], w_own[local_j, f])
                part = jnp.dot(probs[j], weight, preferred_element_type=F32)
                acc[jnp.minimum(slot, slots)] += part.astype(BF16).astype(F32)
            return carry

        lax.fori_loop(0, divide(count_ref[piece] + BATCH - 1, BATCH), add, 0)

        def drain(i, mass):
            block = acc[i]
            out[i] = block.astype(BF16)
            return mass + block

        mass = lax.fori_loop(0, slots, drain, mass, unroll=4)
    part = rows_from_columns([jnp.sum(mass, axis=1, keepdims=True)])

    @pl.when(step == 0)
    def _():
        mass_ref[...] = part

    @pl.when(step > 0)
    def _():
        mass_ref[...] += part


def teacher_probs(x_own, x_peer, stats):
    rows, cols = x_own.shape
    return pl.pallas_call(
        probs_kernel,
        in_specs=[VMEM_SPEC] * (2 + len(stats)),
        out_specs=VMEM_SPEC,
        out_shape=jax.ShapeDtypeStruct((2 * cols // LANES, rows, LANES), BF16),
        compiler_params=params(16),
        cost_estimate=COST,
        name="teacher_probs",
    )(x_own, x_peer, *stats)


def chip_sums(spot, lists, counts, probs, w_own, w_peer, first, n_out, steps, slots):
    rows = probs.shape[1]
    fan = w_own.shape[1]
    whole = lambda shape: pl.BlockSpec(shape, lambda s: (0,) * len(shape))
    out = pltpu.HBM((steps * slots, rows, LANES), BF16)
    return pl.pallas_call(
        functools.partial(sums_kernel, first=first, fan=fan, pieces=counts.shape[0] // 2),
        grid=(steps,),
        in_specs=[SMEM_SPEC] * 3 + [VMEM_SPEC] * 3,
        out_specs=[pl.BlockSpec((slots, rows, LANES), lambda s: (s, 0, 0))] * n_out + [whole((8, rows))],
        out_shape=[out] * n_out + [jax.ShapeDtypeStruct((8, rows), F32)],
        scratch_shapes=[pltpu.VMEM((slots + 1, rows, LANES), F32)],
        compiler_params=params(32),
        cost_estimate=COST,
        name="chip_sums",
    )(spot, lists, counts, probs, w_own, w_peer)


def logits_kernel(spot_ref, after_ref, near_ref, far_ref, head_ref, *refs):
    out_ref, turned_ref, everyone = refs
    n_tok = out_ref.shape[0]
    half = near_ref.shape[0] // n_tok
    del after_ref

    @pl.when(pl.program_id(0) == 0)
    def _():
        core = spot_ref[0]
        for r in range(n_tok):
            source = slice(r * half, (r + 1) * half)
            for side, ref in ((core, near_ref), (1 - core, far_ref)):
                start = pl.multiple_of((2 * r + side) * half, half)
                everyone[pl.ds(start, half), :] = ref[source, :]

    result = jnp.dot(everyone[...], head_ref[...], preferred_element_type=F32)
    for r in range(n_tok):
        out_ref[r] = result[2 * r * half : 2 * (r + 1) * half, :]
    part = turned_ref.shape[0]
    start = pl.multiple_of(pl.program_id(0) * part, part)
    turned_ref[...] = everyone[:, pl.ds(start, part)].T


def student_logits(spot, after, near, far, head, n_tok):
    every, depth = 2 * near.shape[0], near.shape[1]
    rows = every // n_tok
    cols = head.shape[1]
    tile = 256
    whole = lambda shape: pl.BlockSpec(shape, lambda i: (0, 0))
    return pl.pallas_call(
        logits_kernel,
        grid=(cols // tile,),
        in_specs=[SMEM_SPEC, pl.BlockSpec(memory_space=pl.ANY), whole(near.shape), whole(far.shape)]
        + [pl.BlockSpec((depth, tile), lambda i: (0, i))],
        out_specs=[pl.BlockSpec((n_tok, rows, tile), lambda i: (0, 0, i))]
        + [pl.BlockSpec((depth * tile // cols, every), lambda i: (i, 0))],
        out_shape=[pltpu.HBM((n_tok, rows, cols), F32), pltpu.HBM((depth, every), BF16)],
        scratch_shapes=[pltpu.VMEM((every, depth), BF16)],
        compiler_params=params(40),
        cost_estimate=COST,
        name="student_logits",
    )(spot, after, near, far, pltpu.with_memory_space_constraint(head, pltpu.HBM))


def student_kernel(spot_ref, labels_ref, mass_ref, logits_ref, *outs):
    n_tok, rows, cols = logits_ref.shape
    lane = lax.broadcasted_iota(jnp.int32, (rows, LANES), 1)
    for r, out in enumerate(outs):
        t = spot_ref[0] ^ r
        label = labels_ref[t] - spot_ref[1]
        top = jnp.full((rows, LANES), -jnp.inf, F32)
        hit = jnp.zeros((rows, LANES), F32)
        for b in range(0, cols, LANES):
            block = logits_ref[t, :, b : b + LANES]
            top = jnp.maximum(top, block)
            hit = hit + jnp.where(lane == label - b, block, 0.0)
        top = jnp.max(top, axis=1, keepdims=True)
        total = jnp.zeros((rows, LANES), F32)
        for b in range(0, cols, LANES):
            total = total + jnp.exp(logits_ref[t, :, b : b + LANES] - top)
        total = jnp.sum(total, axis=1, keepdims=True)
        hit = jnp.sum(hit, axis=1, keepdims=True)
        out[...] = rows_from_columns([jnp.zeros_like(hit), top, total, hit])
    outs[0][0:1, :] = mass_ref[0:1, :]


def student_stats(spot, label_columns, mass, logits):
    n_tok, rows, _ = logits.shape
    return pl.pallas_call(
        student_kernel,
        in_specs=[SMEM_SPEC] + [VMEM_SPEC] * 3,
        out_specs=[VMEM_SPEC] * n_tok,
        out_shape=[jax.ShapeDtypeStruct((8, rows), F32)] * n_tok,
        compiler_params=params(16),
        cost_estimate=COST,
        name="student_stats",
    )(spot, label_columns, mass, logits)


def merge_kernel(*refs):
    stats, out = refs[:-1], refs[-1]
    parts = split_rows(stats)
    mass = tree(jnp.add, [r[0] for r in parts])
    top, total = total_at(parts, 1, 2)
    hit = tree(jnp.add, [r[3] for r in parts])
    out[...] = jnp.concatenate([mass, top, total, hit, jnp.zeros((4, top.shape[1]), F32)], axis=0)


def merge_stats(stats):
    return pl.pallas_call(
        merge_kernel,
        in_specs=[VMEM_SPEC] * len(stats),
        out_specs=VMEM_SPEC,
        out_shape=jax.ShapeDtypeStruct(stats[0].shape, F32),
        compiler_params=params(1),
        cost_estimate=COST,
        name="merge_stats",
    )(*stats)


def totals_kernel(*refs):
    stats, (columns, loss_ref) = refs[:-2], refs[-2:]
    parts = split_rows(stats)
    mass = tree(jnp.add, [r[0] for r in parts])
    top, total = total_at(parts, 1, 2)
    log_total = top + jnp.log(total)
    label_logit = tree(jnp.add, [r[3] for r in parts])
    columns[...] = columns_from_rows([mass + 1.0, log_total])
    loss_ref[...] = mass * log_total + log_total - label_logit


def token_totals(stats):
    rows = stats[0].shape[1]
    return pl.pallas_call(
        totals_kernel,
        in_specs=[VMEM_SPEC] * len(stats),
        out_specs=[VMEM_SPEC] * 2,
        out_shape=[jax.ShapeDtypeStruct((rows, LANES), F32), jax.ShapeDtypeStruct((1, rows), F32)],
        compiler_params=params(16),
        cost_estimate=COST,
        name="token_totals",
    )(*stats)


def grad_kernel(tok_ref, base_ref, labels_ref, columns, *refs, n_sums):
    sums = refs[:n_sums]
    logits_ref, *grads, inner_ref, inner = refs[n_sums:]
    step = pl.program_id(0)
    _, rows, cols = logits_ref.shape

    @pl.when(step == 0)
    def _():
        inner[...] = jnp.zeros_like(inner)

    lane = lax.broadcasted_iota(jnp.int32, (rows, LANES), 1)
    lift, log_total = columns[:, 0:1], columns[:, 1:2]
    label = labels_ref[...] - base_ref[token_group(step, tok_ref, len(grads))]
    for r in range(len(grads)):

        @pl.when(step == r)
        def _():
            running = inner[...]
            for b in range(cols // LANES):
                place = slice(b * LANES, (b + 1) * LANES)
                target = functools.reduce(
                    jnp.add, [ref[z, b].astype(F32) for ref in sums for z in range(ref.shape[0])]
                )
                score = logits_ref[0, :, place]
                running = running + target * score
                hit = jnp.where(lane == label - b * LANES, 1.0, 0.0)
                grads[r][:, place] = (lift * jnp.exp(score - log_total) - target - hit).astype(BF16)
            inner[...] = running

    @pl.when(step == pl.num_programs(0) - 1)
    def _():
        inner_ref[...] = rows_from_columns([jnp.sum(inner[...], axis=1, keepdims=True)])[0:1, :]


def token_group(step, tok_ref, n_tok):
    return tok_ref[0] ^ (n_tok - 1 - step)


def grad_logits(tok, base, label_column, columns, sums, logits):
    n_tok, rows, cols = logits.shape
    per = cols // LANES
    whole = lambda shape: pl.BlockSpec(shape, lambda t, tok_ref: (0,) * len(shape))
    group = lambda t, tok_ref: token_group(t, tok_ref, n_tok)
    return pl.pallas_call(
        functools.partial(grad_kernel, n_sums=len(sums)),
        grid_spec=pltpu.PrefetchScalarGridSpec(
            num_scalar_prefetch=1,
            grid=(n_tok,),
            in_specs=[SMEM_SPEC, whole(label_column.shape), whole(columns.shape)]
            + [pl.BlockSpec((s.shape[0], per, rows, LANES), lambda t, r: (0, group(t, r), 0, 0)) for s in sums]
            + [pl.BlockSpec((1, rows, cols), lambda t, r: (group(t, r), 0, 0))],
            out_specs=[whole((rows, cols))] * n_tok + [whole((1, rows))],
            scratch_shapes=[pltpu.VMEM((rows, LANES), F32)],
        ),
        out_shape=[pltpu.HBM((rows, cols), BF16)] * n_tok + [jax.ShapeDtypeStruct((1, rows), F32)],
        compiler_params=params(24),
        cost_estimate=COST,
        name="grad_logits",
    )(tok, base, label_column, columns, *sums, logits)


def product_kernel(tok_ref, a_ref, *refs):
    pieces, o_ref, b_ref = refs[:-2], refs[-2], refs[-1]
    rows = pieces[0].shape[0]

    @pl.when(pl.program_id(0) == 0)
    def _():
        for r, piece in enumerate(pieces):
            start = pl.multiple_of(token_group(r, tok_ref, len(pieces)) * rows, rows)
            b_ref[pl.ds(start, rows), :] = piece[...]

    o_ref[...] = jnp.dot(a_ref[...], b_ref[...], preferred_element_type=F32).astype(o_ref.dtype)


def head_product(tok, a, pieces):
    m, k = a.shape
    rows, n = pieces[0].shape
    tile = m // 4
    return pl.pallas_call(
        product_kernel,
        grid=(m // tile,),
        in_specs=[SMEM_SPEC, pl.BlockSpec((tile, k), lambda i: (i, 0))]
        + [pl.BlockSpec((rows, n), lambda i: (0, 0))] * len(pieces),
        out_specs=pl.BlockSpec((tile, n), lambda i: (i, 0)),
        out_shape=jax.ShapeDtypeStruct((m, n), BF16),
        scratch_shapes=[pltpu.VMEM((k, n), BF16)],
        compiler_params=params(32),
        cost_estimate=COST,
        name="head_product",
    )(tok, pltpu.with_memory_space_constraint(a, pltpu.HBM), *pieces)


def swap(x, axis, mask):
    return lax.ppermute(x, axis, [(i, i ^ mask) for i in range(lax.axis_size(axis))])


def gather_chips(x):
    n = lax.axis_size("vocab")
    if n > 8:
        lines = [[2 * z + c for z in range(n // 2)] for c in range(2)]
        everything = lax.all_gather(x, "vocab", axis=0, axis_index_groups=lines)
        return [everything[z] for z in range(n // 2)]
    return [x] + [swap(x, "vocab", r) for r in range(2, n, 2)]


def gather_cores(x):
    chips = gather_chips(x)
    return chips + [swap(chip, "vocab", 1) for chip in chips]


def half_rows(hidden, spot, n_tok):
    half = hidden.shape[0] // 2
    own = lax.dynamic_slice_in_dim(hidden, spot[0] * half, half)
    return jnp.broadcast_to(own, (n_tok,) + own.shape)


def plus(a, b):
    return (a.astype(F32) + b.astype(F32)).astype(BF16)


def exchange_tok(x):
    return lax.all_to_all(x, "tok", split_axis=0, concat_axis=0, tiled=True)


def send(x, hops):
    return lax.ppermute(x, "vocab", [(2 * a + c, 2 * b + c) for a, b in hops for c in range(2)])


def local(teacher_logits, hidden, new_head, labels, map_target, map_weight):
    rows = teacher_logits.shape[0]
    block = map_weight.shape[2]
    n_tok = lax.axis_size("tok")
    n_vocab = lax.axis_size("vocab")
    n_z = n_vocab // 2
    new_cols = new_head.shape[1]
    per = new_cols // block
    tok = lax.axis_index("tok")
    vocab = lax.axis_index("vocab")
    spot = jnp.stack([vocab % 2, vocab // 2]).astype(jnp.int32)
    slots = n_tok * per
    in_line = n_z == 4

    owner = map_target // per
    owner_vocab = owner % n_vocab
    owner_z = owner_vocab // 2
    if in_line:
        z = vocab // 2
        outer = (owner_z == 0) | (owner_z == n_z - 1)
        near_place = jnp.where(owner_z == z, 3, 2)
        place = jnp.where((owner_z // 2) == (z // 2), near_place, jnp.where(outer, 0, 1))
    else:
        place = owner_z
    slot = (owner // n_vocab) * per + map_target % per
    code = (((owner_vocab % 2) * n_z + place) * SLOT_BASE + slot).astype(jnp.int32).reshape(-1)

    peer_logits = swap(teacher_logits, "vocab", 1)
    peer_code = swap(code, "vocab", 1)
    peer_weight = swap(map_weight, "vocab", 1)
    teacher = teacher_stats(teacher_logits)
    totals = gather_cores(teacher)
    lists, counts = plan(code, peer_code, 2 * n_z)
    probs = teacher_probs(teacher_logits, peer_logits, totals)

    if in_line:
        inward, across, outward = [(0, 1), (3, 2)], [(1, 2), (2, 1)], [(1, 0), (2, 3)]
        far_outer, mass_a = chip_sums(spot, lists, counts, probs, map_weight, peer_weight, 0, 1, 1, slots)
        first = send(far_outer, inward)
        rows_in, mass_a = lax.optimization_barrier((hidden, mass_a))
        copies, probs = lax.optimization_barrier((half_rows(rows_in, spot, n_tok), probs))
        near = exchange_tok(copies)
        far_inner, beside, own, mass_b = chip_sums(
            spot, lists, counts, probs, map_weight, peer_weight, 1, 3, 1, slots
        )
        second = send(far_inner, inward)
        first, mass = lax.optimization_barrier((first, mass_a + mass_b))
        merged = plus(far_outer, first)
        crossed_outer = send(merged, across)
        near, waited, merged = lax.optimization_barrier((near, beside, merged))
        third = send(waited, inward)
    else:
        sums, mass = chip_sums(spot, lists, counts, probs, map_weight, peer_weight, 0, 1, n_z, slots)
        lines = [[2 * z + c for z in range(n_z)] for c in range(2)]
        sums = lax.all_to_all(
            sums.reshape(n_z, slots, rows, block),
            "vocab",
            split_axis=0,
            concat_axis=0,
            axis_index_groups=lines,
            tiled=True,
        )
        sums = [sums]
        near = exchange_tok(half_rows(hidden, spot, n_tok))

    near = near.reshape(n_tok * (rows // 2), -1)
    far = swap(near, "vocab", 1)
    scores, turned = student_logits(spot, mass, near, far, new_head, n_tok)
    base = (jnp.arange(n_tok, dtype=jnp.int32) * n_vocab + vocab) * new_cols
    own_base = (tok * n_vocab + vocab) * new_cols
    label_columns = labels.reshape(n_tok, rows, 1)
    label_column = lax.dynamic_index_in_dim(label_columns, tok, keepdims=False)
    place = jnp.stack([tok, own_base]).astype(jnp.int32)
    student = student_stats(place, label_columns, mass, scores)
    student = merge_stats([student[0]] + [swap(student[r], "tok", r) for r in range(1, n_tok)])
    student = merge_stats([student, swap(student, "vocab", 1)])
    scores = exchange_tok(scores)
    if in_line:
        second, turned = lax.optimization_barrier((second, turned))
        merged_inner = plus(far_inner, second)
        crossed_inner = send(merged_inner, across)
        crossed_outer, merged_inner = lax.optimization_barrier((crossed_outer, merged_inner))
        merged_near = plus(beside, crossed_outer)
        arrived = send(merged_near, outward)
        student, scores, merged_near = lax.optimization_barrier((student, scores, merged_near))
        sums = [x[None] for x in (own, third, crossed_inner, arrived)]
    stats = gather_chips(student)

    group = tok.astype(jnp.int32).reshape(1)
    columns, base_loss = token_totals(stats)
    *grads, inner = grad_logits(group, base, label_column, columns, sums, scores)
    grads = [swap(x, "tok", n_tok - 1 - r) for r, x in enumerate(grads[:-1])] + [grads[-1]]
    mask = 1
    while mask < n_vocab:
        inner = inner + swap(inner, "vocab", mask)
        mask *= 2
    return ((base_loss - inner).reshape(rows), head_product(group, turned, grads))


def solution(mesh):
    return jax.shard_map(
        local,
        mesh=mesh,
        in_specs=(
            P("tok", "vocab"),
            P("tok", None),
            P(None, ("tok", "vocab")),
            P(),
            P("vocab", None),
            P("vocab", None, None, None),
        ),
        out_specs=(P("tok"), P(None, ("tok", "vocab"))),
        check_vma=False,
    )
```

```python
import functools

import jax
import jax.numpy as jnp
from jax import lax
from jax.experimental import pallas as pl
from jax.experimental.pallas import tpu as pltpu
from jax.sharding import PartitionSpec as P

F32 = jnp.float32
BF16 = jnp.bfloat16
LANES = 128
BATCH = 8
COST = pl.CostEstimate(flops=1024, bytes_accessed=1024, transcendentals=0)
SLOT_BITS = 10
SLOT_BASE = 1 << SLOT_BITS
SMEM_SPEC = pl.BlockSpec(memory_space=pltpu.SMEM)
VMEM_SPEC = pl.BlockSpec(memory_space=pltpu.VMEM)


def params(mebibytes):
    return pltpu.CompilerParams(vmem_limit_bytes=mebibytes * 1024 * 1024)


def in_hbm(x):
    return pltpu.with_memory_space_constraint(x, pltpu.HBM)


def tree(op, items):
    while len(items) > 1:
        items = [op(items[i], items[i + 1]) if i + 1 < len(items) else items[i] for i in range(0, len(items), 2)]
    return items[0]


def total_at(rows_of, top_row, total_row):
    top = tree(jnp.maximum, [r[top_row] for r in rows_of])
    total = tree(jnp.add, [r[total_row] * jnp.exp(r[top_row] - top) for r in rows_of])
    return top, total


def split_rows(refs):
    return [[ref[k : k + 1, :] for k in range(8)] for ref in refs]


def rows_from_columns(columns):
    n = columns[0].shape[0]
    lane = lax.broadcasted_iota(jnp.int32, (n, LANES), 1)
    tile = jnp.zeros((n, LANES), F32)
    for place, column in enumerate(columns):
        tile = jnp.where(lane == place, column, tile)
    return tile.T[0:8, :]


def columns_from_rows(rows):
    n = rows[0].shape[1]
    return jnp.concatenate(rows + [jnp.zeros((LANES - len(rows), n), F32)], axis=0).T


def teacher_kernel(x_ref, stat_ref):
    rows, cols = x_ref.shape
    places = range(0, cols, LANES)
    read = lambda place: x_ref[:, place : place + LANES].astype(F32)
    top = jnp.full((rows, LANES), -jnp.inf, F32)
    for place in places:
        top = jnp.maximum(top, read(place))
    top = jnp.max(top, axis=1, keepdims=True)
    total = jnp.zeros((rows, LANES), F32)
    for place in places:
        total = total + jnp.exp(read(place) - top)
    stat_ref[...] = rows_from_columns([top, jnp.sum(total, axis=1, keepdims=True)])


def teacher_stats(x):
    return pl.pallas_call(
        teacher_kernel,
        in_specs=[VMEM_SPEC],
        out_specs=VMEM_SPEC,
        out_shape=jax.ShapeDtypeStruct((8, x.shape[0]), F32),
        compiler_params=params(6),
        cost_estimate=COST,
        name="teacher_stats",
    )(x)


def divide(x, n):
    return lax.shift_right_logical(x, n.bit_length() - 1) if n & (n - 1) == 0 else x // n


def plan_kernel(own_ref, peer_ref, list_ref, count_ref):
    lists = count_ref.shape[0]
    entries = own_ref.shape[0]
    for p in range(lists):
        count_ref[p] = 0

    def visit(i, carry):
        for side, ref in enumerate((own_ref, peer_ref)):
            code = ref[i]
            row = lax.shift_right_logical(code, SLOT_BITS)
            n = count_ref[row]
            list_ref[row, n] = (side * entries + i) * SLOT_BASE + (code & (SLOT_BASE - 1))
            count_ref[row] = n + 1
        return carry

    lax.fori_loop(0, entries, visit, 0, unroll=8)
    for p in range(lists):
        n = count_ref[p]
        for k in range(BATCH - 1):
            list_ref[p, n + k] = SLOT_BASE - 1


def plan(own_code, peer_code, lists):
    room = 2 * own_code.size + BATCH
    return pl.pallas_call(
        plan_kernel,
        in_specs=[SMEM_SPEC] * 2,
        out_specs=[SMEM_SPEC] * 2,
        out_shape=[jax.ShapeDtypeStruct((lists, room), jnp.int32), jax.ShapeDtypeStruct((lists,), jnp.int32)],
        compiler_params=params(1),
        cost_estimate=COST,
        name="entry_lists",
    )(own_code, peer_code)


def probs_kernel(x_own, x_peer, *refs):
    stats, (probs, columns) = refs[:-2], refs[-2:]

    @pl.when(pl.program_id(0) == 0)
    def _():
        top, total = total_at(split_rows(stats), 0, 1)
        columns[...] = columns_from_rows([top, 1.0 / total])

    top, scale = columns[:, 0:1], columns[:, 1:2]
    for side, x in enumerate((x_own, x_peer)):
        for j in range(x.shape[1] // LANES):
            raised = jnp.exp(x[:, j * LANES : (j + 1) * LANES].astype(F32) - top)
            probs[side, j] = (raised * scale).astype(BF16)


def sums_kernel(spot_ref, list_ref, count_ref, probs, w_own, w_peer, *refs, first, fan, pieces):
    outs, mass_ref, acc = refs[:-2], refs[-2], refs[-1]
    step = pl.program_id(0)
    slots, rows, _ = outs[0].shape
    side = w_own.shape[0] * fan
    mass = jnp.zeros((rows, LANES), F32)
    for k, out in enumerate(outs):
        piece = spot_ref[0] * pieces + first + k + step
        acc[...] = jnp.zeros_like(acc)

        def add(i, carry):
            parts = []
            for u in range(BATCH):
                item = list_ref[piece, i * BATCH + u]
                slot = item & (SLOT_BASE - 1)
                entry = lax.shift_right_logical(item, SLOT_BITS)
                weight = jnp.where(entry < side, 0, 1)
                parts.append((entry, slot, weight))
            for entry, slot, peer in parts:
                j = divide(entry, fan)
                f = entry - j * fan
                local_j = j - peer * (side // fan)
                weight = jnp.where(peer == 1, w_peer[local_j, f], w_own[local_j, f])
                part = jnp.dot(probs[j], weight, preferred_element_type=F32)
                acc[jnp.minimum(slot, slots)] += part.astype(BF16).astype(F32)
            return carry

        lax.fori_loop(0, divide(count_ref[piece] + BATCH - 1, BATCH), add, 0)

        def drain(i, mass):
            block = acc[i]
            out[i] = block.astype(BF16)
            return mass + block

        mass = lax.fori_loop(0, slots, drain, mass, unroll=4)
    part = rows_from_columns([jnp.sum(mass, axis=1, keepdims=True)])

    @pl.when(step == 0)
    def _():
        mass_ref[...] = part

    @pl.when(step > 0)
    def _():
        mass_ref[...] += part


def teacher_probs(x_own, x_peer, stats):
    rows, cols = x_own.shape
    steps = 4
    blocks = cols // LANES
    part = pl.BlockSpec((rows, cols // steps), lambda i: (0, i))
    probs = pl.pallas_call(
        probs_kernel,
        grid=(steps,),
        in_specs=[part, part] + [pl.BlockSpec(s.shape, lambda i: (0, 0)) for s in stats],
        out_specs=pl.BlockSpec((2, blocks // steps, rows, LANES), lambda i: (0, i, 0, 0)),
        out_shape=jax.ShapeDtypeStruct((2, blocks, rows, LANES), BF16),
        scratch_shapes=[pltpu.VMEM((rows, LANES), F32)],
        compiler_params=params(8),
        cost_estimate=COST,
        name="teacher_probs",
    )(in_hbm(x_own), in_hbm(x_peer), *stats)
    return probs.reshape(2 * blocks, rows, LANES)


def chip_sums(spot, lists, counts, probs, w_own, w_peer, first, n_out, steps, slots):
    rows = probs.shape[1]
    fan = w_own.shape[1]
    whole = lambda shape: pl.BlockSpec(shape, lambda s: (0,) * len(shape))
    out = pltpu.HBM((steps * slots, rows, LANES), BF16)
    return pl.pallas_call(
        functools.partial(sums_kernel, first=first, fan=fan, pieces=counts.shape[0] // 2),
        grid=(steps,),
        in_specs=[SMEM_SPEC] * 3 + [VMEM_SPEC] * 3,
        out_specs=[pl.BlockSpec((slots, rows, LANES), lambda s: (s, 0, 0))] * n_out + [whole((8, rows))],
        out_shape=[out] * n_out + [jax.ShapeDtypeStruct((8, rows), F32)],
        scratch_shapes=[pltpu.VMEM((slots + 1, rows, LANES), F32)],
        compiler_params=params(24),
        cost_estimate=COST,
        name="chip_sums",
    )(spot, lists, counts, probs, w_own, w_peer)


def logits_kernel(spot_ref, after_ref, near_ref, far_ref, head_ref, *refs):
    out_ref, turned_ref, everyone = refs
    n_tok = out_ref.shape[0]
    half = near_ref.shape[0] // n_tok
    del after_ref

    @pl.when(pl.program_id(0) == 0)
    def _():
        core = spot_ref[0]
        for r in range(n_tok):
            source = slice(r * half, (r + 1) * half)
            for side, ref in ((core, near_ref), (1 - core, far_ref)):
                start = pl.multiple_of((2 * r + side) * half, half)
                everyone[pl.ds(start, half), :] = ref[source, :]

    result = jnp.dot(everyone[...], head_ref[...], preferred_element_type=F32)
    for r in range(n_tok):
        out_ref[r] = result[2 * r * half : 2 * (r + 1) * half, :]
    part = turned_ref.shape[0]
    start = pl.multiple_of(pl.program_id(0) * part, part)
    turned_ref[...] = everyone[:, pl.ds(start, part)].T


def student_logits(spot, after, near, far, head, n_tok):
    every, depth = 2 * near.shape[0], near.shape[1]
    rows = every // n_tok
    cols = head.shape[1]
    tile = 256
    whole = lambda shape: pl.BlockSpec(shape, lambda i: (0, 0))
    return pl.pallas_call(
        logits_kernel,
        grid=(cols // tile,),
        in_specs=[SMEM_SPEC, pl.BlockSpec(memory_space=pl.ANY), whole(near.shape), whole(far.shape)]
        + [pl.BlockSpec((depth, tile), lambda i: (0, i))],
        out_specs=[pl.BlockSpec((n_tok, rows, tile), lambda i: (0, 0, i))]
        + [pl.BlockSpec((depth * tile // cols, every), lambda i: (i, 0))],
        out_shape=[pltpu.HBM((n_tok, rows, cols), F32), pltpu.HBM((depth, every), BF16)],
        scratch_shapes=[pltpu.VMEM((every, depth), BF16)],
        compiler_params=params(30),
        cost_estimate=COST,
        name="student_logits",
    )(spot, after, near, far, in_hbm(head))


def student_kernel(base_ref, labels_ref, mass_ref, logits_ref, stat_ref):
    n_tok, rows, cols = logits_ref.shape
    lane = lax.broadcasted_iota(jnp.int32, (rows, LANES), 1)
    label = labels_ref[...]
    top = jnp.full((rows, LANES), -jnp.inf, F32)
    hit = jnp.zeros((rows, LANES), F32)
    for t in range(n_tok):
        for b in range(0, cols, LANES):
            block = logits_ref[t, :, b : b + LANES]
            top = jnp.maximum(top, block)
            hit = hit + jnp.where(lane == label - (base_ref[t] + b), block, 0.0)
    top = jnp.max(top, axis=1, keepdims=True)
    total = jnp.zeros((rows, LANES), F32)
    for t in range(n_tok):
        for b in range(0, cols, LANES):
            total = total + jnp.exp(logits_ref[t, :, b : b + LANES] - top)
    total = jnp.sum(total, axis=1, keepdims=True)
    hit = jnp.sum(hit, axis=1, keepdims=True)
    stat_ref[...] = rows_from_columns([jnp.zeros_like(hit), top, total, hit])
    stat_ref[0:1, :] = mass_ref[0:1, :]


def student_stats(base, label_column, mass, logits):
    return pl.pallas_call(
        student_kernel,
        in_specs=[SMEM_SPEC] + [VMEM_SPEC] * 3,
        out_specs=VMEM_SPEC,
        out_shape=jax.ShapeDtypeStruct(mass.shape, F32),
        compiler_params=params(10),
        cost_estimate=COST,
        name="student_stats",
    )(base, label_column, mass, logits)


def merge_kernel(*refs):
    stats, out = refs[:-1], refs[-1]
    parts = split_rows(stats)
    mass = tree(jnp.add, [r[0] for r in parts])
    top, total = total_at(parts, 1, 2)
    hit = tree(jnp.add, [r[3] for r in parts])
    out[...] = jnp.concatenate([mass, top, total, hit, jnp.zeros((4, top.shape[1]), F32)], axis=0)


def merge_stats(stats):
    return pl.pallas_call(
        merge_kernel,
        in_specs=[VMEM_SPEC] * len(stats),
        out_specs=VMEM_SPEC,
        out_shape=jax.ShapeDtypeStruct(stats[0].shape, F32),
        compiler_params=params(1),
        cost_estimate=COST,
        name="merge_stats",
    )(*stats)


def totals_kernel(*refs):
    stats, (columns, loss_ref) = refs[:-2], refs[-2:]
    parts = split_rows(stats)
    mass = tree(jnp.add, [r[0] for r in parts])
    top, total = total_at(parts, 1, 2)
    log_total = top + jnp.log(total)
    label_logit = tree(jnp.add, [r[3] for r in parts])
    columns[...] = columns_from_rows([mass + 1.0, log_total])
    loss_ref[...] = mass * log_total + log_total - label_logit


def token_totals(stats):
    rows = stats[0].shape[1]
    return pl.pallas_call(
        totals_kernel,
        in_specs=[VMEM_SPEC] * len(stats),
        out_specs=[VMEM_SPEC] * 2,
        out_shape=[jax.ShapeDtypeStruct((rows, LANES), F32), jax.ShapeDtypeStruct((1, rows), F32)],
        compiler_params=params(2),
        cost_estimate=COST,
        name="token_totals",
    )(*stats)


def grad_kernel(tok_ref, base_ref, labels_ref, columns, *refs, n_sums):
    sums = refs[:n_sums]
    logits_ref, *grads, inner_ref, inner = refs[n_sums:]
    step = pl.program_id(0)
    _, rows, cols = logits_ref.shape

    @pl.when(step == 0)
    def _():
        inner[...] = jnp.zeros_like(inner)

    lane = lax.broadcasted_iota(jnp.int32, (rows, LANES), 1)
    lift, log_total = columns[:, 0:1], columns[:, 1:2]
    label = labels_ref[...] - base_ref[token_group(step, tok_ref, len(grads))]
    for r in range(len(grads)):

        @pl.when(step == r)
        def _():
            running = inner[...]
            for b in range(cols // LANES):
                place = slice(b * LANES, (b + 1) * LANES)
                target = functools.reduce(
                    jnp.add, [ref[z, b].astype(F32) for ref in sums for z in range(ref.shape[0])]
                )
                score = logits_ref[0, :, place]
                running = running + target * score
                hit = jnp.where(lane == label - b * LANES, 1.0, 0.0)
                grads[r][:, place] = (lift * jnp.exp(score - log_total) - target - hit).astype(BF16)
            inner[...] = running

    @pl.when(step == pl.num_programs(0) - 1)
    def _():
        inner_ref[...] = rows_from_columns([jnp.sum(inner[...], axis=1, keepdims=True)])[0:1, :]


def token_group(step, tok_ref, n_tok):
    return tok_ref[0] ^ (n_tok - 1 - step)


def grad_logits(tok, base, label_column, columns, sums, logits):
    n_tok, rows, cols = logits.shape
    per = cols // LANES
    whole = lambda shape: pl.BlockSpec(shape, lambda t, tok_ref: (0,) * len(shape))
    group = lambda t, tok_ref: token_group(t, tok_ref, n_tok)
    return pl.pallas_call(
        functools.partial(grad_kernel, n_sums=len(sums)),
        grid_spec=pltpu.PrefetchScalarGridSpec(
            num_scalar_prefetch=1,
            grid=(n_tok,),
            in_specs=[SMEM_SPEC, whole(label_column.shape), whole(columns.shape)]
            + [pl.BlockSpec((s.shape[0], per, rows, LANES), lambda t, r: (0, group(t, r), 0, 0)) for s in sums]
            + [pl.BlockSpec((1, rows, cols), lambda t, r: (group(t, r), 0, 0))],
            out_specs=[whole((rows, cols))] * n_tok + [whole((1, rows))],
            scratch_shapes=[pltpu.VMEM((rows, LANES), F32)],
        ),
        out_shape=[pltpu.HBM((rows, cols), BF16)] * n_tok + [jax.ShapeDtypeStruct((1, rows), F32)],
        compiler_params=params(14),
        cost_estimate=COST,
        name="grad_logits",
    )(tok, base, label_column, columns, *sums, logits)


def product_kernel(tok_ref, a_ref, *refs):
    pieces, o_ref, b_ref = refs[:-2], refs[-2], refs[-1]
    rows = pieces[0].shape[0]

    @pl.when(pl.program_id(0) == 0)
    def _():
        for r, piece in enumerate(pieces):
            start = pl.multiple_of(token_group(r, tok_ref, len(pieces)) * rows, rows)
            b_ref[pl.ds(start, rows), :] = piece[...]

    o_ref[...] = jnp.dot(a_ref[...], b_ref[...], preferred_element_type=F32).astype(o_ref.dtype)


def head_product(tok, a, pieces):
    m, k = a.shape
    rows, n = pieces[0].shape
    tile = m // 4
    return pl.pallas_call(
        product_kernel,
        grid=(m // tile,),
        in_specs=[SMEM_SPEC, pl.BlockSpec((tile, k), lambda i: (i, 0))]
        + [pl.BlockSpec((rows, n), lambda i: (0, 0))] * len(pieces),
        out_specs=pl.BlockSpec((tile, n), lambda i: (i, 0)),
        out_shape=jax.ShapeDtypeStruct((m, n), BF16),
        scratch_shapes=[pltpu.VMEM((k, n), BF16)],
        compiler_params=params(20),
        cost_estimate=COST,
        name="head_product",
    )(tok, in_hbm(a), *pieces)


def swap(x, axis, mask):
    return lax.ppermute(x, axis, [(i, i ^ mask) for i in range(lax.axis_size(axis))])


def gather_chips(x):
    n = lax.axis_size("vocab")
    if n > 8:
        lines = [[2 * z + c for z in range(n // 2)] for c in range(2)]
        everything = lax.all_gather(x, "vocab", axis=0, axis_index_groups=lines)
        return [everything[z] for z in range(n // 2)]
    return [x] + [swap(x, "vocab", r) for r in range(2, n, 2)]


def gather_cores(x):
    chips = gather_chips(x)
    return chips + [swap(chip, "vocab", 1) for chip in chips]


def half_rows(hidden, spot, n_tok):
    half = hidden.shape[0] // 2
    own = lax.dynamic_slice_in_dim(hidden, spot[0] * half, half)
    return jnp.broadcast_to(own, (n_tok,) + own.shape)


def plus(a, b):
    return (a.astype(F32) + b.astype(F32)).astype(BF16)


def exchange_tok(x):
    return lax.all_to_all(x, "tok", split_axis=0, concat_axis=0, tiled=True)


def send(x, hops):
    return lax.ppermute(x, "vocab", [(2 * a + c, 2 * b + c) for a, b in hops for c in range(2)])


def local(teacher_logits, hidden, new_head, labels, map_target, map_weight):
    rows = teacher_logits.shape[0]
    block = map_weight.shape[2]
    n_tok = lax.axis_size("tok")
    n_vocab = lax.axis_size("vocab")
    n_z = n_vocab // 2
    new_cols = new_head.shape[1]
    per = new_cols // block
    tok = lax.axis_index("tok")
    vocab = lax.axis_index("vocab")
    spot = jnp.stack([vocab % 2, vocab // 2]).astype(jnp.int32)
    slots = n_tok * per
    in_line = n_z == 4

    owner = map_target // per
    owner_vocab = owner % n_vocab
    owner_z = owner_vocab // 2
    if in_line:
        z = vocab // 2
        outer = (owner_z == 0) | (owner_z == n_z - 1)
        near_place = jnp.where(owner_z == z, 3, 2)
        place = jnp.where((owner_z // 2) == (z // 2), near_place, jnp.where(outer, 0, 1))
    else:
        place = owner_z
    slot = (owner // n_vocab) * per + map_target % per
    code = (((owner_vocab % 2) * n_z + place) * SLOT_BASE + slot).astype(jnp.int32).reshape(-1)

    peer_logits = swap(teacher_logits, "vocab", 1)
    peer_code = swap(code, "vocab", 1)
    peer_weight = swap(map_weight, "vocab", 1)
    teacher = teacher_stats(teacher_logits)
    totals = gather_cores(teacher)
    lists, counts = plan(code, peer_code, 2 * n_z)
    probs = teacher_probs(teacher_logits, peer_logits, totals)

    if in_line:
        inward, across, beyond = [(0, 1), (3, 2)], [(1, 2), (2, 1)], [(1, 3), (2, 0)]
        far_outer, mass_a = chip_sums(spot, lists, counts, probs, map_weight, peer_weight, 0, 1, 1, slots)
        first = send(far_outer, inward)
        rows_in, mass_a = lax.optimization_barrier((hidden, mass_a))
        copies, probs = lax.optimization_barrier((half_rows(rows_in, spot, n_tok), probs))
        near = exchange_tok(copies)
        far_inner, beside, own, mass_b = chip_sums(
            spot, lists, counts, probs, map_weight, peer_weight, 1, 3, 1, slots
        )
        second = send(far_inner, inward)
        first, mass = lax.optimization_barrier((first, mass_a + mass_b))
        merged = plus(far_outer, first)
        arrived = send(merged, beyond)
        near, waited, merged = lax.optimization_barrier((near, beside, merged))
        third = swap(waited, "vocab", 2)
    else:
        sums, mass = chip_sums(spot, lists, counts, probs, map_weight, peer_weight, 0, 1, n_z, slots)
        lines = [[2 * z + c for z in range(n_z)] for c in range(2)]
        sums = lax.all_to_all(
            sums.reshape(n_z, slots, rows, block),
            "vocab",
            split_axis=0,
            concat_axis=0,
            axis_index_groups=lines,
            tiled=True,
        )
        sums = [sums]
        near = exchange_tok(half_rows(hidden, spot, n_tok))

    near = near.reshape(n_tok * (rows // 2), -1)
    far = swap(near, "vocab", 1)
    scores, turned = student_logits(spot, mass, near, far, new_head, n_tok)
    base = (jnp.arange(n_tok, dtype=jnp.int32) * n_vocab + vocab) * new_cols
    label_column = lax.dynamic_slice_in_dim(labels, tok * rows, rows).reshape(rows, 1)
    scores = exchange_tok(scores)
    if in_line:
        second, turned = lax.optimization_barrier((second, turned))
        merged_inner = plus(far_inner, second)
        crossed = send(merged_inner, across)
        scores, merged_inner = lax.optimization_barrier((scores, merged_inner))
        sums = [x[None] for x in (own, third, crossed, arrived)]
    student = student_stats(base, label_column, mass, scores)
    student = merge_stats([student, swap(student, "vocab", 1)])
    stats = gather_chips(student)

    group = tok.astype(jnp.int32).reshape(1)
    columns, base_loss = token_totals(stats)
    *grads, inner = grad_logits(group, base, label_column, columns, sums, scores)
    grads = [swap(x, "tok", n_tok - 1 - r) for r, x in enumerate(grads[:-1])] + [grads[-1]]
    mask = 1
    while mask < n_vocab:
        inner = inner + swap(inner, "vocab", mask)
        mask *= 2
    return ((base_loss - inner).reshape(rows), head_product(group, turned, grads))


def solution(mesh):
    return jax.shard_map(
        local,
        mesh=mesh,
        in_specs=(
            P("tok", "vocab"),
            P("tok", None),
            P(None, ("tok", "vocab")),
            P(),
            P("vocab", None),
            P("vocab", None, None, None),
        ),
        out_specs=(P("tok"), P(None, ("tok", "vocab"))),
        check_vma=False,
    )
```

```python
import functools

import jax
import jax.numpy as jnp
from jax import lax
from jax.experimental import pallas as pl
from jax.experimental.pallas import tpu as pltpu
from jax.sharding import PartitionSpec as P

F32 = jnp.float32
BF16 = jnp.bfloat16
LANES = 128
BATCH = 8
COST = pl.CostEstimate(flops=1024, bytes_accessed=1024, transcendentals=0)
SLOT_BITS = 10
SLOT_BASE = 1 << SLOT_BITS
SMEM_SPEC = pl.BlockSpec(memory_space=pltpu.SMEM)
VMEM_SPEC = pl.BlockSpec(memory_space=pltpu.VMEM)


def params(mebibytes):
    return pltpu.CompilerParams(vmem_limit_bytes=mebibytes * 1024 * 1024)


def in_hbm(x):
    return pltpu.with_memory_space_constraint(x, pltpu.HBM)


def tree(op, items):
    while len(items) > 1:
        items = [op(items[i], items[i + 1]) if i + 1 < len(items) else items[i] for i in range(0, len(items), 2)]
    return items[0]


def total_at(rows_of, top_row, total_row):
    top = tree(jnp.maximum, [r[top_row] for r in rows_of])
    total = tree(jnp.add, [r[total_row] * jnp.exp(r[top_row] - top) for r in rows_of])
    return top, total


def split_rows(refs):
    return [[ref[k : k + 1, :] for k in range(8)] for ref in refs]


def rows_from_columns(columns):
    n = columns[0].shape[0]
    lane = lax.broadcasted_iota(jnp.int32, (n, LANES), 1)
    tile = jnp.zeros((n, LANES), F32)
    for place, column in enumerate(columns):
        tile = jnp.where(lane == place, column, tile)
    return tile.T[0:8, :]


def columns_from_rows(rows):
    n = rows[0].shape[1]
    return jnp.concatenate(rows + [jnp.zeros((LANES - len(rows), n), F32)], axis=0).T


def teacher_kernel(x_ref, stat_ref):
    rows, cols = x_ref.shape
    places = range(0, cols, LANES)
    read = lambda place: x_ref[:, place : place + LANES].astype(F32)
    top = jnp.full((rows, LANES), -jnp.inf, F32)
    for place in places:
        top = jnp.maximum(top, read(place))
    top = jnp.max(top, axis=1, keepdims=True)
    total = jnp.zeros((rows, LANES), F32)
    for place in places:
        total = total + jnp.exp(read(place) - top)
    stat_ref[...] = rows_from_columns([top, jnp.sum(total, axis=1, keepdims=True)])


def teacher_stats(x):
    return pl.pallas_call(
        teacher_kernel,
        in_specs=[VMEM_SPEC],
        out_specs=VMEM_SPEC,
        out_shape=jax.ShapeDtypeStruct((8, x.shape[0]), F32),
        compiler_params=params(6),
        cost_estimate=COST,
        name="teacher_stats",
    )(x)


def divide(x, n):
    return lax.shift_right_logical(x, n.bit_length() - 1) if n & (n - 1) == 0 else x // n


def plan_kernel(own_ref, peer_ref, list_ref, count_ref):
    lists = count_ref.shape[0]
    entries = own_ref.shape[0]
    for p in range(lists):
        count_ref[p] = 0

    def visit(i, carry):
        for side, ref in enumerate((own_ref, peer_ref)):
            code = ref[i]
            row = lax.shift_right_logical(code, SLOT_BITS)
            n = count_ref[row]
            list_ref[row, n] = (side * entries + i) * SLOT_BASE + (code & (SLOT_BASE - 1))
            count_ref[row] = n + 1
        return carry

    lax.fori_loop(0, entries, visit, 0, unroll=8)
    for p in range(lists):
        n = count_ref[p]
        for k in range(BATCH - 1):
            list_ref[p, n + k] = SLOT_BASE - 1


def plan(own_code, peer_code, lists):
    room = 2 * own_code.size + BATCH
    return pl.pallas_call(
        plan_kernel,
        in_specs=[SMEM_SPEC] * 2,
        out_specs=[SMEM_SPEC] * 2,
        out_shape=[jax.ShapeDtypeStruct((lists, room), jnp.int32), jax.ShapeDtypeStruct((lists,), jnp.int32)],
        compiler_params=params(1),
        cost_estimate=COST,
        name="entry_lists",
    )(own_code, peer_code)


def probs_kernel(x_own, x_peer, *refs):
    stats, (probs, columns) = refs[:-2], refs[-2:]

    @pl.when(pl.program_id(0) == 0)
    def _():
        top, total = total_at(split_rows(stats), 0, 1)
        columns[...] = columns_from_rows([top, 1.0 / total])

    top, scale = columns[:, 0:1], columns[:, 1:2]
    for side, x in enumerate((x_own, x_peer)):
        for j in range(x.shape[1] // LANES):
            raised = jnp.exp(x[:, j * LANES : (j + 1) * LANES].astype(F32) - top)
            probs[side, j] = (raised * scale).astype(BF16)


def sums_kernel(spot_ref, list_ref, count_ref, probs, w_own, w_peer, *refs, first, fan, pieces):
    outs, mass_ref, acc = refs[:-2], refs[-2], refs[-1]
    step = pl.program_id(0)
    slots, rows, _ = outs[0].shape
    side = w_own.shape[0] * fan
    mass = jnp.zeros((rows, LANES), F32)
    for k, out in enumerate(outs):
        piece = spot_ref[0] * pieces + first + k + step
        acc[...] = jnp.zeros_like(acc)

        def add(i, carry):
            parts = []
            for u in range(BATCH):
                item = list_ref[piece, i * BATCH + u]
                slot = item & (SLOT_BASE - 1)
                entry = lax.shift_right_logical(item, SLOT_BITS)
                weight = jnp.where(entry < side, 0, 1)
                parts.append((entry, slot, weight))
            for entry, slot, peer in parts:
                j = divide(entry, fan)
                f = entry - j * fan
                local_j = j - peer * (side // fan)
                weight = jnp.where(peer == 1, w_peer[local_j, f], w_own[local_j, f])
                part = jnp.dot(probs[j], weight, preferred_element_type=F32)
                acc[jnp.minimum(slot, slots)] += part.astype(BF16).astype(F32)
            return carry

        lax.fori_loop(0, divide(count_ref[piece] + BATCH - 1, BATCH), add, 0)

        def drain(i, mass):
            block = acc[i]
            out[i] = block.astype(BF16)
            return mass + block

        mass = lax.fori_loop(0, slots, drain, mass, unroll=4)
    part = rows_from_columns([jnp.sum(mass, axis=1, keepdims=True)])

    @pl.when(step == 0)
    def _():
        mass_ref[...] = part

    @pl.when(step > 0)
    def _():
        mass_ref[...] += part


def teacher_probs(x_own, x_peer, stats):
    rows, cols = x_own.shape
    steps = 4
    blocks = cols // LANES
    part = pl.BlockSpec((rows, cols // steps), lambda i: (0, i))
    probs = pl.pallas_call(
        probs_kernel,
        grid=(steps,),
        in_specs=[part, part] + [pl.BlockSpec(s.shape, lambda i: (0, 0)) for s in stats],
        out_specs=pl.BlockSpec((2, blocks // steps, rows, LANES), lambda i: (0, i, 0, 0)),
        out_shape=jax.ShapeDtypeStruct((2, blocks, rows, LANES), BF16),
        scratch_shapes=[pltpu.VMEM((rows, LANES), F32)],
        compiler_params=params(8),
        cost_estimate=COST,
        name="teacher_probs",
    )(in_hbm(x_own), in_hbm(x_peer), *stats)
    return probs.reshape(2 * blocks, rows, LANES)


def chip_sums(spot, lists, counts, probs, w_own, w_peer, first, n_out, steps, slots):
    rows = probs.shape[1]
    fan = w_own.shape[1]
    whole = lambda shape: pl.BlockSpec(shape, lambda s: (0,) * len(shape))
    out = pltpu.HBM((steps * slots, rows, LANES), BF16)
    return pl.pallas_call(
        functools.partial(sums_kernel, first=first, fan=fan, pieces=counts.shape[0] // 2),
        grid=(steps,),
        in_specs=[SMEM_SPEC] * 3 + [VMEM_SPEC] * 3,
        out_specs=[pl.BlockSpec((slots, rows, LANES), lambda s: (s, 0, 0))] * n_out + [whole((8, rows))],
        out_shape=[out] * n_out + [jax.ShapeDtypeStruct((8, rows), F32)],
        scratch_shapes=[pltpu.VMEM((slots + 1, rows, LANES), F32)],
        compiler_params=params(24),
        cost_estimate=COST,
        name="chip_sums",
    )(spot, lists, counts, probs, w_own, w_peer)


def logits_kernel(spot_ref, after_ref, near_ref, far_ref, head_ref, *refs):
    out_ref, turned_ref, everyone = refs
    n_tok = out_ref.shape[0]
    half = near_ref.shape[0] // n_tok
    del after_ref

    @pl.when(pl.program_id(0) == 0)
    def _():
        core = spot_ref[0]
        for r in range(n_tok):
            source = slice(r * half, (r + 1) * half)
            for side, ref in ((core, near_ref), (1 - core, far_ref)):
                start = pl.multiple_of((2 * r + side) * half, half)
                everyone[pl.ds(start, half), :] = ref[source, :]

    result = jnp.dot(everyone[...], head_ref[...], preferred_element_type=F32)
    for r in range(n_tok):
        out_ref[r] = result[2 * r * half : 2 * (r + 1) * half, :]
    part = turned_ref.shape[0]
    start = pl.multiple_of(pl.program_id(0) * part, part)
    turned_ref[...] = everyone[:, pl.ds(start, part)].T


def student_logits(spot, after, near, far, head, n_tok):
    every, depth = 2 * near.shape[0], near.shape[1]
    rows = every // n_tok
    cols = head.shape[1]
    tile = 256
    whole = lambda shape: pl.BlockSpec(shape, lambda i: (0, 0))
    return pl.pallas_call(
        logits_kernel,
        grid=(cols // tile,),
        in_specs=[SMEM_SPEC, pl.BlockSpec(memory_space=pl.ANY), whole(near.shape), whole(far.shape)]
        + [pl.BlockSpec((depth, tile), lambda i: (0, i))],
        out_specs=[pl.BlockSpec((n_tok, rows, tile), lambda i: (0, 0, i))]
        + [pl.BlockSpec((depth * tile // cols, every), lambda i: (i, 0))],
        out_shape=[pltpu.HBM((n_tok, rows, cols), F32), pltpu.HBM((depth, every), BF16)],
        scratch_shapes=[pltpu.VMEM((every, depth), BF16)],
        compiler_params=params(30),
        cost_estimate=COST,
        name="student_logits",
    )(spot, after, near, far, in_hbm(head))


def student_kernel(base_ref, labels_ref, mass_ref, logits_ref, stat_ref):
    n_tok, rows, cols = logits_ref.shape
    lane = lax.broadcasted_iota(jnp.int32, (rows, LANES), 1)
    label = labels_ref[...]
    top = jnp.full((rows, LANES), -jnp.inf, F32)
    hit = jnp.zeros((rows, LANES), F32)
    for t in range(n_tok):
        for b in range(0, cols, LANES):
            block = logits_ref[t, :, b : b + LANES]
            top = jnp.maximum(top, block)
            hit = hit + jnp.where(lane == label - (base_ref[t] + b), block, 0.0)
    top = jnp.max(top, axis=1, keepdims=True)
    total = jnp.zeros((rows, LANES), F32)
    for t in range(n_tok):
        for b in range(0, cols, LANES):
            total = total + jnp.exp(logits_ref[t, :, b : b + LANES] - top)
    total = jnp.sum(total, axis=1, keepdims=True)
    hit = jnp.sum(hit, axis=1, keepdims=True)
    stat_ref[...] = rows_from_columns([jnp.zeros_like(hit), top, total, hit])
    stat_ref[0:1, :] = mass_ref[0:1, :]


def student_stats(base, label_column, mass, logits):
    return pl.pallas_call(
        student_kernel,
        in_specs=[SMEM_SPEC] + [VMEM_SPEC] * 3,
        out_specs=VMEM_SPEC,
        out_shape=jax.ShapeDtypeStruct(mass.shape, F32),
        compiler_params=params(10),
        cost_estimate=COST,
        name="student_stats",
    )(base, label_column, mass, logits)


def merge_kernel(*refs):
    stats, out = refs[:-1], refs[-1]
    parts = split_rows(stats)
    mass = tree(jnp.add, [r[0] for r in parts])
    top, total = total_at(parts, 1, 2)
    hit = tree(jnp.add, [r[3] for r in parts])
    out[...] = jnp.concatenate([mass, top, total, hit, jnp.zeros((4, top.shape[1]), F32)], axis=0)


def merge_stats(stats):
    return pl.pallas_call(
        merge_kernel,
        in_specs=[VMEM_SPEC] * len(stats),
        out_specs=VMEM_SPEC,
        out_shape=jax.ShapeDtypeStruct(stats[0].shape, F32),
        compiler_params=params(1),
        cost_estimate=COST,
        name="merge_stats",
    )(*stats)


def totals_kernel(*refs):
    stats, (columns, loss_ref) = refs[:-2], refs[-2:]
    parts = split_rows(stats)
    mass = tree(jnp.add, [r[0] for r in parts])
    top, total = total_at(parts, 1, 2)
    log_total = top + jnp.log(total)
    label_logit = tree(jnp.add, [r[3] for r in parts])
    columns[...] = columns_from_rows([mass + 1.0, log_total])
    loss_ref[...] = mass * log_total + log_total - label_logit


def token_totals(stats):
    rows = stats[0].shape[1]
    return pl.pallas_call(
        totals_kernel,
        in_specs=[VMEM_SPEC] * len(stats),
        out_specs=[VMEM_SPEC] * 2,
        out_shape=[jax.ShapeDtypeStruct((rows, LANES), F32), jax.ShapeDtypeStruct((1, rows), F32)],
        compiler_params=params(2),
        cost_estimate=COST,
        name="token_totals",
    )(*stats)


def grad_kernel(tok_ref, base_ref, labels_ref, columns, *refs, n_sums):
    sums = refs[:n_sums]
    logits_ref, *grads, inner_ref, inner = refs[n_sums:]
    step = pl.program_id(0)
    _, rows, cols = logits_ref.shape

    @pl.when(step == 0)
    def _():
        inner[...] = jnp.zeros_like(inner)

    lane = lax.broadcasted_iota(jnp.int32, (rows, LANES), 1)
    lift, log_total = columns[:, 0:1], columns[:, 1:2]
    label = labels_ref[...] - base_ref[token_group(step, tok_ref, len(grads))]
    for r in range(len(grads)):

        @pl.when(step == r)
        def _():
            running = inner[...]
            for b in range(cols // LANES):
                place = slice(b * LANES, (b + 1) * LANES)
                target = functools.reduce(
                    jnp.add, [ref[z, b].astype(F32) for ref in sums for z in range(ref.shape[0])]
                )
                score = logits_ref[0, :, place]
                running = running + target * score
                hit = jnp.where(lane == label - b * LANES, 1.0, 0.0)
                grads[r][:, place] = (lift * jnp.exp(score - log_total) - target - hit).astype(BF16)
            inner[...] = running

    @pl.when(step == pl.num_programs(0) - 1)
    def _():
        inner_ref[...] = rows_from_columns([jnp.sum(inner[...], axis=1, keepdims=True)])[0:1, :]


def token_group(step, tok_ref, n_tok):
    return tok_ref[0] ^ (n_tok - 1 - step)


def grad_logits(tok, base, label_column, columns, sums, logits):
    n_tok, rows, cols = logits.shape
    per = cols // LANES
    whole = lambda shape: pl.BlockSpec(shape, lambda t, tok_ref: (0,) * len(shape))
    group = lambda t, tok_ref: token_group(t, tok_ref, n_tok)
    return pl.pallas_call(
        functools.partial(grad_kernel, n_sums=len(sums)),
        grid_spec=pltpu.PrefetchScalarGridSpec(
            num_scalar_prefetch=1,
            grid=(n_tok,),
            in_specs=[SMEM_SPEC, whole(label_column.shape), whole(columns.shape)]
            + [pl.BlockSpec((s.shape[0], per, rows, LANES), lambda t, r: (0, group(t, r), 0, 0)) for s in sums]
            + [pl.BlockSpec((1, rows, cols), lambda t, r: (group(t, r), 0, 0))],
            out_specs=[whole((rows, cols))] * n_tok + [whole((1, rows))],
            scratch_shapes=[pltpu.VMEM((rows, LANES), F32)],
        ),
        out_shape=[pltpu.HBM((rows, cols), BF16)] * n_tok + [jax.ShapeDtypeStruct((1, rows), F32)],
        compiler_params=params(14),
        cost_estimate=COST,
        name="grad_logits",
    )(tok, base, label_column, columns, *sums, logits)


def product_kernel(tok_ref, a_ref, *refs):
    pieces, o_ref, b_ref = refs[:-2], refs[-2], refs[-1]
    rows = pieces[0].shape[0]

    @pl.when(pl.program_id(0) == 0)
    def _():
        for r, piece in enumerate(pieces):
            start = pl.multiple_of(token_group(r, tok_ref, len(pieces)) * rows, rows)
            b_ref[pl.ds(start, rows), :] = piece[...]

    o_ref[...] = jnp.dot(a_ref[...], b_ref[...], preferred_element_type=F32).astype(o_ref.dtype)


def head_product(tok, a, pieces):
    m, k = a.shape
    rows, n = pieces[0].shape
    tile = m // 6
    return pl.pallas_call(
        product_kernel,
        grid=(m // tile,),
        in_specs=[SMEM_SPEC, pl.BlockSpec((tile, k), lambda i: (i, 0))]
        + [pl.BlockSpec((rows, n), lambda i: (0, 0))] * len(pieces),
        out_specs=pl.BlockSpec((tile, n), lambda i: (i, 0)),
        out_shape=jax.ShapeDtypeStruct((m, n), BF16),
        scratch_shapes=[pltpu.VMEM((k, n), BF16)],
        compiler_params=params(20),
        cost_estimate=COST,
        name="head_product",
    )(tok, in_hbm(a), *pieces[:-1], in_hbm(pieces[-1]))


def swap(x, axis, mask):
    return lax.ppermute(x, axis, [(i, i ^ mask) for i in range(lax.axis_size(axis))])


def gather_chips(x):
    n = lax.axis_size("vocab")
    if n > 8:
        lines = [[2 * z + c for z in range(n // 2)] for c in range(2)]
        everything = lax.all_gather(x, "vocab", axis=0, axis_index_groups=lines)
        return [everything[z] for z in range(n // 2)]
    return [x] + [swap(x, "vocab", r) for r in range(2, n, 2)]


def gather_cores(x):
    chips = gather_chips(x)
    return chips + [swap(chip, "vocab", 1) for chip in chips]


def half_rows(hidden, spot, n_tok):
    half = hidden.shape[0] // 2
    own = lax.dynamic_slice_in_dim(hidden, spot[0] * half, half)
    return jnp.broadcast_to(own, (n_tok,) + own.shape)


def plus(a, b):
    return (a.astype(F32) + b.astype(F32)).astype(BF16)


def exchange_tok(x):
    return lax.all_to_all(x, "tok", split_axis=0, concat_axis=0, tiled=True)


def send(x, hops):
    return lax.ppermute(x, "vocab", [(2 * a + c, 2 * b + c) for a, b in hops for c in range(2)])


def local(teacher_logits, hidden, new_head, labels, map_target, map_weight):
    rows = teacher_logits.shape[0]
    block = map_weight.shape[2]
    n_tok = lax.axis_size("tok")
    n_vocab = lax.axis_size("vocab")
    n_z = n_vocab // 2
    new_cols = new_head.shape[1]
    per = new_cols // block
    tok = lax.axis_index("tok")
    vocab = lax.axis_index("vocab")
    spot = jnp.stack([vocab % 2, vocab // 2]).astype(jnp.int32)
    slots = n_tok * per
    in_line = n_z == 4

    owner = map_target // per
    owner_vocab = owner % n_vocab
    owner_z = owner_vocab // 2
    if in_line:
        z = vocab // 2
        outer = (owner_z == 0) | (owner_z == n_z - 1)
        near_place = jnp.where(owner_z == z, 3, 2)
        place = jnp.where((owner_z // 2) == (z // 2), near_place, jnp.where(outer, 0, 1))
    else:
        place = owner_z
    slot = (owner // n_vocab) * per + map_target % per
    code = (((owner_vocab % 2) * n_z + place) * SLOT_BASE + slot).astype(jnp.int32).reshape(-1)

    peer_logits = swap(teacher_logits, "vocab", 1)
    peer_code = swap(code, "vocab", 1)
    peer_weight = swap(map_weight, "vocab", 1)
    teacher = teacher_stats(teacher_logits)
    totals = gather_cores(teacher)
    lists, counts = plan(code, peer_code, 2 * n_z)
    probs = teacher_probs(teacher_logits, peer_logits, totals)

    if in_line:
        inward, across, beyond = [(0, 1), (3, 2)], [(1, 2), (2, 1)], [(1, 3), (2, 0)]
        far_outer, mass_a = chip_sums(spot, lists, counts, probs, map_weight, peer_weight, 0, 1, 1, slots)
        first = send(far_outer, inward)
        rows_in, mass_a = lax.optimization_barrier((hidden, mass_a))
        copies, probs = lax.optimization_barrier((half_rows(rows_in, spot, n_tok), probs))
        near = exchange_tok(copies)
        far_inner, beside, own, mass_b = chip_sums(
            spot, lists, counts, probs, map_weight, peer_weight, 1, 3, 1, slots
        )
        second = send(far_inner, inward)
        first, mass = lax.optimization_barrier((first, mass_a + mass_b))
        merged = plus(far_outer, first)
        arrived = send(merged, beyond)
        near, waited, merged = lax.optimization_barrier((near, beside, merged))
        third = swap(waited, "vocab", 2)
    else:
        sums, mass = chip_sums(spot, lists, counts, probs, map_weight, peer_weight, 0, 1, n_z, slots)
        lines = [[2 * z + c for z in range(n_z)] for c in range(2)]
        sums = lax.all_to_all(
            sums.reshape(n_z, slots, rows, block),
            "vocab",
            split_axis=0,
            concat_axis=0,
            axis_index_groups=lines,
            tiled=True,
        )
        sums = [sums]
        near = exchange_tok(half_rows(hidden, spot, n_tok))

    near = near.reshape(n_tok * (rows // 2), -1)
    far = swap(near, "vocab", 1)
    scores, turned = student_logits(spot, mass, near, far, new_head, n_tok)
    base = (jnp.arange(n_tok, dtype=jnp.int32) * n_vocab + vocab) * new_cols
    label_column = lax.dynamic_slice_in_dim(labels, tok * rows, rows).reshape(rows, 1)
    scores = exchange_tok(scores)
    if in_line:
        second, arrived, turned = lax.optimization_barrier((second, arrived, turned))
        merged_inner = plus(far_inner, second)
        crossed = send(merged_inner, across)
        scores, merged_inner = lax.optimization_barrier((scores, merged_inner))
        sums = [x[None] for x in (own, third, crossed, arrived)]
    student = student_stats(base, label_column, mass, scores)
    student = merge_stats([student, swap(student, "vocab", 1)])
    stats = gather_chips(student)

    group = tok.astype(jnp.int32).reshape(1)
    columns, base_loss = token_totals(stats)
    *grads, inner = grad_logits(group, base, label_column, columns, sums, scores)
    grads = [swap(x, "tok", n_tok - 1 - r) for r, x in enumerate(grads[:-1])] + [grads[-1]]
    mask = 1
    while mask < n_vocab:
        inner = inner + swap(inner, "vocab", mask)
        mask *= 2
    return ((base_loss - inner).reshape(rows), head_product(group, turned, grads))


def solution(mesh):
    return jax.shard_map(
        local,
        mesh=mesh,
        in_specs=(
            P("tok", "vocab"),
            P("tok", None),
            P(None, ("tok", "vocab")),
            P(),
            P("vocab", None),
            P("vocab", None, None, None),
        ),
        out_specs=(P("tok"), P(None, ("tok", "vocab"))),
        check_vma=False,
    )
```

```python
import functools

import jax
import jax.numpy as jnp
from jax import lax
from jax.experimental import pallas as pl
from jax.experimental.pallas import tpu as pltpu
from jax.sharding import PartitionSpec as P

F32 = jnp.float32
BF16 = jnp.bfloat16
LANES = 128
BATCH = 8
COST = pl.CostEstimate(flops=1024, bytes_accessed=1024, transcendentals=0)
SLOT_BITS = 10
SLOT_BASE = 1 << SLOT_BITS
SMEM_SPEC = pl.BlockSpec(memory_space=pltpu.SMEM)
VMEM_SPEC = pl.BlockSpec(memory_space=pltpu.VMEM)


def params(mebibytes):
    return pltpu.CompilerParams(vmem_limit_bytes=mebibytes * 1024 * 1024)


def in_hbm(x):
    return pltpu.with_memory_space_constraint(x, pltpu.HBM)


def tree(op, items):
    while len(items) > 1:
        items = [op(items[i], items[i + 1]) if i + 1 < len(items) else items[i] for i in range(0, len(items), 2)]
    return items[0]


def total_at(rows_of, top_row, total_row):
    top = tree(jnp.maximum, [r[top_row] for r in rows_of])
    total = tree(jnp.add, [r[total_row] * jnp.exp(r[top_row] - top) for r in rows_of])
    return top, total


def split_rows(refs):
    return [[ref[k : k + 1, :] for k in range(8)] for ref in refs]


def rows_from_columns(columns):
    n = columns[0].shape[0]
    lane = lax.broadcasted_iota(jnp.int32, (n, LANES), 1)
    tile = jnp.zeros((n, LANES), F32)
    for place, column in enumerate(columns):
        tile = jnp.where(lane == place, column, tile)
    return tile.T[0:8, :]


def columns_from_rows(rows):
    n = rows[0].shape[1]
    return jnp.concatenate(rows + [jnp.zeros((LANES - len(rows), n), F32)], axis=0).T


def teacher_kernel(x_ref, stat_ref):
    rows, cols = x_ref.shape
    places = range(0, cols, LANES)
    read = lambda place: x_ref[:, place : place + LANES].astype(F32)
    top = jnp.full((rows, LANES), -jnp.inf, F32)
    for place in places:
        top = jnp.maximum(top, read(place))
    top = jnp.max(top, axis=1, keepdims=True)
    total = jnp.zeros((rows, LANES), F32)
    for place in places:
        total = total + jnp.exp(read(place) - top)
    stat_ref[...] = rows_from_columns([top, jnp.sum(total, axis=1, keepdims=True)])


def teacher_stats(x):
    return pl.pallas_call(
        teacher_kernel,
        in_specs=[VMEM_SPEC],
        out_specs=VMEM_SPEC,
        out_shape=jax.ShapeDtypeStruct((8, x.shape[0]), F32),
        compiler_params=params(6),
        cost_estimate=COST,
        name="teacher_stats",
    )(x)


def divide(x, n):
    return lax.shift_right_logical(x, n.bit_length() - 1) if n & (n - 1) == 0 else x // n


def plan_kernel(own_ref, peer_ref, list_ref, count_ref):
    lists = count_ref.shape[0]
    entries = own_ref.shape[0]
    for p in range(lists):
        count_ref[p] = 0

    def visit(i, carry):
        for side, ref in enumerate((own_ref, peer_ref)):
            code = ref[i]
            row = lax.shift_right_logical(code, SLOT_BITS)
            n = count_ref[row]
            list_ref[row, n] = (side * entries + i) * SLOT_BASE + (code & (SLOT_BASE - 1))
            count_ref[row] = n + 1
        return carry

    lax.fori_loop(0, entries, visit, 0, unroll=8)
    for p in range(lists):
        n = count_ref[p]
        for k in range(BATCH - 1):
            list_ref[p, n + k] = SLOT_BASE - 1


def plan(own_code, peer_code, lists):
    room = 2 * own_code.size + BATCH
    return pl.pallas_call(
        plan_kernel,
        in_specs=[SMEM_SPEC] * 2,
        out_specs=[SMEM_SPEC] * 2,
        out_shape=[jax.ShapeDtypeStruct((lists, room), jnp.int32), jax.ShapeDtypeStruct((lists,), jnp.int32)],
        compiler_params=params(1),
        cost_estimate=COST,
        name="entry_lists",
    )(own_code, peer_code)


def probs_kernel(x_own, x_peer, *refs):
    stats, (probs, columns) = refs[:-2], refs[-2:]

    @pl.when(pl.program_id(0) == 0)
    def _():
        top, total = total_at(split_rows(stats), 0, 1)
        columns[...] = columns_from_rows([top, 1.0 / total])

    top, scale = columns[:, 0:1], columns[:, 1:2]
    for side, x in enumerate((x_own, x_peer)):
        for j in range(x.shape[1] // LANES):
            raised = jnp.exp(x[:, j * LANES : (j + 1) * LANES].astype(F32) - top)
            probs[side, j] = (raised * scale).astype(BF16)


def sums_kernel(spot_ref, list_ref, count_ref, probs, w_own, w_peer, *refs, first, fan, pieces):
    outs, mass_ref, acc = refs[:-2], refs[-2], refs[-1]
    step = pl.program_id(0)
    slots, rows, _ = outs[0].shape
    side = w_own.shape[0] * fan
    mass = jnp.zeros((rows, LANES), F32)
    for k, out in enumerate(outs):
        piece = spot_ref[0] * pieces + first + k + step
        acc[...] = jnp.zeros_like(acc)

        def add(i, carry):
            parts = []
            for u in range(BATCH):
                item = list_ref[piece, i * BATCH + u]
                slot = item & (SLOT_BASE - 1)
                entry = lax.shift_right_logical(item, SLOT_BITS)
                weight = jnp.where(entry < side, 0, 1)
                parts.append((entry, slot, weight))
            for entry, slot, peer in parts:
                j = divide(entry, fan)
                f = entry - j * fan
                local_j = j - peer * (side // fan)
                weight = jnp.where(peer == 1, w_peer[local_j, f], w_own[local_j, f])
                part = jnp.dot(probs[j], weight, preferred_element_type=F32)
                acc[jnp.minimum(slot, slots)] += part.astype(BF16).astype(F32)
            return carry

        lax.fori_loop(0, divide(count_ref[piece] + BATCH - 1, BATCH), add, 0)

        def drain(i, mass):
            block = acc[i]
            out[i] = block.astype(BF16)
            return mass + block

        mass = lax.fori_loop(0, slots, drain, mass, unroll=4)
    part = rows_from_columns([jnp.sum(mass, axis=1, keepdims=True)])

    @pl.when(step == 0)
    def _():
        mass_ref[...] = part

    @pl.when(step > 0)
    def _():
        mass_ref[...] += part


def teacher_probs(x_own, x_peer, stats):
    rows, cols = x_own.shape
    steps = 4
    blocks = cols // LANES
    part = pl.BlockSpec((rows, cols // steps), lambda i: (0, i))
    probs = pl.pallas_call(
        probs_kernel,
        grid=(steps,),
        in_specs=[part, part] + [pl.BlockSpec(s.shape, lambda i: (0, 0)) for s in stats],
        out_specs=pl.BlockSpec((2, blocks // steps, rows, LANES), lambda i: (0, i, 0, 0)),
        out_shape=jax.ShapeDtypeStruct((2, blocks, rows, LANES), BF16),
        scratch_shapes=[pltpu.VMEM((rows, LANES), F32)],
        compiler_params=params(8),
        cost_estimate=COST,
        name="teacher_probs",
    )(in_hbm(x_own), in_hbm(x_peer), *stats)
    return probs.reshape(2 * blocks, rows, LANES)


def chip_sums(spot, lists, counts, probs, w_own, w_peer, first, n_out, steps, slots):
    rows = probs.shape[1]
    fan = w_own.shape[1]
    whole = lambda shape: pl.BlockSpec(shape, lambda s: (0,) * len(shape))
    out = pltpu.HBM((steps * slots, rows, LANES), BF16)
    return pl.pallas_call(
        functools.partial(sums_kernel, first=first, fan=fan, pieces=counts.shape[0] // 2),
        grid=(steps,),
        in_specs=[SMEM_SPEC] * 3 + [VMEM_SPEC] * 3,
        out_specs=[pl.BlockSpec((slots, rows, LANES), lambda s: (s, 0, 0))] * n_out + [whole((8, rows))],
        out_shape=[out] * n_out + [jax.ShapeDtypeStruct((8, rows), F32)],
        scratch_shapes=[pltpu.VMEM((slots + 1, rows, LANES), F32)],
        compiler_params=params(24),
        cost_estimate=COST,
        name="chip_sums",
    )(spot, lists, counts, probs, w_own, w_peer)


def logits_kernel(place_ref, after_ref, own_ref, *refs):
    n_other = (len(refs) - 4) // 2
    near, far, (head_ref, out_ref, turned_ref, everyone) = refs[:n_other], refs[n_other : 2 * n_other], refs[-4:]
    rows = own_ref.shape[0]
    half = rows // 2
    del after_ref

    @pl.when(pl.program_id(0) == 0)
    def _():
        core, tok = place_ref[0], place_ref[1]
        everyone[pl.ds(pl.multiple_of(tok * rows, rows), rows), :] = own_ref[...]
        for r in range(n_other):
            start = (tok ^ (r + 1)) * rows
            everyone[pl.ds(pl.multiple_of(start + core * half, half), half), :] = near[r][...]
            everyone[pl.ds(pl.multiple_of(start + (1 - core) * half, half), half), :] = far[r][...]

    result = jnp.dot(everyone[...], head_ref[...], preferred_element_type=F32)
    for t in range(out_ref.shape[0]):
        out_ref[t] = result[t * rows : (t + 1) * rows, :]
    part = turned_ref.shape[0]
    start = pl.multiple_of(pl.program_id(0) * part, part)
    turned_ref[...] = everyone[:, pl.ds(start, part)].T


def student_logits(place, after, own, near, far, head):
    rows, depth = own.shape
    n_tok = len(near) + 1
    every = n_tok * rows
    cols = head.shape[1]
    tile = 256
    whole = lambda shape: pl.BlockSpec(shape, lambda i: (0, 0))
    return pl.pallas_call(
        logits_kernel,
        grid=(cols // tile,),
        in_specs=[SMEM_SPEC, pl.BlockSpec(memory_space=pl.ANY), whole(own.shape)]
        + [whole(x.shape) for x in near + far]
        + [pl.BlockSpec((depth, tile), lambda i: (0, i))],
        out_specs=[
            pl.BlockSpec((n_tok, rows, tile), lambda i: (0, 0, i)),
            pl.BlockSpec((depth * tile // cols, every), lambda i: (i, 0)),
        ],
        out_shape=[pltpu.HBM((n_tok, rows, cols), F32), pltpu.HBM((depth, every), BF16)],
        scratch_shapes=[pltpu.VMEM((every, depth), BF16)],
        compiler_params=params(32),
        cost_estimate=COST,
        name="student_logits",
    )(place, after, own, *near, *far, in_hbm(head))


def student_kernel(base_ref, labels_ref, mass_ref, logits_ref, stat_ref):
    n_tok, rows, cols = logits_ref.shape
    lane = lax.broadcasted_iota(jnp.int32, (rows, LANES), 1)
    label = labels_ref[...]
    top = jnp.full((rows, LANES), -jnp.inf, F32)
    hit = jnp.zeros((rows, LANES), F32)
    for t in range(n_tok):
        for b in range(0, cols, LANES):
            block = logits_ref[t, :, b : b + LANES]
            top = jnp.maximum(top, block)
            hit = hit + jnp.where(lane == label - (base_ref[t] + b), block, 0.0)
    top = jnp.max(top, axis=1, keepdims=True)
    total = jnp.zeros((rows, LANES), F32)
    for t in range(n_tok):
        for b in range(0, cols, LANES):
            total = total + jnp.exp(logits_ref[t, :, b : b + LANES] - top)
    total = jnp.sum(total, axis=1, keepdims=True)
    hit = jnp.sum(hit, axis=1, keepdims=True)
    stat_ref[...] = rows_from_columns([jnp.zeros_like(hit), top, total, hit])
    stat_ref[0:1, :] = mass_ref[0:1, :]


def student_stats(base, label_column, mass, logits):
    return pl.pallas_call(
        student_kernel,
        in_specs=[SMEM_SPEC] + [VMEM_SPEC] * 3,
        out_specs=VMEM_SPEC,
        out_shape=jax.ShapeDtypeStruct(mass.shape, F32),
        compiler_params=params(10),
        cost_estimate=COST,
        name="student_stats",
    )(base, label_column, mass, logits)


def merge_kernel(*refs):
    stats, out = refs[:-1], refs[-1]
    parts = split_rows(stats)
    mass = tree(jnp.add, [r[0] for r in parts])
    top, total = total_at(parts, 1, 2)
    hit = tree(jnp.add, [r[3] for r in parts])
    out[...] = jnp.concatenate([mass, top, total, hit, jnp.zeros((4, top.shape[1]), F32)], axis=0)


def merge_stats(stats):
    return pl.pallas_call(
        merge_kernel,
        in_specs=[VMEM_SPEC] * len(stats),
        out_specs=VMEM_SPEC,
        out_shape=jax.ShapeDtypeStruct(stats[0].shape, F32),
        compiler_params=params(1),
        cost_estimate=COST,
        name="merge_stats",
    )(*stats)


def totals_kernel(*refs):
    stats, (columns, loss_ref) = refs[:-2], refs[-2:]
    parts = split_rows(stats)
    mass = tree(jnp.add, [r[0] for r in parts])
    top, total = total_at(parts, 1, 2)
    log_total = top + jnp.log(total)
    label_logit = tree(jnp.add, [r[3] for r in parts])
    columns[...] = columns_from_rows([mass + 1.0, log_total])
    loss_ref[...] = mass * log_total + log_total - label_logit


def token_totals(stats):
    rows = stats[0].shape[1]
    return pl.pallas_call(
        totals_kernel,
        in_specs=[VMEM_SPEC] * len(stats),
        out_specs=[VMEM_SPEC] * 2,
        out_shape=[jax.ShapeDtypeStruct((rows, LANES), F32), jax.ShapeDtypeStruct((1, rows), F32)],
        compiler_params=params(2),
        cost_estimate=COST,
        name="token_totals",
    )(*stats)


def grad_kernel(tok_ref, base_ref, labels_ref, columns, *refs, n_sums):
    sums = refs[:n_sums]
    logits_ref, *grads, inner_ref, inner = refs[n_sums:]
    step = pl.program_id(0)
    _, rows, cols = logits_ref.shape

    @pl.when(step == 0)
    def _():
        inner[...] = jnp.zeros_like(inner)

    lane = lax.broadcasted_iota(jnp.int32, (rows, LANES), 1)
    lift, log_total = columns[:, 0:1], columns[:, 1:2]
    label = labels_ref[...] - base_ref[token_group(step, tok_ref, len(grads))]
    for r in range(len(grads)):

        @pl.when(step == r)
        def _():
            running = inner[...]
            for b in range(cols // LANES):
                place = slice(b * LANES, (b + 1) * LANES)
                target = functools.reduce(
                    jnp.add, [ref[z, b].astype(F32) for ref in sums for z in range(ref.shape[0])]
                )
                score = logits_ref[0, :, place]
                running = running + target * score
                hit = jnp.where(lane == label - b * LANES, 1.0, 0.0)
                grads[r][:, place] = (lift * jnp.exp(score - log_total) - target - hit).astype(BF16)
            inner[...] = running

    @pl.when(step == pl.num_programs(0) - 1)
    def _():
        inner_ref[...] = rows_from_columns([jnp.sum(inner[...], axis=1, keepdims=True)])[0:1, :]


def token_group(step, tok_ref, n_tok):
    return tok_ref[0] ^ (n_tok - 1 - step)


def grad_logits(tok, base, label_column, columns, sums, logits):
    n_tok, rows, cols = logits.shape
    per = cols // LANES
    whole = lambda shape: pl.BlockSpec(shape, lambda t, tok_ref: (0,) * len(shape))
    group = lambda t, tok_ref: token_group(t, tok_ref, n_tok)
    return pl.pallas_call(
        functools.partial(grad_kernel, n_sums=len(sums)),
        grid_spec=pltpu.PrefetchScalarGridSpec(
            num_scalar_prefetch=1,
            grid=(n_tok,),
            in_specs=[SMEM_SPEC, whole(label_column.shape), whole(columns.shape)]
            + [pl.BlockSpec((s.shape[0], per, rows, LANES), lambda t, r: (0, group(t, r), 0, 0)) for s in sums]
            + [pl.BlockSpec((1, rows, cols), lambda t, r: (group(t, r), 0, 0))],
            out_specs=[whole((rows, cols))] * n_tok + [whole((1, rows))],
            scratch_shapes=[pltpu.VMEM((rows, LANES), F32)],
        ),
        out_shape=[pltpu.HBM((rows, cols), BF16)] * n_tok + [jax.ShapeDtypeStruct((1, rows), F32)],
        compiler_params=params(14),
        cost_estimate=COST,
        name="grad_logits",
    )(tok, base, label_column, columns, *sums, logits)


def product_kernel(tok_ref, a_ref, *refs):
    pieces, o_ref, b_ref = refs[:-2], refs[-2], refs[-1]
    rows = pieces[0].shape[0]
    m, n = pl.program_id(0), pl.program_id(1)

    @pl.when((m == 0) & (n == 0))
    def _():
        for r, piece in enumerate(pieces):
            start = pl.multiple_of(token_group(r, tok_ref, len(pieces)) * rows, rows)
            for part in range(b_ref.shape[0]):
                b_ref[part, pl.ds(start, rows), :] = piece[:, part * b_ref.shape[2] : (part + 1) * b_ref.shape[2]]

    o_ref[...] = jnp.dot(a_ref[...], b_ref[n], preferred_element_type=F32).astype(o_ref.dtype)


def head_product(tok, a, pieces):
    m, k = a.shape
    rows, n = pieces[0].shape
    steps = 2
    return pl.pallas_call(
        product_kernel,
        grid=(steps, steps),
        in_specs=[SMEM_SPEC, pl.BlockSpec((m // steps, k), lambda i, j: (i, 0))]
        + [pl.BlockSpec((rows, n), lambda i, j: (0, 0))] * len(pieces),
        out_specs=pl.BlockSpec((m // steps, n // steps), lambda i, j: (i, j)),
        out_shape=jax.ShapeDtypeStruct((m, n), BF16),
        scratch_shapes=[pltpu.VMEM((steps, k, n // steps), BF16)],
        compiler_params=params(30),
        cost_estimate=COST,
        name="head_product",
    )(tok, in_hbm(a), *pieces[:-1], in_hbm(pieces[-1]))


def swap(x, axis, mask):
    return lax.ppermute(x, axis, [(i, i ^ mask) for i in range(lax.axis_size(axis))])


def gather_chips(x):
    n = lax.axis_size("vocab")
    if n > 8:
        lines = [[2 * z + c for z in range(n // 2)] for c in range(2)]
        everything = lax.all_gather(x, "vocab", axis=0, axis_index_groups=lines)
        return [everything[z] for z in range(n // 2)]
    return [x] + [swap(x, "vocab", r) for r in range(2, n, 2)]


def gather_cores(x):
    chips = gather_chips(x)
    return chips + [swap(chip, "vocab", 1) for chip in chips]


def plus(a, b):
    return (a.astype(F32) + b.astype(F32)).astype(BF16)


def exchange_tok(x):
    return lax.all_to_all(x, "tok", split_axis=0, concat_axis=0, tiled=True)


def send(x, hops):
    return lax.ppermute(x, "vocab", [(2 * a + c, 2 * b + c) for a, b in hops for c in range(2)])


def local(teacher_logits, hidden, new_head, labels, map_target, map_weight):
    rows = teacher_logits.shape[0]
    block = map_weight.shape[2]
    n_tok = lax.axis_size("tok")
    n_vocab = lax.axis_size("vocab")
    n_z = n_vocab // 2
    new_cols = new_head.shape[1]
    per = new_cols // block
    tok = lax.axis_index("tok")
    vocab = lax.axis_index("vocab")
    spot = jnp.stack([vocab % 2, vocab // 2]).astype(jnp.int32)
    slots = n_tok * per
    in_line = n_z == 4

    owner = map_target // per
    owner_vocab = owner % n_vocab
    owner_z = owner_vocab // 2
    if in_line:
        z = vocab // 2
        outer = (owner_z == 0) | (owner_z == n_z - 1)
        near_place = jnp.where(owner_z == z, 3, 2)
        place = jnp.where((owner_z // 2) == (z // 2), near_place, jnp.where(outer, 0, 1))
    else:
        place = owner_z
    slot = (owner // n_vocab) * per + map_target % per
    code = (((owner_vocab % 2) * n_z + place) * SLOT_BASE + slot).astype(jnp.int32).reshape(-1)

    peer_logits = swap(teacher_logits, "vocab", 1)
    peer_code = swap(code, "vocab", 1)
    peer_weight = swap(map_weight, "vocab", 1)
    teacher = teacher_stats(teacher_logits)
    totals = gather_cores(teacher)
    lists, counts = plan(code, peer_code, 2 * n_z)
    probs = teacher_probs(teacher_logits, peer_logits, totals)

    half = lax.dynamic_slice_in_dim(hidden, spot[0] * (rows // 2), rows // 2)
    if in_line:
        inward, across, beyond = [(0, 1), (3, 2)], [(1, 2), (2, 1)], [(1, 3), (2, 0)]
        far_outer, mass_a = chip_sums(spot, lists, counts, probs, map_weight, peer_weight, 0, 1, 1, slots)
        first = send(far_outer, inward)
        half, probs, mass_a = lax.optimization_barrier((half, probs, mass_a))
        near = [swap(half, "tok", r) for r in range(1, n_tok)]
        far_inner, beside, own, mass_b = chip_sums(
            spot, lists, counts, probs, map_weight, peer_weight, 1, 3, 1, slots
        )
        second = send(far_inner, inward)
        first, mass = lax.optimization_barrier((first, mass_a + mass_b))
        merged = plus(far_outer, first)
        arrived = send(merged, beyond)
        *near, waited, merged = lax.optimization_barrier((*near, beside, merged))
        third = swap(waited, "vocab", 2)
    else:
        sums, mass = chip_sums(spot, lists, counts, probs, map_weight, peer_weight, 0, 1, n_z, slots)
        lines = [[2 * z + c for z in range(n_z)] for c in range(2)]
        sums = lax.all_to_all(
            sums.reshape(n_z, slots, rows, block),
            "vocab",
            split_axis=0,
            concat_axis=0,
            axis_index_groups=lines,
            tiled=True,
        )
        sums = [sums]
        near = [swap(half, "tok", r) for r in range(1, n_tok)]

    far = [swap(x, "vocab", 1) for x in near]
    where = jnp.stack([vocab % 2, tok]).astype(jnp.int32)
    scores, turned = student_logits(where, mass, hidden, near, far, new_head)
    base = (jnp.arange(n_tok, dtype=jnp.int32) * n_vocab + vocab) * new_cols
    label_column = lax.dynamic_slice_in_dim(labels, tok * rows, rows).reshape(rows, 1)
    scores = exchange_tok(scores)
    if in_line:
        second, arrived, turned = lax.optimization_barrier((second, arrived, turned))
        merged_inner = plus(far_inner, second)
        crossed = send(merged_inner, across)
        scores, merged_inner = lax.optimization_barrier((scores, merged_inner))
        sums = [x[None] for x in (own, third, crossed, arrived)]
    student = student_stats(base, label_column, mass, scores)
    student = merge_stats([student, swap(student, "vocab", 1)])
    stats = gather_chips(student)

    group = tok.astype(jnp.int32).reshape(1)
    columns, base_loss = token_totals(stats)
    *grads, inner = grad_logits(group, base, label_column, columns, sums, scores)
    grads = [swap(x, "tok", n_tok - 1 - r) for r, x in enumerate(grads[:-1])] + [grads[-1]]
    mask = 1
    while mask < n_vocab:
        inner = inner + swap(inner, "vocab", mask)
        mask *= 2
    return ((base_loss - inner).reshape(rows), head_product(group, turned, grads))


def solution(mesh):
    return jax.shard_map(
        local,
        mesh=mesh,
        in_specs=(
            P("tok", "vocab"),
            P("tok", None),
            P(None, ("tok", "vocab")),
            P(),
            P("vocab", None),
            P("vocab", None, None, None),
        ),
        out_specs=(P("tok"), P(None, ("tok", "vocab"))),
        check_vma=False,
    )
```

```python
import functools

import jax
import jax.numpy as jnp
from jax import lax
from jax.experimental import pallas as pl
from jax.experimental.pallas import tpu as pltpu
from jax.sharding import PartitionSpec as P

F32 = jnp.float32
BF16 = jnp.bfloat16
LANES = 128
BATCH = 8
COST = pl.CostEstimate(flops=1024, bytes_accessed=1024, transcendentals=0)
SLOT_BITS = 10
SLOT_BASE = 1 << SLOT_BITS
SMEM_SPEC = pl.BlockSpec(memory_space=pltpu.SMEM)
VMEM_SPEC = pl.BlockSpec(memory_space=pltpu.VMEM)


def params(mebibytes):
    return pltpu.CompilerParams(vmem_limit_bytes=mebibytes * 1024 * 1024)


def in_hbm(x):
    return pltpu.with_memory_space_constraint(x, pltpu.HBM)


def in_vmem(x):
    return pltpu.with_memory_space_constraint(x, pltpu.VMEM)


def tree(op, items):
    while len(items) > 1:
        items = [op(items[i], items[i + 1]) if i + 1 < len(items) else items[i] for i in range(0, len(items), 2)]
    return items[0]


def total_at(rows_of, top_row, total_row):
    top = tree(jnp.maximum, [r[top_row] for r in rows_of])
    total = tree(jnp.add, [r[total_row] * jnp.exp(r[top_row] - top) for r in rows_of])
    return top, total


def split_rows(refs):
    return [[ref[k : k + 1, :] for k in range(8)] for ref in refs]


def rows_from_columns(columns):
    n = columns[0].shape[0]
    lane = lax.broadcasted_iota(jnp.int32, (n, LANES), 1)
    tile = jnp.zeros((n, LANES), F32)
    for place, column in enumerate(columns):
        tile = jnp.where(lane == place, column, tile)
    return tile.T[0:8, :]


def columns_from_rows(rows):
    n = rows[0].shape[1]
    return jnp.concatenate(rows + [jnp.zeros((LANES - len(rows), n), F32)], axis=0).T


def teacher_kernel(x_ref, stat_ref):
    rows, cols = x_ref.shape
    places = range(0, cols, LANES)
    read = lambda place: x_ref[:, place : place + LANES].astype(F32)
    top = jnp.full((rows, LANES), -jnp.inf, F32)
    for place in places:
        top = jnp.maximum(top, read(place))
    top = jnp.max(top, axis=1, keepdims=True)
    total = jnp.zeros((rows, LANES), F32)
    for place in places:
        total = total + jnp.exp(read(place) - top)
    stat_ref[...] = rows_from_columns([top, jnp.sum(total, axis=1, keepdims=True)])


def teacher_stats(x):
    return pl.pallas_call(
        teacher_kernel,
        in_specs=[VMEM_SPEC],
        out_specs=VMEM_SPEC,
        out_shape=jax.ShapeDtypeStruct((8, x.shape[0]), F32),
        compiler_params=params(6),
        cost_estimate=COST,
        name="teacher_stats",
    )(x)


def divide(x, n):
    return lax.shift_right_logical(x, n.bit_length() - 1) if n & (n - 1) == 0 else x // n


def plan_kernel(own_ref, peer_ref, list_ref, count_ref):
    lists = count_ref.shape[0]
    entries = own_ref.shape[0]
    for p in range(lists):
        count_ref[p] = 0

    def visit(i, carry):
        for side, ref in enumerate((own_ref, peer_ref)):
            code = ref[i]
            row = lax.shift_right_logical(code, SLOT_BITS)
            n = count_ref[row]
            list_ref[row, n] = (side * entries + i) * SLOT_BASE + (code & (SLOT_BASE - 1))
            count_ref[row] = n + 1
        return carry

    lax.fori_loop(0, entries, visit, 0, unroll=8)
    for p in range(lists):
        n = count_ref[p]
        for k in range(BATCH - 1):
            list_ref[p, n + k] = SLOT_BASE - 1


def plan(own_code, peer_code, lists):
    room = 2 * own_code.size + BATCH
    return pl.pallas_call(
        plan_kernel,
        in_specs=[SMEM_SPEC] * 2,
        out_specs=[SMEM_SPEC] * 2,
        out_shape=[jax.ShapeDtypeStruct((lists, room), jnp.int32), jax.ShapeDtypeStruct((lists,), jnp.int32)],
        compiler_params=params(1),
        cost_estimate=COST,
        name="entry_lists",
    )(own_code, peer_code)


def probs_kernel(x_own, x_peer, *refs):
    stats, (probs, columns) = refs[:-2], refs[-2:]

    @pl.when(pl.program_id(0) == 0)
    def _():
        top, total = total_at(split_rows(stats), 0, 1)
        columns[...] = columns_from_rows([top, 1.0 / total])

    top, scale = columns[:, 0:1], columns[:, 1:2]
    for side, x in enumerate((x_own, x_peer)):
        for j in range(x.shape[1] // LANES):
            raised = jnp.exp(x[:, j * LANES : (j + 1) * LANES].astype(F32) - top)
            probs[side, j] = (raised * scale).astype(BF16)


def sums_kernel(spot_ref, list_ref, count_ref, probs, w_own, w_peer, *refs, first, fan, pieces):
    outs, mass_ref, acc = refs[:-2], refs[-2], refs[-1]
    step = pl.program_id(0)
    slots, rows, _ = outs[0].shape
    side = w_own.shape[0] * fan
    mass = jnp.zeros((rows, LANES), F32)
    for k, out in enumerate(outs):
        piece = spot_ref[0] * pieces + first + k + step
        acc[...] = jnp.zeros_like(acc)

        def add(i, carry):
            parts = []
            for u in range(BATCH):
                item = list_ref[piece, i * BATCH + u]
                slot = item & (SLOT_BASE - 1)
                entry = lax.shift_right_logical(item, SLOT_BITS)
                weight = jnp.where(entry < side, 0, 1)
                parts.append((entry, slot, weight))
            for entry, slot, peer in parts:
                j = divide(entry, fan)
                f = entry - j * fan
                local_j = j - peer * (side // fan)
                weight = jnp.where(peer == 1, w_peer[local_j, f], w_own[local_j, f])
                part = jnp.dot(probs[j], weight, preferred_element_type=F32)
                acc[jnp.minimum(slot, slots)] += part.astype(BF16).astype(F32)
            return carry

        lax.fori_loop(0, divide(count_ref[piece] + BATCH - 1, BATCH), add, 0)

        def drain(i, mass):
            block = acc[i]
            out[i] = block.astype(BF16)
            return mass + block

        mass = lax.fori_loop(0, slots, drain, mass, unroll=4)
    part = rows_from_columns([jnp.sum(mass, axis=1, keepdims=True)])

    @pl.when(step == 0)
    def _():
        mass_ref[...] = part

    @pl.when(step > 0)
    def _():
        mass_ref[...] += part


def teacher_probs(x_own, x_peer, stats):
    rows, cols = x_own.shape
    steps = 4
    blocks = cols // LANES
    part = pl.BlockSpec((rows, cols // steps), lambda i: (0, i))
    probs = pl.pallas_call(
        probs_kernel,
        grid=(steps,),
        in_specs=[part, part] + [pl.BlockSpec(s.shape, lambda i: (0, 0)) for s in stats],
        out_specs=pl.BlockSpec((2, blocks // steps, rows, LANES), lambda i: (0, i, 0, 0)),
        out_shape=jax.ShapeDtypeStruct((2, blocks, rows, LANES), BF16),
        scratch_shapes=[pltpu.VMEM((rows, LANES), F32)],
        compiler_params=params(8),
        cost_estimate=COST,
        name="teacher_probs",
    )(in_hbm(x_own), in_hbm(x_peer), *stats)
    return probs.reshape(2 * blocks, rows, LANES)


def chip_sums(spot, lists, counts, probs, w_own, w_peer, first, n_out, steps, slots):
    rows = probs.shape[1]
    fan = w_own.shape[1]
    whole = lambda shape: pl.BlockSpec(shape, lambda s: (0,) * len(shape))
    out = pltpu.HBM((steps * slots, rows, LANES), BF16)
    return pl.pallas_call(
        functools.partial(sums_kernel, first=first, fan=fan, pieces=counts.shape[0] // 2),
        grid=(steps,),
        in_specs=[SMEM_SPEC] * 3 + [VMEM_SPEC] * 3,
        out_specs=[pl.BlockSpec((slots, rows, LANES), lambda s: (s, 0, 0))] * n_out + [whole((8, rows))],
        out_shape=[out] * n_out + [jax.ShapeDtypeStruct((8, rows), F32)],
        scratch_shapes=[pltpu.VMEM((slots + 1, rows, LANES), F32)],
        compiler_params=params(24),
        cost_estimate=COST,
        name="chip_sums",
    )(spot, lists, counts, probs, w_own, w_peer)


def logits_kernel(place_ref, after_ref, own_ref, *refs):
    n_other = (len(refs) - 4) // 2
    near, far, (head_ref, out_ref, turned_ref, everyone) = refs[:n_other], refs[n_other : 2 * n_other], refs[-4:]
    rows = own_ref.shape[0]
    half = rows // 2
    del after_ref

    @pl.when(pl.program_id(0) == 0)
    def _():
        core = place_ref[0]
        everyone[0:rows, :] = own_ref[...]
        for r in range(n_other):
            start = (r + 1) * rows
            everyone[pl.ds(pl.multiple_of(start + core * half, half), half), :] = near[r][...]
            everyone[pl.ds(pl.multiple_of(start + (1 - core) * half, half), half), :] = far[r][...]

    result = jnp.dot(everyone[...], head_ref[...], preferred_element_type=F32)
    for r in range(n_other + 1):
        out_ref[place_ref[1] ^ r] = result[r * rows : (r + 1) * rows, :]
    part = turned_ref.shape[0] // pl.num_programs(0)
    start = pl.multiple_of(pl.program_id(0) * part, part)
    turned_ref[pl.ds(start, part), :] = everyone[:, pl.ds(start, part)].T


def student_logits(place, after, own, near, far, head):
    rows, depth = own.shape
    n_tok = len(near) + 1
    every = n_tok * rows
    cols = head.shape[1]
    tile = 256
    whole = lambda shape: pl.BlockSpec(shape, lambda i: (0, 0))
    return pl.pallas_call(
        logits_kernel,
        grid=(cols // tile,),
        in_specs=[SMEM_SPEC, pl.BlockSpec(memory_space=pl.ANY), whole(own.shape)]
        + [whole(x.shape) for x in near + far]
        + [pl.BlockSpec((depth, tile), lambda i: (0, i))],
        out_specs=[
            pl.BlockSpec((n_tok, rows, tile), lambda i: (0, 0, i)),
            VMEM_SPEC,
        ],
        out_shape=[pltpu.HBM((n_tok, rows, cols), F32), pltpu.VMEM((depth, every), BF16)],
        scratch_shapes=[pltpu.VMEM((every, depth), BF16)],
        compiler_params=params(32),
        cost_estimate=COST,
        name="student_logits",
    )(place, after, own, *near, *far, in_hbm(head))


def student_kernel(base_ref, labels_ref, mass_ref, logits_ref, stat_ref):
    n_tok, rows, cols = logits_ref.shape
    lane = lax.broadcasted_iota(jnp.int32, (rows, LANES), 1)
    label = labels_ref[...]
    top = jnp.full((rows, LANES), -jnp.inf, F32)
    hit = jnp.zeros((rows, LANES), F32)
    for t in range(n_tok):
        for b in range(0, cols, LANES):
            block = logits_ref[t, :, b : b + LANES]
            top = jnp.maximum(top, block)
            hit = hit + jnp.where(lane == label - (base_ref[t] + b), block, 0.0)
    top = jnp.max(top, axis=1, keepdims=True)
    total = jnp.zeros((rows, LANES), F32)
    for t in range(n_tok):
        for b in range(0, cols, LANES):
            total = total + jnp.exp(logits_ref[t, :, b : b + LANES] - top)
    total = jnp.sum(total, axis=1, keepdims=True)
    hit = jnp.sum(hit, axis=1, keepdims=True)
    stat_ref[...] = rows_from_columns([jnp.zeros_like(hit), top, total, hit])
    stat_ref[0:1, :] = mass_ref[0:1, :]


def student_stats(base, label_column, mass, logits):
    return pl.pallas_call(
        student_kernel,
        in_specs=[SMEM_SPEC] + [VMEM_SPEC] * 3,
        out_specs=VMEM_SPEC,
        out_shape=jax.ShapeDtypeStruct(mass.shape, F32),
        compiler_params=params(10),
        cost_estimate=COST,
        name="student_stats",
    )(base, label_column, mass, logits)


def merge_kernel(*refs):
    stats, out = refs[:-1], refs[-1]
    parts = split_rows(stats)
    mass = tree(jnp.add, [r[0] for r in parts])
    top, total = total_at(parts, 1, 2)
    hit = tree(jnp.add, [r[3] for r in parts])
    out[...] = jnp.concatenate([mass, top, total, hit, jnp.zeros((4, top.shape[1]), F32)], axis=0)


def merge_stats(stats):
    return pl.pallas_call(
        merge_kernel,
        in_specs=[VMEM_SPEC] * len(stats),
        out_specs=VMEM_SPEC,
        out_shape=jax.ShapeDtypeStruct(stats[0].shape, F32),
        compiler_params=params(1),
        cost_estimate=COST,
        name="merge_stats",
    )(*stats)


def totals_kernel(*refs):
    stats, (columns, loss_ref) = refs[:-2], refs[-2:]
    parts = split_rows(stats)
    mass = tree(jnp.add, [r[0] for r in parts])
    top, total = total_at(parts, 1, 2)
    log_total = top + jnp.log(total)
    label_logit = tree(jnp.add, [r[3] for r in parts])
    columns[...] = columns_from_rows([mass + 1.0, log_total])
    loss_ref[...] = mass * log_total + log_total - label_logit


def token_totals(stats):
    rows = stats[0].shape[1]
    return pl.pallas_call(
        totals_kernel,
        in_specs=[VMEM_SPEC] * len(stats),
        out_specs=[VMEM_SPEC] * 2,
        out_shape=[jax.ShapeDtypeStruct((rows, LANES), F32), jax.ShapeDtypeStruct((1, rows), F32)],
        compiler_params=params(2),
        cost_estimate=COST,
        name="token_totals",
    )(*stats)


def grad_kernel(tok_ref, base_ref, labels_ref, columns, *refs, n_sums):
    sums = refs[:n_sums]
    logits_ref, *grads, inner_ref, inner = refs[n_sums:]
    step = pl.program_id(0)
    _, rows, cols = logits_ref.shape

    @pl.when(step == 0)
    def _():
        inner[...] = jnp.zeros_like(inner)

    lane = lax.broadcasted_iota(jnp.int32, (rows, LANES), 1)
    lift, log_total = columns[:, 0:1], columns[:, 1:2]
    label = labels_ref[...] - base_ref[token_group(step, tok_ref, len(grads))]
    for r in range(len(grads)):

        @pl.when(step == r)
        def _():
            running = inner[...]
            for b in range(cols // LANES):
                place = slice(b * LANES, (b + 1) * LANES)
                target = functools.reduce(
                    jnp.add, [ref[z, b].astype(F32) for ref in sums for z in range(ref.shape[0])]
                )
                score = logits_ref[0, :, place]
                running = running + target * score
                hit = jnp.where(lane == label - b * LANES, 1.0, 0.0)
                grads[r][:, place] = (lift * jnp.exp(score - log_total) - target - hit).astype(BF16)
            inner[...] = running

    @pl.when(step == pl.num_programs(0) - 1)
    def _():
        inner_ref[...] = rows_from_columns([jnp.sum(inner[...], axis=1, keepdims=True)])[0:1, :]


def token_group(step, tok_ref, n_tok):
    return tok_ref[0] ^ ((step + 1) % n_tok)


def grad_logits(tok, base, label_column, columns, sums, logits):
    n_tok, rows, cols = logits.shape
    per = cols // LANES
    whole = lambda shape: pl.BlockSpec(shape, lambda t, tok_ref: (0,) * len(shape))
    group = lambda t, tok_ref: token_group(t, tok_ref, n_tok)
    return pl.pallas_call(
        functools.partial(grad_kernel, n_sums=len(sums)),
        grid_spec=pltpu.PrefetchScalarGridSpec(
            num_scalar_prefetch=1,
            grid=(n_tok,),
            in_specs=[SMEM_SPEC, whole(label_column.shape), whole(columns.shape)]
            + [pl.BlockSpec((s.shape[0], per, rows, LANES), lambda t, r: (0, group(t, r), 0, 0)) for s in sums]
            + [pl.BlockSpec((1, rows, cols), lambda t, r: (group(t, r), 0, 0))],
            out_specs=[whole((rows, cols))] * n_tok + [whole((1, rows))],
            scratch_shapes=[pltpu.VMEM((rows, LANES), F32)],
        ),
        out_shape=[pltpu.HBM((rows, cols), BF16)] * n_tok + [jax.ShapeDtypeStruct((1, rows), F32)],
        compiler_params=params(14),
        cost_estimate=COST,
        name="grad_logits",
    )(tok, base, label_column, columns, *sums, logits)


def stack_pieces(pieces, b_ref):
    rows = pieces[0].shape[0]

    @pl.when(pl.program_id(0) == 0)
    def _():
        for r, piece in enumerate(pieces):
            b_ref[r * rows : (r + 1) * rows, :] = piece[...]


def product_part(a_ref, b_ref, first):
    tile = a_ref.shape[0] // pl.num_programs(0)
    rows = pl.ds(pl.multiple_of(pl.program_id(0) * tile, tile), tile)
    return rows, jnp.dot(a_ref[rows, first : first + b_ref.shape[0]], b_ref[...], preferred_element_type=F32)


def first_product_kernel(a_ref, *refs):
    pieces, (acc_ref, b_ref) = refs[:-2], refs[-2:]
    stack_pieces(pieces, b_ref)
    rows, part = product_part(a_ref, b_ref, 0)
    acc_ref[rows, :] = part


def last_product_kernel(a_ref, acc_ref, *refs):
    pieces, (o_ref, end_ref, b_ref) = refs[:-3], refs[-3:]
    stack_pieces(pieces, b_ref)
    rows, part = product_part(a_ref, b_ref, a_ref.shape[1] - b_ref.shape[0])
    o_ref[...] = (acc_ref[rows, :] + part).astype(o_ref.dtype)
    end_ref[...] = jnp.zeros_like(end_ref)


def first_product(a, pieces):
    rows, n = pieces[0].shape
    return pl.pallas_call(
        first_product_kernel,
        grid=(4,),
        in_specs=[VMEM_SPEC] + [pl.BlockSpec((rows, n), lambda i: (0, 0))] * len(pieces),
        out_specs=VMEM_SPEC,
        out_shape=pltpu.VMEM((a.shape[0], n), F32),
        scratch_shapes=[pltpu.VMEM((len(pieces) * rows, n), BF16)],
        compiler_params=params(16),
        cost_estimate=COST,
        name="first_product",
    )(in_vmem(a), in_hbm(pieces[0]), *pieces[1:])


def last_product(a, acc, pieces):
    m = a.shape[0]
    rows, n = pieces[0].shape
    steps = 4
    return pl.pallas_call(
        last_product_kernel,
        grid=(steps,),
        in_specs=[VMEM_SPEC] * 2 + [pl.BlockSpec((rows, n), lambda i: (0, 0))] * len(pieces),
        out_specs=[pl.BlockSpec((m // steps, n), lambda i: (i, 0)), pl.BlockSpec((1, rows), lambda i: (0, 0))],
        out_shape=[jax.ShapeDtypeStruct((m, n), BF16), jax.ShapeDtypeStruct((1, rows), F32)],
        scratch_shapes=[pltpu.VMEM((len(pieces) * rows, n), BF16)],
        compiler_params=params(20),
        cost_estimate=COST,
        name="last_product",
    )(in_vmem(a), in_vmem(acc), *pieces)


def swap(x, axis, mask):
    return lax.ppermute(x, axis, [(i, i ^ mask) for i in range(lax.axis_size(axis))])


def gather_chips(x):
    n = lax.axis_size("vocab")
    if n > 8:
        lines = [[2 * z + c for z in range(n // 2)] for c in range(2)]
        everything = lax.all_gather(x, "vocab", axis=0, axis_index_groups=lines)
        return [everything[z] for z in range(n // 2)]
    return [x] + [swap(x, "vocab", r) for r in range(2, n, 2)]


def gather_cores(x):
    chips = gather_chips(x)
    return chips + [swap(chip, "vocab", 1) for chip in chips]


def plus(a, b):
    return (a.astype(F32) + b.astype(F32)).astype(BF16)


def exchange_tok(x):
    return lax.all_to_all(x, "tok", split_axis=0, concat_axis=0, tiled=True)


def send(x, hops):
    return lax.ppermute(x, "vocab", [(2 * a + c, 2 * b + c) for a, b in hops for c in range(2)])


def local(teacher_logits, hidden, new_head, labels, map_target, map_weight):
    rows = teacher_logits.shape[0]
    block = map_weight.shape[2]
    n_tok = lax.axis_size("tok")
    n_vocab = lax.axis_size("vocab")
    n_z = n_vocab // 2
    new_cols = new_head.shape[1]
    per = new_cols // block
    tok = lax.axis_index("tok")
    vocab = lax.axis_index("vocab")
    spot = jnp.stack([vocab % 2, vocab // 2]).astype(jnp.int32)
    slots = n_tok * per
    in_line = n_z == 4

    owner = map_target // per
    owner_vocab = owner % n_vocab
    owner_z = owner_vocab // 2
    if in_line:
        z = vocab // 2
        outer = (owner_z == 0) | (owner_z == n_z - 1)
        near_place = jnp.where(owner_z == z, 3, 2)
        place = jnp.where((owner_z // 2) == (z // 2), near_place, jnp.where(outer, 0, 1))
    else:
        place = owner_z
    slot = (owner // n_vocab) * per + map_target % per
    code = (((owner_vocab % 2) * n_z + place) * SLOT_BASE + slot).astype(jnp.int32).reshape(-1)

    peer_logits = swap(teacher_logits, "vocab", 1)
    peer_code = swap(code, "vocab", 1)
    peer_weight = swap(map_weight, "vocab", 1)
    teacher = teacher_stats(teacher_logits)
    totals = gather_cores(teacher)
    lists, counts = plan(code, peer_code, 2 * n_z)
    probs = teacher_probs(teacher_logits, peer_logits, totals)

    half = lax.dynamic_slice_in_dim(hidden, spot[0] * (rows // 2), rows // 2)
    if in_line:
        inward, across, beyond = [(0, 1), (3, 2)], [(1, 2), (2, 1)], [(1, 3), (2, 0)]
        far_outer, mass_a = chip_sums(spot, lists, counts, probs, map_weight, peer_weight, 0, 1, 1, slots)
        first = send(far_outer, inward)
        half, probs, mass_a = lax.optimization_barrier((half, probs, mass_a))
        near = [swap(half, "tok", r) for r in range(1, n_tok)]
        far_inner, beside, own, mass_b = chip_sums(
            spot, lists, counts, probs, map_weight, peer_weight, 1, 3, 1, slots
        )
        second = send(far_inner, inward)
        first, mass = lax.optimization_barrier((first, mass_a + mass_b))
        merged = plus(far_outer, first)
        arrived = send(merged, beyond)
        *near, waited, merged = lax.optimization_barrier((*near, beside, merged))
        third = swap(waited, "vocab", 2)
    else:
        sums, mass = chip_sums(spot, lists, counts, probs, map_weight, peer_weight, 0, 1, n_z, slots)
        lines = [[2 * z + c for z in range(n_z)] for c in range(2)]
        sums = lax.all_to_all(
            sums.reshape(n_z, slots, rows, block),
            "vocab",
            split_axis=0,
            concat_axis=0,
            axis_index_groups=lines,
            tiled=True,
        )
        sums = [sums]
        near = [swap(half, "tok", r) for r in range(1, n_tok)]

    far = [swap(x, "vocab", 1) for x in near]
    where = jnp.stack([vocab % 2, tok]).astype(jnp.int32)
    scores, turned = student_logits(where, mass, hidden, near, far, new_head)
    base = (jnp.arange(n_tok, dtype=jnp.int32) * n_vocab + vocab) * new_cols
    label_column = lax.dynamic_slice_in_dim(labels, tok * rows, rows).reshape(rows, 1)
    scores = exchange_tok(scores)
    if in_line:
        second, arrived, turned = lax.optimization_barrier((second, arrived, turned))
        merged_inner = plus(far_inner, second)
        crossed = send(merged_inner, across)
        scores, merged_inner = lax.optimization_barrier((scores, merged_inner))
        sums = [x[None] for x in (own, third, crossed, arrived)]
    student = student_stats(base, label_column, mass, scores)
    student = merge_stats([student, swap(student, "vocab", 1)])
    stats = gather_chips(student)

    group = tok.astype(jnp.int32).reshape(1)
    columns, base_loss = token_totals(stats)
    *grads, inner = grad_logits(group, base, label_column, columns, sums, scores)
    grads = [grads[-1]] + [swap(x, "tok", r + 1) for r, x in enumerate(grads[:-1])]
    split = n_tok // 2
    acc = first_product(turned, grads[:split])
    head_grad, end = last_product(turned, acc, grads[split:])
    mask = 1
    while mask < n_vocab:
        other = swap(inner, "vocab", mask)
        inner = inner + other
        mask *= 2
    return ((base_loss - inner + end).reshape(rows), head_grad)


def solution(mesh):
    return jax.shard_map(
        local,
        mesh=mesh,
        in_specs=(
            P("tok", "vocab"),
            P("tok", None),
            P(None, ("tok", "vocab")),
            P(),
            P("vocab", None),
            P("vocab", None, None, None),
        ),
        out_specs=(P("tok"), P(None, ("tok", "vocab"))),
        check_vma=False,
    )
```

```python
import functools

import jax
import jax.numpy as jnp
from jax import lax
from jax.experimental import pallas as pl
from jax.experimental.pallas import tpu as pltpu
from jax.sharding import PartitionSpec as P

F32 = jnp.float32
BF16 = jnp.bfloat16
LANES = 128
BATCH = 8
COST = pl.CostEstimate(flops=1024, bytes_accessed=1024, transcendentals=0)
SLOT_BITS = 10
SLOT_BASE = 1 << SLOT_BITS
SMEM_SPEC = pl.BlockSpec(memory_space=pltpu.SMEM)
VMEM_SPEC = pl.BlockSpec(memory_space=pltpu.VMEM)


def params(mebibytes):
    return pltpu.CompilerParams(vmem_limit_bytes=mebibytes * 1024 * 1024)


def in_hbm(x):
    return pltpu.with_memory_space_constraint(x, pltpu.HBM)


def in_vmem(x):
    return pltpu.with_memory_space_constraint(x, pltpu.VMEM)


def tree(op, items):
    while len(items) > 1:
        items = [op(items[i], items[i + 1]) if i + 1 < len(items) else items[i] for i in range(0, len(items), 2)]
    return items[0]


def total_at(rows_of, top_row, total_row):
    top = tree(jnp.maximum, [r[top_row] for r in rows_of])
    total = tree(jnp.add, [r[total_row] * jnp.exp(r[top_row] - top) for r in rows_of])
    return top, total


def split_rows(refs):
    return [[ref[k : k + 1, :] for k in range(8)] for ref in refs]


def rows_from_columns(columns):
    n = columns[0].shape[0]
    lane = lax.broadcasted_iota(jnp.int32, (n, LANES), 1)
    tile = jnp.zeros((n, LANES), F32)
    for place, column in enumerate(columns):
        tile = jnp.where(lane == place, column, tile)
    return tile.T[0:8, :]


def columns_from_rows(rows):
    n = rows[0].shape[1]
    return jnp.concatenate(rows + [jnp.zeros((LANES - len(rows), n), F32)], axis=0).T


def teacher_kernel(x_ref, stat_ref):
    rows, cols = x_ref.shape
    places = range(0, cols, LANES)
    read = lambda place: x_ref[:, place : place + LANES].astype(F32)
    top = jnp.full((rows, LANES), -jnp.inf, F32)
    for place in places:
        top = jnp.maximum(top, read(place))
    top = jnp.max(top, axis=1, keepdims=True)
    total = jnp.zeros((rows, LANES), F32)
    for place in places:
        total = total + jnp.exp(read(place) - top)
    stat_ref[...] = rows_from_columns([top, jnp.sum(total, axis=1, keepdims=True)])


def teacher_stats(x):
    return pl.pallas_call(
        teacher_kernel,
        in_specs=[VMEM_SPEC],
        out_specs=VMEM_SPEC,
        out_shape=jax.ShapeDtypeStruct((8, x.shape[0]), F32),
        compiler_params=params(6),
        cost_estimate=COST,
        name="teacher_stats",
    )(x)


def divide(x, n):
    return lax.shift_right_logical(x, n.bit_length() - 1) if n & (n - 1) == 0 else x // n


def plan_kernel(own_ref, peer_ref, list_ref, count_ref):
    lists = count_ref.shape[0]
    entries = own_ref.shape[0]
    for p in range(lists):
        count_ref[p] = 0

    def visit(i, carry):
        for side, ref in enumerate((own_ref, peer_ref)):
            code = ref[i]
            row = lax.shift_right_logical(code, SLOT_BITS)
            n = count_ref[row]
            list_ref[row, n] = (side * entries + i) * SLOT_BASE + (code & (SLOT_BASE - 1))
            count_ref[row] = n + 1
        return carry

    lax.fori_loop(0, entries, visit, 0, unroll=8)
    for p in range(lists):
        n = count_ref[p]
        for k in range(BATCH - 1):
            list_ref[p, n + k] = SLOT_BASE - 1


def plan(own_code, peer_code, lists):
    room = 2 * own_code.size + BATCH
    return pl.pallas_call(
        plan_kernel,
        in_specs=[SMEM_SPEC] * 2,
        out_specs=[SMEM_SPEC] * 2,
        out_shape=[jax.ShapeDtypeStruct((lists, room), jnp.int32), jax.ShapeDtypeStruct((lists,), jnp.int32)],
        compiler_params=params(1),
        cost_estimate=COST,
        name="entry_lists",
    )(own_code, peer_code)


def probs_kernel(x_own, x_peer, *refs):
    stats, (probs, columns) = refs[:-2], refs[-2:]

    @pl.when(pl.program_id(0) == 0)
    def _():
        top, total = total_at(split_rows(stats), 0, 1)
        columns[...] = columns_from_rows([top, 1.0 / total])

    top, scale = columns[:, 0:1], columns[:, 1:2]
    for side, x in enumerate((x_own, x_peer)):
        for j in range(x.shape[1] // LANES):
            raised = jnp.exp(x[:, j * LANES : (j + 1) * LANES].astype(F32) - top)
            probs[side, j] = (raised * scale).astype(BF16)


def sums_kernel(spot_ref, list_ref, count_ref, probs, w_own, w_peer, *refs, first, fan, pieces):
    outs, mass_ref, acc = refs[:-2], refs[-2], refs[-1]
    step = pl.program_id(0)
    slots, rows, _ = outs[0].shape
    side = w_own.shape[0] * fan
    mass = jnp.zeros((rows, LANES), F32)
    for k, out in enumerate(outs):
        piece = spot_ref[0] * pieces + first + k + step
        acc[...] = jnp.zeros_like(acc)

        def add(i, carry):
            parts = []
            for u in range(BATCH):
                item = list_ref[piece, i * BATCH + u]
                slot = item & (SLOT_BASE - 1)
                entry = lax.shift_right_logical(item, SLOT_BITS)
                weight = jnp.where(entry < side, 0, 1)
                parts.append((entry, slot, weight))
            for entry, slot, peer in parts:
                j = divide(entry, fan)
                f = entry - j * fan
                local_j = j - peer * (side // fan)
                weight = jnp.where(peer == 1, w_peer[local_j, f], w_own[local_j, f])
                part = jnp.dot(probs[j], weight, preferred_element_type=F32)
                acc[jnp.minimum(slot, slots)] += part.astype(BF16).astype(F32)
            return carry

        lax.fori_loop(0, divide(count_ref[piece] + BATCH - 1, BATCH), add, 0)

        def drain(i, mass):
            block = acc[i]
            out[i] = block.astype(BF16)
            return mass + block

        mass = lax.fori_loop(0, slots, drain, mass, unroll=4)
    part = rows_from_columns([jnp.sum(mass, axis=1, keepdims=True)])

    @pl.when(step == 0)
    def _():
        mass_ref[...] = part

    @pl.when(step > 0)
    def _():
        mass_ref[...] += part


def teacher_probs(x_own, x_peer, stats):
    rows, cols = x_own.shape
    steps = 4
    blocks = cols // LANES
    part = pl.BlockSpec((rows, cols // steps), lambda i: (0, i))
    probs = pl.pallas_call(
        probs_kernel,
        grid=(steps,),
        in_specs=[part, part] + [pl.BlockSpec(s.shape, lambda i: (0, 0)) for s in stats],
        out_specs=pl.BlockSpec((2, blocks // steps, rows, LANES), lambda i: (0, i, 0, 0)),
        out_shape=jax.ShapeDtypeStruct((2, blocks, rows, LANES), BF16),
        scratch_shapes=[pltpu.VMEM((rows, LANES), F32)],
        compiler_params=params(8),
        cost_estimate=COST,
        name="teacher_probs",
    )(in_hbm(x_own), x_peer, *stats)
    return probs.reshape(2 * blocks, rows, LANES)


def chip_sums(spot, lists, counts, probs, w_own, w_peer, first, n_out, steps, slots):
    rows = probs.shape[1]
    fan = w_own.shape[1]
    whole = lambda shape: pl.BlockSpec(shape, lambda s: (0,) * len(shape))
    out = pltpu.HBM((steps * slots, rows, LANES), BF16)
    return pl.pallas_call(
        functools.partial(sums_kernel, first=first, fan=fan, pieces=counts.shape[0] // 2),
        grid=(steps,),
        in_specs=[SMEM_SPEC] * 3 + [VMEM_SPEC] * 3,
        out_specs=[pl.BlockSpec((slots, rows, LANES), lambda s: (s, 0, 0))] * n_out + [whole((8, rows))],
        out_shape=[out] * n_out + [jax.ShapeDtypeStruct((8, rows), F32)],
        scratch_shapes=[pltpu.VMEM((slots + 1, rows, LANES), F32)],
        compiler_params=params(24),
        cost_estimate=COST,
        name="chip_sums",
    )(spot, lists, counts, probs, w_own, w_peer)


def logits_kernel(place_ref, after_ref, own_ref, *refs):
    n_other = (len(refs) - 4) // 2
    near, far, (head_ref, out_ref, turned_ref, everyone) = refs[:n_other], refs[n_other : 2 * n_other], refs[-4:]
    rows = own_ref.shape[0]
    half = rows // 2
    del after_ref

    @pl.when(pl.program_id(0) == 0)
    def _():
        core = place_ref[0]
        everyone[0:rows, :] = own_ref[...]
        for r in range(n_other):
            start = (r + 1) * rows
            everyone[pl.ds(pl.multiple_of(start + core * half, half), half), :] = near[r][...]
            everyone[pl.ds(pl.multiple_of(start + (1 - core) * half, half), half), :] = far[r][...]

    result = jnp.dot(everyone[...], head_ref[...], preferred_element_type=F32)
    for r in range(n_other + 1):
        out_ref[place_ref[1] ^ r] = result[r * rows : (r + 1) * rows, :]
    part = turned_ref.shape[0]
    start = pl.multiple_of(pl.program_id(0) * part, part)
    turned_ref[...] = everyone[:, pl.ds(start, part)].T


def student_logits(place, after, own, near, far, head):
    rows, depth = own.shape
    n_tok = len(near) + 1
    every = n_tok * rows
    cols = head.shape[1]
    tile = 256
    whole = lambda shape: pl.BlockSpec(shape, lambda i: (0, 0))
    return pl.pallas_call(
        logits_kernel,
        grid=(cols // tile,),
        in_specs=[SMEM_SPEC, pl.BlockSpec(memory_space=pl.ANY), whole(own.shape)]
        + [whole(x.shape) for x in near + far]
        + [pl.BlockSpec((depth, tile), lambda i: (0, i))],
        out_specs=[
            pl.BlockSpec((n_tok, rows, tile), lambda i: (0, 0, i)),
            pl.BlockSpec((depth * tile // cols, every), lambda i: (i, 0)),
        ],
        out_shape=[pltpu.HBM((n_tok, rows, cols), F32), pltpu.HBM((depth, every), BF16)],
        scratch_shapes=[pltpu.VMEM((every, depth), BF16)],
        compiler_params=params(32),
        cost_estimate=COST,
        name="student_logits",
    )(place, after, own, *near, *far, in_hbm(head))


def student_kernel(base_ref, labels_ref, mass_ref, logits_ref, stat_ref):
    n_tok, rows, cols = logits_ref.shape
    lane = lax.broadcasted_iota(jnp.int32, (rows, LANES), 1)
    label = labels_ref[...]
    top = jnp.full((rows, LANES), -jnp.inf, F32)
    hit = jnp.zeros((rows, LANES), F32)
    for t in range(n_tok):
        for b in range(0, cols, LANES):
            block = logits_ref[t, :, b : b + LANES]
            top = jnp.maximum(top, block)
            hit = hit + jnp.where(lane == label - (base_ref[t] + b), block, 0.0)
    top = jnp.max(top, axis=1, keepdims=True)
    total = jnp.zeros((rows, LANES), F32)
    for t in range(n_tok):
        for b in range(0, cols, LANES):
            total = total + jnp.exp(logits_ref[t, :, b : b + LANES] - top)
    total = jnp.sum(total, axis=1, keepdims=True)
    hit = jnp.sum(hit, axis=1, keepdims=True)
    stat_ref[...] = rows_from_columns([jnp.zeros_like(hit), top, total, hit])
    stat_ref[0:1, :] = mass_ref[0:1, :]


def student_stats(base, label_column, mass, logits):
    return pl.pallas_call(
        student_kernel,
        in_specs=[SMEM_SPEC] + [VMEM_SPEC] * 3,
        out_specs=VMEM_SPEC,
        out_shape=jax.ShapeDtypeStruct(mass.shape, F32),
        compiler_params=params(10),
        cost_estimate=COST,
        name="student_stats",
    )(base, label_column, mass, logits)


def merge_kernel(*refs):
    stats, out = refs[:-1], refs[-1]
    parts = split_rows(stats)
    mass = tree(jnp.add, [r[0] for r in parts])
    top, total = total_at(parts, 1, 2)
    hit = tree(jnp.add, [r[3] for r in parts])
    out[...] = jnp.concatenate([mass, top, total, hit, jnp.zeros((4, top.shape[1]), F32)], axis=0)


def merge_stats(stats):
    return pl.pallas_call(
        merge_kernel,
        in_specs=[VMEM_SPEC] * len(stats),
        out_specs=VMEM_SPEC,
        out_shape=jax.ShapeDtypeStruct(stats[0].shape, F32),
        compiler_params=params(1),
        cost_estimate=COST,
        name="merge_stats",
    )(*stats)


def totals_kernel(*refs):
    stats, (columns, loss_ref) = refs[:-2], refs[-2:]
    parts = split_rows(stats)
    mass = tree(jnp.add, [r[0] for r in parts])
    top, total = total_at(parts, 1, 2)
    log_total = top + jnp.log(total)
    label_logit = tree(jnp.add, [r[3] for r in parts])
    columns[...] = columns_from_rows([mass + 1.0, log_total])
    loss_ref[...] = mass * log_total + log_total - label_logit


def token_totals(stats):
    rows = stats[0].shape[1]
    return pl.pallas_call(
        totals_kernel,
        in_specs=[VMEM_SPEC] * len(stats),
        out_specs=[VMEM_SPEC] * 2,
        out_shape=[jax.ShapeDtypeStruct((rows, LANES), F32), jax.ShapeDtypeStruct((1, rows), F32)],
        compiler_params=params(2),
        cost_estimate=COST,
        name="token_totals",
    )(*stats)


def grad_kernel(tok_ref, base_ref, labels_ref, columns, *refs, n_sums, groups):
    sums = refs[:n_sums]
    logits_ref, *grads, inner_ref, inner = refs[n_sums:]
    step = pl.program_id(0)
    _, rows, cols = logits_ref.shape

    @pl.when(step == 0)
    def _():
        inner[...] = jnp.zeros_like(inner)

    lane = lax.broadcasted_iota(jnp.int32, (rows, LANES), 1)
    lift, log_total = columns[:, 0:1], columns[:, 1:2]
    label = labels_ref[...] - base_ref[token_group(step, tok_ref, groups)]
    for r in range(len(grads)):

        @pl.when(step == r)
        def _():
            running = inner[...]
            for b in range(cols // LANES):
                place = slice(b * LANES, (b + 1) * LANES)
                target = functools.reduce(
                    jnp.add, [ref[z, b].astype(F32) for ref in sums for z in range(ref.shape[0])]
                )
                score = logits_ref[0, :, place]
                running = running + target * score
                hit = jnp.where(lane == label - b * LANES, 1.0, 0.0)
                grads[r][:, place] = (lift * jnp.exp(score - log_total) - target - hit).astype(BF16)
            inner[...] = running

    @pl.when(step == pl.num_programs(0) - 1)
    def _():
        inner_ref[...] = rows_from_columns([jnp.sum(inner[...], axis=1, keepdims=True)])[0:1, :]


def token_group(step, tok_ref, groups):
    first, last = groups
    return tok_ref[0] ^ (first + step * (last - first))


def grad_logits(tok, base, label_column, columns, sums, logits, groups):
    n_tok, rows, cols = logits.shape
    per = cols // LANES
    whole = lambda shape: pl.BlockSpec(shape, lambda t, tok_ref: (0,) * len(shape))
    group = lambda t, tok_ref: token_group(t, tok_ref, groups)
    n_out = len(groups)
    return pl.pallas_call(
        functools.partial(grad_kernel, n_sums=len(sums), groups=groups),
        grid_spec=pltpu.PrefetchScalarGridSpec(
            num_scalar_prefetch=1,
            grid=(n_out,),
            in_specs=[SMEM_SPEC, whole(label_column.shape), whole(columns.shape)]
            + [pl.BlockSpec((s.shape[0], per, rows, LANES), lambda t, r: (0, group(t, r), 0, 0)) for s in sums]
            + [pl.BlockSpec((1, rows, cols), lambda t, r: (group(t, r), 0, 0))],
            out_specs=[whole((rows, cols))] * n_out + [whole((1, rows))],
            scratch_shapes=[pltpu.VMEM((rows, LANES), F32)],
        ),
        out_shape=[pltpu.HBM((rows, cols), BF16)] * n_out + [jax.ShapeDtypeStruct((1, rows), F32)],
        compiler_params=params(14),
        cost_estimate=COST,
        name="grad_logits",
    )(tok, base, label_column, columns, *sums, logits)


def stack_pieces(pieces, b_ref):
    rows = pieces[0].shape[0]

    @pl.when(pl.program_id(0) == 0)
    def _():
        for r, piece in enumerate(pieces):
            b_ref[r * rows : (r + 1) * rows, :] = piece[...]


def product_part(a_ref, b_ref, first):
    tile = a_ref.shape[0] // pl.num_programs(0)
    rows = pl.ds(pl.multiple_of(pl.program_id(0) * tile, tile), tile)
    return rows, jnp.dot(a_ref[rows, first : first + b_ref.shape[0]], b_ref[...], preferred_element_type=F32)


def first_product_kernel(a_ref, *refs):
    pieces, (acc_ref, b_ref) = refs[:-2], refs[-2:]
    stack_pieces(pieces, b_ref)
    rows, part = product_part(a_ref, b_ref, 0)
    acc_ref[rows, :] = part


def last_product_kernel(a_ref, acc_ref, *refs):
    pieces, (o_ref, end_ref, b_ref) = refs[:-3], refs[-3:]
    stack_pieces(pieces, b_ref)
    rows, part = product_part(a_ref, b_ref, a_ref.shape[1] - b_ref.shape[0])
    o_ref[...] = (acc_ref[rows, :] + part).astype(o_ref.dtype)
    end_ref[...] = jnp.zeros_like(end_ref)


def first_product(a, pieces):
    rows, n = pieces[0].shape
    return pl.pallas_call(
        first_product_kernel,
        grid=(4,),
        in_specs=[VMEM_SPEC] + [pl.BlockSpec((rows, n), lambda i: (0, 0))] * len(pieces),
        out_specs=VMEM_SPEC,
        out_shape=pltpu.VMEM((a.shape[0], n), F32),
        scratch_shapes=[pltpu.VMEM((len(pieces) * rows, n), BF16)],
        compiler_params=params(16),
        cost_estimate=COST,
        name="first_product",
    )(in_vmem(a), in_hbm(pieces[0]), *pieces[1:])


def last_product(a, acc, pieces):
    m = a.shape[0]
    rows, n = pieces[0].shape
    steps = 4
    return pl.pallas_call(
        last_product_kernel,
        grid=(steps,),
        in_specs=[VMEM_SPEC] * 2 + [pl.BlockSpec((rows, n), lambda i: (0, 0))] * len(pieces),
        out_specs=[pl.BlockSpec((m // steps, n), lambda i: (i, 0)), pl.BlockSpec((1, rows), lambda i: (0, 0))],
        out_shape=[jax.ShapeDtypeStruct((m, n), BF16), jax.ShapeDtypeStruct((1, rows), F32)],
        scratch_shapes=[pltpu.VMEM((len(pieces) * rows, n), BF16)],
        compiler_params=params(20),
        cost_estimate=COST,
        name="last_product",
    )(in_vmem(a), in_vmem(acc), *pieces)


def swap(x, axis, mask):
    return lax.ppermute(x, axis, [(i, i ^ mask) for i in range(lax.axis_size(axis))])


def gather_chips(x):
    n = lax.axis_size("vocab")
    if n > 8:
        lines = [[2 * z + c for z in range(n // 2)] for c in range(2)]
        everything = lax.all_gather(x, "vocab", axis=0, axis_index_groups=lines)
        return [everything[z] for z in range(n // 2)]
    return [x] + [swap(x, "vocab", r) for r in range(2, n, 2)]


def gather_cores(x):
    chips = gather_chips(x)
    return chips + [swap(chip, "vocab", 1) for chip in chips]


def plus(a, b):
    return (a.astype(F32) + b.astype(F32)).astype(BF16)


def exchange_tok(x):
    return lax.all_to_all(x, "tok", split_axis=0, concat_axis=0, tiled=True)


def send(x, hops):
    return lax.ppermute(x, "vocab", [(2 * a + c, 2 * b + c) for a, b in hops for c in range(2)])


def local(teacher_logits, hidden, new_head, labels, map_target, map_weight):
    rows = teacher_logits.shape[0]
    block = map_weight.shape[2]
    n_tok = lax.axis_size("tok")
    n_vocab = lax.axis_size("vocab")
    n_z = n_vocab // 2
    new_cols = new_head.shape[1]
    per = new_cols // block
    tok = lax.axis_index("tok")
    vocab = lax.axis_index("vocab")
    spot = jnp.stack([vocab % 2, vocab // 2]).astype(jnp.int32)
    slots = n_tok * per
    in_line = n_z == 4

    owner = map_target // per
    owner_vocab = owner % n_vocab
    owner_z = owner_vocab // 2
    if in_line:
        z = vocab // 2
        outer = (owner_z == 0) | (owner_z == n_z - 1)
        near_place = jnp.where(owner_z == z, 3, 2)
        place = jnp.where((owner_z // 2) == (z // 2), near_place, jnp.where(outer, 0, 1))
    else:
        place = owner_z
    slot = (owner // n_vocab) * per + map_target % per
    code = (((owner_vocab % 2) * n_z + place) * SLOT_BASE + slot).astype(jnp.int32).reshape(-1)

    peer_logits = swap(teacher_logits, "vocab", 1)
    peer_code = swap(code, "vocab", 1)
    peer_weight = swap(map_weight, "vocab", 1)
    teacher = teacher_stats(teacher_logits)
    totals = gather_cores(teacher)
    lists, counts = plan(code, peer_code, 2 * n_z)
    probs = teacher_probs(teacher_logits, peer_logits, totals)

    half = lax.dynamic_slice_in_dim(hidden, spot[0] * (rows // 2), rows // 2)
    if in_line:
        inward, across, beyond = [(0, 1), (3, 2)], [(1, 2), (2, 1)], [(1, 3), (2, 0)]
        far_outer, mass_a = chip_sums(spot, lists, counts, probs, map_weight, peer_weight, 0, 1, 1, slots)
        first = send(far_outer, inward)
        half, probs, mass_a = lax.optimization_barrier((half, probs, mass_a))
        near = [swap(half, "tok", r) for r in range(1, n_tok)]
        far_inner, beside, own, mass_b = chip_sums(
            spot, lists, counts, probs, map_weight, peer_weight, 1, 3, 1, slots
        )
        second = send(far_inner, inward)
        first, mass = lax.optimization_barrier((first, mass_a + mass_b))
        merged = plus(far_outer, first)
        arrived = send(merged, beyond)
        *near, waited, merged = lax.optimization_barrier((*near, beside, merged))
        third = swap(waited, "vocab", 2)
    else:
        sums, mass = chip_sums(spot, lists, counts, probs, map_weight, peer_weight, 0, 1, n_z, slots)
        lines = [[2 * z + c for z in range(n_z)] for c in range(2)]
        sums = lax.all_to_all(
            sums.reshape(n_z, slots, rows, block),
            "vocab",
            split_axis=0,
            concat_axis=0,
            axis_index_groups=lines,
            tiled=True,
        )
        sums = [sums]
        near = [swap(half, "tok", r) for r in range(1, n_tok)]

    far = [swap(x, "vocab", 1) for x in near]
    where = jnp.stack([vocab % 2, tok]).astype(jnp.int32)
    scores, turned = student_logits(where, mass, hidden, near, far, new_head)
    base = (jnp.arange(n_tok, dtype=jnp.int32) * n_vocab + vocab) * new_cols
    label_column = lax.dynamic_slice_in_dim(labels, tok * rows, rows).reshape(rows, 1)
    scores = exchange_tok(scores)
    if in_line:
        second, turned = lax.optimization_barrier((second, turned))
        merged_inner, arrived = lax.optimization_barrier((plus(far_inner, second), arrived))
        crossed = send(merged_inner, across)
        scores, merged_inner = lax.optimization_barrier((scores, merged_inner))
        sums = [x[None] for x in (own, third, crossed, arrived)]
    student = student_stats(base, label_column, mass, scores)
    student = merge_stats([student, swap(student, "vocab", 1)])
    stats = gather_chips(student)

    group = tok.astype(jnp.int32).reshape(1)
    columns, base_loss = token_totals(stats)
    grad_args = (group, base, label_column, columns, sums, scores)
    beside_x, across_xy, inner = grad_logits(*grad_args, (1, 3))
    beside_x, across_xy = swap(beside_x, "tok", 1), swap(across_xy, "tok", 3)
    beside_y, here, inner_b = grad_logits(*grad_args, (2, 0))
    beside_y = swap(beside_y, "tok", 2)
    inner = inner + inner_b
    acc = first_product(turned, [here, beside_x])
    head_grad, end = last_product(turned, acc, [beside_y, across_xy])
    mask = 1
    while mask < n_vocab:
        other = swap(inner, "vocab", mask)
        inner = inner + other
        mask *= 2
    return ((base_loss - inner + end).reshape(rows), head_grad)


def solution(mesh):
    return jax.shard_map(
        local,
        mesh=mesh,
        in_specs=(
            P("tok", "vocab"),
            P("tok", None),
            P(None, ("tok", "vocab")),
            P(),
            P("vocab", None),
            P("vocab", None, None, None),
        ),
        out_specs=(P("tok"), P(None, ("tok", "vocab"))),
        check_vma=False,
    )
```

```python
import functools

import jax
import jax.numpy as jnp
from jax import lax
from jax.experimental import pallas as pl
from jax.experimental.pallas import tpu as pltpu
from jax.sharding import PartitionSpec as P

F32 = jnp.float32
BF16 = jnp.bfloat16
LANES = 128
BATCH = 8
COST = pl.CostEstimate(flops=1024, bytes_accessed=1024, transcendentals=0)
SLOT_BITS = 10
SLOT_BASE = 1 << SLOT_BITS
SMEM_SPEC = pl.BlockSpec(memory_space=pltpu.SMEM)
VMEM_SPEC = pl.BlockSpec(memory_space=pltpu.VMEM)


def params(mebibytes):
    return pltpu.CompilerParams(vmem_limit_bytes=mebibytes * 1024 * 1024)


def in_hbm(x):
    return pltpu.with_memory_space_constraint(x, pltpu.HBM)


def in_vmem(x):
    return pltpu.with_memory_space_constraint(x, pltpu.VMEM)


def tree(op, items):
    while len(items) > 1:
        items = [op(items[i], items[i + 1]) if i + 1 < len(items) else items[i] for i in range(0, len(items), 2)]
    return items[0]


def total_at(rows_of, top_row, total_row):
    top = tree(jnp.maximum, [r[top_row] for r in rows_of])
    total = tree(jnp.add, [r[total_row] * jnp.exp(r[top_row] - top) for r in rows_of])
    return top, total


def split_rows(refs):
    return [[ref[k : k + 1, :] for k in range(8)] for ref in refs]


def rows_from_columns(columns):
    n = columns[0].shape[0]
    lane = lax.broadcasted_iota(jnp.int32, (n, LANES), 1)
    tile = jnp.zeros((n, LANES), F32)
    for place, column in enumerate(columns):
        tile = jnp.where(lane == place, column, tile)
    return tile.T[0:8, :]


def columns_from_rows(rows):
    n = rows[0].shape[1]
    return jnp.concatenate(rows + [jnp.zeros((LANES - len(rows), n), F32)], axis=0).T


def teacher_kernel(x_ref, stat_ref):
    rows, cols = x_ref.shape
    places = range(0, cols, LANES)
    read = lambda place: x_ref[:, place : place + LANES].astype(F32)
    top = jnp.full((rows, LANES), -jnp.inf, F32)
    for place in places:
        top = jnp.maximum(top, read(place))
    top = jnp.max(top, axis=1, keepdims=True)
    total = jnp.zeros((rows, LANES), F32)
    for place in places:
        total = total + jnp.exp(read(place) - top)
    stat_ref[...] = rows_from_columns([top, jnp.sum(total, axis=1, keepdims=True)])


def teacher_stats(x):
    return pl.pallas_call(
        teacher_kernel,
        in_specs=[VMEM_SPEC],
        out_specs=VMEM_SPEC,
        out_shape=jax.ShapeDtypeStruct((8, x.shape[0]), F32),
        compiler_params=params(6),
        cost_estimate=COST,
        name="teacher_stats",
    )(x)


def divide(x, n):
    return lax.shift_right_logical(x, n.bit_length() - 1) if n & (n - 1) == 0 else x // n


def plan_kernel(own_ref, peer_ref, list_ref, count_ref):
    lists = count_ref.shape[0]
    entries = own_ref.shape[0]
    for p in range(lists):
        count_ref[p] = 0

    def visit(i, carry):
        for side, ref in enumerate((own_ref, peer_ref)):
            code = ref[i]
            row = lax.shift_right_logical(code, SLOT_BITS)
            n = count_ref[row]
            list_ref[row, n] = (side * entries + i) * SLOT_BASE + (code & (SLOT_BASE - 1))
            count_ref[row] = n + 1
        return carry

    lax.fori_loop(0, entries, visit, 0, unroll=8)
    for p in range(lists):
        n = count_ref[p]
        for k in range(BATCH - 1):
            list_ref[p, n + k] = SLOT_BASE - 1


def plan(own_code, peer_code, lists):
    room = 2 * own_code.size + BATCH
    return pl.pallas_call(
        plan_kernel,
        in_specs=[SMEM_SPEC] * 2,
        out_specs=[SMEM_SPEC] * 2,
        out_shape=[jax.ShapeDtypeStruct((lists, room), jnp.int32), jax.ShapeDtypeStruct((lists,), jnp.int32)],
        compiler_params=params(1),
        cost_estimate=COST,
        name="entry_lists",
    )(own_code, peer_code)


def probs_kernel(x_own, x_peer, *refs):
    stats, (probs, columns) = refs[:-2], refs[-2:]

    @pl.when(pl.program_id(0) == 0)
    def _():
        top, total = total_at(split_rows(stats), 0, 1)
        columns[...] = columns_from_rows([top, 1.0 / total])

    top, scale = columns[:, 0:1], columns[:, 1:2]
    for side, x in enumerate((x_own, x_peer)):
        for j in range(x.shape[1] // LANES):
            raised = jnp.exp(x[:, j * LANES : (j + 1) * LANES].astype(F32) - top)
            probs[side, j] = (raised * scale).astype(BF16)


def sums_kernel(spot_ref, list_ref, count_ref, probs, w_own, w_peer, *refs, first, fan, pieces):
    outs, mass_ref, acc = refs[:-2], refs[-2], refs[-1]
    step = pl.program_id(0)
    slots, rows, _ = outs[0].shape
    side = w_own.shape[0] * fan
    mass = jnp.zeros((rows, LANES), F32)
    for k, out in enumerate(outs):
        piece = spot_ref[0] * pieces + first + k + step
        acc[...] = jnp.zeros_like(acc)

        def add(i, carry):
            parts = []
            for u in range(BATCH):
                item = list_ref[piece, i * BATCH + u]
                slot = item & (SLOT_BASE - 1)
                entry = lax.shift_right_logical(item, SLOT_BITS)
                weight = jnp.where(entry < side, 0, 1)
                parts.append((entry, slot, weight))
            for entry, slot, peer in parts:
                j = divide(entry, fan)
                f = entry - j * fan
                local_j = j - peer * (side // fan)
                weight = jnp.where(peer == 1, w_peer[local_j, f], w_own[local_j, f])
                part = jnp.dot(probs[j], weight, preferred_element_type=F32)
                acc[jnp.minimum(slot, slots)] += part.astype(BF16).astype(F32)
            return carry

        lax.fori_loop(0, divide(count_ref[piece] + BATCH - 1, BATCH), add, 0)

        def drain(i, mass):
            block = acc[i]
            out[i] = block.astype(BF16)
            return mass + block

        mass = lax.fori_loop(0, slots, drain, mass, unroll=4)
    part = rows_from_columns([jnp.sum(mass, axis=1, keepdims=True)])

    @pl.when(step == 0)
    def _():
        mass_ref[...] = part

    @pl.when(step > 0)
    def _():
        mass_ref[...] += part


def teacher_probs(x_own, x_peer, stats):
    rows, cols = x_own.shape
    steps = 4
    blocks = cols // LANES
    part = pl.BlockSpec((rows, cols // steps), lambda i: (0, i))
    probs = pl.pallas_call(
        probs_kernel,
        grid=(steps,),
        in_specs=[part, part] + [pl.BlockSpec(s.shape, lambda i: (0, 0)) for s in stats],
        out_specs=pl.BlockSpec((2, blocks // steps, rows, LANES), lambda i: (0, i, 0, 0)),
        out_shape=jax.ShapeDtypeStruct((2, blocks, rows, LANES), BF16),
        scratch_shapes=[pltpu.VMEM((rows, LANES), F32)],
        compiler_params=params(8),
        cost_estimate=COST,
        name="teacher_probs",
    )(in_hbm(x_own), x_peer, *stats)
    return probs.reshape(2 * blocks, rows, LANES)


def chip_sums(spot, lists, counts, probs, w_own, w_peer, first, n_out, steps, slots):
    rows = probs.shape[1]
    fan = w_own.shape[1]
    whole = lambda shape: pl.BlockSpec(shape, lambda s: (0,) * len(shape))
    out = pltpu.HBM((steps * slots, rows, LANES), BF16)
    return pl.pallas_call(
        functools.partial(sums_kernel, first=first, fan=fan, pieces=counts.shape[0] // 2),
        grid=(steps,),
        in_specs=[SMEM_SPEC] * 3 + [VMEM_SPEC] * 3,
        out_specs=[pl.BlockSpec((slots, rows, LANES), lambda s: (s, 0, 0))] * n_out + [whole((8, rows))],
        out_shape=[out] * n_out + [jax.ShapeDtypeStruct((8, rows), F32)],
        scratch_shapes=[pltpu.VMEM((slots + 1, rows, LANES), F32)],
        compiler_params=params(24),
        cost_estimate=COST,
        name="chip_sums",
    )(spot, lists, counts, probs, w_own, w_peer)


def logits_kernel(place_ref, after_ref, own_ref, *refs):
    n_other = (len(refs) - 4) // 2
    near, far, (head_ref, out_ref, turned_ref, everyone) = refs[:n_other], refs[n_other : 2 * n_other], refs[-4:]
    rows = own_ref.shape[0]
    half = rows // 2
    del after_ref

    @pl.when(pl.program_id(0) == 0)
    def _():
        core = place_ref[0]
        everyone[0:rows, :] = own_ref[...]
        for r in range(n_other):
            start = (r + 1) * rows
            everyone[pl.ds(pl.multiple_of(start + core * half, half), half), :] = near[r][...]
            everyone[pl.ds(pl.multiple_of(start + (1 - core) * half, half), half), :] = far[r][...]

    result = jnp.dot(everyone[...], head_ref[...], preferred_element_type=F32)
    for r in range(n_other + 1):
        out_ref[place_ref[1] ^ r] = result[r * rows : (r + 1) * rows, :]
    part = turned_ref.shape[0]
    start = pl.multiple_of(pl.program_id(0) * part, part)
    turned_ref[...] = everyone[:, pl.ds(start, part)].T


def student_logits(place, after, own, near, far, head):
    rows, depth = own.shape
    n_tok = len(near) + 1
    every = n_tok * rows
    cols = head.shape[1]
    tile = 256
    whole = lambda shape: pl.BlockSpec(shape, lambda i: (0, 0))
    return pl.pallas_call(
        logits_kernel,
        grid=(cols // tile,),
        in_specs=[SMEM_SPEC, pl.BlockSpec(memory_space=pl.ANY), whole(own.shape)]
        + [whole(x.shape) for x in near + far]
        + [pl.BlockSpec((depth, tile), lambda i: (0, i))],
        out_specs=[
            pl.BlockSpec((n_tok, rows, tile), lambda i: (0, 0, i)),
            pl.BlockSpec((depth * tile // cols, every), lambda i: (i, 0)),
        ],
        out_shape=[pltpu.HBM((n_tok, rows, cols), F32), pltpu.HBM((depth, every), BF16)],
        scratch_shapes=[pltpu.VMEM((every, depth), BF16)],
        compiler_params=params(32),
        cost_estimate=COST,
        name="student_logits",
    )(place, after, own, *near, *far, head)


def student_kernel(base_ref, labels_ref, mass_ref, logits_ref, stat_ref):
    n_tok, rows, cols = logits_ref.shape
    lane = lax.broadcasted_iota(jnp.int32, (rows, LANES), 1)
    label = labels_ref[...]
    top = jnp.full((rows, LANES), -jnp.inf, F32)
    hit = jnp.zeros((rows, LANES), F32)
    for t in range(n_tok):
        for b in range(0, cols, LANES):
            block = logits_ref[t, :, b : b + LANES]
            top = jnp.maximum(top, block)
            hit = hit + jnp.where(lane == label - (base_ref[t] + b), block, 0.0)
    top = jnp.max(top, axis=1, keepdims=True)
    total = jnp.zeros((rows, LANES), F32)
    for t in range(n_tok):
        for b in range(0, cols, LANES):
            total = total + jnp.exp(logits_ref[t, :, b : b + LANES] - top)
    total = jnp.sum(total, axis=1, keepdims=True)
    hit = jnp.sum(hit, axis=1, keepdims=True)
    stat_ref[...] = rows_from_columns([jnp.zeros_like(hit), top, total, hit])
    stat_ref[0:1, :] = mass_ref[0:1, :]


def student_stats(base, label_column, mass, logits):
    return pl.pallas_call(
        student_kernel,
        in_specs=[SMEM_SPEC] + [VMEM_SPEC] * 3,
        out_specs=VMEM_SPEC,
        out_shape=jax.ShapeDtypeStruct(mass.shape, F32),
        compiler_params=params(10),
        cost_estimate=COST,
        name="student_stats",
    )(base, label_column, mass, logits)


def merge_kernel(*refs):
    stats, out = refs[:-1], refs[-1]
    parts = split_rows(stats)
    mass = tree(jnp.add, [r[0] for r in parts])
    top, total = total_at(parts, 1, 2)
    hit = tree(jnp.add, [r[3] for r in parts])
    out[...] = jnp.concatenate([mass, top, total, hit, jnp.zeros((4, top.shape[1]), F32)], axis=0)


def merge_stats(stats):
    return pl.pallas_call(
        merge_kernel,
        in_specs=[VMEM_SPEC] * len(stats),
        out_specs=VMEM_SPEC,
        out_shape=jax.ShapeDtypeStruct(stats[0].shape, F32),
        compiler_params=params(1),
        cost_estimate=COST,
        name="merge_stats",
    )(*stats)


def totals_kernel(*refs):
    stats, (columns, loss_ref) = refs[:-2], refs[-2:]
    parts = split_rows(stats)
    mass = tree(jnp.add, [r[0] for r in parts])
    top, total = total_at(parts, 1, 2)
    log_total = top + jnp.log(total)
    label_logit = tree(jnp.add, [r[3] for r in parts])
    columns[...] = columns_from_rows([mass + 1.0, log_total])
    loss_ref[...] = mass * log_total + log_total - label_logit


def token_totals(stats):
    rows = stats[0].shape[1]
    return pl.pallas_call(
        totals_kernel,
        in_specs=[VMEM_SPEC] * len(stats),
        out_specs=[VMEM_SPEC] * 2,
        out_shape=[jax.ShapeDtypeStruct((rows, LANES), F32), jax.ShapeDtypeStruct((1, rows), F32)],
        compiler_params=params(2),
        cost_estimate=COST,
        name="token_totals",
    )(*stats)


def grad_kernel(tok_ref, base_ref, labels_ref, columns, *refs, n_sums, groups):
    sums = refs[:n_sums]
    logits_ref, *grads, inner_ref, inner = refs[n_sums:]
    step = pl.program_id(0)
    _, rows, cols = logits_ref.shape

    @pl.when(step == 0)
    def _():
        inner[...] = jnp.zeros_like(inner)

    lane = lax.broadcasted_iota(jnp.int32, (rows, LANES), 1)
    lift, log_total = columns[:, 0:1], columns[:, 1:2]
    label = labels_ref[...] - base_ref[token_group(step, tok_ref, groups)]
    for r in range(len(grads)):

        @pl.when(step == r)
        def _():
            running = inner[...]
            for b in range(cols // LANES):
                place = slice(b * LANES, (b + 1) * LANES)
                target = functools.reduce(
                    jnp.add, [ref[z, b].astype(F32) for ref in sums for z in range(ref.shape[0])]
                )
                score = logits_ref[0, :, place]
                running = running + target * score
                hit = jnp.where(lane == label - b * LANES, 1.0, 0.0)
                grads[r][:, place] = (lift * jnp.exp(score - log_total) - target - hit).astype(BF16)
            inner[...] = running

    @pl.when(step == pl.num_programs(0) - 1)
    def _():
        inner_ref[...] = rows_from_columns([jnp.sum(inner[...], axis=1, keepdims=True)])[0:1, :]


def token_group(step, tok_ref, groups):
    first, last = groups
    return tok_ref[0] ^ (first + step * (last - first))


def grad_logits(tok, base, label_column, columns, sums, logits, groups):
    n_tok, rows, cols = logits.shape
    per = cols // LANES
    whole = lambda shape: pl.BlockSpec(shape, lambda t, tok_ref: (0,) * len(shape))
    group = lambda t, tok_ref: token_group(t, tok_ref, groups)
    n_out = len(groups)
    return pl.pallas_call(
        functools.partial(grad_kernel, n_sums=len(sums), groups=groups),
        grid_spec=pltpu.PrefetchScalarGridSpec(
            num_scalar_prefetch=1,
            grid=(n_out,),
            in_specs=[SMEM_SPEC, whole(label_column.shape), whole(columns.shape)]
            + [pl.BlockSpec((s.shape[0], per, rows, LANES), lambda t, r: (0, group(t, r), 0, 0)) for s in sums]
            + [pl.BlockSpec((1, rows, cols), lambda t, r: (group(t, r), 0, 0))],
            out_specs=[whole((rows, cols))] * n_out + [whole((1, rows))],
            scratch_shapes=[pltpu.VMEM((rows, LANES), F32)],
        ),
        out_shape=[pltpu.HBM((rows, cols), BF16)] * n_out + [jax.ShapeDtypeStruct((1, rows), F32)],
        compiler_params=params(14),
        cost_estimate=COST,
        name="grad_logits",
    )(tok, base, label_column, columns, *sums, logits)


def stack_pieces(pieces, b_ref):
    rows = pieces[0].shape[0]

    @pl.when(pl.program_id(0) == 0)
    def _():
        for r, piece in enumerate(pieces):
            b_ref[r * rows : (r + 1) * rows, :] = piece[...]


def product_part(a_ref, b_ref, first):
    tile = a_ref.shape[0] // pl.num_programs(0)
    rows = pl.ds(pl.multiple_of(pl.program_id(0) * tile, tile), tile)
    return rows, jnp.dot(a_ref[rows, first : first + b_ref.shape[0]], b_ref[...], preferred_element_type=F32)


def first_product_kernel(a_ref, *refs):
    pieces, (acc_ref, b_ref) = refs[:-2], refs[-2:]
    stack_pieces(pieces, b_ref)
    rows, part = product_part(a_ref, b_ref, 0)
    acc_ref[rows, :] = part


def last_product_kernel(a_ref, acc_ref, *refs):
    pieces, (o_ref, end_ref, b_ref) = refs[:-3], refs[-3:]
    stack_pieces(pieces, b_ref)
    rows, part = product_part(a_ref, b_ref, a_ref.shape[1] - b_ref.shape[0])
    o_ref[...] = (acc_ref[rows, :] + part).astype(o_ref.dtype)
    end_ref[...] = jnp.zeros_like(end_ref)


def first_product(a, pieces):
    rows, n = pieces[0].shape
    return pl.pallas_call(
        first_product_kernel,
        grid=(4,),
        in_specs=[VMEM_SPEC] + [pl.BlockSpec((rows, n), lambda i: (0, 0))] * len(pieces),
        out_specs=VMEM_SPEC,
        out_shape=pltpu.VMEM((a.shape[0], n), F32),
        scratch_shapes=[pltpu.VMEM((len(pieces) * rows, n), BF16)],
        compiler_params=params(16),
        cost_estimate=COST,
        name="first_product",
    )(in_vmem(a), in_hbm(pieces[0]), *pieces[1:])


def last_product(a, acc, pieces):
    m = a.shape[0]
    rows, n = pieces[0].shape
    steps = 4
    return pl.pallas_call(
        last_product_kernel,
        grid=(steps,),
        in_specs=[VMEM_SPEC] * 2 + [pl.BlockSpec((rows, n), lambda i: (0, 0))] * len(pieces),
        out_specs=[pl.BlockSpec((m // steps, n), lambda i: (i, 0)), pl.BlockSpec((1, rows), lambda i: (0, 0))],
        out_shape=[jax.ShapeDtypeStruct((m, n), BF16), jax.ShapeDtypeStruct((1, rows), F32)],
        scratch_shapes=[pltpu.VMEM((len(pieces) * rows, n), BF16)],
        compiler_params=params(20),
        cost_estimate=COST,
        name="last_product",
    )(in_vmem(a), in_vmem(acc), *pieces)


def swap(x, axis, mask):
    return lax.ppermute(x, axis, [(i, i ^ mask) for i in range(lax.axis_size(axis))])


def gather_chips(x):
    n = lax.axis_size("vocab")
    if n > 8:
        lines = [[2 * z + c for z in range(n // 2)] for c in range(2)]
        everything = lax.all_gather(x, "vocab", axis=0, axis_index_groups=lines)
        return [everything[z] for z in range(n // 2)]
    return [x] + [swap(x, "vocab", r) for r in range(2, n, 2)]


def gather_cores(x):
    chips = gather_chips(x)
    return chips + [swap(chip, "vocab", 1) for chip in chips]


def plus(a, b):
    return (a.astype(F32) + b.astype(F32)).astype(BF16)


def exchange_tok(x):
    return lax.all_to_all(x, "tok", split_axis=0, concat_axis=0, tiled=True)


def send(x, hops):
    return lax.ppermute(x, "vocab", [(2 * a + c, 2 * b + c) for a, b in hops for c in range(2)])


def local(teacher_logits, hidden, new_head, labels, map_target, map_weight):
    rows = teacher_logits.shape[0]
    block = map_weight.shape[2]
    n_tok = lax.axis_size("tok")
    n_vocab = lax.axis_size("vocab")
    n_z = n_vocab // 2
    new_cols = new_head.shape[1]
    per = new_cols // block
    tok = lax.axis_index("tok")
    vocab = lax.axis_index("vocab")
    spot = jnp.stack([vocab % 2, vocab // 2]).astype(jnp.int32)
    slots = n_tok * per
    in_line = n_z == 4

    owner = map_target // per
    owner_vocab = owner % n_vocab
    owner_z = owner_vocab // 2
    if in_line:
        z = vocab // 2
        outer = (owner_z == 0) | (owner_z == n_z - 1)
        near_place = jnp.where(owner_z == z, 3, 2)
        place = jnp.where((owner_z // 2) == (z // 2), near_place, jnp.where(outer, 0, 1))
    else:
        place = owner_z
    slot = (owner // n_vocab) * per + map_target % per
    code = (((owner_vocab % 2) * n_z + place) * SLOT_BASE + slot).astype(jnp.int32).reshape(-1)

    peer_logits = swap(teacher_logits, "vocab", 1)
    peer_code = swap(code, "vocab", 1)
    peer_weight = swap(map_weight, "vocab", 1)
    teacher = teacher_stats(teacher_logits)
    totals = gather_cores(teacher)
    lists, counts = plan(code, peer_code, 2 * n_z)
    probs = teacher_probs(teacher_logits, peer_logits, totals)

    half = lax.dynamic_slice_in_dim(hidden, spot[0] * (rows // 2), rows // 2)
    if in_line:
        inward, across, beyond = [(0, 1), (3, 2)], [(1, 2), (2, 1)], [(1, 3), (2, 0)]
        far_outer, mass_a = chip_sums(spot, lists, counts, probs, map_weight, peer_weight, 0, 1, 1, slots)
        first = send(far_outer, inward)
        half, probs, mass_a = lax.optimization_barrier((half, probs, mass_a))
        near = [swap(half, "tok", r) for r in range(1, n_tok)]
        far_inner, beside, own, mass_b = chip_sums(
            spot, lists, counts, probs, map_weight, peer_weight, 1, 3, 1, slots
        )
        second = send(far_inner, inward)
        first, mass = lax.optimization_barrier((first, mass_a + mass_b))
        merged = plus(far_outer, first)
        arrived = send(merged, beyond)
        *near, waited, merged = lax.optimization_barrier((*near, beside, merged))
        third = swap(waited, "vocab", 2)
    else:
        sums, mass = chip_sums(spot, lists, counts, probs, map_weight, peer_weight, 0, 1, n_z, slots)
        lines = [[2 * z + c for z in range(n_z)] for c in range(2)]
        sums = lax.all_to_all(
            sums.reshape(n_z, slots, rows, block),
            "vocab",
            split_axis=0,
            concat_axis=0,
            axis_index_groups=lines,
            tiled=True,
        )
        sums = [sums]
        near = [swap(half, "tok", r) for r in range(1, n_tok)]

    far = [swap(x, "vocab", 1) for x in near]
    where = jnp.stack([vocab % 2, tok]).astype(jnp.int32)
    scores, turned = student_logits(where, mass, hidden, near, far, new_head)
    base = (jnp.arange(n_tok, dtype=jnp.int32) * n_vocab + vocab) * new_cols
    label_column = lax.dynamic_slice_in_dim(labels, tok * rows, rows).reshape(rows, 1)
    scores = exchange_tok(scores)
    if in_line:
        second, arrived, turned = lax.optimization_barrier((second, arrived, turned))
        merged_inner = plus(far_inner, second)
        crossed = send(merged_inner, across)
        scores, merged_inner = lax.optimization_barrier((scores, merged_inner))
        sums = [x[None] for x in (own, third, crossed, arrived)]
    student = student_stats(base, label_column, mass, scores)
    student = merge_stats([student, swap(student, "vocab", 1)])
    stats = gather_chips(student)

    group = tok.astype(jnp.int32).reshape(1)
    columns, base_loss = token_totals(stats)
    grad_args = (group, base, label_column, columns, sums, scores)
    beside_x, across_xy, inner = grad_logits(*grad_args, (1, 3))
    beside_x, across_xy = swap(beside_x, "tok", 1), swap(across_xy, "tok", 3)
    beside_y, here, inner_b = grad_logits(*grad_args, (2, 0))
    beside_y = swap(beside_y, "tok", 2)
    inner = inner + inner_b
    acc = first_product(turned, [here, beside_x])
    head_grad, end = last_product(turned, acc, [beside_y, across_xy])
    mask = 1
    while mask < n_vocab:
        other = swap(inner, "vocab", mask)
        inner = inner + other
        mask *= 2
    return ((base_loss - inner + end).reshape(rows), head_grad)


def solution(mesh):
    return jax.shard_map(
        local,
        mesh=mesh,
        in_specs=(
            P("tok", "vocab"),
            P("tok", None),
            P(None, ("tok", "vocab")),
            P(),
            P("vocab", None),
            P("vocab", None, None, None),
        ),
        out_specs=(P("tok"), P(None, ("tok", "vocab"))),
        check_vma=False,
    )
```

```python
import functools

import jax
import jax.numpy as jnp
from jax import lax
from jax.experimental import pallas as pl
from jax.experimental.pallas import tpu as pltpu
from jax.sharding import PartitionSpec as P

F32 = jnp.float32
BF16 = jnp.bfloat16
LANES = 128
BATCH = 8
COST = pl.CostEstimate(flops=1024, bytes_accessed=1024, transcendentals=0)
SLOT_BITS = 10
SLOT_BASE = 1 << SLOT_BITS
SMEM_SPEC = pl.BlockSpec(memory_space=pltpu.SMEM)
VMEM_SPEC = pl.BlockSpec(memory_space=pltpu.VMEM)


def params(mebibytes):
    return pltpu.CompilerParams(vmem_limit_bytes=mebibytes * 1024 * 1024)


def in_hbm(x):
    return pltpu.with_memory_space_constraint(x, pltpu.HBM)


def in_vmem(x):
    return pltpu.with_memory_space_constraint(x, pltpu.VMEM)


def tree(op, items):
    while len(items) > 1:
        items = [op(items[i], items[i + 1]) if i + 1 < len(items) else items[i] for i in range(0, len(items), 2)]
    return items[0]


def total_at(rows_of, top_row, total_row):
    top = tree(jnp.maximum, [r[top_row] for r in rows_of])
    total = tree(jnp.add, [r[total_row] * jnp.exp(r[top_row] - top) for r in rows_of])
    return top, total


def split_rows(refs):
    return [[ref[k : k + 1, :] for k in range(8)] for ref in refs]


def rows_from_columns(columns):
    n = columns[0].shape[0]
    lane = lax.broadcasted_iota(jnp.int32, (n, LANES), 1)
    tile = jnp.zeros((n, LANES), F32)
    for place, column in enumerate(columns):
        tile = jnp.where(lane == place, column, tile)
    return tile.T[0:8, :]


def columns_from_rows(rows):
    n = rows[0].shape[1]
    return jnp.concatenate(rows + [jnp.zeros((LANES - len(rows), n), F32)], axis=0).T


def teacher_kernel(x_ref, stat_ref):
    rows, cols = x_ref.shape
    places = range(0, cols, LANES)
    read = lambda place: x_ref[:, place : place + LANES].astype(F32)
    top = jnp.full((rows, LANES), -jnp.inf, F32)
    for place in places:
        top = jnp.maximum(top, read(place))
    top = jnp.max(top, axis=1, keepdims=True)
    total = jnp.zeros((rows, LANES), F32)
    for place in places:
        total = total + jnp.exp(read(place) - top)
    stat_ref[...] = rows_from_columns([jnp.zeros_like(top), top, jnp.sum(total, axis=1, keepdims=True)])


def teacher_stats(x):
    return pl.pallas_call(
        teacher_kernel,
        in_specs=[VMEM_SPEC],
        out_specs=VMEM_SPEC,
        out_shape=jax.ShapeDtypeStruct((8, x.shape[0]), F32),
        compiler_params=params(6),
        cost_estimate=COST,
        name="teacher_stats",
    )(x)


def divide(x, n):
    return lax.shift_right_logical(x, n.bit_length() - 1) if n & (n - 1) == 0 else x // n


def plan_kernel(own_ref, peer_ref, list_ref, count_ref):
    lists = count_ref.shape[0]
    entries = own_ref.shape[0]
    for p in range(lists):
        count_ref[p] = 0

    def visit(i, carry):
        for side, ref in enumerate((own_ref, peer_ref)):
            code = ref[i]
            row = lax.shift_right_logical(code, SLOT_BITS)
            n = count_ref[row]
            list_ref[row, n] = (side * entries + i) * SLOT_BASE + (code & (SLOT_BASE - 1))
            count_ref[row] = n + 1
        return carry

    lax.fori_loop(0, entries, visit, 0, unroll=8)
    for p in range(lists):
        n = count_ref[p]
        for k in range(BATCH - 1):
            list_ref[p, n + k] = SLOT_BASE - 1


def plan(own_code, peer_code, lists):
    room = 2 * own_code.size + BATCH
    return pl.pallas_call(
        plan_kernel,
        in_specs=[SMEM_SPEC] * 2,
        out_specs=[SMEM_SPEC] * 2,
        out_shape=[jax.ShapeDtypeStruct((lists, room), jnp.int32), jax.ShapeDtypeStruct((lists,), jnp.int32)],
        compiler_params=params(1),
        cost_estimate=COST,
        name="entry_lists",
    )(own_code, peer_code)


def probs_kernel(x_own, x_peer, *refs):
    stats, (probs, columns) = refs[:-2], refs[-2:]

    @pl.when(pl.program_id(0) == 0)
    def _():
        top, total = total_at(split_rows(stats), 1, 2)
        columns[...] = columns_from_rows([top, 1.0 / total])

    top, scale = columns[:, 0:1], columns[:, 1:2]
    for side, x in enumerate((x_own, x_peer)):
        for j in range(x.shape[1] // LANES):
            raised = jnp.exp(x[:, j * LANES : (j + 1) * LANES].astype(F32) - top)
            probs[side, j] = (raised * scale).astype(BF16)


def sums_kernel(spot_ref, list_ref, count_ref, probs, w_own, w_peer, *refs, first, fan, pieces):
    outs, mass_ref, acc = refs[:-2], refs[-2], refs[-1]
    step = pl.program_id(0)
    slots, rows, _ = outs[0].shape
    side = w_own.shape[0] * fan
    mass = jnp.zeros((rows, LANES), F32)
    for k, out in enumerate(outs):
        piece = spot_ref[0] * pieces + first + k + step
        acc[...] = jnp.zeros_like(acc)

        def add(i, carry):
            parts = []
            for u in range(BATCH):
                item = list_ref[piece, i * BATCH + u]
                slot = item & (SLOT_BASE - 1)
                entry = lax.shift_right_logical(item, SLOT_BITS)
                weight = jnp.where(entry < side, 0, 1)
                parts.append((entry, slot, weight))
            for entry, slot, peer in parts:
                j = divide(entry, fan)
                f = entry - j * fan
                local_j = j - peer * (side // fan)
                weight = jnp.where(peer == 1, w_peer[local_j, f], w_own[local_j, f])
                part = jnp.dot(probs[j], weight, preferred_element_type=F32)
                acc[jnp.minimum(slot, slots)] += part.astype(BF16).astype(F32)
            return carry

        lax.fori_loop(0, divide(count_ref[piece] + BATCH - 1, BATCH), add, 0)

        def drain(i, mass):
            block = acc[i]
            out[i] = block.astype(BF16)
            return mass + block

        mass = lax.fori_loop(0, slots, drain, mass, unroll=4)
    part = rows_from_columns([jnp.sum(mass, axis=1, keepdims=True)])

    @pl.when(step == 0)
    def _():
        mass_ref[...] = part

    @pl.when(step > 0)
    def _():
        mass_ref[...] += part


def teacher_probs(x_own, x_peer, stats):
    rows, cols = x_own.shape
    steps = 4
    blocks = cols // LANES
    part = pl.BlockSpec((rows, cols // steps), lambda i: (0, i))
    probs = pl.pallas_call(
        probs_kernel,
        grid=(steps,),
        in_specs=[part, part] + [pl.BlockSpec(s.shape, lambda i: (0, 0)) for s in stats],
        out_specs=pl.BlockSpec((2, blocks // steps, rows, LANES), lambda i: (0, i, 0, 0)),
        out_shape=jax.ShapeDtypeStruct((2, blocks, rows, LANES), BF16),
        scratch_shapes=[pltpu.VMEM((rows, LANES), F32)],
        compiler_params=params(8),
        cost_estimate=COST,
        name="teacher_probs",
    )(in_hbm(x_own), x_peer, *stats)
    return probs.reshape(2 * blocks, rows, LANES)


def chip_sums(spot, lists, counts, probs, w_own, w_peer, first, n_out, steps, slots):
    rows = probs.shape[1]
    fan = w_own.shape[1]
    whole = lambda shape: pl.BlockSpec(shape, lambda s: (0,) * len(shape))
    out = pltpu.HBM((steps * slots, rows, LANES), BF16)
    return pl.pallas_call(
        functools.partial(sums_kernel, first=first, fan=fan, pieces=counts.shape[0] // 2),
        grid=(steps,),
        in_specs=[SMEM_SPEC] * 3 + [VMEM_SPEC] * 3,
        out_specs=[pl.BlockSpec((slots, rows, LANES), lambda s: (s, 0, 0))] * n_out + [whole((8, rows))],
        out_shape=[out] * n_out + [jax.ShapeDtypeStruct((8, rows), F32)],
        scratch_shapes=[pltpu.VMEM((slots + 1, rows, LANES), F32)],
        compiler_params=params(24),
        cost_estimate=COST,
        name="chip_sums",
    )(spot, lists, counts, probs, w_own, w_peer)


def stack_rows(place_ref, own_ref, near, far, everyone):
    rows = own_ref.shape[0]
    half = rows // 2
    core = place_ref[0]
    everyone[0:rows, :] = own_ref[...]
    for r in range(len(near)):
        start = (r + 1) * rows
        everyone[pl.ds(pl.multiple_of(start + core * half, half), half), :] = near[r][...]
        everyone[pl.ds(pl.multiple_of(start + (1 - core) * half, half), half), :] = far[r][...]


def logits_kernel(place_ref, after_ref, own_ref, *refs):
    n_other = (len(refs) - 3) // 2
    near, far, (head_ref, out_ref, everyone) = refs[:n_other], refs[n_other : 2 * n_other], refs[-3:]
    rows = own_ref.shape[0]
    del after_ref

    @pl.when(pl.program_id(0) == 0)
    def _():
        stack_rows(place_ref, own_ref, near, far, everyone)

    result = jnp.dot(everyone[...], head_ref[...], preferred_element_type=F32)
    for r in range(n_other + 1):
        out_ref[place_ref[1] ^ r] = result[r * rows : (r + 1) * rows, :]


def turn_kernel(place_ref, own_ref, *refs):
    n_other = (len(refs) - 2) // 2
    near, far, (turned_ref, everyone) = refs[:n_other], refs[n_other : 2 * n_other], refs[-2:]
    stack_rows(place_ref, own_ref, near, far, everyone)
    turned_ref[...] = everyone[...].T


def turned_rows(place, own, near, far):
    rows, depth = own.shape
    every = (len(near) + 1) * rows
    steps = 4
    part = depth // steps
    return pl.pallas_call(
        turn_kernel,
        grid=(steps,),
        in_specs=[SMEM_SPEC] + [pl.BlockSpec((x.shape[0], part), lambda i: (0, i)) for x in (own, *near, *far)],
        out_specs=pl.BlockSpec((part, every), lambda i: (i, 0)),
        out_shape=pltpu.HBM((depth, every), BF16),
        scratch_shapes=[pltpu.VMEM((every, part), BF16)],
        compiler_params=params(12),
        cost_estimate=COST,
        name="turned_rows",
    )(place, own, *near, *far)


def student_logits(place, after, own, near, far, head):
    rows, depth = own.shape
    n_tok = len(near) + 1
    every = n_tok * rows
    cols = head.shape[1]
    tile = 256
    whole = lambda shape: pl.BlockSpec(shape, lambda i: (0, 0))
    return pl.pallas_call(
        logits_kernel,
        grid=(cols // tile,),
        in_specs=[SMEM_SPEC, pl.BlockSpec(memory_space=pl.ANY), whole(own.shape)]
        + [whole(x.shape) for x in near + far]
        + [pl.BlockSpec((depth, tile), lambda i: (0, i))],
        out_specs=pl.BlockSpec((n_tok, rows, tile), lambda i: (0, 0, i)),
        out_shape=pltpu.HBM((n_tok, rows, cols), F32),
        scratch_shapes=[pltpu.VMEM((every, depth), BF16)],
        compiler_params=params(32),
        cost_estimate=COST,
        name="student_logits",
    )(place, after, own, *near, *far, in_hbm(head))


def student_kernel(base_ref, labels_ref, mass_ref, logits_ref, stat_ref):
    n_tok, rows, cols = logits_ref.shape
    lane = lax.broadcasted_iota(jnp.int32, (rows, LANES), 1)
    label = labels_ref[...]
    top = jnp.full((rows, LANES), -jnp.inf, F32)
    hit = jnp.zeros((rows, LANES), F32)
    for t in range(n_tok):
        for b in range(0, cols, LANES):
            block = logits_ref[t, :, b : b + LANES]
            top = jnp.maximum(top, block)
            hit = hit + jnp.where(lane == label - (base_ref[t] + b), block, 0.0)
    top = jnp.max(top, axis=1, keepdims=True)
    total = jnp.zeros((rows, LANES), F32)
    for t in range(n_tok):
        for b in range(0, cols, LANES):
            total = total + jnp.exp(logits_ref[t, :, b : b + LANES] - top)
    total = jnp.sum(total, axis=1, keepdims=True)
    hit = jnp.sum(hit, axis=1, keepdims=True)
    stat_ref[...] = rows_from_columns([jnp.zeros_like(hit), top, total, hit])
    stat_ref[0:1, :] = mass_ref[0:1, :]


def student_stats(base, label_column, mass, logits):
    return pl.pallas_call(
        student_kernel,
        in_specs=[SMEM_SPEC] + [VMEM_SPEC] * 3,
        out_specs=VMEM_SPEC,
        out_shape=jax.ShapeDtypeStruct(mass.shape, F32),
        compiler_params=params(10),
        cost_estimate=COST,
        name="student_stats",
    )(base, label_column, mass, logits)


def merge_kernel(*refs):
    stats, out = refs[:-1], refs[-1]
    parts = split_rows(stats)
    mass = tree(jnp.add, [r[0] for r in parts])
    top, total = total_at(parts, 1, 2)
    hit = tree(jnp.add, [r[3] for r in parts])
    out[...] = jnp.concatenate([mass, top, total, hit, jnp.zeros((4, top.shape[1]), F32)], axis=0)


def merge_stats(stats):
    return pl.pallas_call(
        merge_kernel,
        in_specs=[VMEM_SPEC] * len(stats),
        out_specs=VMEM_SPEC,
        out_shape=jax.ShapeDtypeStruct(stats[0].shape, F32),
        compiler_params=params(1),
        cost_estimate=COST,
        name="merge_stats",
    )(*stats)


def totals_kernel(*refs):
    stats, (columns, loss_ref) = refs[:-2], refs[-2:]
    parts = split_rows(stats)
    mass = tree(jnp.add, [r[0] for r in parts])
    top, total = total_at(parts, 1, 2)
    log_total = top + jnp.log(total)
    label_logit = tree(jnp.add, [r[3] for r in parts])
    columns[...] = columns_from_rows([mass + 1.0, log_total])
    loss_ref[...] = mass * log_total + log_total - label_logit


def token_totals(stats):
    rows = stats[0].shape[1]
    return pl.pallas_call(
        totals_kernel,
        in_specs=[VMEM_SPEC] * len(stats),
        out_specs=[VMEM_SPEC] * 2,
        out_shape=[jax.ShapeDtypeStruct((rows, LANES), F32), jax.ShapeDtypeStruct((1, rows), F32)],
        compiler_params=params(2),
        cost_estimate=COST,
        name="token_totals",
    )(*stats)


def grad_kernel(tok_ref, base_ref, labels_ref, columns, *refs, n_sums, groups):
    sums = refs[:n_sums]
    logits_ref, *grads, inner_ref, inner = refs[n_sums:]
    step = pl.program_id(0)
    _, rows, cols = logits_ref.shape

    @pl.when(step == 0)
    def _():
        inner[...] = jnp.zeros_like(inner)

    lane = lax.broadcasted_iota(jnp.int32, (rows, LANES), 1)
    lift, log_total = columns[:, 0:1], columns[:, 1:2]
    label = labels_ref[...] - base_ref[token_group(step, tok_ref, groups)]
    for r in range(len(grads)):

        @pl.when(step == r)
        def _():
            running = inner[...]
            for b in range(cols // LANES):
                place = slice(b * LANES, (b + 1) * LANES)
                target = functools.reduce(
                    jnp.add, [ref[z, b].astype(F32) for ref in sums for z in range(ref.shape[0])]
                )
                score = logits_ref[0, :, place]
                running = running + target * score
                hit = jnp.where(lane == label - b * LANES, 1.0, 0.0)
                grads[r][:, place] = (lift * jnp.exp(score - log_total) - target - hit).astype(BF16)
            inner[...] = running

    @pl.when(step == pl.num_programs(0) - 1)
    def _():
        inner_ref[...] = rows_from_columns([jnp.sum(inner[...], axis=1, keepdims=True)])[0:1, :]


def token_group(step, tok_ref, groups):
    first, last = groups
    return tok_ref[0] ^ (first + step * (last - first))


def grad_logits(tok, base, label_column, columns, sums, logits, groups):
    n_tok, rows, cols = logits.shape
    per = cols // LANES
    whole = lambda shape: pl.BlockSpec(shape, lambda t, tok_ref: (0,) * len(shape))
    group = lambda t, tok_ref: token_group(t, tok_ref, groups)
    n_out = len(groups)
    return pl.pallas_call(
        functools.partial(grad_kernel, n_sums=len(sums), groups=groups),
        grid_spec=pltpu.PrefetchScalarGridSpec(
            num_scalar_prefetch=1,
            grid=(n_out,),
            in_specs=[SMEM_SPEC, whole(label_column.shape), whole(columns.shape)]
            + [pl.BlockSpec((s.shape[0], per, rows, LANES), lambda t, r: (0, group(t, r), 0, 0)) for s in sums]
            + [pl.BlockSpec((1, rows, cols), lambda t, r: (group(t, r), 0, 0))],
            out_specs=[whole((rows, cols))] * n_out + [whole((1, rows))],
            scratch_shapes=[pltpu.VMEM((rows, LANES), F32)],
        ),
        out_shape=[pltpu.HBM((rows, cols), BF16)] * n_out + [jax.ShapeDtypeStruct((1, rows), F32)],
        compiler_params=params(14),
        cost_estimate=COST,
        name="grad_logits",
    )(tok, base, label_column, columns, *sums, logits)


def stack_pieces(pieces, b_ref):
    rows = pieces[0].shape[0]

    @pl.when(pl.program_id(0) == 0)
    def _():
        for r, piece in enumerate(pieces):
            b_ref[r * rows : (r + 1) * rows, :] = piece[...]


def product_part(a_ref, b_ref, first):
    tile = a_ref.shape[0] // pl.num_programs(0)
    rows = pl.ds(pl.multiple_of(pl.program_id(0) * tile, tile), tile)
    return rows, jnp.dot(a_ref[rows, first : first + b_ref.shape[0]], b_ref[...], preferred_element_type=F32)


def first_product_kernel(a_ref, *refs):
    pieces, (acc_ref, b_ref) = refs[:-2], refs[-2:]
    stack_pieces(pieces, b_ref)
    rows, part = product_part(a_ref, b_ref, 0)
    acc_ref[rows, :] = part


def last_product_kernel(a_ref, acc_ref, *refs):
    pieces, (o_ref, end_ref, b_ref) = refs[:-3], refs[-3:]
    stack_pieces(pieces, b_ref)
    rows, part = product_part(a_ref, b_ref, a_ref.shape[1] - b_ref.shape[0])
    o_ref[...] = (acc_ref[rows, :] + part).astype(o_ref.dtype)
    end_ref[...] = jnp.zeros_like(end_ref)


def first_product(a, pieces):
    rows, n = pieces[0].shape
    return pl.pallas_call(
        first_product_kernel,
        grid=(4,),
        in_specs=[VMEM_SPEC] + [pl.BlockSpec((rows, n), lambda i: (0, 0))] * len(pieces),
        out_specs=VMEM_SPEC,
        out_shape=pltpu.VMEM((a.shape[0], n), F32),
        scratch_shapes=[pltpu.VMEM((len(pieces) * rows, n), BF16)],
        compiler_params=params(16),
        cost_estimate=COST,
        name="first_product",
    )(in_vmem(a), in_hbm(pieces[0]), *pieces[1:])


def last_product(a, acc, pieces):
    m = a.shape[0]
    rows, n = pieces[0].shape
    steps = 4
    return pl.pallas_call(
        last_product_kernel,
        grid=(steps,),
        in_specs=[VMEM_SPEC] * 2 + [pl.BlockSpec((rows, n), lambda i: (0, 0))] * len(pieces),
        out_specs=[pl.BlockSpec((m // steps, n), lambda i: (i, 0)), pl.BlockSpec((1, rows), lambda i: (0, 0))],
        out_shape=[jax.ShapeDtypeStruct((m, n), BF16), jax.ShapeDtypeStruct((1, rows), F32)],
        scratch_shapes=[pltpu.VMEM((len(pieces) * rows, n), BF16)],
        compiler_params=params(20),
        cost_estimate=COST,
        name="last_product",
    )(in_vmem(a), in_vmem(acc), *pieces)


def swap(x, axis, mask):
    return lax.ppermute(x, axis, [(i, i ^ mask) for i in range(lax.axis_size(axis))])


def gather_chips(x):
    n = lax.axis_size("vocab")
    if n > 8:
        lines = [[2 * z + c for z in range(n // 2)] for c in range(2)]
        everything = lax.all_gather(x, "vocab", axis=0, axis_index_groups=lines)
        return [everything[z] for z in range(n // 2)]
    return [x] + [swap(x, "vocab", r) for r in range(2, n, 2)]


def butterfly(tile):
    tiles, mask = [tile], 1
    while mask < lax.axis_size("vocab"):
        tile = merge_stats(tiles) if len(tiles) > 1 else tile
        tiles = [tile, swap(tile, "vocab", mask)]
        mask *= 2
    return tiles


def exchange_tok(x):
    return lax.all_to_all(x, "tok", split_axis=0, concat_axis=0, tiled=True)


def plus(a, b):
    return (a.astype(F32) + b.astype(F32)).astype(BF16)


def exchange_tok(x):
    return lax.all_to_all(x, "tok", split_axis=0, concat_axis=0, tiled=True)


def send(x, hops):
    return lax.ppermute(x, "vocab", [(2 * a + c, 2 * b + c) for a, b in hops for c in range(2)])


def local(teacher_logits, hidden, new_head, labels, map_target, map_weight):
    rows = teacher_logits.shape[0]
    block = map_weight.shape[2]
    n_tok = lax.axis_size("tok")
    n_vocab = lax.axis_size("vocab")
    n_z = n_vocab // 2
    new_cols = new_head.shape[1]
    per = new_cols // block
    tok = lax.axis_index("tok")
    vocab = lax.axis_index("vocab")
    spot = jnp.stack([vocab % 2, vocab // 2]).astype(jnp.int32)
    slots = n_tok * per
    in_line = n_z == 4

    owner = map_target // per
    owner_vocab = owner % n_vocab
    owner_z = owner_vocab // 2
    if in_line:
        z = vocab // 2
        outer = (owner_z == 0) | (owner_z == n_z - 1)
        near_place = jnp.where(owner_z == z, 3, 2)
        place = jnp.where((owner_z // 2) == (z // 2), near_place, jnp.where(outer, 0, 1))
    else:
        place = owner_z
    slot = (owner // n_vocab) * per + map_target % per
    code = (((owner_vocab % 2) * n_z + place) * SLOT_BASE + slot).astype(jnp.int32).reshape(-1)

    peer_logits = swap(teacher_logits, "vocab", 1)
    peer_code = swap(code, "vocab", 1)
    peer_weight = swap(map_weight, "vocab", 1)
    totals = butterfly(teacher_stats(teacher_logits))
    lists, counts = plan(code, peer_code, 2 * n_z)
    probs = teacher_probs(teacher_logits, peer_logits, totals)

    half = lax.dynamic_slice_in_dim(hidden, spot[0] * (rows // 2), rows // 2)
    if in_line:
        inward, across, beyond = [(0, 1), (3, 2)], [(1, 2), (2, 1)], [(1, 3), (2, 0)]
        far_outer, mass_a = chip_sums(spot, lists, counts, probs, map_weight, peer_weight, 0, 1, 1, slots)
        first = send(far_outer, inward)
        half, probs, mass_a = lax.optimization_barrier((half, probs, mass_a))
        near = [swap(half, "tok", r) for r in range(1, n_tok)]
        far_inner, beside, own, mass_b = chip_sums(
            spot, lists, counts, probs, map_weight, peer_weight, 1, 3, 1, slots
        )
        second = send(far_inner, inward)
        first, mass = lax.optimization_barrier((first, mass_a + mass_b))
        merged = plus(far_outer, first)
        arrived = send(merged, beyond)
        *near, waited, merged = lax.optimization_barrier((*near, beside, merged))
        third = swap(waited, "vocab", 2)
    else:
        sums, mass = chip_sums(spot, lists, counts, probs, map_weight, peer_weight, 0, 1, n_z, slots)
        lines = [[2 * z + c for z in range(n_z)] for c in range(2)]
        sums = lax.all_to_all(
            sums.reshape(n_z, slots, rows, block),
            "vocab",
            split_axis=0,
            concat_axis=0,
            axis_index_groups=lines,
            tiled=True,
        )
        sums = [sums]
        near = [swap(half, "tok", r) for r in range(1, n_tok)]

    far = [swap(x, "vocab", 1) for x in near]
    where = jnp.stack([vocab % 2, tok]).astype(jnp.int32)
    logits = student_logits(where, mass, hidden, near, far, new_head)
    base = (jnp.arange(n_tok, dtype=jnp.int32) * n_vocab + vocab) * new_cols
    label_column = lax.dynamic_slice_in_dim(labels, tok * rows, rows).reshape(rows, 1)
    scores = exchange_tok(logits)
    if in_line:
        second, arrived, logits = lax.optimization_barrier((second, arrived, logits))
        merged_inner = plus(far_inner, second)
        crossed = send(merged_inner, across)
        where, merged_inner = lax.optimization_barrier((where, merged_inner))
        turned = turned_rows(where, hidden, near, far)
        scores, merged_inner, turned = lax.optimization_barrier((scores, merged_inner, turned))
        sums = [x[None] for x in (own, third, crossed, arrived)]
    else:
        turned = turned_rows(where, hidden, near, far)
    student = student_stats(base, label_column, mass, scores)
    student = merge_stats([student, swap(student, "vocab", 1)])
    stats = gather_chips(student)

    group = tok.astype(jnp.int32).reshape(1)
    columns, base_loss = token_totals(stats)
    grad_args = (group, base, label_column, columns, sums, scores)
    beside_x, across_xy, inner = grad_logits(*grad_args, (1, 3))
    beside_x, across_xy = swap(beside_x, "tok", 1), swap(across_xy, "tok", 3)
    beside_y, here, inner_b = grad_logits(*grad_args, (2, 0))
    beside_y = swap(beside_y, "tok", 2)
    inner = inner + inner_b
    acc = first_product(turned, [here, beside_x])
    head_grad, end = last_product(turned, acc, [beside_y, across_xy])
    mask = 1
    while mask < n_vocab:
        other = swap(inner, "vocab", mask)
        inner = inner + other
        mask *= 2
    return ((base_loss - inner + end).reshape(rows), head_grad)


def solution(mesh):
    return jax.shard_map(
        local,
        mesh=mesh,
        in_specs=(
            P("tok", "vocab"),
            P("tok", None),
            P(None, ("tok", "vocab")),
            P(),
            P("vocab", None),
            P("vocab", None, None, None),
        ),
        out_specs=(P("tok"), P(None, ("tok", "vocab"))),
        check_vma=False,
    )
```

```python
import functools

import jax
import jax.numpy as jnp
from jax import lax
from jax.experimental import pallas as pl
from jax.experimental.pallas import tpu as pltpu
from jax.sharding import PartitionSpec as P

F32 = jnp.float32
BF16 = jnp.bfloat16
LANES = 128
BATCH = 8
COST = pl.CostEstimate(flops=1024, bytes_accessed=1024, transcendentals=0)
SLOT_BITS = 10
SLOT_BASE = 1 << SLOT_BITS
SMEM_SPEC = pl.BlockSpec(memory_space=pltpu.SMEM)
VMEM_SPEC = pl.BlockSpec(memory_space=pltpu.VMEM)


def params(mebibytes):
    return pltpu.CompilerParams(vmem_limit_bytes=mebibytes * 1024 * 1024)


def in_hbm(x):
    return pltpu.with_memory_space_constraint(x, pltpu.HBM)


def in_vmem(x):
    return pltpu.with_memory_space_constraint(x, pltpu.VMEM)


def tree(op, items):
    while len(items) > 1:
        items = [op(items[i], items[i + 1]) if i + 1 < len(items) else items[i] for i in range(0, len(items), 2)]
    return items[0]


def total_at(rows_of, top_row, total_row):
    top = tree(jnp.maximum, [r[top_row] for r in rows_of])
    total = tree(jnp.add, [r[total_row] * jnp.exp(r[top_row] - top) for r in rows_of])
    return top, total


def split_rows(refs):
    return [[ref[k : k + 1, :] for k in range(8)] for ref in refs]


def rows_from_columns(columns):
    n = columns[0].shape[0]
    lane = lax.broadcasted_iota(jnp.int32, (n, LANES), 1)
    tile = jnp.zeros((n, LANES), F32)
    for place, column in enumerate(columns):
        tile = jnp.where(lane == place, column, tile)
    return tile.T[0:8, :]


def columns_from_rows(rows):
    n = rows[0].shape[1]
    return jnp.concatenate(rows + [jnp.zeros((LANES - len(rows), n), F32)], axis=0).T


def teacher_kernel(x_ref, stat_ref):
    rows, cols = x_ref.shape
    places = range(0, cols, LANES)
    read = lambda place: x_ref[:, place : place + LANES].astype(F32)
    top = jnp.full((rows, LANES), -jnp.inf, F32)
    for place in places:
        top = jnp.maximum(top, read(place))
    top = jnp.max(top, axis=1, keepdims=True)
    total = jnp.zeros((rows, LANES), F32)
    for place in places:
        total = total + jnp.exp(read(place) - top)
    stat_ref[...] = rows_from_columns([jnp.zeros_like(top), top, jnp.sum(total, axis=1, keepdims=True)])


def teacher_stats(x):
    return pl.pallas_call(
        teacher_kernel,
        in_specs=[VMEM_SPEC],
        out_specs=VMEM_SPEC,
        out_shape=jax.ShapeDtypeStruct((8, x.shape[0]), F32),
        compiler_params=params(6),
        cost_estimate=COST,
        name="teacher_stats",
    )(x)


def divide(x, n):
    return lax.shift_right_logical(x, n.bit_length() - 1) if n & (n - 1) == 0 else x // n


def plan_kernel(own_ref, peer_ref, list_ref, count_ref):
    lists = count_ref.shape[0]
    entries = own_ref.shape[0]
    for p in range(lists):
        count_ref[p] = 0

    def visit(i, carry):
        for side, ref in enumerate((own_ref, peer_ref)):
            code = ref[i]
            row = lax.shift_right_logical(code, SLOT_BITS)
            n = count_ref[row]
            list_ref[row, n] = (side * entries + i) * SLOT_BASE + (code & (SLOT_BASE - 1))
            count_ref[row] = n + 1
        return carry

    lax.fori_loop(0, entries, visit, 0, unroll=8)
    for p in range(lists):
        n = count_ref[p]
        for k in range(BATCH - 1):
            list_ref[p, n + k] = SLOT_BASE - 1


def plan(own_code, peer_code, lists):
    room = 2 * own_code.size + BATCH
    return pl.pallas_call(
        plan_kernel,
        in_specs=[SMEM_SPEC] * 2,
        out_specs=[SMEM_SPEC] * 2,
        out_shape=[jax.ShapeDtypeStruct((lists, room), jnp.int32), jax.ShapeDtypeStruct((lists,), jnp.int32)],
        compiler_params=params(1),
        cost_estimate=COST,
        name="entry_lists",
    )(own_code, peer_code)


def probs_kernel(x_own, x_peer, *refs):
    stats, (probs, columns) = refs[:-2], refs[-2:]

    @pl.when(pl.program_id(0) == 0)
    def _():
        top, total = total_at(split_rows(stats), 1, 2)
        columns[...] = columns_from_rows([top, 1.0 / total])

    top, scale = columns[:, 0:1], columns[:, 1:2]
    for side, x in enumerate((x_own, x_peer)):
        for j in range(x.shape[1] // LANES):
            raised = jnp.exp(x[:, j * LANES : (j + 1) * LANES].astype(F32) - top)
            probs[side, j] = (raised * scale).astype(BF16)


def sums_kernel(spot_ref, list_ref, count_ref, probs, w_own, w_peer, *refs, first, fan, pieces):
    outs, mass_ref, acc = refs[:-2], refs[-2], refs[-1]
    step = pl.program_id(0)
    slots, rows, _ = outs[0].shape
    side = w_own.shape[0] * fan
    mass = jnp.zeros((rows, LANES), F32)
    for k, out in enumerate(outs):
        piece = spot_ref[0] * pieces + first + k + step
        acc[...] = jnp.zeros_like(acc)

        def add(i, carry):
            parts = []
            for u in range(BATCH):
                item = list_ref[piece, i * BATCH + u]
                slot = item & (SLOT_BASE - 1)
                entry = lax.shift_right_logical(item, SLOT_BITS)
                weight = jnp.where(entry < side, 0, 1)
                parts.append((entry, slot, weight))
            for entry, slot, peer in parts:
                j = divide(entry, fan)
                f = entry - j * fan
                local_j = j - peer * (side // fan)
                weight = jnp.where(peer == 1, w_peer[local_j, f], w_own[local_j, f])
                part = jnp.dot(probs[j], weight, preferred_element_type=F32)
                acc[jnp.minimum(slot, slots)] += part.astype(BF16).astype(F32)
            return carry

        lax.fori_loop(0, divide(count_ref[piece] + BATCH - 1, BATCH), add, 0)

        def drain(i, mass):
            block = acc[i]
            out[i] = block.astype(BF16)
            return mass + block

        mass = lax.fori_loop(0, slots, drain, mass, unroll=4)
    part = rows_from_columns([jnp.sum(mass, axis=1, keepdims=True)])

    @pl.when(step == 0)
    def _():
        mass_ref[...] = part

    @pl.when(step > 0)
    def _():
        mass_ref[...] += part


def teacher_probs(x_own, x_peer, stats):
    rows, cols = x_own.shape
    steps = 4
    blocks = cols // LANES
    part = pl.BlockSpec((rows, cols // steps), lambda i: (0, i))
    probs = pl.pallas_call(
        probs_kernel,
        grid=(steps,),
        in_specs=[part, part] + [pl.BlockSpec(s.shape, lambda i: (0, 0)) for s in stats],
        out_specs=pl.BlockSpec((2, blocks // steps, rows, LANES), lambda i: (0, i, 0, 0)),
        out_shape=jax.ShapeDtypeStruct((2, blocks, rows, LANES), BF16),
        scratch_shapes=[pltpu.VMEM((rows, LANES), F32)],
        compiler_params=params(8),
        cost_estimate=COST,
        name="teacher_probs",
    )(in_hbm(x_own), x_peer, *stats)
    return probs.reshape(2 * blocks, rows, LANES)


def chip_sums(spot, lists, counts, probs, w_own, w_peer, first, n_out, steps, slots):
    rows = probs.shape[1]
    fan = w_own.shape[1]
    whole = lambda shape: pl.BlockSpec(shape, lambda s: (0,) * len(shape))
    out = pltpu.HBM((steps * slots, rows, LANES), BF16)
    return pl.pallas_call(
        functools.partial(sums_kernel, first=first, fan=fan, pieces=counts.shape[0] // 2),
        grid=(steps,),
        in_specs=[SMEM_SPEC] * 3 + [VMEM_SPEC] * 3,
        out_specs=[pl.BlockSpec((slots, rows, LANES), lambda s: (s, 0, 0))] * n_out + [whole((8, rows))],
        out_shape=[out] * n_out + [jax.ShapeDtypeStruct((8, rows), F32)],
        scratch_shapes=[pltpu.VMEM((slots + 1, rows, LANES), F32)],
        compiler_params=params(24),
        cost_estimate=COST,
        name="chip_sums",
    )(spot, lists, counts, probs, w_own, w_peer)


def stack_rows(place_ref, own_ref, near, far, everyone):
    rows = own_ref.shape[0]
    half = rows // 2
    core = place_ref[0]
    everyone[0:rows, :] = own_ref[...]
    for r in range(len(near)):
        start = (r + 1) * rows
        everyone[pl.ds(pl.multiple_of(start + core * half, half), half), :] = near[r][...]
        everyone[pl.ds(pl.multiple_of(start + (1 - core) * half, half), half), :] = far[r][...]


def logits_kernel(place_ref, after_ref, own_ref, *refs):
    n_other = (len(refs) - 3) // 2
    near, far, (head_ref, out_ref, everyone) = refs[:n_other], refs[n_other : 2 * n_other], refs[-3:]
    rows = own_ref.shape[0]
    del after_ref

    @pl.when(pl.program_id(0) == 0)
    def _():
        stack_rows(place_ref, own_ref, near, far, everyone)

    result = jnp.dot(everyone[...], head_ref[...], preferred_element_type=F32)
    for r in range(n_other + 1):
        out_ref[place_ref[1] ^ r] = result[r * rows : (r + 1) * rows, :]


def turn_kernel(place_ref, own_ref, *refs):
    n_other = (len(refs) - 2) // 2
    near, far, (turned_ref, everyone) = refs[:n_other], refs[n_other : 2 * n_other], refs[-2:]
    stack_rows(place_ref, own_ref, near, far, everyone)
    turned_ref[...] = everyone[...].T


def turned_rows(place, own, near, far):
    rows, depth = own.shape
    every = (len(near) + 1) * rows
    steps = 4
    part = depth // steps
    return pl.pallas_call(
        turn_kernel,
        grid=(steps,),
        in_specs=[SMEM_SPEC] + [pl.BlockSpec((x.shape[0], part), lambda i: (0, i)) for x in (own, *near, *far)],
        out_specs=pl.BlockSpec((part, every), lambda i: (i, 0)),
        out_shape=pltpu.HBM((depth, every), BF16),
        scratch_shapes=[pltpu.VMEM((every, part), BF16)],
        compiler_params=params(12),
        cost_estimate=COST,
        name="turned_rows",
    )(place, own, *near, *far)


def student_logits(place, after, own, near, far, head):
    rows, depth = own.shape
    n_tok = len(near) + 1
    every = n_tok * rows
    cols = head.shape[1]
    tile = 256
    whole = lambda shape: pl.BlockSpec(shape, lambda i: (0, 0))
    return pl.pallas_call(
        logits_kernel,
        grid=(cols // tile,),
        in_specs=[SMEM_SPEC, pl.BlockSpec(memory_space=pl.ANY), whole(own.shape)]
        + [whole(x.shape) for x in near + far]
        + [pl.BlockSpec((depth, tile), lambda i: (0, i))],
        out_specs=pl.BlockSpec((n_tok, rows, tile), lambda i: (0, 0, i)),
        out_shape=pltpu.HBM((n_tok, rows, cols), F32),
        scratch_shapes=[pltpu.VMEM((every, depth), BF16)],
        compiler_params=params(32),
        cost_estimate=COST,
        name="student_logits",
    )(place, after, own, *near, *far, in_hbm(head))


def student_kernel(base_ref, labels_ref, mass_ref, logits_ref, stat_ref):
    n_tok, rows, cols = logits_ref.shape
    lane = lax.broadcasted_iota(jnp.int32, (rows, LANES), 1)
    label = labels_ref[...]
    top = jnp.full((rows, LANES), -jnp.inf, F32)
    hit = jnp.zeros((rows, LANES), F32)
    for t in range(n_tok):
        for b in range(0, cols, LANES):
            block = logits_ref[t, :, b : b + LANES]
            top = jnp.maximum(top, block)
            hit = hit + jnp.where(lane == label - (base_ref[t] + b), block, 0.0)
    top = jnp.max(top, axis=1, keepdims=True)
    total = jnp.zeros((rows, LANES), F32)
    for t in range(n_tok):
        for b in range(0, cols, LANES):
            total = total + jnp.exp(logits_ref[t, :, b : b + LANES] - top)
    total = jnp.sum(total, axis=1, keepdims=True)
    hit = jnp.sum(hit, axis=1, keepdims=True)
    stat_ref[...] = rows_from_columns([jnp.zeros_like(hit), top, total, hit])
    stat_ref[0:1, :] = mass_ref[0:1, :]


def student_stats(base, label_column, mass, logits):
    return pl.pallas_call(
        student_kernel,
        in_specs=[SMEM_SPEC] + [VMEM_SPEC] * 3,
        out_specs=VMEM_SPEC,
        out_shape=jax.ShapeDtypeStruct(mass.shape, F32),
        compiler_params=params(10),
        cost_estimate=COST,
        name="student_stats",
    )(base, label_column, mass, logits)


def merge_kernel(*refs):
    stats, out = refs[:-1], refs[-1]
    parts = split_rows(stats)
    mass = tree(jnp.add, [r[0] for r in parts])
    top, total = total_at(parts, 1, 2)
    hit = tree(jnp.add, [r[3] for r in parts])
    out[...] = jnp.concatenate([mass, top, total, hit, jnp.zeros((4, top.shape[1]), F32)], axis=0)


def merge_stats(stats):
    return pl.pallas_call(
        merge_kernel,
        in_specs=[VMEM_SPEC] * len(stats),
        out_specs=VMEM_SPEC,
        out_shape=jax.ShapeDtypeStruct(stats[0].shape, F32),
        compiler_params=params(1),
        cost_estimate=COST,
        name="merge_stats",
    )(*stats)


def totals_kernel(*refs):
    stats, (columns, loss_ref) = refs[:-2], refs[-2:]
    parts = split_rows(stats)
    mass = tree(jnp.add, [r[0] for r in parts])
    top, total = total_at(parts, 1, 2)
    log_total = top + jnp.log(total)
    label_logit = tree(jnp.add, [r[3] for r in parts])
    columns[...] = columns_from_rows([mass + 1.0, log_total])
    loss_ref[...] = mass * log_total + log_total - label_logit


def token_totals(stats):
    rows = stats[0].shape[1]
    return pl.pallas_call(
        totals_kernel,
        in_specs=[VMEM_SPEC] * len(stats),
        out_specs=[VMEM_SPEC] * 2,
        out_shape=[jax.ShapeDtypeStruct((rows, LANES), F32), jax.ShapeDtypeStruct((1, rows), F32)],
        compiler_params=params(2),
        cost_estimate=COST,
        name="token_totals",
    )(*stats)


def grad_kernel(tok_ref, base_ref, labels_ref, columns, *refs, n_sums, groups):
    sums = refs[:n_sums]
    logits_ref, *grads, inner_ref, inner = refs[n_sums:]
    step = pl.program_id(0)
    _, rows, cols = logits_ref.shape

    @pl.when(step == 0)
    def _():
        inner[...] = jnp.zeros_like(inner)

    lane = lax.broadcasted_iota(jnp.int32, (rows, LANES), 1)
    lift, log_total = columns[:, 0:1], columns[:, 1:2]
    label = labels_ref[...] - base_ref[token_group(step, tok_ref, groups)]
    for r in range(len(grads)):

        @pl.when(step == r)
        def _():
            running = inner[...]
            for b in range(cols // LANES):
                place = slice(b * LANES, (b + 1) * LANES)
                target = functools.reduce(
                    jnp.add, [ref[z, b].astype(F32) for ref in sums for z in range(ref.shape[0])]
                )
                score = logits_ref[0, :, place]
                running = running + target * score
                hit = jnp.where(lane == label - b * LANES, 1.0, 0.0)
                grads[r][:, place] = (lift * jnp.exp(score - log_total) - target - hit).astype(BF16)
            inner[...] = running

    @pl.when(step == pl.num_programs(0) - 1)
    def _():
        inner_ref[...] = rows_from_columns([jnp.sum(inner[...], axis=1, keepdims=True)])[0:1, :]


def token_group(step, tok_ref, groups):
    r = groups[0]
    for i in range(1, len(groups)):
        r = jnp.where(step == i, groups[i], r)
    return tok_ref[0] ^ r


def grad_logits(tok, base, label_column, columns, sums, logits, groups):
    n_tok, rows, cols = logits.shape
    per = cols // LANES
    whole = lambda shape: pl.BlockSpec(shape, lambda t, tok_ref: (0,) * len(shape))
    group = lambda t, tok_ref: token_group(t, tok_ref, groups)
    n_out = len(groups)
    return pl.pallas_call(
        functools.partial(grad_kernel, n_sums=len(sums), groups=groups),
        grid_spec=pltpu.PrefetchScalarGridSpec(
            num_scalar_prefetch=1,
            grid=(n_out,),
            in_specs=[SMEM_SPEC, whole(label_column.shape), whole(columns.shape)]
            + [pl.BlockSpec((s.shape[0], per, rows, LANES), lambda t, r: (0, group(t, r), 0, 0)) for s in sums]
            + [pl.BlockSpec((1, rows, cols), lambda t, r: (group(t, r), 0, 0))],
            out_specs=[whole((rows, cols))] * n_out + [whole((1, rows))],
            scratch_shapes=[pltpu.VMEM((rows, LANES), F32)],
        ),
        out_shape=[pltpu.HBM((rows, cols), BF16)] * n_out + [jax.ShapeDtypeStruct((1, rows), F32)],
        compiler_params=params(14),
        cost_estimate=COST,
        name="grad_logits",
    )(tok, base, label_column, columns, *sums, logits)


def stack_pieces(pieces, b_ref):
    rows = pieces[0].shape[0]

    @pl.when(pl.program_id(0) == 0)
    def _():
        for r, piece in enumerate(pieces):
            b_ref[r * rows : (r + 1) * rows, :] = piece[...]


def product_part(a_ref, b_ref, first):
    tile = a_ref.shape[0] // pl.num_programs(0)
    rows = pl.ds(pl.multiple_of(pl.program_id(0) * tile, tile), tile)
    return rows, jnp.dot(a_ref[rows, first : first + b_ref.shape[0]], b_ref[...], preferred_element_type=F32)


def first_product_kernel(a_ref, *refs):
    pieces, (acc_ref, end_ref, b_ref) = refs[:-3], refs[-3:]
    stack_pieces(pieces, b_ref)
    rows, part = product_part(a_ref, b_ref, 0)
    acc_ref[rows, :] = part
    end_ref[...] = jnp.zeros_like(end_ref)


def last_product_kernel(a_ref, acc_ref, *refs):
    pieces, (o_ref, end_ref, b_ref) = refs[:-3], refs[-3:]
    stack_pieces(pieces, b_ref)
    rows, part = product_part(a_ref, b_ref, a_ref.shape[1] - b_ref.shape[0])
    o_ref[...] = (acc_ref[rows, :] + part).astype(o_ref.dtype)
    end_ref[...] = jnp.zeros_like(end_ref)


def first_product(a, pieces):
    rows, n = pieces[0].shape
    return pl.pallas_call(
        first_product_kernel,
        grid=(4,),
        in_specs=[VMEM_SPEC] + [pl.BlockSpec((rows, n), lambda i: (0, 0))] * len(pieces),
        out_specs=[VMEM_SPEC, pl.BlockSpec((1, rows), lambda i: (0, 0))],
        out_shape=[pltpu.VMEM((a.shape[0], n), F32), jax.ShapeDtypeStruct((1, rows), F32)],
        scratch_shapes=[pltpu.VMEM((len(pieces) * rows, n), BF16)],
        compiler_params=params(16),
        cost_estimate=COST,
        name="first_product",
    )(in_vmem(a), in_hbm(pieces[0]), *pieces[1:])


def last_product(a, acc, pieces):
    m = a.shape[0]
    rows, n = pieces[0].shape
    steps = 4
    return pl.pallas_call(
        last_product_kernel,
        grid=(steps,),
        in_specs=[VMEM_SPEC] * 2 + [pl.BlockSpec((rows, n), lambda i: (0, 0))] * len(pieces),
        out_specs=[pl.BlockSpec((m // steps, n), lambda i: (i, 0)), pl.BlockSpec((1, rows), lambda i: (0, 0))],
        out_shape=[jax.ShapeDtypeStruct((m, n), BF16), jax.ShapeDtypeStruct((1, rows), F32)],
        scratch_shapes=[pltpu.VMEM((len(pieces) * rows, n), BF16)],
        compiler_params=params(20),
        cost_estimate=COST,
        name="last_product",
    )(in_vmem(a), in_vmem(acc), *pieces)


def swap(x, axis, mask):
    return lax.ppermute(x, axis, [(i, i ^ mask) for i in range(lax.axis_size(axis))])


def gather_chips(x):
    n = lax.axis_size("vocab")
    if n > 8:
        lines = [[2 * z + c for z in range(n // 2)] for c in range(2)]
        everything = lax.all_gather(x, "vocab", axis=0, axis_index_groups=lines)
        return [everything[z] for z in range(n // 2)]
    return [x] + [swap(x, "vocab", r) for r in range(2, n, 2)]


def butterfly(tile):
    n = lax.axis_size("vocab")
    tiles, masks = [tile], [1 << k for k in range(1, n.bit_length() - 1)] + [1]
    for mask in masks:
        tile = merge_stats(tiles) if len(tiles) > 1 else tile
        tiles = [tile, swap(tile, "vocab", mask)]
    return tiles


def exchange_tok(x):
    return lax.all_to_all(x, "tok", split_axis=0, concat_axis=0, tiled=True)


def plus(a, b):
    return (a.astype(F32) + b.astype(F32)).astype(BF16)


def exchange_tok(x):
    return lax.all_to_all(x, "tok", split_axis=0, concat_axis=0, tiled=True)


def send(x, hops):
    return lax.ppermute(x, "vocab", [(2 * a + c, 2 * b + c) for a, b in hops for c in range(2)])


def local(teacher_logits, hidden, new_head, labels, map_target, map_weight):
    rows = teacher_logits.shape[0]
    block = map_weight.shape[2]
    n_tok = lax.axis_size("tok")
    n_vocab = lax.axis_size("vocab")
    n_z = n_vocab // 2
    new_cols = new_head.shape[1]
    per = new_cols // block
    tok = lax.axis_index("tok")
    vocab = lax.axis_index("vocab")
    spot = jnp.stack([vocab % 2, vocab // 2]).astype(jnp.int32)
    slots = n_tok * per
    in_line = n_z == 4

    owner = map_target // per
    owner_vocab = owner % n_vocab
    owner_z = owner_vocab // 2
    if in_line:
        z = vocab // 2
        outer = (owner_z == 0) | (owner_z == n_z - 1)
        near_place = jnp.where(owner_z == z, 3, 2)
        place = jnp.where((owner_z // 2) == (z // 2), near_place, jnp.where(outer, 0, 1))
    else:
        place = owner_z
    slot = (owner // n_vocab) * per + map_target % per
    code = (((owner_vocab % 2) * n_z + place) * SLOT_BASE + slot).astype(jnp.int32).reshape(-1)

    peer_logits = swap(teacher_logits, "vocab", 1)
    peer_code = swap(code, "vocab", 1)
    peer_weight = swap(map_weight, "vocab", 1)
    totals = butterfly(teacher_stats(teacher_logits))
    lists, counts = plan(code, peer_code, 2 * n_z)
    probs = teacher_probs(teacher_logits, peer_logits, totals)

    half = lax.dynamic_slice_in_dim(hidden, spot[0] * (rows // 2), rows // 2)
    if in_line:
        inward, across, beyond = [(0, 1), (3, 2)], [(1, 2), (2, 1)], [(1, 3), (2, 0)]
        far_outer, mass_a = chip_sums(spot, lists, counts, probs, map_weight, peer_weight, 0, 1, 1, slots)
        first = send(far_outer, inward)
        half, probs, mass_a = lax.optimization_barrier((half, probs, mass_a))
        near = [swap(half, "tok", r) for r in range(1, n_tok)]
        far_inner, beside, own, mass_b = chip_sums(
            spot, lists, counts, probs, map_weight, peer_weight, 1, 3, 1, slots
        )
        second = send(far_inner, inward)
        first, mass = lax.optimization_barrier((first, mass_a + mass_b))
        merged = plus(far_outer, first)
        arrived = send(merged, beyond)
        *near, waited, merged = lax.optimization_barrier((*near, beside, merged))
        third = swap(waited, "vocab", 2)
    else:
        sums, mass = chip_sums(spot, lists, counts, probs, map_weight, peer_weight, 0, 1, n_z, slots)
        lines = [[2 * z + c for z in range(n_z)] for c in range(2)]
        sums = lax.all_to_all(
            sums.reshape(n_z, slots, rows, block),
            "vocab",
            split_axis=0,
            concat_axis=0,
            axis_index_groups=lines,
            tiled=True,
        )
        sums = [sums]
        near = [swap(half, "tok", r) for r in range(1, n_tok)]

    far = [swap(x, "vocab", 1) for x in near]
    where = jnp.stack([vocab % 2, tok]).astype(jnp.int32)
    logits = student_logits(where, mass, hidden, near, far, new_head)
    base = (jnp.arange(n_tok, dtype=jnp.int32) * n_vocab + vocab) * new_cols
    label_column = lax.dynamic_slice_in_dim(labels, tok * rows, rows).reshape(rows, 1)
    scores = exchange_tok(logits)
    if in_line:
        second, arrived, logits = lax.optimization_barrier((second, arrived, logits))
        merged_inner = plus(far_inner, second)
        crossed = send(merged_inner, across)
        where, merged_inner = lax.optimization_barrier((where, merged_inner))
        turned = turned_rows(where, hidden, near[-1:] + near[:-1], far[-1:] + far[:-1])
        scores, merged_inner, turned = lax.optimization_barrier((scores, merged_inner, turned))
        sums = [x[None] for x in (own, third, crossed, arrived)]
    else:
        turned = turned_rows(where, hidden, near[-1:] + near[:-1], far[-1:] + far[:-1])
    student = student_stats(base, label_column, mass, scores)
    student = merge_stats([student, swap(student, "vocab", 1)])
    stats = gather_chips(student)

    group = tok.astype(jnp.int32).reshape(1)
    columns, base_loss = token_totals(stats)
    grad_args = (group, base, label_column, columns, sums, scores)
    far_group, inner = grad_logits(*grad_args, (3,))
    far_group = swap(far_group, "tok", 3)
    beside_x, beside_y, here, inner_b = grad_logits(*grad_args, (1, 2, 0))
    beside_x, beside_y = swap(beside_x, "tok", 1), swap(beside_y, "tok", 2)
    inner = inner + inner_b
    acc, middle = first_product(turned, [here, far_group])
    head_grad, end = last_product(turned, acc, [beside_x, beside_y])
    mask = 1
    while mask < n_vocab:
        inner = inner + swap(inner, "vocab", mask)
        if mask == 2:
            inner = inner + middle
        mask *= 2
    return ((base_loss - inner + end).reshape(rows), head_grad)


def solution(mesh):
    return jax.shard_map(
        local,
        mesh=mesh,
        in_specs=(
            P("tok", "vocab"),
            P("tok", None),
            P(None, ("tok", "vocab")),
            P(),
            P("vocab", None),
            P("vocab", None, None, None),
        ),
        out_specs=(P("tok"), P(None, ("tok", "vocab"))),
        check_vma=False,
    )
```

```python
import functools

import jax
import jax.numpy as jnp
from jax import lax
from jax.experimental import pallas as pl
from jax.experimental.pallas import tpu as pltpu
from jax.sharding import PartitionSpec as P

F32 = jnp.float32
BF16 = jnp.bfloat16
LANES = 128
BATCH = 8
COST = pl.CostEstimate(flops=1024, bytes_accessed=1024, transcendentals=0)
SLOT_BITS = 10
SLOT_BASE = 1 << SLOT_BITS
SMEM_SPEC = pl.BlockSpec(memory_space=pltpu.SMEM)
VMEM_SPEC = pl.BlockSpec(memory_space=pltpu.VMEM)


def params(mebibytes):
    return pltpu.CompilerParams(vmem_limit_bytes=mebibytes * 1024 * 1024)


def in_hbm(x):
    return pltpu.with_memory_space_constraint(x, pltpu.HBM)


def in_vmem(x):
    return pltpu.with_memory_space_constraint(x, pltpu.VMEM)


def tree(op, items):
    while len(items) > 1:
        items = [op(items[i], items[i + 1]) if i + 1 < len(items) else items[i] for i in range(0, len(items), 2)]
    return items[0]


def total_at(rows_of, top_row, total_row):
    top = tree(jnp.maximum, [r[top_row] for r in rows_of])
    total = tree(jnp.add, [r[total_row] * jnp.exp(r[top_row] - top) for r in rows_of])
    return top, total


def split_rows(refs):
    return [[ref[k : k + 1, :] for k in range(8)] for ref in refs]


def rows_from_columns(columns):
    n = columns[0].shape[0]
    lane = lax.broadcasted_iota(jnp.int32, (n, LANES), 1)
    tile = jnp.zeros((n, LANES), F32)
    for place, column in enumerate(columns):
        tile = jnp.where(lane == place, column, tile)
    return tile.T[0:8, :]


def columns_from_rows(rows):
    n = rows[0].shape[1]
    return jnp.concatenate(rows + [jnp.zeros((LANES - len(rows), n), F32)], axis=0).T


def teacher_kernel(x_ref, stat_ref):
    rows, cols = x_ref.shape
    places = range(0, cols, LANES)
    read = lambda place: x_ref[:, place : place + LANES].astype(F32)
    top = jnp.full((rows, LANES), -jnp.inf, F32)
    for place in places:
        top = jnp.maximum(top, read(place))
    top = jnp.max(top, axis=1, keepdims=True)
    total = jnp.zeros((rows, LANES), F32)
    for place in places:
        total = total + jnp.exp(read(place) - top)
    stat_ref[...] = rows_from_columns([jnp.zeros_like(top), top, jnp.sum(total, axis=1, keepdims=True)])


def teacher_stats(x):
    return pl.pallas_call(
        teacher_kernel,
        in_specs=[VMEM_SPEC],
        out_specs=VMEM_SPEC,
        out_shape=jax.ShapeDtypeStruct((8, x.shape[0]), F32),
        compiler_params=params(6),
        cost_estimate=COST,
        name="teacher_stats",
    )(x)


def divide(x, n):
    return lax.shift_right_logical(x, n.bit_length() - 1) if n & (n - 1) == 0 else x // n


def plan_kernel(own_ref, peer_ref, list_ref):
    lists, room = list_ref.shape
    codes = [own_ref[...], peer_ref[...]]
    n = codes[0].shape[1]
    rows = [lax.shift_right_logical(code, SLOT_BITS) for code in codes]
    across = [jnp.broadcast_to(row.astype(F32), (n, n)) for row in rows]
    down = [x.T for x in across]
    before = lax.broadcasted_iota(jnp.int32, (n, n), 1) < lax.broadcasted_iota(jnp.int32, (n, n), 0)
    count = lambda mask: jnp.sum(jnp.where(mask, 1.0, 0.0), axis=1, keepdims=True)
    ranks = [count((down[0] == across[0]) & before)]
    ranks.append(count((down[1] == across[1]) & before) + count(down[1] == across[0]))
    place = lax.broadcasted_iota(jnp.int32, (n, room), 1).astype(F32)
    entry = lax.broadcasted_iota(jnp.int32, (lists, n), 1).astype(F32)
    entries = slots = jnp.zeros((lists, room), F32)
    counts = jnp.zeros((lists, 1), F32)
    for side, code in enumerate(codes):
        member = jnp.broadcast_to(rows[side], (lists, n)) == lax.broadcasted_iota(jnp.int32, (lists, n), 0)
        slot = jnp.broadcast_to(code & (SLOT_BASE - 1), (lists, n)).astype(F32)
        here = jnp.where(place == ranks[side], 1.0, 0.0).astype(BF16)
        pick = lambda x: jnp.dot(jnp.where(member, x, 0.0).astype(BF16), here, preferred_element_type=F32)
        entries = entries + pick(entry + side * n)
        slots = slots + pick(slot)
        counts = counts + count(member)
    column = lax.broadcasted_iota(jnp.int32, (lists, room), 1)
    counts = counts.astype(jnp.int32)
    items = entries.astype(jnp.int32) * SLOT_BASE + slots.astype(jnp.int32)
    items = jnp.where(column < counts, items, SLOT_BASE - 1)
    list_ref[...] = jnp.where(column == room - 1, counts, items)


def plan(own_code, peer_code, lists):
    n = own_code.size
    room = 3 * LANES
    return pl.pallas_call(
        plan_kernel,
        in_specs=[VMEM_SPEC] * 2,
        out_specs=VMEM_SPEC,
        out_shape=jax.ShapeDtypeStruct((lists, room), jnp.int32),
        compiler_params=params(4),
        cost_estimate=COST,
        name="entry_lists",
    )(own_code.reshape(1, n), peer_code.reshape(1, n))


def probs_kernel(x_own, x_peer, *refs):
    stats, (probs, columns) = refs[:-2], refs[-2:]

    @pl.when(pl.program_id(0) == 0)
    def _():
        top, total = total_at(split_rows(stats), 1, 2)
        columns[...] = columns_from_rows([top, 1.0 / total])

    top, scale = columns[:, 0:1], columns[:, 1:2]
    for side, x in enumerate((x_own, x_peer)):
        for j in range(x.shape[1] // LANES):
            raised = jnp.exp(x[:, j * LANES : (j + 1) * LANES].astype(F32) - top)
            probs[side, j] = (raised * scale).astype(BF16)


def sums_kernel(spot_ref, list_ref, probs, w_own, w_peer, *refs, first, fan, pieces):
    outs, mass_ref, acc = refs[:-2], refs[-2], refs[-1]
    step = pl.program_id(0)
    slots, rows, _ = outs[0].shape
    side = w_own.shape[0] * fan
    mass = jnp.zeros((rows, LANES), F32)
    for k, out in enumerate(outs):
        piece = spot_ref[0] * pieces + first + k + step
        acc[...] = jnp.zeros_like(acc)

        def add(i, carry):
            parts = []
            for u in range(BATCH):
                item = list_ref[piece, i * BATCH + u]
                slot = item & (SLOT_BASE - 1)
                entry = lax.shift_right_logical(item, SLOT_BITS)
                weight = jnp.where(entry < side, 0, 1)
                parts.append((entry, slot, weight))
            for entry, slot, peer in parts:
                j = divide(entry, fan)
                f = entry - j * fan
                local_j = j - peer * (side // fan)
                weight = jnp.where(peer == 1, w_peer[local_j, f], w_own[local_j, f])
                part = jnp.dot(probs[j], weight, preferred_element_type=F32)
                acc[jnp.minimum(slot, slots)] += part.astype(BF16).astype(F32)
            return carry

        lax.fori_loop(0, divide(list_ref[piece, list_ref.shape[1] - 1] + BATCH - 1, BATCH), add, 0)

        def drain(i, mass):
            block = acc[i]
            out[i] = block.astype(BF16)
            return mass + block

        mass = lax.fori_loop(0, slots, drain, mass, unroll=4)
    part = rows_from_columns([jnp.sum(mass, axis=1, keepdims=True)])

    @pl.when(step == 0)
    def _():
        mass_ref[...] = part

    @pl.when(step > 0)
    def _():
        mass_ref[...] += part


def teacher_probs(x_own, x_peer, stats):
    rows, cols = x_own.shape
    steps = 4
    blocks = cols // LANES
    part = pl.BlockSpec((rows, cols // steps), lambda i: (0, i))
    probs = pl.pallas_call(
        probs_kernel,
        grid=(steps,),
        in_specs=[part, part] + [pl.BlockSpec(s.shape, lambda i: (0, 0)) for s in stats],
        out_specs=pl.BlockSpec((2, blocks // steps, rows, LANES), lambda i: (0, i, 0, 0)),
        out_shape=jax.ShapeDtypeStruct((2, blocks, rows, LANES), BF16),
        scratch_shapes=[pltpu.VMEM((rows, LANES), F32)],
        compiler_params=params(8),
        cost_estimate=COST,
        name="teacher_probs",
    )(in_hbm(x_own), x_peer, *stats)
    return probs.reshape(2 * blocks, rows, LANES)


def chip_sums(spot, lists, probs, w_own, w_peer, first, n_out, steps, slots):
    rows = probs.shape[1]
    fan = w_own.shape[1]
    whole = lambda shape: pl.BlockSpec(shape, lambda s: (0,) * len(shape))
    out = pltpu.HBM((steps * slots, rows, LANES), BF16)
    return pl.pallas_call(
        functools.partial(sums_kernel, first=first, fan=fan, pieces=lists.shape[0] // 2),
        grid=(steps,),
        in_specs=[SMEM_SPEC] * 2 + [VMEM_SPEC] * 3,
        out_specs=[pl.BlockSpec((slots, rows, LANES), lambda s: (s, 0, 0))] * n_out + [whole((8, rows))],
        out_shape=[out] * n_out + [jax.ShapeDtypeStruct((8, rows), F32)],
        scratch_shapes=[pltpu.VMEM((slots + 1, rows, LANES), F32)],
        compiler_params=params(24),
        cost_estimate=COST,
        name="chip_sums",
    )(spot, lists, probs, w_own, w_peer)


def stack_rows(place_ref, own_ref, near, far, everyone):
    rows = own_ref.shape[0]
    half = rows // 2
    core = place_ref[0]
    everyone[0:rows, :] = own_ref[...]
    for r in range(len(near)):
        start = (r + 1) * rows
        everyone[pl.ds(pl.multiple_of(start + core * half, half), half), :] = near[r][...]
        everyone[pl.ds(pl.multiple_of(start + (1 - core) * half, half), half), :] = far[r][...]


def logits_kernel(place_ref, after_ref, own_ref, *refs):
    n_other = (len(refs) - 3) // 2
    near, far, (head_ref, out_ref, everyone) = refs[:n_other], refs[n_other : 2 * n_other], refs[-3:]
    rows = own_ref.shape[0]
    del after_ref

    @pl.when(pl.program_id(0) == 0)
    def _():
        stack_rows(place_ref, own_ref, near, far, everyone)

    result = jnp.dot(everyone[...], head_ref[...], preferred_element_type=F32)
    for r in range(n_other + 1):
        out_ref[place_ref[1] ^ r] = result[r * rows : (r + 1) * rows, :]


def turn_kernel(place_ref, own_ref, *refs):
    n_other = (len(refs) - 2) // 2
    near, far, (turned_ref, everyone) = refs[:n_other], refs[n_other : 2 * n_other], refs[-2:]
    stack_rows(place_ref, own_ref, near, far, everyone)
    turned_ref[...] = everyone[...].T


def turned_rows(place, own, near, far):
    rows, depth = own.shape
    every = (len(near) + 1) * rows
    steps = 4
    part = depth // steps
    return pl.pallas_call(
        turn_kernel,
        grid=(steps,),
        in_specs=[SMEM_SPEC] + [pl.BlockSpec((x.shape[0], part), lambda i: (0, i)) for x in (own, *near, *far)],
        out_specs=pl.BlockSpec((part, every), lambda i: (i, 0)),
        out_shape=pltpu.HBM((depth, every), BF16),
        scratch_shapes=[pltpu.VMEM((every, part), BF16)],
        compiler_params=params(12),
        cost_estimate=COST,
        name="turned_rows",
    )(place, own, *near, *far)


def student_logits(place, after, own, near, far, head):
    rows, depth = own.shape
    n_tok = len(near) + 1
    every = n_tok * rows
    cols = head.shape[1]
    tile = 256
    whole = lambda shape: pl.BlockSpec(shape, lambda i: (0, 0))
    return pl.pallas_call(
        logits_kernel,
        grid=(cols // tile,),
        in_specs=[SMEM_SPEC, pl.BlockSpec(memory_space=pl.ANY), whole(own.shape)]
        + [whole(x.shape) for x in near + far]
        + [pl.BlockSpec((depth, tile), lambda i: (0, i))],
        out_specs=pl.BlockSpec((n_tok, rows, tile), lambda i: (0, 0, i)),
        out_shape=pltpu.HBM((n_tok, rows, cols), F32),
        scratch_shapes=[pltpu.VMEM((every, depth), BF16)],
        compiler_params=params(32),
        cost_estimate=COST,
        name="student_logits",
    )(place, after, own, *near, *far, in_hbm(head))


def student_kernel(base_ref, labels_ref, mass_ref, logits_ref, stat_ref):
    n_tok, rows, cols = logits_ref.shape
    lane = lax.broadcasted_iota(jnp.int32, (rows, LANES), 1)
    label = labels_ref[...]
    top = jnp.full((rows, LANES), -jnp.inf, F32)
    hit = jnp.zeros((rows, LANES), F32)
    for t in range(n_tok):
        for b in range(0, cols, LANES):
            block = logits_ref[t, :, b : b + LANES]
            top = jnp.maximum(top, block)
            hit = hit + jnp.where(lane == label - (base_ref[t] + b), block, 0.0)
    top = jnp.max(top, axis=1, keepdims=True)
    total = jnp.zeros((rows, LANES), F32)
    for t in range(n_tok):
        for b in range(0, cols, LANES):
            total = total + jnp.exp(logits_ref[t, :, b : b + LANES] - top)
    total = jnp.sum(total, axis=1, keepdims=True)
    hit = jnp.sum(hit, axis=1, keepdims=True)
    stat_ref[...] = rows_from_columns([jnp.zeros_like(hit), top, total, hit])
    stat_ref[0:1, :] = mass_ref[0:1, :]


def student_stats(base, label_column, mass, logits):
    return pl.pallas_call(
        student_kernel,
        in_specs=[SMEM_SPEC] + [VMEM_SPEC] * 3,
        out_specs=VMEM_SPEC,
        out_shape=jax.ShapeDtypeStruct(mass.shape, F32),
        compiler_params=params(10),
        cost_estimate=COST,
        name="student_stats",
    )(base, label_column, mass, logits)


def merge_kernel(*refs):
    stats, out = refs[:-1], refs[-1]
    parts = split_rows(stats)
    mass = tree(jnp.add, [r[0] for r in parts])
    top, total = total_at(parts, 1, 2)
    hit = tree(jnp.add, [r[3] for r in parts])
    out[...] = jnp.concatenate([mass, top, total, hit, jnp.zeros((4, top.shape[1]), F32)], axis=0)


def merge_stats(stats):
    return pl.pallas_call(
        merge_kernel,
        in_specs=[VMEM_SPEC] * len(stats),
        out_specs=VMEM_SPEC,
        out_shape=jax.ShapeDtypeStruct(stats[0].shape, F32),
        compiler_params=params(1),
        cost_estimate=COST,
        name="merge_stats",
    )(*stats)


def totals_kernel(*refs):
    stats, (columns, loss_ref) = refs[:-2], refs[-2:]
    parts = split_rows(stats)
    mass = tree(jnp.add, [r[0] for r in parts])
    top, total = total_at(parts, 1, 2)
    log_total = top + jnp.log(total)
    label_logit = tree(jnp.add, [r[3] for r in parts])
    columns[...] = columns_from_rows([mass + 1.0, log_total])
    loss_ref[...] = mass * log_total + log_total - label_logit


def token_totals(stats):
    rows = stats[0].shape[1]
    return pl.pallas_call(
        totals_kernel,
        in_specs=[VMEM_SPEC] * len(stats),
        out_specs=[VMEM_SPEC] * 2,
        out_shape=[jax.ShapeDtypeStruct((rows, LANES), F32), jax.ShapeDtypeStruct((1, rows), F32)],
        compiler_params=params(2),
        cost_estimate=COST,
        name="token_totals",
    )(*stats)


def grad_kernel(tok_ref, base_ref, labels_ref, columns, *refs, n_sums, groups):
    sums = refs[:n_sums]
    logits_ref, *grads, inner_ref, inner = refs[n_sums:]
    step = pl.program_id(0)
    _, rows, cols = logits_ref.shape

    @pl.when(step == 0)
    def _():
        inner[...] = jnp.zeros_like(inner)

    lane = lax.broadcasted_iota(jnp.int32, (rows, LANES), 1)
    lift, log_total = columns[:, 0:1], columns[:, 1:2]
    label = labels_ref[...] - base_ref[token_group(step, tok_ref, groups)]
    for r in range(len(grads)):

        @pl.when(step == r)
        def _():
            running = inner[...]
            for b in range(cols // LANES):
                place = slice(b * LANES, (b + 1) * LANES)
                target = functools.reduce(
                    jnp.add, [ref[z, b].astype(F32) for ref in sums for z in range(ref.shape[0])]
                )
                score = logits_ref[0, :, place]
                running = running + target * score
                hit = jnp.where(lane == label - b * LANES, 1.0, 0.0)
                grads[r][:, place] = (lift * jnp.exp(score - log_total) - target - hit).astype(BF16)
            inner[...] = running

    @pl.when(step == pl.num_programs(0) - 1)
    def _():
        inner_ref[...] = rows_from_columns([jnp.sum(inner[...], axis=1, keepdims=True)])[0:1, :]


def token_group(step, tok_ref, groups):
    r = groups[0]
    for i in range(1, len(groups)):
        r = jnp.where(step == i, groups[i], r)
    return tok_ref[0] ^ r


def grad_logits(tok, base, label_column, columns, sums, logits, groups):
    n_tok, rows, cols = logits.shape
    per = cols // LANES
    whole = lambda shape: pl.BlockSpec(shape, lambda t, tok_ref: (0,) * len(shape))
    group = lambda t, tok_ref: token_group(t, tok_ref, groups)
    n_out = len(groups)
    return pl.pallas_call(
        functools.partial(grad_kernel, n_sums=len(sums), groups=groups),
        grid_spec=pltpu.PrefetchScalarGridSpec(
            num_scalar_prefetch=1,
            grid=(n_out,),
            in_specs=[SMEM_SPEC, whole(label_column.shape), whole(columns.shape)]
            + [pl.BlockSpec((s.shape[0], per, rows, LANES), lambda t, r: (0, group(t, r), 0, 0)) for s in sums]
            + [pl.BlockSpec((1, rows, cols), lambda t, r: (group(t, r), 0, 0))],
            out_specs=[whole((rows, cols))] * n_out + [whole((1, rows))],
            scratch_shapes=[pltpu.VMEM((rows, LANES), F32)],
        ),
        out_shape=[pltpu.HBM((rows, cols), BF16)] * n_out + [jax.ShapeDtypeStruct((1, rows), F32)],
        compiler_params=params(14),
        cost_estimate=COST,
        name="grad_logits",
    )(tok, base, label_column, columns, *sums, logits)


def stack_pieces(pieces, b_ref):
    rows = pieces[0].shape[0]

    @pl.when(pl.program_id(0) == 0)
    def _():
        for r, piece in enumerate(pieces):
            b_ref[r * rows : (r + 1) * rows, :] = piece[...]


def product_part(a_ref, b_ref, first):
    tile = a_ref.shape[0] // pl.num_programs(0)
    rows = pl.ds(pl.multiple_of(pl.program_id(0) * tile, tile), tile)
    return rows, jnp.dot(a_ref[rows, first : first + b_ref.shape[0]], b_ref[...], preferred_element_type=F32)


def first_product_kernel(a_ref, *refs):
    pieces, (acc_ref, end_ref, b_ref) = refs[:-3], refs[-3:]
    stack_pieces(pieces, b_ref)
    rows, part = product_part(a_ref, b_ref, 0)
    acc_ref[rows, :] = part
    end_ref[...] = jnp.zeros_like(end_ref)


def last_product_kernel(a_ref, acc_ref, *refs):
    pieces, (o_ref, end_ref, b_ref) = refs[:-3], refs[-3:]
    stack_pieces(pieces, b_ref)
    rows, part = product_part(a_ref, b_ref, a_ref.shape[1] - b_ref.shape[0])
    o_ref[...] = (acc_ref[rows, :] + part).astype(o_ref.dtype)
    end_ref[...] = jnp.zeros_like(end_ref)


def first_product(a, pieces):
    rows, n = pieces[0].shape
    return pl.pallas_call(
        first_product_kernel,
        grid=(4,),
        in_specs=[VMEM_SPEC] + [pl.BlockSpec((rows, n), lambda i: (0, 0))] * len(pieces),
        out_specs=[VMEM_SPEC, pl.BlockSpec((1, rows), lambda i: (0, 0))],
        out_shape=[pltpu.VMEM((a.shape[0], n), F32), jax.ShapeDtypeStruct((1, rows), F32)],
        scratch_shapes=[pltpu.VMEM((len(pieces) * rows, n), BF16)],
        compiler_params=params(16),
        cost_estimate=COST,
        name="first_product",
    )(in_vmem(a), in_hbm(pieces[0]), *pieces[1:])


def last_product(a, acc, pieces):
    m = a.shape[0]
    rows, n = pieces[0].shape
    steps = 4
    return pl.pallas_call(
        last_product_kernel,
        grid=(steps,),
        in_specs=[VMEM_SPEC] * 2 + [pl.BlockSpec((rows, n), lambda i: (0, 0))] * len(pieces),
        out_specs=[pl.BlockSpec((m // steps, n), lambda i: (i, 0)), pl.BlockSpec((1, rows), lambda i: (0, 0))],
        out_shape=[jax.ShapeDtypeStruct((m, n), BF16), jax.ShapeDtypeStruct((1, rows), F32)],
        scratch_shapes=[pltpu.VMEM((len(pieces) * rows, n), BF16)],
        compiler_params=params(20),
        cost_estimate=COST,
        name="last_product",
    )(in_vmem(a), in_vmem(acc), *pieces)


def swap(x, axis, mask):
    return lax.ppermute(x, axis, [(i, i ^ mask) for i in range(lax.axis_size(axis))])


def gather_chips(x):
    n = lax.axis_size("vocab")
    if n > 8:
        lines = [[2 * z + c for z in range(n // 2)] for c in range(2)]
        everything = lax.all_gather(x, "vocab", axis=0, axis_index_groups=lines)
        return [everything[z] for z in range(n // 2)]
    return [x] + [swap(x, "vocab", r) for r in range(2, n, 2)]


def butterfly(tile):
    n = lax.axis_size("vocab")
    tiles, masks = [tile], [1 << k for k in range(1, n.bit_length() - 1)] + [1]
    for mask in masks:
        tile = merge_stats(tiles) if len(tiles) > 1 else tile
        tiles = [tile, swap(tile, "vocab", mask)]
    return tiles


def exchange_tok(x):
    return lax.all_to_all(x, "tok", split_axis=0, concat_axis=0, tiled=True)


def plus(a, b):
    return (a.astype(F32) + b.astype(F32)).astype(BF16)


def exchange_tok(x):
    return lax.all_to_all(x, "tok", split_axis=0, concat_axis=0, tiled=True)


def send(x, hops):
    return lax.ppermute(x, "vocab", [(2 * a + c, 2 * b + c) for a, b in hops for c in range(2)])


def local(teacher_logits, hidden, new_head, labels, map_target, map_weight):
    rows = teacher_logits.shape[0]
    block = map_weight.shape[2]
    n_tok = lax.axis_size("tok")
    n_vocab = lax.axis_size("vocab")
    n_z = n_vocab // 2
    new_cols = new_head.shape[1]
    per = new_cols // block
    tok = lax.axis_index("tok")
    vocab = lax.axis_index("vocab")
    spot = jnp.stack([vocab % 2, vocab // 2]).astype(jnp.int32)
    slots = n_tok * per
    in_line = n_z == 4

    owner = map_target // per
    owner_vocab = owner % n_vocab
    owner_z = owner_vocab // 2
    if in_line:
        z = vocab // 2
        outer = (owner_z == 0) | (owner_z == n_z - 1)
        near_place = jnp.where(owner_z == z, 3, 2)
        place = jnp.where((owner_z // 2) == (z // 2), near_place, jnp.where(outer, 0, 1))
    else:
        place = owner_z
    slot = (owner // n_vocab) * per + map_target % per
    code = (((owner_vocab % 2) * n_z + place) * SLOT_BASE + slot).astype(jnp.int32).reshape(-1)

    peer_logits = swap(teacher_logits, "vocab", 1)
    peer_code = swap(code, "vocab", 1)
    peer_weight = swap(map_weight, "vocab", 1)
    totals = butterfly(teacher_stats(teacher_logits))
    lists = plan(code, peer_code, 2 * n_z)
    probs = teacher_probs(teacher_logits, peer_logits, totals)

    half = lax.dynamic_slice_in_dim(hidden, spot[0] * (rows // 2), rows // 2)
    if in_line:
        inward, across, beyond = [(0, 1), (3, 2)], [(1, 2), (2, 1)], [(1, 3), (2, 0)]
        far_outer, mass_a = chip_sums(spot, lists, probs, map_weight, peer_weight, 0, 1, 1, slots)
        first = send(far_outer, inward)
        half, probs, mass_a = lax.optimization_barrier((half, probs, mass_a))
        near = [swap(half, "tok", r) for r in range(1, n_tok)]
        far_inner, beside, own, mass_b = chip_sums(
            spot, lists, probs, map_weight, peer_weight, 1, 3, 1, slots
        )
        second = send(far_inner, inward)
        first, mass = lax.optimization_barrier((first, mass_a + mass_b))
        merged = plus(far_outer, first)
        arrived = send(merged, beyond)
        *near, waited, merged = lax.optimization_barrier((*near, beside, merged))
        third = swap(waited, "vocab", 2)
    else:
        sums, mass = chip_sums(spot, lists, probs, map_weight, peer_weight, 0, 1, n_z, slots)
        lines = [[2 * z + c for z in range(n_z)] for c in range(2)]
        sums = lax.all_to_all(
            sums.reshape(n_z, slots, rows, block),
            "vocab",
            split_axis=0,
            concat_axis=0,
            axis_index_groups=lines,
            tiled=True,
        )
        sums = [sums]
        near = [swap(half, "tok", r) for r in range(1, n_tok)]

    far = [swap(x, "vocab", 1) for x in near]
    where = jnp.stack([vocab % 2, tok]).astype(jnp.int32)
    logits = student_logits(where, mass, hidden, near, far, new_head)
    base = (jnp.arange(n_tok, dtype=jnp.int32) * n_vocab + vocab) * new_cols
    label_column = lax.dynamic_slice_in_dim(labels, tok * rows, rows).reshape(rows, 1)
    scores = exchange_tok(logits)
    if in_line:
        second, arrived, logits = lax.optimization_barrier((second, arrived, logits))
        merged_inner = plus(far_inner, second)
        crossed = send(merged_inner, across)
        where, merged_inner = lax.optimization_barrier((where, merged_inner))
        turned = turned_rows(where, hidden, near[-1:] + near[:-1], far[-1:] + far[:-1])
        scores, merged_inner, turned = lax.optimization_barrier((scores, merged_inner, turned))
        sums = [x[None] for x in (own, third, crossed, arrived)]
    else:
        turned = turned_rows(where, hidden, near[-1:] + near[:-1], far[-1:] + far[:-1])
    student = student_stats(base, label_column, mass, scores)
    student = merge_stats([student, swap(student, "vocab", 1)])
    stats = gather_chips(student)

    group = tok.astype(jnp.int32).reshape(1)
    columns, base_loss = token_totals(stats)
    grad_args = (group, base, label_column, columns, sums, scores)
    far_group, inner = grad_logits(*grad_args, (3,))
    far_group = swap(far_group, "tok", 3)
    beside_x, beside_y, here, inner_b = grad_logits(*grad_args, (1, 2, 0))
    beside_x, beside_y = swap(beside_x, "tok", 1), swap(beside_y, "tok", 2)
    inner = inner + inner_b
    acc, middle = first_product(turned, [here, far_group])
    head_grad, end = last_product(turned, acc, [beside_x, beside_y])
    mask = 1
    while mask < n_vocab:
        inner = inner + swap(inner, "vocab", mask)
        if mask == 2:
            inner = inner + middle
        mask *= 2
    return ((base_loss - inner + end).reshape(rows), head_grad)


def solution(mesh):
    return jax.shard_map(
        local,
        mesh=mesh,
        in_specs=(
            P("tok", "vocab"),
            P("tok", None),
            P(None, ("tok", "vocab")),
            P(),
            P("vocab", None),
            P("vocab", None, None, None),
        ),
        out_specs=(P("tok"), P(None, ("tok", "vocab"))),
        check_vma=False,
    )
```

```python
import functools

import jax
import jax.numpy as jnp
from jax import lax
from jax.experimental import pallas as pl
from jax.experimental.pallas import tpu as pltpu
from jax.sharding import PartitionSpec as P

F32 = jnp.float32
BF16 = jnp.bfloat16
LANES = 128
BATCH = 8
COST = pl.CostEstimate(flops=1024, bytes_accessed=1024, transcendentals=0)
SLOT_BITS = 10
SLOT_BASE = 1 << SLOT_BITS
SMEM_SPEC = pl.BlockSpec(memory_space=pltpu.SMEM)
VMEM_SPEC = pl.BlockSpec(memory_space=pltpu.VMEM)


def params(mebibytes):
    return pltpu.CompilerParams(vmem_limit_bytes=mebibytes * 1024 * 1024)


def in_hbm(x):
    return pltpu.with_memory_space_constraint(x, pltpu.HBM)


def in_vmem(x):
    return pltpu.with_memory_space_constraint(x, pltpu.VMEM)


def tree(op, items):
    while len(items) > 1:
        items = [op(items[i], items[i + 1]) if i + 1 < len(items) else items[i] for i in range(0, len(items), 2)]
    return items[0]


def total_at(rows_of, top_row, total_row):
    top = tree(jnp.maximum, [r[top_row] for r in rows_of])
    total = tree(jnp.add, [r[total_row] * jnp.exp(r[top_row] - top) for r in rows_of])
    return top, total


def split_rows(refs):
    return [[ref[k : k + 1, :] for k in range(8)] for ref in refs]


def rows_from_columns(columns):
    n = columns[0].shape[0]
    lane = lax.broadcasted_iota(jnp.int32, (n, LANES), 1)
    tile = jnp.zeros((n, LANES), F32)
    for place, column in enumerate(columns):
        tile = jnp.where(lane == place, column, tile)
    return tile.T[0:8, :]


def columns_from_rows(rows):
    n = rows[0].shape[1]
    return jnp.concatenate(rows + [jnp.zeros((LANES - len(rows), n), F32)], axis=0).T


def teacher_kernel(x_ref, stat_ref):
    rows, cols = x_ref.shape
    places = range(0, cols, LANES)
    read = lambda place: x_ref[:, place : place + LANES].astype(F32)
    top = jnp.full((rows, LANES), -jnp.inf, F32)
    for place in places:
        top = jnp.maximum(top, read(place))
    top = jnp.max(top, axis=1, keepdims=True)
    total = jnp.zeros((rows, LANES), F32)
    for place in places:
        total = total + jnp.exp(read(place) - top)
    stat_ref[...] = rows_from_columns([jnp.zeros_like(top), top, jnp.sum(total, axis=1, keepdims=True)])


def teacher_stats(x):
    return pl.pallas_call(
        teacher_kernel,
        in_specs=[VMEM_SPEC],
        out_specs=VMEM_SPEC,
        out_shape=jax.ShapeDtypeStruct((8, x.shape[0]), F32),
        compiler_params=params(6),
        cost_estimate=COST,
        name="teacher_stats",
    )(x)


def divide(x, n):
    return lax.shift_right_logical(x, n.bit_length() - 1) if n & (n - 1) == 0 else x // n


def plan_kernel(own_ref, peer_ref, list_ref):
    lists, room = list_ref.shape
    codes = [own_ref[...], peer_ref[...]]
    n = codes[0].shape[1]
    rows = [lax.shift_right_logical(code, SLOT_BITS) for code in codes]
    across = [jnp.broadcast_to(row.astype(F32), (n, n)) for row in rows]
    down = [x.T for x in across]
    before = lax.broadcasted_iota(jnp.int32, (n, n), 1) < lax.broadcasted_iota(jnp.int32, (n, n), 0)
    count = lambda mask: jnp.sum(jnp.where(mask, 1.0, 0.0), axis=1, keepdims=True)
    ranks = [count((down[0] == across[0]) & before)]
    ranks.append(count((down[1] == across[1]) & before) + count(down[1] == across[0]))
    place = lax.broadcasted_iota(jnp.int32, (n, room), 1).astype(F32)
    entry = lax.broadcasted_iota(jnp.int32, (lists, n), 1).astype(F32)
    entries = slots = jnp.zeros((lists, room), F32)
    counts = jnp.zeros((lists, 1), F32)
    for side, code in enumerate(codes):
        member = jnp.broadcast_to(rows[side], (lists, n)) == lax.broadcasted_iota(jnp.int32, (lists, n), 0)
        slot = jnp.broadcast_to(code & (SLOT_BASE - 1), (lists, n)).astype(F32)
        here = jnp.where(place == ranks[side], 1.0, 0.0).astype(BF16)
        pick = lambda x: jnp.dot(jnp.where(member, x, 0.0).astype(BF16), here, preferred_element_type=F32)
        entries = entries + pick(entry + side * n)
        slots = slots + pick(slot)
        counts = counts + count(member)
    column = lax.broadcasted_iota(jnp.int32, (lists, room), 1)
    counts = counts.astype(jnp.int32)
    items = entries.astype(jnp.int32) * SLOT_BASE + slots.astype(jnp.int32)
    items = jnp.where(column < counts, items, SLOT_BASE - 1)
    list_ref[...] = jnp.where(column == room - 1, counts, items)


def plan(own_code, peer_code, lists):
    n = own_code.size
    room = 3 * LANES
    return pl.pallas_call(
        plan_kernel,
        in_specs=[VMEM_SPEC] * 2,
        out_specs=VMEM_SPEC,
        out_shape=jax.ShapeDtypeStruct((lists, room), jnp.int32),
        compiler_params=params(4),
        cost_estimate=COST,
        name="entry_lists",
    )(own_code.reshape(1, n), peer_code.reshape(1, n))


def probs_kernel(x_own, x_peer, *refs):
    stats, (probs, columns) = refs[:-2], refs[-2:]

    @pl.when(pl.program_id(0) == 0)
    def _():
        top, total = total_at(split_rows(stats), 1, 2)
        columns[...] = columns_from_rows([top, 1.0 / total])

    top, scale = columns[:, 0:1], columns[:, 1:2]
    for side, x in enumerate((x_own, x_peer)):
        for j in range(x.shape[1] // LANES):
            raised = jnp.exp(x[:, j * LANES : (j + 1) * LANES].astype(F32) - top)
            probs[side, j] = (raised * scale).astype(BF16)


def sums_kernel(spot_ref, list_ref, probs, w_own, w_peer, *refs, first, fan, pieces):
    outs, mass_ref, acc = refs[:-2], refs[-2], refs[-1]
    step = pl.program_id(0)
    slots, rows, _ = outs[0].shape
    side = w_own.shape[0] * fan
    mass = jnp.zeros((rows, LANES), F32)
    for k, out in enumerate(outs):
        piece = spot_ref[0] * pieces + first + k + step
        acc[...] = jnp.zeros_like(acc)

        def add(i, carry):
            parts = []
            for u in range(BATCH):
                item = list_ref[piece, i * BATCH + u]
                slot = item & (SLOT_BASE - 1)
                entry = lax.shift_right_logical(item, SLOT_BITS)
                weight = jnp.where(entry < side, 0, 1)
                parts.append((entry, slot, weight))
            for entry, slot, peer in parts:
                j = divide(entry, fan)
                f = entry - j * fan
                local_j = j - peer * (side // fan)
                weight = jnp.where(peer == 1, w_peer[local_j, f], w_own[local_j, f])
                part = jnp.dot(probs[j], weight, preferred_element_type=F32)
                acc[jnp.minimum(slot, slots)] += part.astype(BF16).astype(F32)
            return carry

        lax.fori_loop(0, divide(list_ref[piece, list_ref.shape[1] - 1] + BATCH - 1, BATCH), add, 0)

        def drain(i, mass):
            block = acc[i]
            out[i] = block.astype(BF16)
            return mass + block

        mass = lax.fori_loop(0, slots, drain, mass, unroll=4)
    part = rows_from_columns([jnp.sum(mass, axis=1, keepdims=True)])

    @pl.when(step == 0)
    def _():
        mass_ref[...] = part

    @pl.when(step > 0)
    def _():
        mass_ref[...] += part


def teacher_probs(x_own, x_peer, stats):
    rows, cols = x_own.shape
    steps = 4
    blocks = cols // LANES
    part = pl.BlockSpec((rows, cols // steps), lambda i: (0, i))
    probs = pl.pallas_call(
        probs_kernel,
        grid=(steps,),
        in_specs=[part, part] + [pl.BlockSpec(s.shape, lambda i: (0, 0)) for s in stats],
        out_specs=pl.BlockSpec((2, blocks // steps, rows, LANES), lambda i: (0, i, 0, 0)),
        out_shape=jax.ShapeDtypeStruct((2, blocks, rows, LANES), BF16),
        scratch_shapes=[pltpu.VMEM((rows, LANES), F32)],
        compiler_params=params(8),
        cost_estimate=COST,
        name="teacher_probs",
    )(in_hbm(x_own), x_peer, *stats)
    return probs.reshape(2 * blocks, rows, LANES)


def chip_sums(spot, lists, probs, w_own, w_peer, first, n_out, steps, slots):
    rows = probs.shape[1]
    fan = w_own.shape[1]
    whole = lambda shape: pl.BlockSpec(shape, lambda s: (0,) * len(shape))
    out = pltpu.HBM((steps * slots, rows, LANES), BF16)
    return pl.pallas_call(
        functools.partial(sums_kernel, first=first, fan=fan, pieces=lists.shape[0] // 2),
        grid=(steps,),
        in_specs=[SMEM_SPEC] * 2 + [VMEM_SPEC] * 3,
        out_specs=[pl.BlockSpec((slots, rows, LANES), lambda s: (s, 0, 0))] * n_out + [whole((8, rows))],
        out_shape=[out] * n_out + [jax.ShapeDtypeStruct((8, rows), F32)],
        scratch_shapes=[pltpu.VMEM((slots + 1, rows, LANES), F32)],
        compiler_params=params(24),
        cost_estimate=COST,
        name="chip_sums",
    )(spot, lists, probs, w_own, w_peer)


def stack_rows(place_ref, own_ref, near, far, everyone):
    rows = own_ref.shape[0]
    half = rows // 2
    core = place_ref[0]
    everyone[0:rows, :] = own_ref[...]
    for r in range(len(near)):
        start = (r + 1) * rows
        everyone[pl.ds(pl.multiple_of(start + core * half, half), half), :] = near[r][...]
        everyone[pl.ds(pl.multiple_of(start + (1 - core) * half, half), half), :] = far[r][...]


def logits_kernel(place_ref, after_ref, own_ref, *refs):
    n_other = (len(refs) - 3) // 2
    near, far, (head_ref, out_ref, everyone) = refs[:n_other], refs[n_other : 2 * n_other], refs[-3:]
    rows = own_ref.shape[0]
    del after_ref

    @pl.when(pl.program_id(0) == 0)
    def _():
        stack_rows(place_ref, own_ref, near, far, everyone)

    result = jnp.dot(everyone[...], head_ref[...], preferred_element_type=F32)
    for r in range(n_other + 1):
        out_ref[place_ref[1] ^ r] = result[r * rows : (r + 1) * rows, :]


def turn_kernel(place_ref, own_ref, *refs):
    n_other = (len(refs) - 2) // 2
    near, far, (turned_ref, everyone) = refs[:n_other], refs[n_other : 2 * n_other], refs[-2:]
    stack_rows(place_ref, own_ref, near, far, everyone)
    turned_ref[...] = everyone[...].T


def turned_rows(place, own, near, far):
    rows, depth = own.shape
    every = (len(near) + 1) * rows
    steps = 4
    part = depth // steps
    return pl.pallas_call(
        turn_kernel,
        grid=(steps,),
        in_specs=[SMEM_SPEC] + [pl.BlockSpec((x.shape[0], part), lambda i: (0, i)) for x in (own, *near, *far)],
        out_specs=pl.BlockSpec((part, every), lambda i: (i, 0)),
        out_shape=pltpu.HBM((depth, every), BF16),
        scratch_shapes=[pltpu.VMEM((every, part), BF16)],
        compiler_params=params(12),
        cost_estimate=COST,
        name="turned_rows",
    )(place, own, *near, *far)


def student_logits(place, after, own, near, far, head):
    rows, depth = own.shape
    n_tok = len(near) + 1
    every = n_tok * rows
    cols = head.shape[1]
    tile = 256
    whole = lambda shape: pl.BlockSpec(shape, lambda i: (0, 0))
    return pl.pallas_call(
        logits_kernel,
        grid=(cols // tile,),
        in_specs=[SMEM_SPEC, pl.BlockSpec(memory_space=pl.ANY), whole(own.shape)]
        + [whole(x.shape) for x in near + far]
        + [pl.BlockSpec((depth, tile), lambda i: (0, i))],
        out_specs=pl.BlockSpec((n_tok, rows, tile), lambda i: (0, 0, i)),
        out_shape=pltpu.HBM((n_tok, rows, cols), F32),
        scratch_shapes=[pltpu.VMEM((every, depth), BF16)],
        compiler_params=params(32),
        cost_estimate=COST,
        name="student_logits",
    )(place, after, own, *near, *far, in_hbm(head))


def student_kernel(base_ref, labels_ref, mass_ref, logits_ref, stat_ref):
    n_tok, rows, cols = logits_ref.shape
    lane = lax.broadcasted_iota(jnp.int32, (rows, LANES), 1)
    label = labels_ref[...]
    top = jnp.full((rows, LANES), -jnp.inf, F32)
    hit = jnp.zeros((rows, LANES), F32)
    for t in range(n_tok):
        for b in range(0, cols, LANES):
            block = logits_ref[t, :, b : b + LANES]
            top = jnp.maximum(top, block)
            hit = hit + jnp.where(lane == label - (base_ref[t] + b), block, 0.0)
    top = jnp.max(top, axis=1, keepdims=True)
    total = jnp.zeros((rows, LANES), F32)
    for t in range(n_tok):
        for b in range(0, cols, LANES):
            total = total + jnp.exp(logits_ref[t, :, b : b + LANES] - top)
    total = jnp.sum(total, axis=1, keepdims=True)
    hit = jnp.sum(hit, axis=1, keepdims=True)
    stat_ref[...] = rows_from_columns([jnp.zeros_like(hit), top, total, hit])
    stat_ref[0:1, :] = mass_ref[0:1, :]


def student_stats(base, label_column, mass, logits):
    return pl.pallas_call(
        student_kernel,
        in_specs=[SMEM_SPEC] + [VMEM_SPEC] * 3,
        out_specs=VMEM_SPEC,
        out_shape=jax.ShapeDtypeStruct(mass.shape, F32),
        compiler_params=params(10),
        cost_estimate=COST,
        name="student_stats",
    )(base, label_column, mass, logits)


def merge_kernel(*refs):
    stats, out = refs[:-1], refs[-1]
    parts = split_rows(stats)
    mass = tree(jnp.add, [r[0] for r in parts])
    top, total = total_at(parts, 1, 2)
    hit = tree(jnp.add, [r[3] for r in parts])
    out[...] = jnp.concatenate([mass, top, total, hit, jnp.zeros((4, top.shape[1]), F32)], axis=0)


def merge_stats(stats):
    return pl.pallas_call(
        merge_kernel,
        in_specs=[VMEM_SPEC] * len(stats),
        out_specs=VMEM_SPEC,
        out_shape=jax.ShapeDtypeStruct(stats[0].shape, F32),
        compiler_params=params(1),
        cost_estimate=COST,
        name="merge_stats",
    )(*stats)


def totals_kernel(*refs):
    stats, (columns, loss_ref) = refs[:-2], refs[-2:]
    parts = split_rows(stats)
    mass = tree(jnp.add, [r[0] for r in parts])
    top, total = total_at(parts, 1, 2)
    log_total = top + jnp.log(total)
    label_logit = tree(jnp.add, [r[3] for r in parts])
    columns[...] = columns_from_rows([mass + 1.0, log_total])
    loss_ref[...] = mass * log_total + log_total - label_logit


def token_totals(stats):
    rows = stats[0].shape[1]
    return pl.pallas_call(
        totals_kernel,
        in_specs=[VMEM_SPEC] * len(stats),
        out_specs=[VMEM_SPEC] * 2,
        out_shape=[jax.ShapeDtypeStruct((rows, LANES), F32), jax.ShapeDtypeStruct((1, rows), F32)],
        compiler_params=params(2),
        cost_estimate=COST,
        name="token_totals",
    )(*stats)


def grad_kernel(tok_ref, base_ref, labels_ref, columns, *refs, n_sums, groups):
    sums = refs[:n_sums]
    logits_ref, *grads, inner_ref, inner = refs[n_sums:]
    step = pl.program_id(0)
    _, rows, cols = logits_ref.shape

    @pl.when(step == 0)
    def _():
        inner[...] = jnp.zeros_like(inner)

    lane = lax.broadcasted_iota(jnp.int32, (rows, LANES), 1)
    lift, log_total = columns[:, 0:1], columns[:, 1:2]
    label = labels_ref[...] - base_ref[token_group(step, tok_ref, groups)]
    for r in range(len(grads)):

        @pl.when(step == r)
        def _():
            running = inner[...]
            for b in range(cols // LANES):
                place = slice(b * LANES, (b + 1) * LANES)
                target = functools.reduce(
                    jnp.add, [ref[z, b].astype(F32) for ref in sums for z in range(ref.shape[0])]
                )
                score = logits_ref[0, :, place]
                running = running + target * score
                hit = jnp.where(lane == label - b * LANES, 1.0, 0.0)
                grads[r][:, place] = (lift * jnp.exp(score - log_total) - target - hit).astype(BF16)
            inner[...] = running

    @pl.when(step == pl.num_programs(0) - 1)
    def _():
        inner_ref[...] = rows_from_columns([jnp.sum(inner[...], axis=1, keepdims=True)])[0:1, :]


def token_group(step, tok_ref, groups):
    r = groups[0]
    for i in range(1, len(groups)):
        r = jnp.where(step == i, groups[i], r)
    return tok_ref[0] ^ r


def grad_logits(tok, base, label_column, columns, sums, logits, groups):
    n_tok, rows, cols = logits.shape
    per = cols // LANES
    whole = lambda shape: pl.BlockSpec(shape, lambda t, tok_ref: (0,) * len(shape))
    group = lambda t, tok_ref: token_group(t, tok_ref, groups)
    n_out = len(groups)
    return pl.pallas_call(
        functools.partial(grad_kernel, n_sums=len(sums), groups=groups),
        grid_spec=pltpu.PrefetchScalarGridSpec(
            num_scalar_prefetch=1,
            grid=(n_out,),
            in_specs=[SMEM_SPEC, whole(label_column.shape), whole(columns.shape)]
            + [pl.BlockSpec((s.shape[0], per, rows, LANES), lambda t, r: (0, group(t, r), 0, 0)) for s in sums]
            + [pl.BlockSpec((1, rows, cols), lambda t, r: (group(t, r), 0, 0))],
            out_specs=[whole((rows, cols))] * n_out + [whole((1, rows))],
            scratch_shapes=[pltpu.VMEM((rows, LANES), F32)],
        ),
        out_shape=[pltpu.HBM((rows, cols), BF16)] * n_out + [jax.ShapeDtypeStruct((1, rows), F32)],
        compiler_params=params(14),
        cost_estimate=COST,
        name="grad_logits",
    )(tok, base, label_column, columns, *sums, logits)


def stack_pieces(pieces, b_ref):
    rows = pieces[0].shape[0]

    @pl.when(pl.program_id(0) == 0)
    def _():
        for r, piece in enumerate(pieces):
            b_ref[r * rows : (r + 1) * rows, :] = piece[...]


def product_part(a_ref, b_ref, first):
    tile = a_ref.shape[0] // pl.num_programs(0)
    rows = pl.ds(pl.multiple_of(pl.program_id(0) * tile, tile), tile)
    return rows, jnp.dot(a_ref[rows, first : first + b_ref.shape[0]], b_ref[...], preferred_element_type=F32)


def first_product_kernel(a_ref, *refs):
    pieces, (acc_ref, end_ref, b_ref) = refs[:-3], refs[-3:]
    stack_pieces(pieces, b_ref)
    rows, part = product_part(a_ref, b_ref, 0)
    acc_ref[rows, :] = part
    end_ref[...] = jnp.zeros_like(end_ref)


def last_product_kernel(a_ref, acc_ref, *refs):
    pieces, (o_ref, end_ref, b_ref) = refs[:-3], refs[-3:]
    stack_pieces(pieces, b_ref)
    rows, part = product_part(a_ref, b_ref, a_ref.shape[1] - b_ref.shape[0])
    o_ref[...] = (acc_ref[rows, :] + part).astype(o_ref.dtype)
    end_ref[...] = jnp.zeros_like(end_ref)


def first_product(a, pieces):
    rows, n = pieces[0].shape
    return pl.pallas_call(
        first_product_kernel,
        grid=(4,),
        in_specs=[VMEM_SPEC] + [pl.BlockSpec((rows, n), lambda i: (0, 0))] * len(pieces),
        out_specs=[VMEM_SPEC, pl.BlockSpec((1, rows), lambda i: (0, 0))],
        out_shape=[pltpu.VMEM((a.shape[0], n), F32), jax.ShapeDtypeStruct((1, rows), F32)],
        scratch_shapes=[pltpu.VMEM((len(pieces) * rows, n), BF16)],
        compiler_params=params(16),
        cost_estimate=COST,
        name="first_product",
    )(in_vmem(a), in_hbm(pieces[0]), *pieces[1:])


def last_product(a, acc, pieces):
    m = a.shape[0]
    rows, n = pieces[0].shape
    steps = 4
    return pl.pallas_call(
        last_product_kernel,
        grid=(steps,),
        in_specs=[VMEM_SPEC] * 2 + [pl.BlockSpec((rows, n), lambda i: (0, 0))] * len(pieces),
        out_specs=[pl.BlockSpec((m // steps, n), lambda i: (i, 0)), pl.BlockSpec((1, rows), lambda i: (0, 0))],
        out_shape=[jax.ShapeDtypeStruct((m, n), BF16), jax.ShapeDtypeStruct((1, rows), F32)],
        scratch_shapes=[pltpu.VMEM((len(pieces) * rows, n), BF16)],
        compiler_params=params(20),
        cost_estimate=COST,
        name="last_product",
    )(in_vmem(a), in_vmem(acc), *pieces)


def swap(x, axis, mask):
    return lax.ppermute(x, axis, [(i, i ^ mask) for i in range(lax.axis_size(axis))])


def gather_chips(x):
    n = lax.axis_size("vocab")
    if n > 8:
        lines = [[2 * z + c for z in range(n // 2)] for c in range(2)]
        everything = lax.all_gather(x, "vocab", axis=0, axis_index_groups=lines)
        return [everything[z] for z in range(n // 2)]
    return [x] + [swap(x, "vocab", r) for r in range(2, n, 2)]


def butterfly(tile):
    n = lax.axis_size("vocab")
    tiles, masks = [tile], [1 << k for k in range(1, n.bit_length() - 1)] + [1]
    for mask in masks:
        tile = merge_stats(tiles) if len(tiles) > 1 else tile
        tiles = [tile, swap(tile, "vocab", mask)]
    return tiles


def exchange_tok(x):
    return lax.all_to_all(x, "tok", split_axis=0, concat_axis=0, tiled=True)


def merge_sums_kernel(a_ref, b_ref, o_ref):
    o_ref[...] = (a_ref[...].astype(F32) + b_ref[...].astype(F32)).astype(BF16)


def merge_sums(a, b):
    spec = pl.BlockSpec((a.shape[0] // 2,) + a.shape[1:], lambda i: (i, 0, 0))
    return pl.pallas_call(
        merge_sums_kernel,
        grid=(2,),
        in_specs=[spec, spec],
        out_specs=spec,
        out_shape=pltpu.HBM(a.shape, BF16),
        compiler_params=params(8),
        cost_estimate=COST,
        name="merge_sums",
    )(in_hbm(a), b)


def plus(a, b):
    return (a.astype(F32) + b.astype(F32)).astype(BF16)


def exchange_tok(x):
    return lax.all_to_all(x, "tok", split_axis=0, concat_axis=0, tiled=True)


def send(x, hops):
    return lax.ppermute(x, "vocab", [(2 * a + c, 2 * b + c) for a, b in hops for c in range(2)])


def local(teacher_logits, hidden, new_head, labels, map_target, map_weight):
    rows = teacher_logits.shape[0]
    block = map_weight.shape[2]
    n_tok = lax.axis_size("tok")
    n_vocab = lax.axis_size("vocab")
    n_z = n_vocab // 2
    new_cols = new_head.shape[1]
    per = new_cols // block
    tok = lax.axis_index("tok")
    vocab = lax.axis_index("vocab")
    spot = jnp.stack([vocab % 2, vocab // 2]).astype(jnp.int32)
    slots = n_tok * per
    in_line = n_z == 4

    owner = map_target // per
    owner_vocab = owner % n_vocab
    owner_z = owner_vocab // 2
    if in_line:
        z = vocab // 2
        outer = (owner_z == 0) | (owner_z == n_z - 1)
        near_place = jnp.where(owner_z == z, 3, 2)
        place = jnp.where((owner_z // 2) == (z // 2), near_place, jnp.where(outer, 0, 1))
    else:
        place = owner_z
    slot = (owner // n_vocab) * per + map_target % per
    code = (((owner_vocab % 2) * n_z + place) * SLOT_BASE + slot).astype(jnp.int32).reshape(-1)

    peer_logits = swap(teacher_logits, "vocab", 1)
    peer_code = swap(code, "vocab", 1)
    peer_weight = swap(map_weight, "vocab", 1)
    totals = butterfly(teacher_stats(teacher_logits))
    lists = plan(code, peer_code, 2 * n_z)
    probs = teacher_probs(teacher_logits, peer_logits, totals)

    half = lax.dynamic_slice_in_dim(hidden, spot[0] * (rows // 2), rows // 2)
    if in_line:
        inward, across, beyond = [(0, 1), (3, 2)], [(1, 2), (2, 1)], [(1, 3), (2, 0)]
        far_outer, mass_a = chip_sums(spot, lists, probs, map_weight, peer_weight, 0, 1, 1, slots)
        first = send(far_outer, inward)
        half, probs, mass_a = lax.optimization_barrier((half, probs, mass_a))
        near = [swap(half, "tok", r) for r in range(1, n_tok)]
        far_inner, beside, own, mass_b = chip_sums(
            spot, lists, probs, map_weight, peer_weight, 1, 3, 1, slots
        )
        second = send(far_inner, inward)
        first, mass = lax.optimization_barrier((first, mass_a + mass_b))
        merged = plus(far_outer, first)
        arrived = send(merged, beyond)
        *near, waited, merged = lax.optimization_barrier((*near, beside, merged))
        third = swap(waited, "vocab", 2)
    else:
        sums, mass = chip_sums(spot, lists, probs, map_weight, peer_weight, 0, 1, n_z, slots)
        lines = [[2 * z + c for z in range(n_z)] for c in range(2)]
        sums = lax.all_to_all(
            sums.reshape(n_z, slots, rows, block),
            "vocab",
            split_axis=0,
            concat_axis=0,
            axis_index_groups=lines,
            tiled=True,
        )
        sums = [sums]
        near = [swap(half, "tok", r) for r in range(1, n_tok)]

    far = [swap(x, "vocab", 1) for x in near]
    where = jnp.stack([vocab % 2, tok]).astype(jnp.int32)
    logits = student_logits(where, mass, hidden, near, far, new_head)
    base = (jnp.arange(n_tok, dtype=jnp.int32) * n_vocab + vocab) * new_cols
    label_column = lax.dynamic_slice_in_dim(labels, tok * rows, rows).reshape(rows, 1)
    scores = exchange_tok(logits)
    if in_line:
        second, logits = lax.optimization_barrier((second, logits))
        merged_inner, arrived = lax.optimization_barrier((merge_sums(far_inner, second), arrived))
        crossed = send(merged_inner, across)
        where, merged_inner = lax.optimization_barrier((where, merged_inner))
        turned = turned_rows(where, hidden, near[-1:] + near[:-1], far[-1:] + far[:-1])
        scores, merged_inner, turned = lax.optimization_barrier((scores, merged_inner, turned))
        sums = [x[None] for x in (own, third, crossed, arrived)]
    else:
        turned = turned_rows(where, hidden, near[-1:] + near[:-1], far[-1:] + far[:-1])
    student = student_stats(base, label_column, mass, scores)
    student = merge_stats([student, swap(student, "vocab", 1)])
    stats = gather_chips(student)

    group = tok.astype(jnp.int32).reshape(1)
    columns, base_loss = token_totals(stats)
    grad_args = (group, base, label_column, columns, sums, scores)
    far_group, inner = grad_logits(*grad_args, (3,))
    far_group = swap(far_group, "tok", 3)
    beside_x, beside_y, here, inner_b = grad_logits(*grad_args, (1, 2, 0))
    beside_x, beside_y = swap(beside_x, "tok", 1), swap(beside_y, "tok", 2)
    inner = inner + inner_b
    acc, middle = first_product(turned, [here, far_group])
    head_grad, end = last_product(turned, acc, [beside_x, beside_y])
    mask = 1
    while mask < n_vocab:
        inner = inner + swap(inner, "vocab", mask)
        if mask == 2:
            inner = inner + middle
        mask *= 2
    return ((base_loss - inner + end).reshape(rows), head_grad)


def solution(mesh):
    return jax.shard_map(
        local,
        mesh=mesh,
        in_specs=(
            P("tok", "vocab"),
            P("tok", None),
            P(None, ("tok", "vocab")),
            P(),
            P("vocab", None),
            P("vocab", None, None, None),
        ),
        out_specs=(P("tok"), P(None, ("tok", "vocab"))),
        check_vma=False,
    )
```

```python
import functools

import jax
import jax.numpy as jnp
from jax import lax
from jax.experimental import pallas as pl
from jax.experimental.pallas import tpu as pltpu
from jax.sharding import PartitionSpec as P

F32 = jnp.float32
BF16 = jnp.bfloat16
LANES = 128
BATCH = 8
COST = pl.CostEstimate(flops=1024, bytes_accessed=1024, transcendentals=0)
SLOT_BITS = 10
SLOT_BASE = 1 << SLOT_BITS
SMEM_SPEC = pl.BlockSpec(memory_space=pltpu.SMEM)
VMEM_SPEC = pl.BlockSpec(memory_space=pltpu.VMEM)


def params(mebibytes):
    return pltpu.CompilerParams(vmem_limit_bytes=mebibytes * 1024 * 1024)


def in_hbm(x):
    return pltpu.with_memory_space_constraint(x, pltpu.HBM)


def in_vmem(x):
    return pltpu.with_memory_space_constraint(x, pltpu.VMEM)


def tree(op, items):
    while len(items) > 1:
        items = [op(items[i], items[i + 1]) if i + 1 < len(items) else items[i] for i in range(0, len(items), 2)]
    return items[0]


def total_at(rows_of, top_row, total_row):
    top = tree(jnp.maximum, [r[top_row] for r in rows_of])
    total = tree(jnp.add, [r[total_row] * jnp.exp(r[top_row] - top) for r in rows_of])
    return top, total


def split_rows(refs):
    return [[ref[k : k + 1, :] for k in range(8)] for ref in refs]


def rows_from_columns(columns):
    n = columns[0].shape[0]
    lane = lax.broadcasted_iota(jnp.int32, (n, LANES), 1)
    tile = jnp.zeros((n, LANES), F32)
    for place, column in enumerate(columns):
        tile = jnp.where(lane == place, column, tile)
    return tile.T[0:8, :]


def columns_from_rows(rows):
    n = rows[0].shape[1]
    return jnp.concatenate(rows + [jnp.zeros((LANES - len(rows), n), F32)], axis=0).T


def teacher_kernel(x_ref, stat_ref):
    rows, cols = x_ref.shape
    places = range(0, cols, LANES)
    read = lambda place: x_ref[:, place : place + LANES].astype(F32)
    top = jnp.full((rows, LANES), -jnp.inf, F32)
    for place in places:
        top = jnp.maximum(top, read(place))
    top = jnp.max(top, axis=1, keepdims=True)
    total = jnp.zeros((rows, LANES), F32)
    for place in places:
        total = total + jnp.exp(read(place) - top)
    stat_ref[...] = rows_from_columns([jnp.zeros_like(top), top, jnp.sum(total, axis=1, keepdims=True)])


def teacher_stats(x):
    return pl.pallas_call(
        teacher_kernel,
        in_specs=[VMEM_SPEC],
        out_specs=VMEM_SPEC,
        out_shape=jax.ShapeDtypeStruct((8, x.shape[0]), F32),
        compiler_params=params(6),
        cost_estimate=COST,
        name="teacher_stats",
    )(x)


def divide(x, n):
    return lax.shift_right_logical(x, n.bit_length() - 1) if n & (n - 1) == 0 else x // n


def plan_kernel(own_ref, peer_ref, list_ref):
    lists, room = list_ref.shape
    codes = [own_ref[...], peer_ref[...]]
    n = codes[0].shape[1]
    rows = [lax.shift_right_logical(code, SLOT_BITS) for code in codes]
    across = [jnp.broadcast_to(row.astype(F32), (n, n)) for row in rows]
    down = [x.T for x in across]
    before = lax.broadcasted_iota(jnp.int32, (n, n), 1) < lax.broadcasted_iota(jnp.int32, (n, n), 0)
    count = lambda mask: jnp.sum(jnp.where(mask, 1.0, 0.0), axis=1, keepdims=True)
    ranks = [count((down[0] == across[0]) & before)]
    ranks.append(count((down[1] == across[1]) & before) + count(down[1] == across[0]))
    place = lax.broadcasted_iota(jnp.int32, (n, room), 1).astype(F32)
    entry = lax.broadcasted_iota(jnp.int32, (lists, n), 1).astype(F32)
    entries = slots = jnp.zeros((lists, room), F32)
    counts = jnp.zeros((lists, 1), F32)
    for side, code in enumerate(codes):
        member = jnp.broadcast_to(rows[side], (lists, n)) == lax.broadcasted_iota(jnp.int32, (lists, n), 0)
        slot = jnp.broadcast_to(code & (SLOT_BASE - 1), (lists, n)).astype(F32)
        here = jnp.where(place == ranks[side], 1.0, 0.0).astype(BF16)
        pick = lambda x: jnp.dot(jnp.where(member, x, 0.0).astype(BF16), here, preferred_element_type=F32)
        entries = entries + pick(entry + side * n)
        slots = slots + pick(slot)
        counts = counts + count(member)
    column = lax.broadcasted_iota(jnp.int32, (lists, room), 1)
    counts = counts.astype(jnp.int32)
    items = entries.astype(jnp.int32) * SLOT_BASE + slots.astype(jnp.int32)
    items = jnp.where(column < counts, items, SLOT_BASE - 1)
    list_ref[...] = jnp.where(column == room - 1, counts, items)


def plan(own_code, peer_code, lists):
    n = own_code.size
    room = 3 * LANES
    return pl.pallas_call(
        plan_kernel,
        in_specs=[VMEM_SPEC] * 2,
        out_specs=VMEM_SPEC,
        out_shape=jax.ShapeDtypeStruct((lists, room), jnp.int32),
        compiler_params=params(4),
        cost_estimate=COST,
        name="entry_lists",
    )(own_code.reshape(1, n), peer_code.reshape(1, n))


def probs_kernel(x_own, x_peer, *refs):
    stats, (probs, columns) = refs[:-2], refs[-2:]

    @pl.when(pl.program_id(0) == 0)
    def _():
        top, total = total_at(split_rows(stats), 1, 2)
        columns[...] = columns_from_rows([top, 1.0 / total])

    top, scale = columns[:, 0:1], columns[:, 1:2]
    for side, x in enumerate((x_own, x_peer)):
        for j in range(x.shape[1] // LANES):
            raised = jnp.exp(x[:, j * LANES : (j + 1) * LANES].astype(F32) - top)
            probs[side, j] = (raised * scale).astype(BF16)


def sums_kernel(spot_ref, list_ref, probs, w_own, w_peer, *refs, first, fan, pieces):
    outs, mass_ref, acc = refs[:-2], refs[-2], refs[-1]
    step = pl.program_id(0)
    slots, rows, _ = outs[0].shape
    side = w_own.shape[0] * fan
    mass = jnp.zeros((rows, LANES), F32)
    for k, out in enumerate(outs):
        piece = spot_ref[0] * pieces + first + k + step
        acc[...] = jnp.zeros_like(acc)

        def add(i, carry):
            parts = []
            for u in range(BATCH):
                item = list_ref[piece, i * BATCH + u]
                slot = item & (SLOT_BASE - 1)
                entry = lax.shift_right_logical(item, SLOT_BITS)
                weight = jnp.where(entry < side, 0, 1)
                parts.append((entry, slot, weight))
            for entry, slot, peer in parts:
                j = divide(entry, fan)
                f = entry - j * fan
                local_j = j - peer * (side // fan)
                weight = jnp.where(peer == 1, w_peer[local_j, f], w_own[local_j, f])
                part = jnp.dot(probs[j], weight, preferred_element_type=F32)
                acc[jnp.minimum(slot, slots)] += part.astype(BF16).astype(F32)
            return carry

        lax.fori_loop(0, divide(list_ref[piece, list_ref.shape[1] - 1] + BATCH - 1, BATCH), add, 0)

        def drain(i, mass):
            block = acc[i]
            out[i] = block.astype(BF16)
            return mass + block

        mass = lax.fori_loop(0, slots, drain, mass, unroll=4)
    part = rows_from_columns([jnp.sum(mass, axis=1, keepdims=True)])

    @pl.when(step == 0)
    def _():
        mass_ref[...] = part

    @pl.when(step > 0)
    def _():
        mass_ref[...] += part


def teacher_probs(x_own, x_peer, stats):
    rows, cols = x_own.shape
    steps = 4
    blocks = cols // LANES
    part = pl.BlockSpec((rows, cols // steps), lambda i: (0, i))
    probs = pl.pallas_call(
        probs_kernel,
        grid=(steps,),
        in_specs=[part, part] + [pl.BlockSpec(s.shape, lambda i: (0, 0)) for s in stats],
        out_specs=pl.BlockSpec((2, blocks // steps, rows, LANES), lambda i: (0, i, 0, 0)),
        out_shape=jax.ShapeDtypeStruct((2, blocks, rows, LANES), BF16),
        scratch_shapes=[pltpu.VMEM((rows, LANES), F32)],
        compiler_params=params(8),
        cost_estimate=COST,
        name="teacher_probs",
    )(in_hbm(x_own), x_peer, *stats)
    return probs.reshape(2 * blocks, rows, LANES)


def chip_sums(spot, lists, probs, w_own, w_peer, first, n_out, steps, slots):
    rows = probs.shape[1]
    fan = w_own.shape[1]
    whole = lambda shape: pl.BlockSpec(shape, lambda s: (0,) * len(shape))
    out = pltpu.HBM((steps * slots, rows, LANES), BF16)
    return pl.pallas_call(
        functools.partial(sums_kernel, first=first, fan=fan, pieces=lists.shape[0] // 2),
        grid=(steps,),
        in_specs=[SMEM_SPEC] * 2 + [VMEM_SPEC] * 3,
        out_specs=[pl.BlockSpec((slots, rows, LANES), lambda s: (s, 0, 0))] * n_out + [whole((8, rows))],
        out_shape=[out] * n_out + [jax.ShapeDtypeStruct((8, rows), F32)],
        scratch_shapes=[pltpu.VMEM((slots + 1, rows, LANES), F32)],
        compiler_params=params(24),
        cost_estimate=COST,
        name="chip_sums",
    )(spot, lists, probs, w_own, w_peer)


def stack_rows(place_ref, own_ref, near, far, everyone):
    rows = own_ref.shape[0]
    half = rows // 2
    core = place_ref[0]
    everyone[0:rows, :] = own_ref[...]
    for r in range(len(near)):
        start = (r + 1) * rows
        everyone[pl.ds(pl.multiple_of(start + core * half, half), half), :] = near[r][...]
        everyone[pl.ds(pl.multiple_of(start + (1 - core) * half, half), half), :] = far[r][...]


def logits_kernel(place_ref, after_ref, own_ref, *refs):
    n_other = (len(refs) - 3) // 2
    near, far, (head_ref, out_ref, everyone) = refs[:n_other], refs[n_other : 2 * n_other], refs[-3:]
    rows = own_ref.shape[0]
    del after_ref

    @pl.when(pl.program_id(0) == 0)
    def _():
        stack_rows(place_ref, own_ref, near, far, everyone)

    result = jnp.dot(everyone[...], head_ref[...], preferred_element_type=F32)
    for r in range(n_other + 1):
        out_ref[place_ref[1] ^ r] = result[r * rows : (r + 1) * rows, :]


def turn_kernel(place_ref, own_ref, *refs):
    n_other = (len(refs) - 2) // 2
    near, far, (turned_ref, everyone) = refs[:n_other], refs[n_other : 2 * n_other], refs[-2:]
    stack_rows(place_ref, own_ref, near, far, everyone)
    turned_ref[...] = everyone[...].T


def turned_rows(place, own, near, far):
    rows, depth = own.shape
    every = (len(near) + 1) * rows
    steps = 4
    part = depth // steps
    return pl.pallas_call(
        turn_kernel,
        grid=(steps,),
        in_specs=[SMEM_SPEC] + [pl.BlockSpec((x.shape[0], part), lambda i: (0, i)) for x in (own, *near, *far)],
        out_specs=pl.BlockSpec((part, every), lambda i: (i, 0)),
        out_shape=pltpu.HBM((depth, every), BF16),
        scratch_shapes=[pltpu.VMEM((every, part), BF16)],
        compiler_params=params(12),
        cost_estimate=COST,
        name="turned_rows",
    )(place, own, *near, *far)


def student_logits(place, after, own, near, far, head):
    rows, depth = own.shape
    n_tok = len(near) + 1
    every = n_tok * rows
    cols = head.shape[1]
    tile = 256
    whole = lambda shape: pl.BlockSpec(shape, lambda i: (0, 0))
    return pl.pallas_call(
        logits_kernel,
        grid=(cols // tile,),
        in_specs=[SMEM_SPEC, pl.BlockSpec(memory_space=pl.ANY), whole(own.shape)]
        + [whole(x.shape) for x in near + far]
        + [pl.BlockSpec((depth, tile), lambda i: (0, i))],
        out_specs=pl.BlockSpec((n_tok, rows, tile), lambda i: (0, 0, i)),
        out_shape=pltpu.HBM((n_tok, rows, cols), F32),
        scratch_shapes=[pltpu.VMEM((every, depth), BF16)],
        compiler_params=params(32),
        cost_estimate=COST,
        name="student_logits",
    )(place, after, own, *near, *far, in_hbm(head))


def student_kernel(base_ref, labels_ref, mass_ref, logits_ref, stat_ref):
    n_tok, rows, cols = logits_ref.shape
    lane = lax.broadcasted_iota(jnp.int32, (rows, LANES), 1)
    label = labels_ref[...]
    top = jnp.full((rows, LANES), -jnp.inf, F32)
    hit = jnp.zeros((rows, LANES), F32)
    for t in range(n_tok):
        for b in range(0, cols, LANES):
            block = logits_ref[t, :, b : b + LANES]
            top = jnp.maximum(top, block)
            hit = hit + jnp.where(lane == label - (base_ref[t] + b), block, 0.0)
    top = jnp.max(top, axis=1, keepdims=True)
    total = jnp.zeros((rows, LANES), F32)
    for t in range(n_tok):
        for b in range(0, cols, LANES):
            total = total + jnp.exp(logits_ref[t, :, b : b + LANES] - top)
    total = jnp.sum(total, axis=1, keepdims=True)
    hit = jnp.sum(hit, axis=1, keepdims=True)
    stat_ref[...] = rows_from_columns([jnp.zeros_like(hit), top, total, hit])
    stat_ref[0:1, :] = mass_ref[0:1, :]


def student_stats(base, label_column, mass, logits):
    return pl.pallas_call(
        student_kernel,
        in_specs=[SMEM_SPEC] + [VMEM_SPEC] * 3,
        out_specs=VMEM_SPEC,
        out_shape=jax.ShapeDtypeStruct(mass.shape, F32),
        compiler_params=params(10),
        cost_estimate=COST,
        name="student_stats",
    )(base, label_column, mass, logits)


def merge_kernel(*refs):
    stats, out = refs[:-1], refs[-1]
    parts = split_rows(stats)
    mass = tree(jnp.add, [r[0] for r in parts])
    top, total = total_at(parts, 1, 2)
    hit = tree(jnp.add, [r[3] for r in parts])
    out[...] = jnp.concatenate([mass, top, total, hit, jnp.zeros((4, top.shape[1]), F32)], axis=0)


def merge_stats(stats):
    return pl.pallas_call(
        merge_kernel,
        in_specs=[VMEM_SPEC] * len(stats),
        out_specs=VMEM_SPEC,
        out_shape=jax.ShapeDtypeStruct(stats[0].shape, F32),
        compiler_params=params(1),
        cost_estimate=COST,
        name="merge_stats",
    )(*stats)


def totals_kernel(*refs):
    stats, (columns, loss_ref) = refs[:-2], refs[-2:]
    parts = split_rows(stats)
    mass = tree(jnp.add, [r[0] for r in parts])
    top, total = total_at(parts, 1, 2)
    log_total = top + jnp.log(total)
    label_logit = tree(jnp.add, [r[3] for r in parts])
    columns[...] = columns_from_rows([mass + 1.0, log_total])
    loss_ref[...] = mass * log_total + log_total - label_logit


def token_totals(stats):
    rows = stats[0].shape[1]
    return pl.pallas_call(
        totals_kernel,
        in_specs=[VMEM_SPEC] * len(stats),
        out_specs=[VMEM_SPEC] * 2,
        out_shape=[jax.ShapeDtypeStruct((rows, LANES), F32), jax.ShapeDtypeStruct((1, rows), F32)],
        compiler_params=params(2),
        cost_estimate=COST,
        name="token_totals",
    )(*stats)


def grad_kernel(tok_ref, base_ref, labels_ref, columns, *refs, n_sums, groups):
    sums = refs[:n_sums]
    logits_ref, *grads, inner_ref, inner = refs[n_sums:]
    step = pl.program_id(0)
    _, rows, cols = logits_ref.shape

    @pl.when(step == 0)
    def _():
        inner[...] = jnp.zeros_like(inner)

    lane = lax.broadcasted_iota(jnp.int32, (rows, LANES), 1)
    lift, log_total = columns[:, 0:1], columns[:, 1:2]
    label = labels_ref[...] - base_ref[token_group(step, tok_ref, groups)]
    for r in range(len(grads)):

        @pl.when(step == r)
        def _():
            running = inner[...]
            for b in range(cols // LANES):
                place = slice(b * LANES, (b + 1) * LANES)
                target = functools.reduce(
                    jnp.add, [ref[z, b].astype(F32) for ref in sums for z in range(ref.shape[0])]
                )
                score = logits_ref[0, :, place]
                running = running + target * score
                hit = jnp.where(lane == label - b * LANES, 1.0, 0.0)
                grads[r][:, place] = (lift * jnp.exp(score - log_total) - target - hit).astype(BF16)
            inner[...] = running

    @pl.when(step == pl.num_programs(0) - 1)
    def _():
        inner_ref[...] = rows_from_columns([jnp.sum(inner[...], axis=1, keepdims=True)])[0:1, :]


def token_group(step, tok_ref, groups):
    r = groups[0]
    for i in range(1, len(groups)):
        r = jnp.where(step == i, groups[i], r)
    return tok_ref[0] ^ r


def grad_logits(tok, base, label_column, columns, sums, logits, groups):
    n_tok, rows, cols = logits.shape
    per = cols // LANES
    whole = lambda shape: pl.BlockSpec(shape, lambda t, tok_ref: (0,) * len(shape))
    group = lambda t, tok_ref: token_group(t, tok_ref, groups)
    n_out = len(groups)
    return pl.pallas_call(
        functools.partial(grad_kernel, n_sums=len(sums), groups=groups),
        grid_spec=pltpu.PrefetchScalarGridSpec(
            num_scalar_prefetch=1,
            grid=(n_out,),
            in_specs=[SMEM_SPEC, whole(label_column.shape), whole(columns.shape)]
            + [pl.BlockSpec((s.shape[0], per, rows, LANES), lambda t, r: (0, group(t, r), 0, 0)) for s in sums]
            + [pl.BlockSpec((1, rows, cols), lambda t, r: (group(t, r), 0, 0))],
            out_specs=[whole((rows, cols))] * n_out + [whole((1, rows))],
            scratch_shapes=[pltpu.VMEM((rows, LANES), F32)],
        ),
        out_shape=[pltpu.HBM((rows, cols), BF16)] * n_out + [jax.ShapeDtypeStruct((1, rows), F32)],
        compiler_params=params(14),
        cost_estimate=COST,
        name="grad_logits",
    )(tok, base, label_column, columns, *sums, logits)


def stack_pieces(pieces, b_ref):
    rows = pieces[0].shape[0]

    @pl.when(pl.program_id(0) == 0)
    def _():
        for r, piece in enumerate(pieces):
            b_ref[r * rows : (r + 1) * rows, :] = piece[...]


def product_part(a_ref, b_ref, first):
    tile = a_ref.shape[0] // pl.num_programs(0)
    rows = pl.ds(pl.multiple_of(pl.program_id(0) * tile, tile), tile)
    return rows, jnp.dot(a_ref[rows, first : first + b_ref.shape[0]], b_ref[...], preferred_element_type=F32)


def first_product_kernel(a_ref, *refs):
    pieces, (acc_ref, end_ref, b_ref) = refs[:-3], refs[-3:]
    stack_pieces(pieces, b_ref)
    rows, part = product_part(a_ref, b_ref, 0)
    acc_ref[rows, :] = part
    end_ref[...] = jnp.zeros_like(end_ref)


def last_product_kernel(a_ref, acc_ref, *refs):
    pieces, (o_ref, end_ref, b_ref) = refs[:-3], refs[-3:]
    stack_pieces(pieces, b_ref)
    rows, part = product_part(a_ref, b_ref, a_ref.shape[1] - b_ref.shape[0])
    o_ref[...] = (acc_ref[rows, :] + part).astype(o_ref.dtype)
    end_ref[...] = jnp.zeros_like(end_ref)


def first_product(a, pieces):
    rows, n = pieces[0].shape
    return pl.pallas_call(
        first_product_kernel,
        grid=(4,),
        in_specs=[VMEM_SPEC] + [pl.BlockSpec((rows, n), lambda i: (0, 0))] * len(pieces),
        out_specs=[VMEM_SPEC, pl.BlockSpec((1, rows), lambda i: (0, 0))],
        out_shape=[pltpu.VMEM((a.shape[0], n), F32), jax.ShapeDtypeStruct((1, rows), F32)],
        scratch_shapes=[pltpu.VMEM((len(pieces) * rows, n), BF16)],
        compiler_params=params(16),
        cost_estimate=COST,
        name="first_product",
    )(in_vmem(a), in_hbm(pieces[0]), *pieces[1:])


def last_product(a, acc, pieces):
    m = a.shape[0]
    rows, n = pieces[0].shape
    steps = 4
    return pl.pallas_call(
        last_product_kernel,
        grid=(steps,),
        in_specs=[VMEM_SPEC] * 2 + [pl.BlockSpec((rows, n), lambda i: (0, 0))] * len(pieces),
        out_specs=[pl.BlockSpec((m // steps, n), lambda i: (i, 0)), pl.BlockSpec((1, rows), lambda i: (0, 0))],
        out_shape=[jax.ShapeDtypeStruct((m, n), BF16), jax.ShapeDtypeStruct((1, rows), F32)],
        scratch_shapes=[pltpu.VMEM((len(pieces) * rows, n), BF16)],
        compiler_params=params(20),
        cost_estimate=COST,
        name="last_product",
    )(in_vmem(a), in_vmem(acc), *pieces)


def swap(x, axis, mask):
    return lax.ppermute(x, axis, [(i, i ^ mask) for i in range(lax.axis_size(axis))])


def gather_chips(x):
    n = lax.axis_size("vocab")
    if n > 8:
        lines = [[2 * z + c for z in range(n // 2)] for c in range(2)]
        everything = lax.all_gather(x, "vocab", axis=0, axis_index_groups=lines)
        return [everything[z] for z in range(n // 2)]
    return [x] + [swap(x, "vocab", r) for r in range(2, n, 2)]


def butterfly(tile):
    n = lax.axis_size("vocab")
    tiles, masks = [tile], [1 << k for k in range(1, n.bit_length() - 1)] + [1]
    for mask in masks:
        tile = merge_stats(tiles) if len(tiles) > 1 else tile
        tiles = [tile, swap(tile, "vocab", mask)]
    return tiles


def exchange_tok(x):
    return lax.all_to_all(x, "tok", split_axis=0, concat_axis=0, tiled=True)


def plus(a, b):
    return (a.astype(F32) + b.astype(F32)).astype(BF16)


def exchange_tok(x):
    return lax.all_to_all(x, "tok", split_axis=0, concat_axis=0, tiled=True)


def send(x, hops):
    return lax.ppermute(x, "vocab", [(2 * a + c, 2 * b + c) for a, b in hops for c in range(2)])


def local(teacher_logits, hidden, new_head, labels, map_target, map_weight):
    rows = teacher_logits.shape[0]
    block = map_weight.shape[2]
    n_tok = lax.axis_size("tok")
    n_vocab = lax.axis_size("vocab")
    n_z = n_vocab // 2
    new_cols = new_head.shape[1]
    per = new_cols // block
    tok = lax.axis_index("tok")
    vocab = lax.axis_index("vocab")
    spot = jnp.stack([vocab % 2, vocab // 2]).astype(jnp.int32)
    slots = n_tok * per
    in_line = n_z == 4

    owner = map_target // per
    owner_vocab = owner % n_vocab
    owner_z = owner_vocab // 2
    if in_line:
        z = vocab // 2
        outer = (owner_z == 0) | (owner_z == n_z - 1)
        near_place = jnp.where(owner_z == z, 3, 2)
        place = jnp.where((owner_z // 2) == (z // 2), near_place, jnp.where(outer, 0, 1))
    else:
        place = owner_z
    slot = (owner // n_vocab) * per + map_target % per
    code = (((owner_vocab % 2) * n_z + place) * SLOT_BASE + slot).astype(jnp.int32).reshape(-1)

    peer_logits = swap(teacher_logits, "vocab", 1)
    peer_code = swap(code, "vocab", 1)
    peer_weight = swap(map_weight, "vocab", 1)
    totals = butterfly(teacher_stats(teacher_logits))
    lists = plan(code, peer_code, 2 * n_z)
    probs = teacher_probs(teacher_logits, peer_logits, totals)

    half = lax.dynamic_slice_in_dim(hidden, spot[0] * (rows // 2), rows // 2)
    if in_line:
        inward, across, beyond = [(0, 1), (3, 2)], [(1, 2), (2, 1)], [(1, 3), (2, 0)]
        far_outer, mass_a = chip_sums(spot, lists, probs, map_weight, peer_weight, 0, 1, 1, slots)
        first = send(far_outer, inward)
        half, probs, mass_a = lax.optimization_barrier((half, probs, mass_a))
        near = [swap(half, "tok", r) for r in range(1, n_tok)]
        far_inner, beside, own, mass_b = chip_sums(
            spot, lists, probs, map_weight, peer_weight, 1, 3, 1, slots
        )
        second = send(far_inner, inward)
        first, mass = lax.optimization_barrier((first, mass_a + mass_b))
        merged = plus(far_outer, first)
        arrived = send(merged, beyond)
        *near, merged = lax.optimization_barrier((*near, merged))
    else:
        sums, mass = chip_sums(spot, lists, probs, map_weight, peer_weight, 0, 1, n_z, slots)
        lines = [[2 * z + c for z in range(n_z)] for c in range(2)]
        sums = lax.all_to_all(
            sums.reshape(n_z, slots, rows, block),
            "vocab",
            split_axis=0,
            concat_axis=0,
            axis_index_groups=lines,
            tiled=True,
        )
        sums = [sums]
        near = [swap(half, "tok", r) for r in range(1, n_tok)]

    far = [swap(x, "vocab", 1) for x in near]
    where = jnp.stack([vocab % 2, tok]).astype(jnp.int32)
    logits = student_logits(where, mass, hidden, near, far, new_head)
    base = (jnp.arange(n_tok, dtype=jnp.int32) * n_vocab + vocab) * new_cols
    label_column = lax.dynamic_slice_in_dim(labels, tok * rows, rows).reshape(rows, 1)
    scores = exchange_tok(logits)
    if in_line:
        second, arrived, logits = lax.optimization_barrier((second, arrived, logits))
        merged_inner = plus(far_inner, second)
        crossed = send(merged_inner, across)
        waited, merged_inner = lax.optimization_barrier((beside, merged_inner))
        third = swap(waited, "vocab", 2)
        where, merged_inner = lax.optimization_barrier((where, merged_inner))
        turned = turned_rows(where, hidden, near[-1:] + near[:-1], far[-1:] + far[:-1])
        scores, merged_inner, turned = lax.optimization_barrier((scores, merged_inner, turned))
        sums = [x[None] for x in (own, third, crossed, arrived)]
    else:
        turned = turned_rows(where, hidden, near[-1:] + near[:-1], far[-1:] + far[:-1])
    student = student_stats(base, label_column, mass, scores)
    student = merge_stats([student, swap(student, "vocab", 1)])
    stats = gather_chips(student)

    group = tok.astype(jnp.int32).reshape(1)
    columns, base_loss = token_totals(stats)
    grad_args = (group, base, label_column, columns, sums, scores)
    far_group, inner = grad_logits(*grad_args, (3,))
    far_group = swap(far_group, "tok", 3)
    beside_x, beside_y, here, inner_b = grad_logits(*grad_args, (1, 2, 0))
    beside_x, beside_y = swap(beside_x, "tok", 1), swap(beside_y, "tok", 2)
    inner = inner + inner_b
    acc, middle = first_product(turned, [here, far_group])
    head_grad, end = last_product(turned, acc, [beside_x, beside_y])
    mask = 1
    while mask < n_vocab:
        inner = inner + swap(inner, "vocab", mask)
        if mask == 2:
            inner = inner + middle
        mask *= 2
    return ((base_loss - inner + end).reshape(rows), head_grad)


def solution(mesh):
    return jax.shard_map(
        local,
        mesh=mesh,
        in_specs=(
            P("tok", "vocab"),
            P("tok", None),
            P(None, ("tok", "vocab")),
            P(),
            P("vocab", None),
            P("vocab", None, None, None),
        ),
        out_specs=(P("tok"), P(None, ("tok", "vocab"))),
        check_vma=False,
    )
```

```python
import functools

import jax
import jax.numpy as jnp
from jax import lax
from jax.experimental import pallas as pl
from jax.experimental.pallas import tpu as pltpu
from jax.sharding import PartitionSpec as P

F32 = jnp.float32
BF16 = jnp.bfloat16
LANES = 128
BATCH = 8
COST = pl.CostEstimate(flops=1024, bytes_accessed=1024, transcendentals=0)
SLOT_BITS = 10
SLOT_BASE = 1 << SLOT_BITS
SMEM_SPEC = pl.BlockSpec(memory_space=pltpu.SMEM)
VMEM_SPEC = pl.BlockSpec(memory_space=pltpu.VMEM)


def params(mebibytes):
    return pltpu.CompilerParams(vmem_limit_bytes=mebibytes * 1024 * 1024)


def in_hbm(x):
    return pltpu.with_memory_space_constraint(x, pltpu.HBM)


def in_vmem(x):
    return pltpu.with_memory_space_constraint(x, pltpu.VMEM)


def tree(op, items):
    while len(items) > 1:
        items = [op(items[i], items[i + 1]) if i + 1 < len(items) else items[i] for i in range(0, len(items), 2)]
    return items[0]


def total_at(rows_of, top_row, total_row):
    top = tree(jnp.maximum, [r[top_row] for r in rows_of])
    total = tree(jnp.add, [r[total_row] * jnp.exp(r[top_row] - top) for r in rows_of])
    return top, total


def split_rows(refs):
    return [[ref[k : k + 1, :] for k in range(8)] for ref in refs]


def rows_from_columns(columns):
    n = columns[0].shape[0]
    lane = lax.broadcasted_iota(jnp.int32, (n, LANES), 1)
    tile = jnp.zeros((n, LANES), F32)
    for place, column in enumerate(columns):
        tile = jnp.where(lane == place, column, tile)
    return tile.T[0:8, :]


def columns_from_rows(rows):
    n = rows[0].shape[1]
    return jnp.concatenate(rows + [jnp.zeros((LANES - len(rows), n), F32)], axis=0).T


def teacher_kernel(x_ref, stat_ref):
    rows, cols = x_ref.shape
    places = range(0, cols, LANES)
    read = lambda place: x_ref[:, place : place + LANES].astype(F32)
    top = jnp.full((rows, LANES), -jnp.inf, F32)
    for place in places:
        top = jnp.maximum(top, read(place))
    top = jnp.max(top, axis=1, keepdims=True)
    total = jnp.zeros((rows, LANES), F32)
    for place in places:
        total = total + jnp.exp(read(place) - top)
    stat_ref[...] = rows_from_columns([jnp.zeros_like(top), top, jnp.sum(total, axis=1, keepdims=True)])


def teacher_stats(x):
    return pl.pallas_call(
        teacher_kernel,
        in_specs=[VMEM_SPEC],
        out_specs=VMEM_SPEC,
        out_shape=jax.ShapeDtypeStruct((8, x.shape[0]), F32),
        compiler_params=params(6),
        cost_estimate=COST,
        name="teacher_stats",
    )(x)


def divide(x, n):
    return lax.shift_right_logical(x, n.bit_length() - 1) if n & (n - 1) == 0 else x // n


def plan_kernel(own_ref, peer_ref, list_ref):
    lists, room = list_ref.shape
    codes = [own_ref[...], peer_ref[...]]
    n = codes[0].shape[1]
    rows = [lax.shift_right_logical(code, SLOT_BITS) for code in codes]
    across = [jnp.broadcast_to(row.astype(F32), (n, n)) for row in rows]
    down = [x.T for x in across]
    before = lax.broadcasted_iota(jnp.int32, (n, n), 1) < lax.broadcasted_iota(jnp.int32, (n, n), 0)
    count = lambda mask: jnp.sum(jnp.where(mask, 1.0, 0.0), axis=1, keepdims=True)
    ranks = [count((down[0] == across[0]) & before)]
    ranks.append(count((down[1] == across[1]) & before) + count(down[1] == across[0]))
    place = lax.broadcasted_iota(jnp.int32, (n, room), 1).astype(F32)
    entry = lax.broadcasted_iota(jnp.int32, (lists, n), 1).astype(F32)
    entries = slots = jnp.zeros((lists, room), F32)
    counts = jnp.zeros((lists, 1), F32)
    for side, code in enumerate(codes):
        member = jnp.broadcast_to(rows[side], (lists, n)) == lax.broadcasted_iota(jnp.int32, (lists, n), 0)
        slot = jnp.broadcast_to(code & (SLOT_BASE - 1), (lists, n)).astype(F32)
        here = jnp.where(place == ranks[side], 1.0, 0.0).astype(BF16)
        pick = lambda x: jnp.dot(jnp.where(member, x, 0.0).astype(BF16), here, preferred_element_type=F32)
        entries = entries + pick(entry + side * n)
        slots = slots + pick(slot)
        counts = counts + count(member)
    column = lax.broadcasted_iota(jnp.int32, (lists, room), 1)
    counts = counts.astype(jnp.int32)
    items = entries.astype(jnp.int32) * SLOT_BASE + slots.astype(jnp.int32)
    items = jnp.where(column < counts, items, SLOT_BASE - 1)
    list_ref[...] = jnp.where(column == room - 1, counts, items)


def plan(own_code, peer_code, lists):
    n = own_code.size
    room = 3 * LANES
    return pl.pallas_call(
        plan_kernel,
        in_specs=[VMEM_SPEC] * 2,
        out_specs=VMEM_SPEC,
        out_shape=jax.ShapeDtypeStruct((lists, room), jnp.int32),
        compiler_params=params(4),
        cost_estimate=COST,
        name="entry_lists",
    )(own_code.reshape(1, n), peer_code.reshape(1, n))


def probs_kernel(x_own, x_peer, *refs):
    stats, (probs, columns) = refs[:-2], refs[-2:]

    @pl.when(pl.program_id(0) == 0)
    def _():
        top, total = total_at(split_rows(stats), 1, 2)
        columns[...] = columns_from_rows([top, 1.0 / total])

    top, scale = columns[:, 0:1], columns[:, 1:2]
    for side, x in enumerate((x_own, x_peer)):
        for j in range(x.shape[1] // LANES):
            raised = jnp.exp(x[:, j * LANES : (j + 1) * LANES].astype(F32) - top)
            probs[side, j] = (raised * scale).astype(BF16)


def sums_kernel(spot_ref, list_ref, probs, w_own, w_peer, *refs, first, fan, pieces):
    outs, mass_ref, acc = refs[:-2], refs[-2], refs[-1]
    step = pl.program_id(0)
    slots, rows, _ = outs[0].shape
    side = w_own.shape[0] * fan
    mass = jnp.zeros((rows, LANES), F32)
    for k, out in enumerate(outs):
        piece = spot_ref[0] * pieces + first + k + step
        acc[...] = jnp.zeros_like(acc)

        def add(i, carry):
            parts = []
            for u in range(BATCH):
                item = list_ref[piece, i * BATCH + u]
                slot = item & (SLOT_BASE - 1)
                entry = lax.shift_right_logical(item, SLOT_BITS)
                weight = jnp.where(entry < side, 0, 1)
                parts.append((entry, slot, weight))
            for entry, slot, peer in parts:
                j = divide(entry, fan)
                f = entry - j * fan
                local_j = j - peer * (side // fan)
                weight = jnp.where(peer == 1, w_peer[local_j, f], w_own[local_j, f])
                part = jnp.dot(probs[j], weight, preferred_element_type=F32)
                acc[jnp.minimum(slot, slots)] += part.astype(BF16).astype(F32)
            return carry

        lax.fori_loop(0, divide(list_ref[piece, list_ref.shape[1] - 1] + BATCH - 1, BATCH), add, 0)

        def drain(i, mass):
            block = acc[i]
            out[i] = block.astype(BF16)
            return mass + block

        mass = lax.fori_loop(0, slots, drain, mass, unroll=4)
    part = rows_from_columns([jnp.sum(mass, axis=1, keepdims=True)])

    @pl.when(step == 0)
    def _():
        mass_ref[...] = part

    @pl.when(step > 0)
    def _():
        mass_ref[...] += part


def teacher_probs(x_own, x_peer, stats):
    rows, cols = x_own.shape
    steps = 2
    blocks = cols // LANES
    part = pl.BlockSpec((rows, cols // steps), lambda i: (0, i))
    probs = pl.pallas_call(
        probs_kernel,
        grid=(steps,),
        in_specs=[part, part] + [pl.BlockSpec(s.shape, lambda i: (0, 0)) for s in stats],
        out_specs=pl.BlockSpec((2, blocks // steps, rows, LANES), lambda i: (0, i, 0, 0)),
        out_shape=jax.ShapeDtypeStruct((2, blocks, rows, LANES), BF16),
        scratch_shapes=[pltpu.VMEM((rows, LANES), F32)],
        compiler_params=params(8),
        cost_estimate=COST,
        name="teacher_probs",
    )(in_hbm(x_own), x_peer, *stats)
    return probs.reshape(2 * blocks, rows, LANES)


def chip_sums(spot, lists, probs, w_own, w_peer, first, n_out, steps, slots):
    rows = probs.shape[1]
    fan = w_own.shape[1]
    whole = lambda shape: pl.BlockSpec(shape, lambda s: (0,) * len(shape))
    out = pltpu.HBM((steps * slots, rows, LANES), BF16)
    return pl.pallas_call(
        functools.partial(sums_kernel, first=first, fan=fan, pieces=lists.shape[0] // 2),
        grid=(steps,),
        in_specs=[SMEM_SPEC] * 2 + [VMEM_SPEC] * 3,
        out_specs=[pl.BlockSpec((slots, rows, LANES), lambda s: (s, 0, 0))] * n_out + [whole((8, rows))],
        out_shape=[out] * n_out + [jax.ShapeDtypeStruct((8, rows), F32)],
        scratch_shapes=[pltpu.VMEM((slots + 1, rows, LANES), F32)],
        compiler_params=params(24),
        cost_estimate=COST,
        name="chip_sums",
    )(spot, lists, probs, w_own, w_peer)


def stack_rows(place_ref, own_ref, near, far, everyone):
    rows = own_ref.shape[0]
    half = rows // 2
    core = place_ref[0]
    everyone[0:rows, :] = own_ref[...]
    for r in range(len(near)):
        start = (r + 1) * rows
        everyone[pl.ds(pl.multiple_of(start + core * half, half), half), :] = near[r][...]
        everyone[pl.ds(pl.multiple_of(start + (1 - core) * half, half), half), :] = far[r][...]


def logits_kernel(place_ref, after_ref, own_ref, *refs):
    n_other = (len(refs) - 3) // 2
    near, far, (head_ref, out_ref, everyone) = refs[:n_other], refs[n_other : 2 * n_other], refs[-3:]
    rows = own_ref.shape[0]
    del after_ref

    @pl.when(pl.program_id(0) == 0)
    def _():
        stack_rows(place_ref, own_ref, near, far, everyone)

    result = jnp.dot(everyone[...], head_ref[...], preferred_element_type=F32)
    for r in range(n_other + 1):
        out_ref[place_ref[1] ^ r] = result[r * rows : (r + 1) * rows, :]


def turn_kernel(place_ref, own_ref, *refs):
    n_other = (len(refs) - 2) // 2
    near, far, (turned_ref, everyone) = refs[:n_other], refs[n_other : 2 * n_other], refs[-2:]
    stack_rows(place_ref, own_ref, near, far, everyone)
    turned_ref[...] = everyone[...].T


def turned_rows(place, own, near, far):
    rows, depth = own.shape
    every = (len(near) + 1) * rows
    steps = 4
    part = depth // steps
    return pl.pallas_call(
        turn_kernel,
        grid=(steps,),
        in_specs=[SMEM_SPEC] + [pl.BlockSpec((x.shape[0], part), lambda i: (0, i)) for x in (own, *near, *far)],
        out_specs=pl.BlockSpec((part, every), lambda i: (i, 0)),
        out_shape=pltpu.HBM((depth, every), BF16),
        scratch_shapes=[pltpu.VMEM((every, part), BF16)],
        compiler_params=params(12),
        cost_estimate=COST,
        name="turned_rows",
    )(place, own, *near, *far)


def student_logits(place, after, own, near, far, head):
    rows, depth = own.shape
    n_tok = len(near) + 1
    every = n_tok * rows
    cols = head.shape[1]
    tile = 256
    whole = lambda shape: pl.BlockSpec(shape, lambda i: (0, 0))
    return pl.pallas_call(
        logits_kernel,
        grid=(cols // tile,),
        in_specs=[SMEM_SPEC, pl.BlockSpec(memory_space=pl.ANY), whole(own.shape)]
        + [whole(x.shape) for x in near + far]
        + [pl.BlockSpec((depth, tile), lambda i: (0, i))],
        out_specs=pl.BlockSpec((n_tok, rows, tile), lambda i: (0, 0, i)),
        out_shape=pltpu.HBM((n_tok, rows, cols), F32),
        scratch_shapes=[pltpu.VMEM((every, depth), BF16)],
        compiler_params=params(32),
        cost_estimate=COST,
        name="student_logits",
    )(place, after, own, *near, *far, in_hbm(head))


def student_kernel(base_ref, labels_ref, mass_ref, logits_ref, stat_ref):
    n_tok, rows, cols = logits_ref.shape
    lane = lax.broadcasted_iota(jnp.int32, (rows, LANES), 1)
    label = labels_ref[...]
    top = jnp.full((rows, LANES), -jnp.inf, F32)
    hit = jnp.zeros((rows, LANES), F32)
    for t in range(n_tok):
        for b in range(0, cols, LANES):
            block = logits_ref[t, :, b : b + LANES]
            top = jnp.maximum(top, block)
            hit = hit + jnp.where(lane == label - (base_ref[t] + b), block, 0.0)
    top = jnp.max(top, axis=1, keepdims=True)
    total = jnp.zeros((rows, LANES), F32)
    for t in range(n_tok):
        for b in range(0, cols, LANES):
            total = total + jnp.exp(logits_ref[t, :, b : b + LANES] - top)
    total = jnp.sum(total, axis=1, keepdims=True)
    hit = jnp.sum(hit, axis=1, keepdims=True)
    stat_ref[...] = rows_from_columns([jnp.zeros_like(hit), top, total, hit])
    stat_ref[0:1, :] = mass_ref[0:1, :]


def student_stats(base, label_column, mass, logits):
    return pl.pallas_call(
        student_kernel,
        in_specs=[SMEM_SPEC] + [VMEM_SPEC] * 3,
        out_specs=VMEM_SPEC,
        out_shape=jax.ShapeDtypeStruct(mass.shape, F32),
        compiler_params=params(10),
        cost_estimate=COST,
        name="student_stats",
    )(base, label_column, mass, logits)


def merge_kernel(*refs):
    stats, out = refs[:-1], refs[-1]
    parts = split_rows(stats)
    mass = tree(jnp.add, [r[0] for r in parts])
    top, total = total_at(parts, 1, 2)
    hit = tree(jnp.add, [r[3] for r in parts])
    out[...] = jnp.concatenate([mass, top, total, hit, jnp.zeros((4, top.shape[1]), F32)], axis=0)


def merge_stats(stats):
    return pl.pallas_call(
        merge_kernel,
        in_specs=[VMEM_SPEC] * len(stats),
        out_specs=VMEM_SPEC,
        out_shape=jax.ShapeDtypeStruct(stats[0].shape, F32),
        compiler_params=params(1),
        cost_estimate=COST,
        name="merge_stats",
    )(*stats)


def totals_kernel(*refs):
    stats, (columns, loss_ref) = refs[:-2], refs[-2:]
    parts = split_rows(stats)
    mass = tree(jnp.add, [r[0] for r in parts])
    top, total = total_at(parts, 1, 2)
    log_total = top + jnp.log(total)
    label_logit = tree(jnp.add, [r[3] for r in parts])
    columns[...] = columns_from_rows([mass + 1.0, log_total])
    loss_ref[...] = mass * log_total + log_total - label_logit


def token_totals(stats):
    rows = stats[0].shape[1]
    return pl.pallas_call(
        totals_kernel,
        in_specs=[VMEM_SPEC] * len(stats),
        out_specs=[VMEM_SPEC] * 2,
        out_shape=[jax.ShapeDtypeStruct((rows, LANES), F32), jax.ShapeDtypeStruct((1, rows), F32)],
        compiler_params=params(2),
        cost_estimate=COST,
        name="token_totals",
    )(*stats)


def grad_kernel(tok_ref, base_ref, labels_ref, columns, *refs, n_sums, groups):
    sums = refs[:n_sums]
    logits_ref, *grads, inner_ref, inner = refs[n_sums:]
    step = pl.program_id(0)
    _, rows, cols = logits_ref.shape

    @pl.when(step == 0)
    def _():
        inner[...] = jnp.zeros_like(inner)

    lane = lax.broadcasted_iota(jnp.int32, (rows, LANES), 1)
    lift, log_total = columns[:, 0:1], columns[:, 1:2]
    label = labels_ref[...] - base_ref[token_group(step, tok_ref, groups)]
    for r in range(len(grads)):

        @pl.when(step == r)
        def _():
            running = inner[...]
            for b in range(cols // LANES):
                place = slice(b * LANES, (b + 1) * LANES)
                target = functools.reduce(
                    jnp.add, [ref[z, b].astype(F32) for ref in sums for z in range(ref.shape[0])]
                )
                score = logits_ref[0, :, place]
                running = running + target * score
                hit = jnp.where(lane == label - b * LANES, 1.0, 0.0)
                grads[r][:, place] = (lift * jnp.exp(score - log_total) - target - hit).astype(BF16)
            inner[...] = running

    @pl.when(step == pl.num_programs(0) - 1)
    def _():
        inner_ref[...] = rows_from_columns([jnp.sum(inner[...], axis=1, keepdims=True)])[0:1, :]


def token_group(step, tok_ref, groups):
    r = groups[0]
    for i in range(1, len(groups)):
        r = jnp.where(step == i, groups[i], r)
    return tok_ref[0] ^ r


def grad_logits(tok, base, label_column, columns, sums, logits, groups):
    n_tok, rows, cols = logits.shape
    per = cols // LANES
    whole = lambda shape: pl.BlockSpec(shape, lambda t, tok_ref: (0,) * len(shape))
    group = lambda t, tok_ref: token_group(t, tok_ref, groups)
    n_out = len(groups)
    return pl.pallas_call(
        functools.partial(grad_kernel, n_sums=len(sums), groups=groups),
        grid_spec=pltpu.PrefetchScalarGridSpec(
            num_scalar_prefetch=1,
            grid=(n_out,),
            in_specs=[SMEM_SPEC, whole(label_column.shape), whole(columns.shape)]
            + [pl.BlockSpec((s.shape[0], per, rows, LANES), lambda t, r: (0, group(t, r), 0, 0)) for s in sums]
            + [pl.BlockSpec((1, rows, cols), lambda t, r: (group(t, r), 0, 0))],
            out_specs=[whole((rows, cols))] * n_out + [whole((1, rows))],
            scratch_shapes=[pltpu.VMEM((rows, LANES), F32)],
        ),
        out_shape=[pltpu.HBM((rows, cols), BF16)] * n_out + [jax.ShapeDtypeStruct((1, rows), F32)],
        compiler_params=params(14),
        cost_estimate=COST,
        name="grad_logits",
    )(tok, base, label_column, columns, *sums, logits)


def stack_pieces(pieces, b_ref):
    rows = pieces[0].shape[0]

    @pl.when(pl.program_id(0) == 0)
    def _():
        for r, piece in enumerate(pieces):
            b_ref[r * rows : (r + 1) * rows, :] = piece[...]


def product_part(a_ref, b_ref, first):
    tile = a_ref.shape[0] // pl.num_programs(0)
    rows = pl.ds(pl.multiple_of(pl.program_id(0) * tile, tile), tile)
    return rows, jnp.dot(a_ref[rows, first : first + b_ref.shape[0]], b_ref[...], preferred_element_type=F32)


def first_product_kernel(a_ref, *refs):
    pieces, (acc_ref, end_ref, b_ref) = refs[:-3], refs[-3:]
    stack_pieces(pieces, b_ref)
    rows, part = product_part(a_ref, b_ref, 0)
    acc_ref[rows, :] = part
    end_ref[...] = jnp.zeros_like(end_ref)


def last_product_kernel(a_ref, acc_ref, *refs):
    pieces, (o_ref, end_ref, b_ref) = refs[:-3], refs[-3:]
    stack_pieces(pieces, b_ref)
    rows, part = product_part(a_ref, b_ref, a_ref.shape[1] - b_ref.shape[0])
    o_ref[...] = (acc_ref[rows, :] + part).astype(o_ref.dtype)
    end_ref[...] = jnp.zeros_like(end_ref)


def first_product(a, pieces):
    rows, n = pieces[0].shape
    return pl.pallas_call(
        first_product_kernel,
        grid=(4,),
        in_specs=[VMEM_SPEC] + [pl.BlockSpec((rows, n), lambda i: (0, 0))] * len(pieces),
        out_specs=[VMEM_SPEC, pl.BlockSpec((1, rows), lambda i: (0, 0))],
        out_shape=[pltpu.VMEM((a.shape[0], n), F32), jax.ShapeDtypeStruct((1, rows), F32)],
        scratch_shapes=[pltpu.VMEM((len(pieces) * rows, n), BF16)],
        compiler_params=params(16),
        cost_estimate=COST,
        name="first_product",
    )(in_vmem(a), in_hbm(pieces[0]), *pieces[1:])


def last_product(a, acc, pieces):
    m = a.shape[0]
    rows, n = pieces[0].shape
    steps = 4
    return pl.pallas_call(
        last_product_kernel,
        grid=(steps,),
        in_specs=[VMEM_SPEC] * 2 + [pl.BlockSpec((rows, n), lambda i: (0, 0))] * len(pieces),
        out_specs=[pl.BlockSpec((m // steps, n), lambda i: (i, 0)), pl.BlockSpec((1, rows), lambda i: (0, 0))],
        out_shape=[jax.ShapeDtypeStruct((m, n), BF16), jax.ShapeDtypeStruct((1, rows), F32)],
        scratch_shapes=[pltpu.VMEM((len(pieces) * rows, n), BF16)],
        compiler_params=params(20),
        cost_estimate=COST,
        name="last_product",
    )(in_vmem(a), in_vmem(acc), *pieces)


def swap(x, axis, mask):
    return lax.ppermute(x, axis, [(i, i ^ mask) for i in range(lax.axis_size(axis))])


def gather_chips(x):
    n = lax.axis_size("vocab")
    if n > 8:
        lines = [[2 * z + c for z in range(n // 2)] for c in range(2)]
        everything = lax.all_gather(x, "vocab", axis=0, axis_index_groups=lines)
        return [everything[z] for z in range(n // 2)]
    return [x] + [swap(x, "vocab", r) for r in range(2, n, 2)]


def butterfly(tile):
    n = lax.axis_size("vocab")
    tiles, masks = [tile], [1 << k for k in range(1, n.bit_length() - 1)] + [1]
    for mask in masks:
        tile = merge_stats(tiles) if len(tiles) > 1 else tile
        tiles = [tile, swap(tile, "vocab", mask)]
    return tiles


def exchange_tok(x):
    return lax.all_to_all(x, "tok", split_axis=0, concat_axis=0, tiled=True)


def plus(a, b):
    return (a.astype(F32) + b.astype(F32)).astype(BF16)


def exchange_tok(x):
    return lax.all_to_all(x, "tok", split_axis=0, concat_axis=0, tiled=True)


def send(x, hops):
    return lax.ppermute(x, "vocab", [(2 * a + c, 2 * b + c) for a, b in hops for c in range(2)])


def local(teacher_logits, hidden, new_head, labels, map_target, map_weight):
    rows = teacher_logits.shape[0]
    block = map_weight.shape[2]
    n_tok = lax.axis_size("tok")
    n_vocab = lax.axis_size("vocab")
    n_z = n_vocab // 2
    new_cols = new_head.shape[1]
    per = new_cols // block
    tok = lax.axis_index("tok")
    vocab = lax.axis_index("vocab")
    spot = jnp.stack([vocab % 2, vocab // 2]).astype(jnp.int32)
    slots = n_tok * per
    in_line = n_z == 4

    owner = map_target // per
    owner_vocab = owner % n_vocab
    owner_z = owner_vocab // 2
    if in_line:
        z = vocab // 2
        outer = (owner_z == 0) | (owner_z == n_z - 1)
        near_place = jnp.where(owner_z == z, 3, 2)
        place = jnp.where((owner_z // 2) == (z // 2), near_place, jnp.where(outer, 0, 1))
    else:
        place = owner_z
    slot = (owner // n_vocab) * per + map_target % per
    code = (((owner_vocab % 2) * n_z + place) * SLOT_BASE + slot).astype(jnp.int32).reshape(-1)

    peer_logits = swap(teacher_logits, "vocab", 1)
    peer_code = swap(code, "vocab", 1)
    peer_weight = swap(map_weight, "vocab", 1)
    totals = butterfly(teacher_stats(teacher_logits))
    lists = plan(code, peer_code, 2 * n_z)
    probs = teacher_probs(teacher_logits, peer_logits, totals)

    half = lax.dynamic_slice_in_dim(hidden, spot[0] * (rows // 2), rows // 2)
    if in_line:
        inward, across, beyond = [(0, 1), (3, 2)], [(1, 2), (2, 1)], [(1, 3), (2, 0)]
        far_outer, mass_a = chip_sums(spot, lists, probs, map_weight, peer_weight, 0, 1, 1, slots)
        first = send(far_outer, inward)
        half, probs, mass_a = lax.optimization_barrier((half, probs, mass_a))
        near = [swap(half, "tok", r) for r in range(1, n_tok)]
        far_inner, beside, own, mass_b = chip_sums(
            spot, lists, probs, map_weight, peer_weight, 1, 3, 1, slots
        )
        second = send(far_inner, inward)
        first, mass = lax.optimization_barrier((first, mass_a + mass_b))
        merged = plus(far_outer, first)
        arrived = send(merged, beyond)
        *near, merged = lax.optimization_barrier((*near, merged))
    else:
        sums, mass = chip_sums(spot, lists, probs, map_weight, peer_weight, 0, 1, n_z, slots)
        lines = [[2 * z + c for z in range(n_z)] for c in range(2)]
        sums = lax.all_to_all(
            sums.reshape(n_z, slots, rows, block),
            "vocab",
            split_axis=0,
            concat_axis=0,
            axis_index_groups=lines,
            tiled=True,
        )
        sums = [sums]
        near = [swap(half, "tok", r) for r in range(1, n_tok)]

    far = [swap(x, "vocab", 1) for x in near]
    where = jnp.stack([vocab % 2, tok]).astype(jnp.int32)
    logits = student_logits(where, mass, hidden, near, far, new_head)
    base = (jnp.arange(n_tok, dtype=jnp.int32) * n_vocab + vocab) * new_cols
    label_column = lax.dynamic_slice_in_dim(labels, tok * rows, rows).reshape(rows, 1)
    scores = exchange_tok(logits)
    if in_line:
        second, arrived, logits = lax.optimization_barrier((second, arrived, logits))
        merged_inner = plus(far_inner, second)
        crossed = send(merged_inner, across)
        waited, merged_inner = lax.optimization_barrier((beside, merged_inner))
        third = swap(waited, "vocab", 2)
        where, merged_inner = lax.optimization_barrier((where, merged_inner))
        turned = turned_rows(where, hidden, near[-1:] + near[:-1], far[-1:] + far[:-1])
        scores, merged_inner, turned = lax.optimization_barrier((scores, merged_inner, turned))
        sums = [x[None] for x in (own, third, crossed, arrived)]
    else:
        turned = turned_rows(where, hidden, near[-1:] + near[:-1], far[-1:] + far[:-1])
    student = student_stats(base, label_column, mass, scores)
    student = merge_stats([student, swap(student, "vocab", 1)])
    stats = gather_chips(student)

    group = tok.astype(jnp.int32).reshape(1)
    columns, base_loss = token_totals(stats)
    grad_args = (group, base, label_column, columns, sums, scores)
    far_group, inner = grad_logits(*grad_args, (3,))
    far_group = swap(far_group, "tok", 3)
    beside_x, beside_y, here, inner_b = grad_logits(*grad_args, (1, 2, 0))
    beside_x, beside_y = swap(beside_x, "tok", 1), swap(beside_y, "tok", 2)
    inner = inner + inner_b
    acc, middle = first_product(turned, [here, far_group])
    head_grad, end = last_product(turned, acc, [beside_x, beside_y])
    mask = 1
    while mask < n_vocab:
        inner = inner + swap(inner, "vocab", mask)
        if mask == 2:
            inner = inner + middle
        mask *= 2
    return ((base_loss - inner + end).reshape(rows), head_grad)


def solution(mesh):
    return jax.shard_map(
        local,
        mesh=mesh,
        in_specs=(
            P("tok", "vocab"),
            P("tok", None),
            P(None, ("tok", "vocab")),
            P(),
            P("vocab", None),
            P("vocab", None, None, None),
        ),
        out_specs=(P("tok"), P(None, ("tok", "vocab"))),
        check_vma=False,
    )
```
